32 devices in a mesh: cls: 8 (over y, x, core), prt: 4 (over z).
Axes of the slice: x: 2, y: 2, z: 4, core: 2. Of those that a mesh axis runs over, the one named last changes fastest.
Arguments:
- particles: bfloat16 [512, 128, 512], P(('cls', 'prt')), may hold values from -20100 to 20100
- references: bfloat16 [512, 128, 512], P('cls'), may hold values from -6 to 6
- owner_groups: int32 [512, 4], P(('cls', 'prt')), may hold values from 0 to 7, all different within a row; in each aligned block of 16 rows (0 to 15, 16 to 31, ...) at most 16 rows name the same one
- class_order: int32 [512, 4, 64], P(('cls', 'prt')), may hold values from 0 to 63, each once within a row
Outputs:
- class_sums: float32 [512, 128, 512], P('cls', 'prt')
- class_weights: float32 [512], P('cls')
- log_norm: float32 [512], P(('cls', 'prt'))
The draws below stay inside these ranges and needn't reach their ends.
Inputs may be any that keep to these rules, and one draw needn't show every extreme that they name: `owner_groups`: each row names 4 different groups. Among the 16 particles of one device, no group is named by more than 16 rows, a bound that some block reaches. `class_order`: each row along the last dimension is a permutation.
All inputs are finite; a program needn't handle non-finite values.
Results may differ from the reference program's by a relative error of at most 0.0029.
Values may be sent and summed in bfloat16 or wider, within the bound.
No kernel may reach another device: no remote copies, remote signals or barrier semaphores. Data moves between devices by JAX's collectives and lax.ppermute only.
A program may use at most 128 MiB of HBM per device.

```python
import math
import jax
import jax.numpy as jnp
import numpy as np
from jax import lax

CYCLES = 128
HARM = 256
CLASSES = 512
ROTS = 36
OWN_TOP = 4
CAND_OWN = 4
PART_DEV = 16
CLS_DEV = 64
CAP = 16
PARTICLES = 512
N_CLS = 8


def draw_particles(key, part):
    base = jnp.clip(jax.random.normal(key, (PARTICLES, CYCLES, 2 * HARM), jnp.float32), -6.0, 6.0)
    return base.astype(jnp.bfloat16)


def draw_references(key, part):
    keys = jax.random.split(jax.random.fold_in(key, 31), 4)
    level = jnp.exp(jax.random.uniform(keys[0], (CYCLES,), jnp.float32, -0.3, 0.3))
    level = level / jnp.sqrt(jnp.mean(level * level))
    base = jnp.clip(jax.random.normal(keys[3], (CLASSES, CYCLES, 2 * HARM), jnp.float32), -4.0, 4.0)
    return (base * level[None, :, None]).astype(jnp.bfloat16)


def assign_block(key, own, number, rows, count, top, reach, slope):
    sequence = jax.random.permutation(key, count)
    packed, common = load_shares(count, rows * top, reach, slope, True), load_shares(count, rows * top, reach, slope, False)
    places = jnp.arange(count)

    def named(lengths, rotation):
        used = int((lengths > 0).sum())
        fixed = max(1, used // 4)
        moved = fixed + (places - fixed + rotation * (used - fixed)) % max(1, count - fixed)
        return jnp.zeros((count,), jnp.int32).at[sequence[jnp.where(places < fixed, places, moved)]].set(jnp.asarray(lengths, jnp.int32))

    lengths = jnp.where(number % 4 == 0, named(packed, number // 4), named(common, number - number // 4 - 1))
    mixed = jax.random.permutation(jax.random.fold_in(own, 3), count)
    source_of, taker = mixed[0:count // 2 * 2:2], mixed[1:count // 2 * 2:2]
    room = jnp.minimum(lengths[source_of] - 1, reach - lengths[taker]) // 2
    room = jnp.where((source_of == sequence[0]) | (taker == sequence[0]) | (lengths[taker] == 0), 0, jnp.maximum(room, 0))
    moved = jax.random.randint(jax.random.fold_in(own, 4), (count // 2,), 0, 1 << 20) % (room + 1)
    lengths = lengths.at[source_of].add(-moved).at[taker].add(moved)
    items = jnp.searchsorted(jnp.cumsum(lengths), jnp.arange(rows * top), side="right").astype(jnp.int32)
    table = items.reshape(top, rows).T
    table = table[jax.random.permutation(jax.random.fold_in(own, 1), rows)]
    rotation = jax.random.randint(jax.random.fold_in(own, 2), (rows, 1), 0, top)
    return jnp.take_along_axis(table, (jnp.arange(top)[None, :] + rotation) % top, axis=1)


def load_shares(count, total, limit, slope, full):
    weights = [(1 << 20) // math.isqrt(standing ** slope) + 1 for standing in range(1, count + 1)]
    largest = limit if full else min(limit, max(-(-total // count), total * weights[0] // sum(weights)))
    least = 1 if total - largest >= count - 1 else 0
    given, surplus = [largest] + [least] * (count - 1), total - largest - least * (count - 1)
    while surplus > 0:
        free = [i for i in range(1, count) if given[i] < largest] or [i for i in range(1, count) if given[i] < limit]
        mass, left = sum([weights[i] for i in free]), surplus
        for i in free:
            more = min(limit - given[i], max(1, left * weights[i] // mass), surplus)
            given[i] = given[i] + more
            surplus = surplus - more
    return np.array(given)


def setup_inputs(seed: int = 0) -> dict:
    streams_of = jax.random.split(jax.random.key(seed), 5)
    particles = draw_particles(jax.random.fold_in(streams_of[4], 71), 0)
    references = draw_references(jax.random.fold_in(streams_of[4], 71), 0)
    owner_groups_keys = jax.random.split(jax.random.fold_in(streams_of[2], 1), PARTICLES // PART_DEV)
    owner_groups_turns = jax.random.permutation(jax.random.fold_in(streams_of[2], 3), PARTICLES // PART_DEV)
    owner_groups = jax.vmap(lambda own, number: assign_block(jax.random.fold_in(streams_of[2], 2), own, number, PART_DEV, N_CLS, OWN_TOP, CAP, 2))(owner_groups_keys, owner_groups_turns).reshape((PARTICLES, OWN_TOP))
    class_order = jax.vmap(lambda own: jax.random.permutation(own, CLS_DEV))(jax.random.split(streams_of[3], PARTICLES * OWN_TOP)).reshape((PARTICLES, OWN_TOP, CLS_DEV)).astype(jnp.int32)
    return {"particles": particles, "references": references, "owner_groups": owner_groups, "class_order": class_order}


def reference(particles, references, owner_groups, class_order):
    groups = CLASSES // N_CLS
    total_cand = OWN_TOP * CAND_OWN
    candidates = (owner_groups[:, :, None] * groups + class_order[:, :, :CAND_OWN]).reshape(PARTICLES, total_cand).astype(jnp.int32)
    harmonic = jnp.arange(HARM, dtype=jnp.float32)
    angles = 2.0 * math.pi * jnp.arange(ROTS, dtype=jnp.float32) / ROTS
    phase = harmonic[:, None] * angles[None, :]
    forward = jnp.concatenate([jnp.cos(phase), jnp.sin(phase)], 0)
    backward = jnp.concatenate([jnp.cos(phase), -jnp.sin(phase)], 0).T
    scale = 2.0 / math.sqrt(CYCLES * 2 * HARM)
    norms = lax.optimization_barrier(jnp.sum(jnp.square(references.astype(jnp.float32)), axis=(1, 2)))
    block = 16
    steps = PARTICLES // block
    part_blocks = particles.reshape(steps, block, CYCLES, 2 * HARM)
    cand_blocks = candidates.reshape(steps, block, total_cand)

    def one_block(carry, inputs):
        sums, weights = carry
        span_part, span_cls = inputs
        chosen = references[span_cls].astype(jnp.float32)
        lanes = span_part.astype(jnp.float32)
        p_re = lanes[..., :HARM]
        p_im = lanes[..., HARM:]
        r_re = chosen[..., :HARM]
        r_im = chosen[..., HARM:]
        x_re = jnp.einsum('brm,bjrm->bjm', p_re, r_re) + jnp.einsum('brm,bjrm->bjm', p_im, r_im)
        x_im = jnp.einsum('brm,bjrm->bjm', p_im, r_re) - jnp.einsum('brm,bjrm->bjm', p_re, r_im)
        cross = jnp.concatenate([x_re, x_im], -1)
        corr = jnp.dot(cross.reshape(-1, 2 * HARM), forward, precision=lax.Precision.HIGHEST).reshape(block, total_cand, ROTS)
        score = (corr - 0.5 * norms[span_cls][:, :, None]) * scale
        top = lax.optimization_barrier(jnp.max(score, axis=(1, 2)))
        lse = top + jnp.log(lax.optimization_barrier(jnp.sum(jnp.exp(score - top[:, None, None]), axis=(1, 2))))
        weight = jnp.exp(score - lse[:, None, None])
        mixed = jnp.dot(weight.reshape(-1, ROTS), backward, precision=lax.Precision.HIGHEST).astype(jnp.bfloat16)
        mixed = lax.optimization_barrier(mixed).astype(jnp.float32).reshape(block, total_cand, 2 * HARM)
        y_re = mixed[:, :, None, :HARM]
        y_im = mixed[:, :, None, HARM:]
        s_re = p_re[:, None] * y_re - p_im[:, None] * y_im
        s_im = p_re[:, None] * y_im + p_im[:, None] * y_re
        added = jnp.concatenate([s_re, s_im], -1).reshape(block * total_cand, CYCLES, 2 * HARM)
        flat_cls = span_cls.reshape(-1)
        sums = sums.at[flat_cls].add(added)
        weights = weights.at[flat_cls].add(lax.optimization_barrier(jnp.sum(weight, axis=2)).reshape(-1))
        return ((sums, weights), lse)
    start = (jnp.zeros((CLASSES, CYCLES, 2 * HARM), jnp.float32), jnp.zeros((CLASSES,), jnp.float32))
    (sums, weights), norm_blocks = lax.scan(one_block, start, (part_blocks, cand_blocks))
    return (sums, weights, norm_blocks.reshape(PARTICLES))
```

```python
import functools
import math

import jax
import jax.numpy as jnp
import numpy as np
from jax import lax
from jax.experimental import pallas as pl
from jax.experimental.pallas import tpu as pltpu
from jax.sharding import PartitionSpec as P

CYCLES = 128
HARM = 256
ROTS = 36
OWN_TOP = 4
CAND_OWN = 4


lowest = -1e30


def spectral_tables():
    harmonic = jnp.arange(HARM, dtype=jnp.float32)
    angles = 2.0 * math.pi * jnp.arange(ROTS, dtype=jnp.float32) / ROTS
    phase = harmonic[:, None] * angles[None, :]
    forward = jnp.concatenate([jnp.cos(phase), jnp.sin(phase)], 0)
    backward = jnp.concatenate([jnp.cos(phase), -jnp.sin(phase)], 0).T
    return (forward, backward)


def class_accumulate(lanes, mixed):
    l_re = lanes[..., :HARM]
    l_im = lanes[..., HARM:]
    y_re = mixed[..., :HARM]
    y_im = mixed[..., HARM:]
    s_re = jnp.einsum("lrm,lcm->crm", l_re, y_re, preferred_element_type=jnp.float32) - jnp.einsum(
        "lrm,lcm->crm", l_im, y_im, preferred_element_type=jnp.float32
    )
    s_im = jnp.einsum("lrm,lcm->crm", l_re, y_im, preferred_element_type=jnp.float32) + jnp.einsum(
        "lrm,lcm->crm", l_im, y_re, preferred_element_type=jnp.float32
    )
    return jnp.concatenate([s_re, s_im], -1)


def dispatch_device(particles, references, owner_groups, class_order):
    n_cls = lax.axis_size("cls")
    count = particles.shape[0]
    groups = references.shape[0]
    cap = max(2, 2 * count * OWN_TOP // n_cls)
    slots = n_cls * cap
    width = 2 * HARM
    flat_owner = owner_groups.reshape(-1)
    owner_hot = (flat_owner[:, None] == jnp.arange(n_cls, dtype=jnp.int32)[None, :]).astype(
        jnp.int32
    )
    before = jnp.cumsum(owner_hot, axis=0) - owner_hot
    rank = jnp.sum(before * owner_hot, axis=1)
    slot_of = flat_owner * cap + rank
    match = slot_of[None, :] == jnp.arange(slots, dtype=jnp.int32)[:, None]
    member = jnp.any(match.reshape(slots, count, OWN_TOP), axis=2)
    filled = jnp.any(member, axis=1)
    dispatch = member.astype(jnp.bfloat16)
    outgoing = jnp.dot(
        dispatch, particles.reshape(count, CYCLES * width), preferred_element_type=jnp.float32
    )
    outgoing = outgoing.astype(jnp.bfloat16).reshape(n_cls, cap, CYCLES, width)
    match_int = match.astype(jnp.int32)
    picks = class_order[:, :, :CAND_OWN].reshape(count * OWN_TOP, CAND_OWN)
    slot_cand = jnp.where(filled[:, None], jnp.dot(match_int, picks), -1)
    owner_rows = jnp.repeat(jnp.arange(count, dtype=jnp.int32), OWN_TOP)
    slot_pid = jnp.where(filled, jnp.dot(match_int, owner_rows), -1)
    labels_out = jnp.concatenate([slot_cand, slot_pid[:, None]], 1).reshape(
        n_cls, cap, CAND_OWN + 1
    )
    arrived, labels = (
        lax.all_to_all(outgoing, "cls", split_axis=0, concat_axis=0, tiled=True),
        lax.all_to_all(labels_out, "cls", split_axis=0, concat_axis=0, tiled=True),
    )
    lanes = arrived.reshape(slots, CYCLES, width)
    labels = labels.reshape(slots, CAND_OWN + 1)
    forward, backward = spectral_tables()
    scale = 2.0 / math.sqrt(CYCLES * width)
    norms = jnp.sum(jnp.square(references.astype(jnp.float32)), axis=(1, 2))
    l_re = lanes[..., :HARM]
    l_im = lanes[..., HARM:]
    r_re = references[..., :HARM]
    r_im = references[..., HARM:]
    x_re = jnp.einsum("lrm,crm->lcm", l_re, r_re, preferred_element_type=jnp.float32) + jnp.einsum(
        "lrm,crm->lcm", l_im, r_im, preferred_element_type=jnp.float32
    )
    x_im = jnp.einsum("lrm,crm->lcm", l_im, r_re, preferred_element_type=jnp.float32) - jnp.einsum(
        "lrm,crm->lcm", l_re, r_im, preferred_element_type=jnp.float32
    )
    cross = jnp.concatenate([x_re, x_im], -1)
    corr = jnp.dot(
        cross.reshape(slots * groups, width), forward, precision=lax.Precision.HIGHEST
    ).reshape(slots, groups, ROTS)
    score = (corr - 0.5 * norms[None, :, None]) * scale
    candidate = jnp.any(
        labels[:, :CAND_OWN, None] == jnp.arange(groups, dtype=jnp.int32)[None, None, :], axis=1
    )
    part_max = jnp.max(jnp.where(candidate[:, :, None], score, lowest), axis=(1, 2))
    part_sum = jnp.sum(
        jnp.where(candidate[:, :, None], jnp.exp(score - part_max[:, None, None]), 0.0), axis=(1, 2)
    )
    sender_ids = labels[:, CAND_OWN].astype(jnp.float32)
    table_max, table_sum, table_ids = (
        lax.all_gather(part_max.reshape(1, n_cls, cap), "cls", axis=0, tiled=True),
        lax.all_gather(part_sum.reshape(1, n_cls, cap), "cls", axis=0, tiled=True),
        lax.all_gather(sender_ids.reshape(1, n_cls, cap), "cls", axis=0, tiled=True),
    )
    local_ids = jnp.arange(count, dtype=jnp.float32)
    hit = table_ids[..., None] == local_ids
    top = jnp.max(jnp.where(hit, table_max[..., None], lowest), axis=(0, 2))
    total = jnp.sum(
        jnp.where(
            hit, table_sum[..., None] * jnp.exp(table_max[..., None] - top[None, :, None, :]), 0.0
        ),
        axis=(0, 2),
    )
    table_norm = top + jnp.log(total)
    slot_ids = labels[:, CAND_OWN].reshape(n_cls, cap)
    slot_norm = jnp.sum(
        jnp.where(
            slot_ids[..., None] == jnp.arange(count, dtype=jnp.int32), table_norm[:, None, :], 0.0
        ),
        axis=2,
    ).reshape(slots)
    own_norm = lax.dynamic_index_in_dim(table_norm, lax.axis_index("cls"), 0, keepdims=False)
    weight = jnp.where(candidate[:, :, None], jnp.exp(score - slot_norm[:, None, None]), 0.0)
    mixed = (
        jnp.dot(weight.reshape(slots * groups, ROTS), backward, precision=lax.Precision.HIGHEST)
        .astype(jnp.bfloat16)
        .reshape(slots, groups, width)
    )
    class_weights = lax.psum(jnp.sum(weight, axis=(0, 2)), "prt")
    partial_sums = class_accumulate(lanes, mixed)
    class_sums = lax.psum_scatter(partial_sums, "prt", scatter_dimension=1, tiled=True)
    return (class_sums, class_weights, own_norm)


LANES = 128


def harmonic_plan():
    half = ROTS // 2
    turns = HARM // ROTS
    tail = HARM - turns * ROTS
    chunk_of = np.zeros(HARM, np.int32)
    side_of = np.zeros(HARM, np.int32)
    for m in range(HARM):
        turn, rest = divmod(m, ROTS)
        if turn == turns:
            chunk_of[m] = half * turns + rest // 2
            side_of[m] = rest % 2
        elif rest < half:
            chunk_of[m] = rest * turns + turn
        else:
            chunk_of[m] = ((ROTS - rest) % half) * turns + turn
            side_of[m] = 1
    return half, turns, tail, chunk_of, side_of


HALF, TURNS, TAIL, CHUNK_OF, SIDE_OF = harmonic_plan()
BODY = HALF * TURNS
CHUNKS = BODY + TAIL // 2
EXTRA = TAIL // 2 + 1
COEF = 2 * HALF * CAND_OWN


def selector():
    return (np.arange(CHUNKS)[:, None] == CHUNK_OF[None, :]).astype(np.float32)


def side_masks():
    return np.stack([SIDE_OF == 0, SIDE_OF == 1]).astype(np.float32)


def unselector():
    sel = selector()
    return np.concatenate([sel * (SIDE_OF == 0), sel * (SIDE_OF == 1)], 0)


def rotation_table():
    table = np.zeros((HALF, 2, CAND_OWN, ROTS, CAND_OWN))
    angle = 2.0 * np.pi * np.arange(ROTS) / ROTS
    for g in range(HALF):
        first = np.cos(g * angle)
        second = np.cos(HALF * angle) if g == 0 else np.sin(g * angle)
        for q in range(CAND_OWN):
            table[g, 0, q, :, q] = first
            table[g, 1, q, :, q] = second
    return table.reshape(COEF, ROTS * CAND_OWN).astype(np.float32)


def nt_dot(a, b):
    return lax.dot_general(a, b, (((1,), (1,)), ((), ())), preferred_element_type=jnp.float32)


def masked_stack(piece, masks):
    parts = []
    for s in range(2):
        for b in range(2):
            parts.append(piece[:, s * HARM : (s + 1) * HARM] * masks[b : b + 1])
    return jnp.concatenate(parts, 0)


def particle_body(x_ref, owner_ref, pick_ref, sel_ref, mask_ref, out_ref, scr):
    count, cycles, _ = x_ref.shape
    n_prt = out_ref.shape[0]
    span = cycles // n_prt
    masks = mask_ref[...]

    def one(n, carry):
        x = x_ref[n]
        w = jnp.concatenate(
            [masked_stack(x[p * span : (p + 1) * span], masks) for p in range(n_prt)], 0
        )
        y = nt_dot(sel_ref[...], w)
        for p in range(n_prt):
            scr[p, pl.ds(pl.multiple_of(n * CHUNKS, CHUNKS), CHUNKS), :] = y[
                :, p * LANES : (p + 1) * LANES
            ]
        return carry

    lax.fori_loop(0, count, one, 0)

    def two(c, carry):
        for p in range(n_prt):
            out_ref[p, c] = scr[p, pl.ds(c, count, stride=CHUNKS), :].astype(jnp.bfloat16)
        return carry

    lax.fori_loop(0, CHUNKS, two, 0)
    lane = lax.broadcasted_iota(jnp.int32, (count, LANES), 1)
    label = jnp.full((count, LANES), -1, jnp.int32)
    for t in range(OWN_TOP):
        mine = (lane // CAND_OWN) == owner_ref[:, t : t + 1]
        for q in range(CAND_OWN):
            at = t * CAND_OWN + q
            label = jnp.where(
                mine & (lane % CAND_OWN == q), pick_ref[:, at : at + 1], label
            )
    label = label.astype(jnp.float32).astype(jnp.bfloat16)
    for p in range(n_prt):
        out_ref[p, CHUNKS] = label


def arrange_particles(particles, owner, picks, n_prt, sel, masks):
    count = particles.shape[0]
    return pl.pallas_call(
        particle_body,
        out_shape=jax.ShapeDtypeStruct((n_prt, CHUNKS + 1, count, LANES), jnp.bfloat16),
        scratch_shapes=[pltpu.VMEM((n_prt, count * CHUNKS, LANES), jnp.float32)],
        compiler_params=pltpu.CompilerParams(vmem_limit_bytes=32 << 20),
        cost_estimate=pl.CostEstimate(
            flops=particles.size * 2 * CHUNKS, bytes_accessed=particles.size * 4, transcendentals=0
        ),
        name="arrange_particles",
    )(particles, owner, picks, sel, masks)


def reference_body(at_ref, x_ref, sel_ref, mask_ref, out_ref, scr):
    rows = x_ref.shape[0]
    masks = mask_ref[...]
    step = 4

    def one(n, carry):
        w = jnp.concatenate([masked_stack(x_ref[n * step + i], masks) for i in range(step)], 0)
        y = nt_dot(sel_ref[...], w)
        for i in range(step):
            scr[pl.ds(pl.multiple_of((n * step + i) * CHUNKS, CHUNKS), CHUNKS), :] = y[
                :, i * LANES : (i + 1) * LANES
            ]
        return carry

    lax.fori_loop(0, rows // step, one, 0)

    def two(c, carry):
        out_ref[c] = scr[pl.ds(c, rows, stride=CHUNKS), :].astype(jnp.bfloat16)
        return carry

    lax.fori_loop(0, CHUNKS, two, 0)


def arrange_references(references, prt, n_prt, sel, masks):
    groups, cycles, width = references.shape
    span = cycles // n_prt
    block = 16
    return pl.pallas_call(
        reference_body,
        grid_spec=pltpu.PrefetchScalarGridSpec(
            num_scalar_prefetch=1,
            grid=(groups // block,),
            in_specs=[
                pl.BlockSpec((block, span, width), lambda i, at: (i, at[0], 0)),
                pl.BlockSpec(sel.shape, lambda i, at: (0, 0)),
                pl.BlockSpec(masks.shape, lambda i, at: (0, 0)),
            ],
            out_specs=pl.BlockSpec((CHUNKS, block, LANES), lambda i, at: (0, i, 0)),
            scratch_shapes=[pltpu.VMEM((block * CHUNKS, LANES), jnp.float32)],
        ),
        out_shape=jax.ShapeDtypeStruct((CHUNKS, groups, LANES), jnp.bfloat16),
        compiler_params=pltpu.CompilerParams(vmem_limit_bytes=32 << 20),
        cost_estimate=pl.CostEstimate(
            flops=groups * span * width * 2 * CHUNKS,
            bytes_accessed=groups * span * width * 4,
            transcendentals=0,
        ),
        name="arrange_references",
    )(prt, references, sel, masks)


def lane_signs():
    lane = lax.broadcasted_iota(jnp.int32, (1, LANES), 1)
    quarter = LANES // 4
    imag = lane >= 2 * quarter
    odd = (lane // quarter) % 2 == 1
    return imag, odd


def lanes_of(ref, first, number):
    parts = []
    for i in range(first, first + number):
        part = ref[:, i]
        parts.append(part.reshape(part.shape[0] * part.shape[1], LANES))
    return jnp.concatenate(parts, 1) if number > 1 else parts[0]


def hot_masks(cand, groups):
    rows = lax.broadcasted_iota(jnp.int32, (groups, cand.shape[1]), 0).astype(jnp.float32)
    return [rows == cand[q : q + 1] for q in range(CAND_OWN)]


def cross_body(at_ref, p_ref, pt_ref, q_ref, qt_ref, coef_ref, cand_ref, acc, norm):
    g = pl.program_id(0)
    groups = q_ref.shape[1]
    imag, odd = lane_signs()
    quarter = LANES // 4
    sign = jnp.where(imag == odd, -1.0, 1.0)

    @pl.when(g == 0)
    def _():
        label = lanes_of(pt_ref, TAIL // 2, 1).astype(jnp.float32).T
        row = lax.broadcasted_iota(jnp.int32, label.shape, 0)
        base = at_ref[0] * CAND_OWN
        for q in range(CAND_OWN):
            cand_ref[q : q + 1, :] = jnp.sum(
                jnp.where(row == base + q, label, 0.0), axis=0, keepdims=True
            )
        cand_ref[CAND_OWN:, :] = jnp.full(
            (cand_ref.shape[0] - CAND_OWN, cand_ref.shape[1]), -1.0, jnp.float32
        )
        total = jnp.zeros((groups, LANES), jnp.float32)
        for i in range(TAIL // 2):
            total += jnp.square(qt_ref[i].astype(jnp.float32))
        norm[...] = total

    first, second = [], []
    total = norm[...]
    for i in range(TURNS):
        q = q_ref[i].astype(jnp.float32)
        total += jnp.square(q)
        turned = pltpu.roll(q, LANES // 2, 1) * sign
        first.append(jnp.where((g == 0) & odd, 0.0, q))
        second.append(jnp.where(g == 0, jnp.where(odd, q, 0.0), turned))
    norm[...] = total
    weights = jnp.concatenate(
        [jnp.concatenate(first, 1), jnp.concatenate(second, 1)], 0
    ).astype(jnp.bfloat16)
    acc[...] = nt_dot(weights, lanes_of(p_ref, 0, TURNS))

    for i in range(TAIL):

        @pl.when(g == i)
        def _():
            q = qt_ref[i // 2].astype(jnp.float32)
            keep = odd if i % 2 else ~odd
            a = jnp.where(keep, q, 0.0)
            b = jnp.where(keep, pltpu.roll(q, LANES // 2, 1) * jnp.where(imag, 1.0, -1.0), 0.0)
            if i == 0:
                b = jnp.zeros_like(b)
            w = jnp.concatenate([a, b], 0).astype(jnp.bfloat16)
            acc[...] += nt_dot(w, lanes_of(pt_ref, i // 2, 1))

    hot = hot_masks(cand_ref[...], groups)
    rows = []
    for ab in range(2):
        part = acc[ab * groups : (ab + 1) * groups, :]
        for q in range(CAND_OWN):
            rows.append(jnp.sum(jnp.where(hot[q], part, 0.0), axis=0, keepdims=True))
    block = 2 * CAND_OWN
    coef_ref[pl.ds(pl.multiple_of(g * block, block), block), :] = jnp.concatenate(rows, 0)

    @pl.when(g == HALF - 1)
    def _():
        half_norm = 0.5 * jnp.sum(norm[...], axis=1, keepdims=True)
        for q in range(CAND_OWN):
            coef_ref[q : q + 1, :] -= jnp.sum(
                jnp.where(hot[q], half_norm, 0.0), axis=0, keepdims=True
            )


def cross_coefficients(gathered, arranged, cls):
    sources, _, count, _ = gathered.shape
    groups = arranged.shape[1]
    total = sources * count
    half_tail = TAIL // 2
    return pl.pallas_call(
        cross_body,
        grid_spec=pltpu.PrefetchScalarGridSpec(
            num_scalar_prefetch=1,
            grid=(HALF,),
            in_specs=[
                pl.BlockSpec((sources, TURNS, count, LANES), lambda g, at: (0, g, 0, 0)),
                pl.BlockSpec(
                    (sources, EXTRA, count, LANES), lambda g, at: (0, BODY // EXTRA, 0, 0)
                ),
                pl.BlockSpec((TURNS, groups, LANES), lambda g, at: (g, 0, 0)),
                pl.BlockSpec((half_tail, groups, LANES), lambda g, at: (BODY // half_tail, 0, 0)),
            ],
            out_specs=[
                pl.BlockSpec((COEF, total), lambda g, at: (0, 0)),
                pl.BlockSpec((2 * CAND_OWN, total), lambda g, at: (0, 0)),
            ],
            scratch_shapes=[
                pltpu.VMEM((2 * groups, total), jnp.float32),
                pltpu.VMEM((groups, LANES), jnp.float32),
            ],
        ),
        out_shape=[
            jax.ShapeDtypeStruct((COEF, total), jnp.float32),
            jax.ShapeDtypeStruct((2 * CAND_OWN, total), jnp.float32),
        ],
        compiler_params=pltpu.CompilerParams(vmem_limit_bytes=48 << 20),
        cost_estimate=pl.CostEstimate(
            flops=4 * gathered.size * groups, bytes_accessed=2 * gathered.size, transcendentals=0
        ),
        name="cross_coefficients",
    )(cls, gathered, gathered, arranged, arranged)


def score_body(coef_ref, cand_ref, table_ref, score_ref, stat_ref, *, scale):
    corr = lax.dot_general(
        table_ref[...],
        coef_ref[...],
        (((0,), (0,)), ((), ())),
        precision=lax.Precision.HIGHEST,
        preferred_element_type=jnp.float32,
    )
    score = jnp.where(cand_ref[0:1, :] >= 0.0, corr * scale, lowest)
    top = jnp.max(score, axis=0, keepdims=True)
    total = jnp.sum(jnp.exp(score - top), axis=0, keepdims=True)
    score_ref[...] = score
    stat_ref[0:1, :] = top
    stat_ref[1:2, :] = jnp.where(cand_ref[0:1, :] >= 0.0, total, 0.0)


def scores(coef, cand, table, scale):
    total = coef.shape[1]
    return pl.pallas_call(
        functools.partial(score_body, scale=scale),
        out_shape=[
            jax.ShapeDtypeStruct((ROTS * CAND_OWN, total), jnp.float32),
            jax.ShapeDtypeStruct((2, total), jnp.float32),
        ],
        name="scores",
    )(coef, cand, table)


def sums_body(
    p_ref, pt_ref, score_ref, cand_ref, stat_ref, table_ref, back_ref,
    out_ref, weight_ref, norm_ref, mix, planes,
):
    i = pl.program_id(0)
    groups = weight_ref.shape[0]
    total = score_ref.shape[1]
    imag, odd = lane_signs()

    @pl.when(i == 0)
    def _():
        tops = [stat_ref[2 * j : 2 * j + 1, :] for j in range(stat_ref.shape[0] // 2)]
        top = functools.reduce(jnp.maximum, tops)
        summed = jnp.zeros_like(top)
        for j, other in enumerate(tops):
            summed += stat_ref[2 * j + 1 : 2 * j + 2, :] * jnp.exp(other - top)
        log_norm = top + jnp.log(summed)
        norm_ref[...] = log_norm
        weight = jnp.where(
            cand_ref[0:1, :] >= 0.0, jnp.exp(score_ref[...] - log_norm), 0.0
        )
        mixed = lax.dot_general(
            table_ref[...],
            weight,
            (((1,), (0,)), ((), ())),
            precision=lax.Precision.HIGHEST,
            preferred_element_type=jnp.float32,
        )
        hot = hot_masks(cand_ref[...], groups)
        summed = jnp.zeros((groups, total), jnp.float32)
        for q in range(CAND_OWN):
            summed += jnp.where(hot[q], mixed[q : q + 1], 0.0)
        weight_ref[...] = jnp.sum(summed, axis=1, keepdims=True)
        mix[...] = mixed

    @pl.when(i < HALF)
    def _():
        hot = hot_masks(cand_ref[...], groups)
        block = 2 * CAND_OWN
        mine = mix[pl.ds(pl.multiple_of(i * block, block), block), :]
        halves = []
        for ab in range(2):
            dense = jnp.zeros((groups, total), jnp.float32)
            for q in range(CAND_OWN):
                at = ab * CAND_OWN + q
                dense = jnp.where(hot[q], mine[at : at + 1], dense)
            halves.append(dense)
        weights = jnp.concatenate(halves, 0).astype(jnp.bfloat16)
        made = jnp.dot(
            weights, lanes_of(p_ref, 0, TURNS), preferred_element_type=jnp.float32
        )
        sign = jnp.where(imag == odd, 1.0, -1.0)
        for t in range(TURNS):
            g1 = made[:groups, t * LANES : (t + 1) * LANES]
            g2 = made[groups:, t * LANES : (t + 1) * LANES]
            value = jnp.where(
                i == 0, jnp.where(odd, g2, g1), g1 + sign * pltpu.roll(g2, LANES // 2, 1)
            )
            start = pl.multiple_of((i * TURNS + t) * groups, groups)
            planes[pl.ds(start, groups), :] = value

        for t in range(TAIL):

            @pl.when(i == t)
            def _():
                made = jnp.dot(
                    weights, lanes_of(pt_ref, t // 2, 1), preferred_element_type=jnp.float32
                )
                g1, g2 = made[:groups], made[groups:]
                value = g1
                if t > 0:
                    value = g1 + jnp.where(imag, -1.0, 1.0) * pltpu.roll(g2, LANES // 2, 1)
                rows = pl.ds((BODY + t // 2) * groups, groups)
                if t % 2:
                    value = jnp.where(odd, value, planes[rows, :])
                planes[rows, :] = value

    @pl.when(i >= HALF)
    def _():
        block, span, _ = out_ref.shape
        first = (i - HALF) * block
        back = back_ref[...]
        for c in range(block):
            turned = planes[pl.ds(first + c, CHUNKS, stride=groups), :].T
            parts = []
            for s in range(2):
                at = 2 * s * span
                parts.append(
                    jnp.concatenate([turned[at : at + span], turned[at + span : at + 2 * span]], 1)
                )
            value = jnp.concatenate(parts, 0)
            high = value.astype(jnp.bfloat16)
            low = (value - high.astype(jnp.float32)).astype(jnp.bfloat16)
            placed = jnp.dot(high, back, preferred_element_type=jnp.float32) + jnp.dot(
                low, back, preferred_element_type=jnp.float32
            )
            out_ref[c, :, :HARM] = placed[:span]
            out_ref[c, :, HARM:] = placed[span:]


def sums(gathered, score, cand, stats, table, back, groups, span):
    sources, _, count, _ = gathered.shape
    total = sources * count
    block = 8
    whole = lambda i: (0, 0)
    return pl.pallas_call(
        sums_body,
        grid=(HALF + groups // block,),
        in_specs=[
            pl.BlockSpec(
                (sources, TURNS, count, LANES), lambda i: (0, jnp.minimum(i, HALF - 1), 0, 0)
            ),
            pl.BlockSpec((sources, EXTRA, count, LANES), lambda i: (0, BODY // EXTRA, 0, 0)),
            pl.BlockSpec(score.shape, whole),
            pl.BlockSpec(cand.shape, whole),
            pl.BlockSpec(stats.shape, whole),
            pl.BlockSpec(table.shape, whole),
            pl.BlockSpec(back.shape, whole),
        ],
        out_specs=[
            pl.BlockSpec(
                (block, span, 2 * HARM), lambda i: (jnp.maximum(i - HALF, 0), 0, 0)
            ),
            pl.BlockSpec((groups, 1), whole),
            pl.BlockSpec((1, total), whole),
        ],
        out_shape=[
            jax.ShapeDtypeStruct((groups, span, 2 * HARM), jnp.float32),
            jax.ShapeDtypeStruct((groups, 1), jnp.float32),
            jax.ShapeDtypeStruct((1, total), jnp.float32),
        ],
        scratch_shapes=[
            pltpu.VMEM((COEF, total), jnp.float32),
            pltpu.VMEM((CHUNKS * groups, LANES), jnp.float32),
        ],
        compiler_params=pltpu.CompilerParams(vmem_limit_bytes=48 << 20),
        cost_estimate=pl.CostEstimate(
            flops=4 * gathered.size * groups,
            bytes_accessed=2 * gathered.size + 8 * groups * span * HARM,
            transcendentals=0,
        ),
        name="sums",
    )(gathered, gathered, score, cand, stats, table, back)


def spread(outgoing):
    arrived = lax.all_to_all(outgoing, "prt", split_axis=0, concat_axis=0, tiled=True)
    return lax.all_gather(arrived, "cls", axis=0, tiled=True)


def gather_device(particles, references, owner_groups, class_order):
    n_cls, n_prt = lax.axis_size("cls"), lax.axis_size("prt")
    cls, prt = lax.axis_index("cls"), lax.axis_index("prt")
    count, cycles, width = particles.shape
    groups = references.shape[0]
    span = cycles // n_prt
    sel = jnp.asarray(selector(), jnp.bfloat16)
    masks = jnp.asarray(side_masks(), jnp.bfloat16)
    back = jnp.asarray(unselector(), jnp.bfloat16)
    table = jnp.asarray(rotation_table())
    picks = class_order[:, :, :CAND_OWN].reshape(count, OWN_TOP * CAND_OWN)
    outgoing = arrange_particles(particles, owner_groups, picks, n_prt, sel, masks)
    gathered = spread(outgoing)
    arranged = arrange_references(references, prt.reshape(1).astype(jnp.int32), n_prt, sel, masks)
    coef, cand = cross_coefficients(gathered, arranged, cls.reshape(1).astype(jnp.int32))
    coef = lax.psum(coef, "prt")
    scale = 2.0 / math.sqrt(cycles * width)
    score, stat = scores(coef, cand, table, scale)
    stats = lax.all_gather(stat, "cls", axis=0, tiled=True)
    class_sums, class_weights, log_norm = sums(
        gathered, score, cand, stats, table, back, groups, span
    )
    own = lax.dynamic_slice(log_norm[0], ((cls * n_prt + prt) * count,), (count,))
    return class_sums, class_weights[:, 0], own


def per_device(particles, references, owner_groups, class_order):
    n_cls, n_prt = lax.axis_size("cls"), lax.axis_size("prt")
    count, cycles, _ = particles.shape
    groups = references.shape[0]
    cap = max(2, 2 * count * OWN_TOP // n_cls)
    fits = 4 * cycles == LANES * n_prt and n_cls * CAND_OWN <= LANES and groups % 16 == 0
    plan = gather_device if cap >= count and fits else dispatch_device
    return plan(particles, references, owner_groups, class_order)


def solution(mesh):
    in_specs = (
        P(("cls", "prt"), None, None),
        P("cls", None, None),
        P(("cls", "prt"), None),
        P(("cls", "prt"), None, None),
    )
    out_specs = (P("cls", "prt", None), P("cls"), P(("cls", "prt")))
    return jax.shard_map(
        per_device, mesh=mesh, in_specs=in_specs, out_specs=out_specs, check_vma=False
    )
```

```python
import functools
import math

import jax
import jax.numpy as jnp
import numpy as np
from jax import lax
from jax.experimental import pallas as pl
from jax.experimental.pallas import tpu as pltpu
from jax.sharding import PartitionSpec as P

CYCLES = 128
HARM = 256
ROTS = 36
OWN_TOP = 4
CAND_OWN = 4


lowest = -1e30


def spectral_tables():
    harmonic = jnp.arange(HARM, dtype=jnp.float32)
    angles = 2.0 * math.pi * jnp.arange(ROTS, dtype=jnp.float32) / ROTS
    phase = harmonic[:, None] * angles[None, :]
    forward = jnp.concatenate([jnp.cos(phase), jnp.sin(phase)], 0)
    backward = jnp.concatenate([jnp.cos(phase), -jnp.sin(phase)], 0).T
    return (forward, backward)


def class_accumulate(lanes, mixed):
    l_re = lanes[..., :HARM]
    l_im = lanes[..., HARM:]
    y_re = mixed[..., :HARM]
    y_im = mixed[..., HARM:]
    s_re = jnp.einsum("lrm,lcm->crm", l_re, y_re, preferred_element_type=jnp.float32) - jnp.einsum(
        "lrm,lcm->crm", l_im, y_im, preferred_element_type=jnp.float32
    )
    s_im = jnp.einsum("lrm,lcm->crm", l_re, y_im, preferred_element_type=jnp.float32) + jnp.einsum(
        "lrm,lcm->crm", l_im, y_re, preferred_element_type=jnp.float32
    )
    return jnp.concatenate([s_re, s_im], -1)


def dispatch_device(particles, references, owner_groups, class_order):
    n_cls = lax.axis_size("cls")
    count = particles.shape[0]
    groups = references.shape[0]
    cap = max(2, 2 * count * OWN_TOP // n_cls)
    slots = n_cls * cap
    width = 2 * HARM
    flat_owner = owner_groups.reshape(-1)
    owner_hot = (flat_owner[:, None] == jnp.arange(n_cls, dtype=jnp.int32)[None, :]).astype(
        jnp.int32
    )
    before = jnp.cumsum(owner_hot, axis=0) - owner_hot
    rank = jnp.sum(before * owner_hot, axis=1)
    slot_of = flat_owner * cap + rank
    match = slot_of[None, :] == jnp.arange(slots, dtype=jnp.int32)[:, None]
    member = jnp.any(match.reshape(slots, count, OWN_TOP), axis=2)
    filled = jnp.any(member, axis=1)
    dispatch = member.astype(jnp.bfloat16)
    outgoing = jnp.dot(
        dispatch, particles.reshape(count, CYCLES * width), preferred_element_type=jnp.float32
    )
    outgoing = outgoing.astype(jnp.bfloat16).reshape(n_cls, cap, CYCLES, width)
    match_int = match.astype(jnp.int32)
    picks = class_order[:, :, :CAND_OWN].reshape(count * OWN_TOP, CAND_OWN)
    slot_cand = jnp.where(filled[:, None], jnp.dot(match_int, picks), -1)
    owner_rows = jnp.repeat(jnp.arange(count, dtype=jnp.int32), OWN_TOP)
    slot_pid = jnp.where(filled, jnp.dot(match_int, owner_rows), -1)
    labels_out = jnp.concatenate([slot_cand, slot_pid[:, None]], 1).reshape(
        n_cls, cap, CAND_OWN + 1
    )
    arrived, labels = (
        lax.all_to_all(outgoing, "cls", split_axis=0, concat_axis=0, tiled=True),
        lax.all_to_all(labels_out, "cls", split_axis=0, concat_axis=0, tiled=True),
    )
    lanes = arrived.reshape(slots, CYCLES, width)
    labels = labels.reshape(slots, CAND_OWN + 1)
    forward, backward = spectral_tables()
    scale = 2.0 / math.sqrt(CYCLES * width)
    norms = jnp.sum(jnp.square(references.astype(jnp.float32)), axis=(1, 2))
    l_re = lanes[..., :HARM]
    l_im = lanes[..., HARM:]
    r_re = references[..., :HARM]
    r_im = references[..., HARM:]
    x_re = jnp.einsum("lrm,crm->lcm", l_re, r_re, preferred_element_type=jnp.float32) + jnp.einsum(
        "lrm,crm->lcm", l_im, r_im, preferred_element_type=jnp.float32
    )
    x_im = jnp.einsum("lrm,crm->lcm", l_im, r_re, preferred_element_type=jnp.float32) - jnp.einsum(
        "lrm,crm->lcm", l_re, r_im, preferred_element_type=jnp.float32
    )
    cross = jnp.concatenate([x_re, x_im], -1)
    corr = jnp.dot(
        cross.reshape(slots * groups, width), forward, precision=lax.Precision.HIGHEST
    ).reshape(slots, groups, ROTS)
    score = (corr - 0.5 * norms[None, :, None]) * scale
    candidate = jnp.any(
        labels[:, :CAND_OWN, None] == jnp.arange(groups, dtype=jnp.int32)[None, None, :], axis=1
    )
    part_max = jnp.max(jnp.where(candidate[:, :, None], score, lowest), axis=(1, 2))
    part_sum = jnp.sum(
        jnp.where(candidate[:, :, None], jnp.exp(score - part_max[:, None, None]), 0.0), axis=(1, 2)
    )
    sender_ids = labels[:, CAND_OWN].astype(jnp.float32)
    table_max, table_sum, table_ids = (
        lax.all_gather(part_max.reshape(1, n_cls, cap), "cls", axis=0, tiled=True),
        lax.all_gather(part_sum.reshape(1, n_cls, cap), "cls", axis=0, tiled=True),
        lax.all_gather(sender_ids.reshape(1, n_cls, cap), "cls", axis=0, tiled=True),
    )
    local_ids = jnp.arange(count, dtype=jnp.float32)
    hit = table_ids[..., None] == local_ids
    top = jnp.max(jnp.where(hit, table_max[..., None], lowest), axis=(0, 2))
    total = jnp.sum(
        jnp.where(
            hit, table_sum[..., None] * jnp.exp(table_max[..., None] - top[None, :, None, :]), 0.0
        ),
        axis=(0, 2),
    )
    table_norm = top + jnp.log(total)
    slot_ids = labels[:, CAND_OWN].reshape(n_cls, cap)
    slot_norm = jnp.sum(
        jnp.where(
            slot_ids[..., None] == jnp.arange(count, dtype=jnp.int32), table_norm[:, None, :], 0.0
        ),
        axis=2,
    ).reshape(slots)
    own_norm = lax.dynamic_index_in_dim(table_norm, lax.axis_index("cls"), 0, keepdims=False)
    weight = jnp.where(candidate[:, :, None], jnp.exp(score - slot_norm[:, None, None]), 0.0)
    mixed = (
        jnp.dot(weight.reshape(slots * groups, ROTS), backward, precision=lax.Precision.HIGHEST)
        .astype(jnp.bfloat16)
        .reshape(slots, groups, width)
    )
    class_weights = lax.psum(jnp.sum(weight, axis=(0, 2)), "prt")
    partial_sums = class_accumulate(lanes, mixed)
    class_sums = lax.psum_scatter(partial_sums, "prt", scatter_dimension=1, tiled=True)
    return (class_sums, class_weights, own_norm)


LANES = 128


def harmonic_plan():
    half = ROTS // 2
    turns = HARM // ROTS
    tail = HARM - turns * ROTS
    chunk_of = np.zeros(HARM, np.int32)
    side_of = np.zeros(HARM, np.int32)
    for m in range(HARM):
        turn, rest = divmod(m, ROTS)
        if turn == turns:
            chunk_of[m] = half * turns + rest // 2
            side_of[m] = rest % 2
        elif rest < half:
            chunk_of[m] = rest * turns + turn
        else:
            chunk_of[m] = ((ROTS - rest) % half) * turns + turn
            side_of[m] = 1
    return half, turns, tail, chunk_of, side_of


HALF, TURNS, TAIL, CHUNK_OF, SIDE_OF = harmonic_plan()
BODY = HALF * TURNS
CHUNKS = BODY + TAIL // 2
EXTRA = TAIL // 2 + 1
COEF = 2 * HALF * CAND_OWN
PIECES = ((0, 4), (4, 9), (9, 14), (14, 18))


def piece_chunks(piece):
    first, last = PIECES[piece]
    chunks = list(range(first * TURNS, last * TURNS))
    if piece == 0:
        chunks += list(range(BODY, CHUNKS + 1))
    return chunks


def selector():
    return (np.arange(CHUNKS)[:, None] == CHUNK_OF[None, :]).astype(np.float32)


def side_masks():
    return np.stack([SIDE_OF == 0, SIDE_OF == 1]).astype(np.float32)


def unselector():
    sel = selector()
    return np.concatenate([sel * (SIDE_OF == 0), sel * (SIDE_OF == 1)], 0)


def rotation_table():
    table = np.zeros((HALF, 2, CAND_OWN, ROTS, CAND_OWN))
    angle = 2.0 * np.pi * np.arange(ROTS) / ROTS
    for g in range(HALF):
        first = np.cos(g * angle)
        second = np.cos(HALF * angle) if g == 0 else np.sin(g * angle)
        for q in range(CAND_OWN):
            table[g, 0, q, :, q] = first
            table[g, 1, q, :, q] = second
    return table.reshape(COEF, ROTS * CAND_OWN).astype(np.float32)


def nt_dot(a, b):
    return lax.dot_general(a, b, (((1,), (1,)), ((), ())), preferred_element_type=jnp.float32)


def masked_stack(piece, masks):
    parts = []
    for s in range(2):
        for b in range(2):
            parts.append(piece[:, s * HARM : (s + 1) * HARM] * masks[b : b + 1])
    return jnp.concatenate(parts, 0)


def particle_body(x_ref, owner_ref, pick_ref, sel_ref, mask_ref, *refs):
    outs, scr = refs[:-1], refs[-1]
    count, cycles, _ = x_ref.shape
    n_prt = outs[0].shape[0]
    span = cycles // n_prt
    masks = mask_ref[...]

    def one(n, carry):
        x = x_ref[n]
        w = jnp.concatenate(
            [masked_stack(x[p * span : (p + 1) * span], masks) for p in range(n_prt)], 0
        )
        y = nt_dot(sel_ref[...], w)
        for p in range(n_prt):
            scr[p, pl.ds(pl.multiple_of(n * CHUNKS, CHUNKS), CHUNKS), :] = y[
                :, p * LANES : (p + 1) * LANES
            ]
        return carry

    lax.fori_loop(0, count, one, 0)

    for piece, out_ref in enumerate(outs):
        chunks = [c for c in piece_chunks(piece) if c < BODY]

        def two(c, carry):
            for p in range(n_prt):
                out_ref[p, c] = scr[p, pl.ds(chunks[0] + c, count, stride=CHUNKS), :].astype(
                    jnp.bfloat16
                )
            return carry

        lax.fori_loop(0, len(chunks), two, 0)
    base = PIECES[0][1] * TURNS
    for c in range(BODY, CHUNKS):
        for p in range(n_prt):
            outs[0][p, base + c - BODY] = scr[p, pl.ds(c, count, stride=CHUNKS), :].astype(
                jnp.bfloat16
            )
    lane = lax.broadcasted_iota(jnp.int32, (count, LANES), 1)
    label = jnp.full((count, LANES), -1, jnp.int32)
    for t in range(OWN_TOP):
        mine = (lane // CAND_OWN) == owner_ref[:, t : t + 1]
        for q in range(CAND_OWN):
            at = t * CAND_OWN + q
            label = jnp.where(
                mine & (lane % CAND_OWN == q), pick_ref[:, at : at + 1], label
            )
    label = label.astype(jnp.float32).astype(jnp.bfloat16)
    for p in range(n_prt):
        outs[0][p, base + CHUNKS - BODY] = label


def arrange_particles(particles, owner, picks, n_prt, sel, masks):
    count = particles.shape[0]
    return pl.pallas_call(
        particle_body,
        out_shape=[
            jax.ShapeDtypeStruct((n_prt, len(piece_chunks(i)), count, LANES), jnp.bfloat16)
            for i in range(len(PIECES))
        ],
        scratch_shapes=[pltpu.VMEM((n_prt, count * CHUNKS, LANES), jnp.float32)],
        compiler_params=pltpu.CompilerParams(vmem_limit_bytes=32 << 20),
        cost_estimate=pl.CostEstimate(
            flops=particles.size * 2 * CHUNKS, bytes_accessed=particles.size * 4, transcendentals=0
        ),
        name="arrange_particles",
    )(particles, owner, picks, sel, masks)


def reference_body(at_ref, x_ref, sel_ref, mask_ref, out_ref, norm_ref, scr):
    rows = x_ref.shape[0]
    masks = mask_ref[...]
    step = 4

    def one(n, carry):
        w = jnp.concatenate([masked_stack(x_ref[n * step + i], masks) for i in range(step)], 0)
        y = nt_dot(sel_ref[...], w)
        for i in range(step):
            scr[pl.ds(pl.multiple_of((n * step + i) * CHUNKS, CHUNKS), CHUNKS), :] = y[
                :, i * LANES : (i + 1) * LANES
            ]
        return carry

    lax.fori_loop(0, rows // step, one, 0)

    def two(c, carry):
        value = scr[pl.ds(c, rows, stride=CHUNKS), :]
        out_ref[c] = value.astype(jnp.bfloat16)
        return carry + value * value

    norm_ref[...] = lax.fori_loop(0, CHUNKS, two, jnp.zeros((rows, LANES), jnp.float32))


def arrange_references(references, prt, n_prt, sel, masks):
    groups, cycles, width = references.shape
    span = cycles // n_prt
    block = 16
    return pl.pallas_call(
        reference_body,
        grid_spec=pltpu.PrefetchScalarGridSpec(
            num_scalar_prefetch=1,
            grid=(groups // block,),
            in_specs=[
                pl.BlockSpec((block, span, width), lambda i, at: (i, at[0], 0)),
                pl.BlockSpec(sel.shape, lambda i, at: (0, 0)),
                pl.BlockSpec(masks.shape, lambda i, at: (0, 0)),
            ],
            out_specs=[
                pl.BlockSpec((CHUNKS, block, LANES), lambda i, at: (0, i, 0)),
                pl.BlockSpec((block, LANES), lambda i, at: (i, 0)),
            ],
            scratch_shapes=[pltpu.VMEM((block * CHUNKS, LANES), jnp.float32)],
        ),
        out_shape=[
            jax.ShapeDtypeStruct((CHUNKS, groups, LANES), jnp.bfloat16),
            jax.ShapeDtypeStruct((groups, LANES), jnp.float32),
        ],
        compiler_params=pltpu.CompilerParams(vmem_limit_bytes=32 << 20),
        cost_estimate=pl.CostEstimate(
            flops=groups * span * width * 2 * CHUNKS,
            bytes_accessed=groups * span * width * 4,
            transcendentals=0,
        ),
        name="arrange_references",
    )(prt, references, sel, masks)


def lane_signs():
    lane = lax.broadcasted_iota(jnp.int32, (1, LANES), 1)
    quarter = LANES // 4
    imag = lane >= 2 * quarter
    odd = (lane // quarter) % 2 == 1
    return imag, odd


def lanes_of(ref, first, number):
    parts = []
    for i in range(first, first + number):
        part = ref[:, i]
        parts.append(part.reshape(part.shape[0] * part.shape[1], LANES))
    return jnp.concatenate(parts, 1) if number > 1 else parts[0]


def hot_masks(cand, groups):
    rows = lax.broadcasted_iota(jnp.int32, (groups, cand.shape[1]), 0).astype(jnp.float32)
    return [rows == cand[q : q + 1] for q in range(CAND_OWN)]


def residue_weights(q_ref, g, special):
    imag, odd = lane_signs()
    sign = jnp.where(imag == odd, -1.0, 1.0)
    first, second = [], []
    for i in range(TURNS):
        q = q_ref[i].astype(jnp.float32)
        turned = pltpu.roll(q, LANES // 2, 1) * sign
        if special:
            first.append(jnp.where((g == 0) & odd, 0.0, q))
            second.append(jnp.where(g == 0, jnp.where(odd, q, 0.0), turned))
        else:
            first.append(q)
            second.append(turned)
    return jnp.concatenate(
        [jnp.concatenate(first, 1), jnp.concatenate(second, 1)], 0
    ).astype(jnp.bfloat16)


def chosen_rows(acc, cand):
    groups = acc.shape[0] // 2
    hot = hot_masks(cand, groups)
    rows = []
    for ab in range(2):
        part = acc[ab * groups : (ab + 1) * groups, :]
        for q in range(CAND_OWN):
            rows.append(jnp.sum(jnp.where(hot[q], part, 0.0), axis=0, keepdims=True))
    return jnp.concatenate(rows, 0)


def cross_first_body(at_ref, p_ref, *refs):
    tails, label_ref = refs[: TAIL // 2], refs[TAIL // 2]
    q_ref, qt_ref, norm_ref, coef_ref, cand_ref, acc = refs[TAIL // 2 + 1 :]
    g = pl.program_id(0)
    groups = q_ref.shape[1]
    imag, odd = lane_signs()

    @pl.when(g == 0)
    def _():
        label = lanes_of(label_ref, 0, 1).astype(jnp.float32).T
        row = lax.broadcasted_iota(jnp.int32, label.shape, 0)
        base = at_ref[0] * CAND_OWN
        for q in range(CAND_OWN):
            cand_ref[q : q + 1, :] = jnp.sum(
                jnp.where(row == base + q, label, 0.0), axis=0, keepdims=True
            )
        cand_ref[CAND_OWN:, :] = jnp.full(
            (cand_ref.shape[0] - CAND_OWN, cand_ref.shape[1]), -1.0, jnp.float32
        )

    acc[...] = nt_dot(residue_weights(q_ref, g, True), lanes_of(p_ref, 0, TURNS))

    for i in range(TAIL):

        @pl.when(g == i)
        def _():
            q = qt_ref[i // 2].astype(jnp.float32)
            keep = odd if i % 2 else ~odd
            a = jnp.where(keep, q, 0.0)
            b = jnp.where(keep, pltpu.roll(q, LANES // 2, 1) * jnp.where(imag, 1.0, -1.0), 0.0)
            if i == 0:
                b = jnp.zeros_like(b)
            w = jnp.concatenate([a, b], 0).astype(jnp.bfloat16)
            acc[...] += nt_dot(w, lanes_of(tails[i // 2], 0, 1))

    @pl.when(g == 0)
    def _():
        acc[:groups, :] -= 0.5 * jnp.sum(norm_ref[...], axis=1, keepdims=True)

    coef_ref[...] = chosen_rows(acc[...], cand_ref[...])


def cross_body(p_ref, q_ref, cand_ref, coef_ref):
    acc = nt_dot(residue_weights(q_ref, None, False), lanes_of(p_ref, 0, TURNS))
    coef_ref[...] = chosen_rows(acc, cand_ref[...])


def cross_cost(gathered, groups):
    return pl.CostEstimate(
        flops=4 * gathered.size * groups, bytes_accessed=2 * gathered.size, transcendentals=0
    )


def extra_specs(sources, count):
    base = PIECES[0][1] * TURNS
    return [
        pl.BlockSpec((sources, 1, count, LANES), lambda g, *at, k=k: (0, base + k, 0, 0))
        for k in range(EXTRA)
    ]


def cross_first(gathered, arranged, norms, cls):
    sources, _, count, _ = gathered.shape
    groups = arranged.shape[1]
    total = sources * count
    half_tail = TAIL // 2
    number = PIECES[0][1]
    block = 2 * CAND_OWN
    return pl.pallas_call(
        cross_first_body,
        grid_spec=pltpu.PrefetchScalarGridSpec(
            num_scalar_prefetch=1,
            grid=(number,),
            in_specs=[
                pl.BlockSpec((sources, TURNS, count, LANES), lambda g, at: (0, g, 0, 0)),
                *extra_specs(sources, count),
                pl.BlockSpec((TURNS, groups, LANES), lambda g, at: (g, 0, 0)),
                pl.BlockSpec((half_tail, groups, LANES), lambda g, at: (BODY // half_tail, 0, 0)),
                pl.BlockSpec((groups, LANES), lambda g, at: (0, 0)),
            ],
            out_specs=[
                pl.BlockSpec((block, total), lambda g, at: (g, 0)),
                pl.BlockSpec((block, total), lambda g, at: (0, 0)),
            ],
            scratch_shapes=[pltpu.VMEM((2 * groups, total), jnp.float32)],
        ),
        out_shape=[
            jax.ShapeDtypeStruct((number * block, total), jnp.float32),
            jax.ShapeDtypeStruct((block, total), jnp.float32),
        ],
        compiler_params=pltpu.CompilerParams(vmem_limit_bytes=48 << 20),
        cost_estimate=cross_cost(gathered, groups),
        name="cross_first",
    )(cls, gathered, *[gathered] * EXTRA, arranged, arranged, norms)


def cross_later(gathered, arranged, cand, piece):
    sources, _, count, _ = gathered.shape
    groups = arranged.shape[1]
    total = sources * count
    first, last = PIECES[piece]
    block = 2 * CAND_OWN
    return pl.pallas_call(
        cross_body,
        grid=(last - first,),
        in_specs=[
            pl.BlockSpec((sources, TURNS, count, LANES), lambda g: (0, g, 0, 0)),
            pl.BlockSpec((TURNS, groups, LANES), lambda g: (first + g, 0, 0)),
            pl.BlockSpec((block, total), lambda g: (0, 0)),
        ],
        out_specs=pl.BlockSpec((block, total), lambda g: (g, 0)),
        out_shape=jax.ShapeDtypeStruct(((last - first) * block, total), jnp.float32),
        compiler_params=pltpu.CompilerParams(vmem_limit_bytes=48 << 20),
        cost_estimate=cross_cost(gathered, groups),
        name="cross_later",
    )(gathered, arranged, cand)


def score_body(*refs, scale):
    *coefs, cand_ref, table_ref, score_ref, stat_ref = refs
    corr = lax.dot_general(
        table_ref[...],
        jnp.concatenate([ref[...] for ref in coefs], 0),
        (((0,), (0,)), ((), ())),
        precision=lax.Precision.HIGHEST,
        preferred_element_type=jnp.float32,
    )
    score = jnp.where(cand_ref[0:1, :] >= 0.0, corr * scale, lowest)
    top = jnp.max(score, axis=0, keepdims=True)
    total = jnp.sum(jnp.exp(score - top), axis=0, keepdims=True)
    score_ref[...] = score
    stat_ref[0:1, :] = top
    stat_ref[1:2, :] = jnp.where(cand_ref[0:1, :] >= 0.0, total, 0.0)


def scores(coefs, cand, table, scale):
    total = cand.shape[1]
    return pl.pallas_call(
        functools.partial(score_body, scale=scale),
        out_shape=[
            jax.ShapeDtypeStruct((ROTS * CAND_OWN, total), jnp.float32),
            jax.ShapeDtypeStruct((2, total), jnp.float32),
        ],
        name="scores",
    )(*coefs, cand, table)


def sums_body(*refs):
    number = len(PIECES)
    pieces, tails = refs[:number], refs[number : number + TAIL // 2]
    score_ref, cand_ref, stat_ref, table_ref, back_ref = refs[number + TAIL // 2 : -5]
    out_ref, weight_ref, norm_ref, mix, planes = refs[-5:]
    i = pl.program_id(0)
    groups = weight_ref.shape[0]
    total = score_ref.shape[1]
    imag, odd = lane_signs()

    @pl.when(i == 0)
    def _():
        tops = [stat_ref[2 * j : 2 * j + 1, :] for j in range(stat_ref.shape[0] // 2)]
        top = functools.reduce(jnp.maximum, tops)
        summed = jnp.zeros_like(top)
        for j, other in enumerate(tops):
            summed += stat_ref[2 * j + 1 : 2 * j + 2, :] * jnp.exp(other - top)
        log_norm = top + jnp.log(summed)
        norm_ref[...] = log_norm
        weight = jnp.where(
            cand_ref[0:1, :] >= 0.0, jnp.exp(score_ref[...] - log_norm), 0.0
        )
        mixed = lax.dot_general(
            table_ref[...],
            weight,
            (((1,), (0,)), ((), ())),
            precision=lax.Precision.HIGHEST,
            preferred_element_type=jnp.float32,
        )
        hot = hot_masks(cand_ref[...], groups)
        summed = jnp.zeros((groups, total), jnp.float32)
        for q in range(CAND_OWN):
            summed += jnp.where(hot[q], mixed[q : q + 1], 0.0)
        weight_ref[...] = jnp.sum(summed, axis=1, keepdims=True)
        mix[...] = mixed

    @pl.when(i < HALF)
    def _():
        hot = hot_masks(cand_ref[...], groups)
        block = 2 * CAND_OWN
        mine = mix[pl.ds(pl.multiple_of(i * block, block), block), :]
        halves = []
        for ab in range(2):
            dense = jnp.zeros((groups, total), jnp.float32)
            for q in range(CAND_OWN):
                at = ab * CAND_OWN + q
                dense = jnp.where(hot[q], mine[at : at + 1], dense)
            halves.append(dense)
        weights = jnp.concatenate(halves, 0).astype(jnp.bfloat16)
        sign = jnp.where(imag == odd, 1.0, -1.0)
        for piece, (first, last) in enumerate(PIECES):

            @pl.when((i >= first) & (i < last))
            def _():
                made = jnp.dot(
                    weights,
                    lanes_of(pieces[piece], 0, TURNS),
                    preferred_element_type=jnp.float32,
                )
                for t in range(TURNS):
                    g1 = made[:groups, t * LANES : (t + 1) * LANES]
                    g2 = made[groups:, t * LANES : (t + 1) * LANES]
                    value = g1 + sign * pltpu.roll(g2, LANES // 2, 1)
                    if piece == 0:
                        value = jnp.where(i == 0, jnp.where(odd, g2, g1), value)
                    start = pl.multiple_of((i * TURNS + t) * groups, groups)
                    planes[pl.ds(start, groups), :] = value

        for t in range(TAIL):

            @pl.when(i == t)
            def _():
                made = jnp.dot(
                    weights, lanes_of(tails[t // 2], 0, 1), preferred_element_type=jnp.float32
                )
                g1, g2 = made[:groups], made[groups:]
                value = g1
                if t > 0:
                    value = g1 + jnp.where(imag, -1.0, 1.0) * pltpu.roll(g2, LANES // 2, 1)
                rows = pl.ds((BODY + t // 2) * groups, groups)
                if t % 2:
                    value = jnp.where(odd, value, planes[rows, :])
                planes[rows, :] = value

    @pl.when(i >= HALF)
    def _():
        block, span, _ = out_ref.shape
        first = (i - HALF) * block
        back = back_ref[...]
        for c in range(block):
            turned = planes[pl.ds(first + c, CHUNKS, stride=groups), :].T
            parts = []
            for s in range(2):
                at = 2 * s * span
                parts.append(
                    jnp.concatenate([turned[at : at + span], turned[at + span : at + 2 * span]], 1)
                )
            value = jnp.concatenate(parts, 0)
            high = value.astype(jnp.bfloat16)
            low = (value - high.astype(jnp.float32)).astype(jnp.bfloat16)
            placed = jnp.dot(high, back, preferred_element_type=jnp.float32) + jnp.dot(
                low, back, preferred_element_type=jnp.float32
            )
            out_ref[c, :, :HARM] = placed[:span]
            out_ref[c, :, HARM:] = placed[span:]


def piece_spec(piece, sources, count):
    first, last = PIECES[piece]
    return pl.BlockSpec(
        (sources, TURNS, count, LANES),
        lambda i: (0, jnp.clip(i, first, last - 1) - first, 0, 0),
    )


def sums(gathered, score, cand, stats, table, back, groups, span):
    sources, _, count, _ = gathered[0].shape
    total = sources * count
    size = sum(piece.size for piece in gathered)
    block = 8
    whole = lambda i: (0, 0)
    return pl.pallas_call(
        sums_body,
        grid=(HALF + groups // block,),
        in_specs=[
            *[piece_spec(piece, sources, count) for piece in range(len(PIECES))],
            *extra_specs(sources, count)[: TAIL // 2],
            pl.BlockSpec(score.shape, whole),
            pl.BlockSpec(cand.shape, whole),
            pl.BlockSpec(stats.shape, whole),
            pl.BlockSpec(table.shape, whole),
            pl.BlockSpec(back.shape, whole),
        ],
        out_specs=[
            pl.BlockSpec(
                (block, span, 2 * HARM), lambda i: (jnp.maximum(i - HALF, 0), 0, 0)
            ),
            pl.BlockSpec((groups, 1), whole),
            pl.BlockSpec((1, total), whole),
        ],
        out_shape=[
            jax.ShapeDtypeStruct((groups, span, 2 * HARM), jnp.float32),
            jax.ShapeDtypeStruct((groups, 1), jnp.float32),
            jax.ShapeDtypeStruct((1, total), jnp.float32),
        ],
        scratch_shapes=[
            pltpu.VMEM((COEF, total), jnp.float32),
            pltpu.VMEM((CHUNKS * groups, LANES), jnp.float32),
        ],
        compiler_params=pltpu.CompilerParams(vmem_limit_bytes=48 << 20),
        cost_estimate=pl.CostEstimate(
            flops=4 * size * groups,
            bytes_accessed=2 * size + 8 * groups * span * HARM,
            transcendentals=0,
        ),
        name="sums",
    )(*gathered, *[gathered[0]] * (TAIL // 2), score, cand, stats, table, back)


def spread(outgoing):
    arrived = lax.all_to_all(outgoing, "prt", split_axis=0, concat_axis=0, tiled=True)
    return lax.all_gather(arrived, "cls", axis=0, tiled=True)


def gather_device(particles, references, owner_groups, class_order):
    n_cls, n_prt = lax.axis_size("cls"), lax.axis_size("prt")
    cls, prt = lax.axis_index("cls"), lax.axis_index("prt")
    count, cycles, width = particles.shape
    groups = references.shape[0]
    span = cycles // n_prt
    sel = jnp.asarray(selector(), jnp.bfloat16)
    masks = jnp.asarray(side_masks(), jnp.bfloat16)
    back = jnp.asarray(unselector(), jnp.bfloat16)
    table = jnp.asarray(rotation_table())
    picks = class_order[:, :, :CAND_OWN].reshape(count, OWN_TOP * CAND_OWN)
    outgoing = arrange_particles(particles, owner_groups, picks, n_prt, sel, masks)
    gathered = [spread(piece) for piece in outgoing]
    arranged, norms = arrange_references(
        references, prt.reshape(1).astype(jnp.int32), n_prt, sel, masks
    )
    coef, cand = cross_first(gathered[0], arranged, norms, cls.reshape(1).astype(jnp.int32))
    coefs = [lax.psum(coef, "prt")]
    for piece in range(1, len(PIECES)):
        coef = cross_later(gathered[piece], arranged, cand, piece)
        coef, coefs[-1] = lax.optimization_barrier((coef, coefs[-1]))
        coefs.append(lax.psum(coef, "prt"))
    scale = 2.0 / math.sqrt(cycles * width)
    score, stat = scores(coefs, cand, table, scale)
    stats = lax.all_gather(stat, "cls", axis=0, tiled=True)
    class_sums, class_weights, log_norm = sums(
        gathered, score, cand, stats, table, back, groups, span
    )
    own = lax.dynamic_slice(log_norm[0], ((cls * n_prt + prt) * count,), (count,))
    return class_sums, class_weights[:, 0], own


def per_device(particles, references, owner_groups, class_order):
    n_cls, n_prt = lax.axis_size("cls"), lax.axis_size("prt")
    count, cycles, _ = particles.shape
    groups = references.shape[0]
    cap = max(2, 2 * count * OWN_TOP // n_cls)
    fits = 4 * cycles == LANES * n_prt and n_cls * CAND_OWN <= LANES and groups % 16 == 0
    plan = gather_device if cap >= count and fits else dispatch_device
    return plan(particles, references, owner_groups, class_order)


def solution(mesh):
    in_specs = (
        P(("cls", "prt"), None, None),
        P("cls", None, None),
        P(("cls", "prt"), None),
        P(("cls", "prt"), None, None),
    )
    out_specs = (P("cls", "prt", None), P("cls"), P(("cls", "prt")))
    return jax.shard_map(
        per_device, mesh=mesh, in_specs=in_specs, out_specs=out_specs, check_vma=False
    )
```

```python
import functools
import math

import jax
import jax.numpy as jnp
import numpy as np
from jax import lax
from jax.experimental import pallas as pl
from jax.experimental.pallas import tpu as pltpu
from jax.sharding import PartitionSpec as P

CYCLES = 128
HARM = 256
ROTS = 36
OWN_TOP = 4
CAND_OWN = 4


lowest = -1e30


def spectral_tables():
    harmonic = jnp.arange(HARM, dtype=jnp.float32)
    angles = 2.0 * math.pi * jnp.arange(ROTS, dtype=jnp.float32) / ROTS
    phase = harmonic[:, None] * angles[None, :]
    forward = jnp.concatenate([jnp.cos(phase), jnp.sin(phase)], 0)
    backward = jnp.concatenate([jnp.cos(phase), -jnp.sin(phase)], 0).T
    return (forward, backward)


def class_accumulate(lanes, mixed):
    l_re = lanes[..., :HARM]
    l_im = lanes[..., HARM:]
    y_re = mixed[..., :HARM]
    y_im = mixed[..., HARM:]
    s_re = jnp.einsum("lrm,lcm->crm", l_re, y_re, preferred_element_type=jnp.float32) - jnp.einsum(
        "lrm,lcm->crm", l_im, y_im, preferred_element_type=jnp.float32
    )
    s_im = jnp.einsum("lrm,lcm->crm", l_re, y_im, preferred_element_type=jnp.float32) + jnp.einsum(
        "lrm,lcm->crm", l_im, y_re, preferred_element_type=jnp.float32
    )
    return jnp.concatenate([s_re, s_im], -1)


def dispatch_device(particles, references, owner_groups, class_order):
    n_cls = lax.axis_size("cls")
    count = particles.shape[0]
    groups = references.shape[0]
    cap = max(2, 2 * count * OWN_TOP // n_cls)
    slots = n_cls * cap
    width = 2 * HARM
    flat_owner = owner_groups.reshape(-1)
    owner_hot = (flat_owner[:, None] == jnp.arange(n_cls, dtype=jnp.int32)[None, :]).astype(
        jnp.int32
    )
    before = jnp.cumsum(owner_hot, axis=0) - owner_hot
    rank = jnp.sum(before * owner_hot, axis=1)
    slot_of = flat_owner * cap + rank
    match = slot_of[None, :] == jnp.arange(slots, dtype=jnp.int32)[:, None]
    member = jnp.any(match.reshape(slots, count, OWN_TOP), axis=2)
    filled = jnp.any(member, axis=1)
    dispatch = member.astype(jnp.bfloat16)
    outgoing = jnp.dot(
        dispatch, particles.reshape(count, CYCLES * width), preferred_element_type=jnp.float32
    )
    outgoing = outgoing.astype(jnp.bfloat16).reshape(n_cls, cap, CYCLES, width)
    match_int = match.astype(jnp.int32)
    picks = class_order[:, :, :CAND_OWN].reshape(count * OWN_TOP, CAND_OWN)
    slot_cand = jnp.where(filled[:, None], jnp.dot(match_int, picks), -1)
    owner_rows = jnp.repeat(jnp.arange(count, dtype=jnp.int32), OWN_TOP)
    slot_pid = jnp.where(filled, jnp.dot(match_int, owner_rows), -1)
    labels_out = jnp.concatenate([slot_cand, slot_pid[:, None]], 1).reshape(
        n_cls, cap, CAND_OWN + 1
    )
    arrived, labels = (
        lax.all_to_all(outgoing, "cls", split_axis=0, concat_axis=0, tiled=True),
        lax.all_to_all(labels_out, "cls", split_axis=0, concat_axis=0, tiled=True),
    )
    lanes = arrived.reshape(slots, CYCLES, width)
    labels = labels.reshape(slots, CAND_OWN + 1)
    forward, backward = spectral_tables()
    scale = 2.0 / math.sqrt(CYCLES * width)
    norms = jnp.sum(jnp.square(references.astype(jnp.float32)), axis=(1, 2))
    l_re = lanes[..., :HARM]
    l_im = lanes[..., HARM:]
    r_re = references[..., :HARM]
    r_im = references[..., HARM:]
    x_re = jnp.einsum("lrm,crm->lcm", l_re, r_re, preferred_element_type=jnp.float32) + jnp.einsum(
        "lrm,crm->lcm", l_im, r_im, preferred_element_type=jnp.float32
    )
    x_im = jnp.einsum("lrm,crm->lcm", l_im, r_re, preferred_element_type=jnp.float32) - jnp.einsum(
        "lrm,crm->lcm", l_re, r_im, preferred_element_type=jnp.float32
    )
    cross = jnp.concatenate([x_re, x_im], -1)
    corr = jnp.dot(
        cross.reshape(slots * groups, width), forward, precision=lax.Precision.HIGHEST
    ).reshape(slots, groups, ROTS)
    score = (corr - 0.5 * norms[None, :, None]) * scale
    candidate = jnp.any(
        labels[:, :CAND_OWN, None] == jnp.arange(groups, dtype=jnp.int32)[None, None, :], axis=1
    )
    part_max = jnp.max(jnp.where(candidate[:, :, None], score, lowest), axis=(1, 2))
    part_sum = jnp.sum(
        jnp.where(candidate[:, :, None], jnp.exp(score - part_max[:, None, None]), 0.0), axis=(1, 2)
    )
    sender_ids = labels[:, CAND_OWN].astype(jnp.float32)
    table_max, table_sum, table_ids = (
        lax.all_gather(part_max.reshape(1, n_cls, cap), "cls", axis=0, tiled=True),
        lax.all_gather(part_sum.reshape(1, n_cls, cap), "cls", axis=0, tiled=True),
        lax.all_gather(sender_ids.reshape(1, n_cls, cap), "cls", axis=0, tiled=True),
    )
    local_ids = jnp.arange(count, dtype=jnp.float32)
    hit = table_ids[..., None] == local_ids
    top = jnp.max(jnp.where(hit, table_max[..., None], lowest), axis=(0, 2))
    total = jnp.sum(
        jnp.where(
            hit, table_sum[..., None] * jnp.exp(table_max[..., None] - top[None, :, None, :]), 0.0
        ),
        axis=(0, 2),
    )
    table_norm = top + jnp.log(total)
    slot_ids = labels[:, CAND_OWN].reshape(n_cls, cap)
    slot_norm = jnp.sum(
        jnp.where(
            slot_ids[..., None] == jnp.arange(count, dtype=jnp.int32), table_norm[:, None, :], 0.0
        ),
        axis=2,
    ).reshape(slots)
    own_norm = lax.dynamic_index_in_dim(table_norm, lax.axis_index("cls"), 0, keepdims=False)
    weight = jnp.where(candidate[:, :, None], jnp.exp(score - slot_norm[:, None, None]), 0.0)
    mixed = (
        jnp.dot(weight.reshape(slots * groups, ROTS), backward, precision=lax.Precision.HIGHEST)
        .astype(jnp.bfloat16)
        .reshape(slots, groups, width)
    )
    class_weights = lax.psum(jnp.sum(weight, axis=(0, 2)), "prt")
    partial_sums = class_accumulate(lanes, mixed)
    class_sums = lax.psum_scatter(partial_sums, "prt", scatter_dimension=1, tiled=True)
    return (class_sums, class_weights, own_norm)


LANES = 128


def harmonic_plan():
    half = ROTS // 2
    turns = HARM // ROTS
    tail = HARM - turns * ROTS
    chunk_of = np.zeros(HARM, np.int32)
    side_of = np.zeros(HARM, np.int32)
    for m in range(HARM):
        turn, rest = divmod(m, ROTS)
        if turn == turns:
            chunk_of[m] = half * turns + rest // 2
            side_of[m] = rest % 2
        elif rest < half:
            chunk_of[m] = rest * turns + turn
        else:
            chunk_of[m] = ((ROTS - rest) % half) * turns + turn
            side_of[m] = 1
    return half, turns, tail, chunk_of, side_of


HALF, TURNS, TAIL, CHUNK_OF, SIDE_OF = harmonic_plan()
BODY = HALF * TURNS
CHUNKS = BODY + TAIL // 2
EXTRA = TAIL // 2 + 1
COEF = 2 * HALF * CAND_OWN
CROSS_STEP = 6
SUM_STEP = 3


def selector():
    return (np.arange(CHUNKS)[:, None] == CHUNK_OF[None, :]).astype(np.float32)


def side_masks():
    return np.stack([SIDE_OF == 0, SIDE_OF == 1]).astype(np.float32)


def unselector():
    sel = selector()
    return np.concatenate([sel * (SIDE_OF == 0), sel * (SIDE_OF == 1)], 0)


def rotation_table():
    table = np.zeros((HALF, 2, CAND_OWN, ROTS, CAND_OWN))
    angle = 2.0 * np.pi * np.arange(ROTS) / ROTS
    for g in range(HALF):
        first = np.cos(g * angle)
        second = np.cos(HALF * angle) if g == 0 else np.sin(g * angle)
        for q in range(CAND_OWN):
            table[g, 0, q, :, q] = first
            table[g, 1, q, :, q] = second
    return table.reshape(COEF, ROTS * CAND_OWN).astype(np.float32)


def nt_dot(a, b):
    return lax.dot_general(a, b, (((1,), (1,)), ((), ())), preferred_element_type=jnp.float32)


def masked_stack(piece, masks):
    parts = []
    for s in range(2):
        for b in range(2):
            parts.append(piece[:, s * HARM : (s + 1) * HARM] * masks[b : b + 1])
    return jnp.concatenate(parts, 0)


def particle_body(at_ref, x_ref, owner_ref, pick_ref, sel_ref, mask_ref, *refs):
    outs, scr = refs[:-1], refs[-1]
    count, cycles, _ = x_ref.shape
    n_prt = len(outs)
    span = cycles // n_prt
    masks = mask_ref[...]

    def one(n, carry):
        parts = []
        for d in range(n_prt):
            start = pl.multiple_of((at_ref[0] ^ d) * span, span)
            parts.append(masked_stack(x_ref[n, pl.ds(start, span), :], masks))
        w = jnp.concatenate(parts, 0)
        y = nt_dot(sel_ref[...], w)
        for p in range(n_prt):
            scr[p, pl.ds(pl.multiple_of(n * CHUNKS, CHUNKS), CHUNKS), :] = y[
                :, p * LANES : (p + 1) * LANES
            ]
        return carry

    lax.fori_loop(0, count, one, 0)

    def two(c, carry):
        for p in range(n_prt):
            outs[p][c] = scr[p, pl.ds(c, count, stride=CHUNKS), :].astype(jnp.bfloat16)
        return carry

    lax.fori_loop(0, CHUNKS, two, 0)
    lane = lax.broadcasted_iota(jnp.int32, (count, LANES), 1)
    label = jnp.full((count, LANES), -1, jnp.int32)
    for t in range(OWN_TOP):
        mine = (lane // CAND_OWN) == owner_ref[:, t : t + 1]
        for q in range(CAND_OWN):
            at = t * CAND_OWN + q
            label = jnp.where(
                mine & (lane % CAND_OWN == q), pick_ref[:, at : at + 1], label
            )
    label = label.astype(jnp.float32).astype(jnp.bfloat16)
    for p in range(n_prt):
        outs[p][CHUNKS] = label


def arrange_particles(prt, particles, owner, picks, n_prt, sel, masks):
    count = particles.shape[0]
    return pl.pallas_call(
        particle_body,
        in_specs=[pl.BlockSpec(memory_space=pltpu.SMEM)] + [pl.BlockSpec(memory_space=pltpu.VMEM)] * 5,
        out_shape=[jax.ShapeDtypeStruct((CHUNKS + 1, count, LANES), jnp.bfloat16)] * n_prt,
        scratch_shapes=[pltpu.VMEM((n_prt, count * CHUNKS, LANES), jnp.float32)],
        compiler_params=pltpu.CompilerParams(vmem_limit_bytes=32 << 20),
        cost_estimate=pl.CostEstimate(
            flops=particles.size * 2 * CHUNKS, bytes_accessed=particles.size * 4, transcendentals=0
        ),
        name="arrange_particles",
    )(prt, particles, owner, picks, sel, masks)


def reference_body(at_ref, x_ref, sel_ref, mask_ref, out_ref, norm_ref, scr):
    rows = x_ref.shape[0]
    masks = mask_ref[...]
    step = 4

    def one(n, carry):
        w = jnp.concatenate([masked_stack(x_ref[n * step + i], masks) for i in range(step)], 0)
        y = nt_dot(sel_ref[...], w)
        for i in range(step):
            scr[pl.ds(pl.multiple_of((n * step + i) * CHUNKS, CHUNKS), CHUNKS), :] = y[
                :, i * LANES : (i + 1) * LANES
            ]
        return carry

    lax.fori_loop(0, rows // step, one, 0)

    def two(c, carry):
        value = scr[pl.ds(c, rows, stride=CHUNKS), :]
        out_ref[c] = value.astype(jnp.bfloat16)
        return carry + value * value

    norm_ref[...] = lax.fori_loop(0, CHUNKS, two, jnp.zeros((rows, LANES), jnp.float32))


def arrange_references(references, prt, n_prt, sel, masks):
    groups, cycles, width = references.shape
    span = cycles // n_prt
    block = 16
    return pl.pallas_call(
        reference_body,
        grid_spec=pltpu.PrefetchScalarGridSpec(
            num_scalar_prefetch=1,
            grid=(groups // block,),
            in_specs=[
                pl.BlockSpec((block, span, width), lambda i, at: (i, at[0], 0)),
                pl.BlockSpec(sel.shape, lambda i, at: (0, 0)),
                pl.BlockSpec(masks.shape, lambda i, at: (0, 0)),
            ],
            out_specs=[
                pl.BlockSpec((CHUNKS, block, LANES), lambda i, at: (0, i, 0)),
                pl.BlockSpec((block, LANES), lambda i, at: (i, 0)),
            ],
            scratch_shapes=[pltpu.VMEM((block * CHUNKS, LANES), jnp.float32)],
        ),
        out_shape=[
            jax.ShapeDtypeStruct((CHUNKS, groups, LANES), jnp.bfloat16),
            jax.ShapeDtypeStruct((groups, LANES), jnp.float32),
        ],
        compiler_params=pltpu.CompilerParams(vmem_limit_bytes=32 << 20),
        cost_estimate=pl.CostEstimate(
            flops=groups * span * width * 2 * CHUNKS,
            bytes_accessed=groups * span * width * 4,
            transcendentals=0,
        ),
        name="arrange_references",
    )(prt, references, sel, masks)


def lane_signs():
    lane = lax.broadcasted_iota(jnp.int32, (1, LANES), 1)
    quarter = LANES // 4
    imag = lane >= 2 * quarter
    odd = (lane // quarter) % 2 == 1
    return imag, odd


def lanes_of(refs, first, number):
    parts = [
        jnp.concatenate([ref[i] for ref in refs], 0) for i in range(first, first + number)
    ]
    return jnp.concatenate(parts, 1) if number > 1 else parts[0]


def hot_masks(cand, groups):
    rows = lax.broadcasted_iota(jnp.int32, (groups, cand.shape[1]), 0).astype(jnp.float32)
    return [rows == cand[q : q + 1] for q in range(CAND_OWN)]


def residue_weights(q_ref, at, g):
    imag, odd = lane_signs()
    sign = jnp.where(imag == odd, -1.0, 1.0)
    first, second = [], []
    for i in range(TURNS):
        q = q_ref[at * TURNS + i].astype(jnp.float32)
        turned = pltpu.roll(q, LANES // 2, 1) * sign
        if at == 0:
            first.append(jnp.where((g == 0) & odd, 0.0, q))
            second.append(jnp.where(g == 0, jnp.where(odd, q, 0.0), turned))
        else:
            first.append(q)
            second.append(turned)
    return jnp.concatenate(
        [jnp.concatenate(first, 1), jnp.concatenate(second, 1)], 0
    ).astype(jnp.bfloat16)


def chosen_rows(acc, cand):
    groups = acc.shape[0] // 2
    hot = hot_masks(cand, groups)
    rows = []
    for ab in range(2):
        part = acc[ab * groups : (ab + 1) * groups, :]
        for q in range(CAND_OWN):
            rows.append(jnp.sum(jnp.where(hot[q], part, 0.0), axis=0, keepdims=True))
    return jnp.concatenate(rows, 0)


def cross_body(at_ref, *refs):
    number = (len(refs) - 6) // 2
    blocks, extras = refs[:number], refs[number : 2 * number]
    q_ref, qt_ref, norm_ref, coef_ref, cand_ref, acc = refs[2 * number :]
    step = pl.program_id(0)
    groups = q_ref.shape[1]
    imag, odd = lane_signs()

    @pl.when(step == 0)
    def _():
        label = lanes_of(extras, TAIL // 2, 1).astype(jnp.float32).T
        row = lax.broadcasted_iota(jnp.int32, label.shape, 0)
        base = at_ref[0] * CAND_OWN
        for q in range(CAND_OWN):
            cand_ref[q : q + 1, :] = jnp.sum(
                jnp.where(row == base + q, label, 0.0), axis=0, keepdims=True
            )
        cand_ref[CAND_OWN:, :] = jnp.full(
            (cand_ref.shape[0] - CAND_OWN, cand_ref.shape[1]), -1.0, jnp.float32
        )

    for u in range(CROSS_STEP):
        g = step * CROSS_STEP + u
        acc[...] = nt_dot(residue_weights(q_ref, u, g), lanes_of(blocks, u * TURNS, TURNS))

        for i in range(TAIL):
            if i % CROSS_STEP != u:
                continue

            @pl.when(g == i)
            def _():
                q = qt_ref[i // 2].astype(jnp.float32)
                keep = odd if i % 2 else ~odd
                a = jnp.where(keep, q, 0.0)
                turned = pltpu.roll(q, LANES // 2, 1) * jnp.where(imag, 1.0, -1.0)
                b = jnp.where(keep, turned, 0.0)
                if i == 0:
                    b = jnp.zeros_like(b)
                w = jnp.concatenate([a, b], 0).astype(jnp.bfloat16)
                acc[...] += nt_dot(w, lanes_of(extras, i // 2, 1))
                if i == 0:
                    acc[:groups, :] -= 0.5 * jnp.sum(norm_ref[...], axis=1, keepdims=True)

        block = 2 * CAND_OWN
        coef_ref[u * block : (u + 1) * block, :] = chosen_rows(acc[...], cand_ref[...])


def cross_coefficients(blocks, arranged, norms, cls):
    count = blocks[0].shape[1]
    groups = arranged.shape[1]
    total = len(blocks) * count
    half_tail = TAIL // 2
    size = blocks[0].size * len(blocks)
    block = 2 * CAND_OWN
    return pl.pallas_call(
        cross_body,
        grid_spec=pltpu.PrefetchScalarGridSpec(
            num_scalar_prefetch=1,
            grid=(HALF // CROSS_STEP,),
            in_specs=[
                *[
                    pl.BlockSpec((CROSS_STEP * TURNS, count, LANES), lambda g, at: (g, 0, 0))
                    for _ in blocks
                ],
                *[
                    pl.BlockSpec((EXTRA, count, LANES), lambda g, at: (BODY // EXTRA, 0, 0))
                    for _ in blocks
                ],
                pl.BlockSpec((CROSS_STEP * TURNS, groups, LANES), lambda g, at: (g, 0, 0)),
                pl.BlockSpec((half_tail, groups, LANES), lambda g, at: (BODY // half_tail, 0, 0)),
                pl.BlockSpec((groups, LANES), lambda g, at: (0, 0)),
            ],
            out_specs=[
                pl.BlockSpec((CROSS_STEP * block, total), lambda g, at: (g, 0)),
                pl.BlockSpec((block, total), lambda g, at: (0, 0)),
            ],
            scratch_shapes=[pltpu.VMEM((2 * groups, total), jnp.float32)],
        ),
        out_shape=[
            jax.ShapeDtypeStruct((COEF, total), jnp.float32),
            jax.ShapeDtypeStruct((block, total), jnp.float32),
        ],
        compiler_params=pltpu.CompilerParams(vmem_limit_bytes=32 << 20),
        cost_estimate=pl.CostEstimate(
            flops=4 * size * groups, bytes_accessed=2 * size, transcendentals=0
        ),
        name="cross_coefficients",
    )(cls, *blocks, *blocks, arranged, arranged, norms)


def score_body(*refs, scale):
    *coefs, cand_ref, table_ref, score_ref, stat_ref = refs
    corr = lax.dot_general(
        table_ref[...],
        functools.reduce(jnp.add, [ref[...] for ref in coefs]),
        (((0,), (0,)), ((), ())),
        precision=lax.Precision.HIGHEST,
        preferred_element_type=jnp.float32,
    )
    score = jnp.where(cand_ref[0:1, :] >= 0.0, corr * scale, lowest)
    top = jnp.max(score, axis=0, keepdims=True)
    total = jnp.sum(jnp.exp(score - top), axis=0, keepdims=True)
    score_ref[...] = score
    stat_ref[0:1, :] = top
    stat_ref[1:2, :] = jnp.where(cand_ref[0:1, :] >= 0.0, total, 0.0)


def scores(coefs, cand, table, scale):
    total = cand.shape[1]
    return pl.pallas_call(
        functools.partial(score_body, scale=scale),
        out_shape=[
            jax.ShapeDtypeStruct((ROTS * CAND_OWN, total), jnp.float32),
            jax.ShapeDtypeStruct((2, total), jnp.float32),
        ],
        name="scores",
    )(*coefs, cand, table)


def swap_blocks(x, distance, width):
    lane = lax.broadcasted_iota(jnp.int32, x.shape, 1)
    bit = 1
    while bit <= distance:
        if distance & bit:
            shift = bit * width
            down = pltpu.roll(x, shift, 1)
            up = pltpu.roll(x, x.shape[1] - shift, 1)
            x = jnp.where((lane // shift) % 2 == 1, down, up)
        bit *= 2
    return x


def weights_body(at_ref, score_ref, cand_ref, stat_ref, table_ref, mix_ref, norm_ref):
    n_cls, _, total = stat_ref.shape
    width = total // n_cls
    tops, parts = [], []
    for e in range(n_cls):
        table = stat_ref[at_ref[0] ^ e]
        table = swap_blocks(jnp.concatenate([table] * 4, 0), e, width)
        tops.append(table[0:1])
        parts.append(table[1:2])
    top = functools.reduce(jnp.maximum, tops)
    summed = jnp.zeros_like(top)
    for other, part in zip(tops, parts):
        summed += part * jnp.exp(other - top)
    log_norm = top + jnp.log(summed)
    norm_ref[...] = log_norm
    weight = jnp.where(cand_ref[0:1, :] >= 0.0, jnp.exp(score_ref[...] - log_norm), 0.0)
    mix_ref[...] = lax.dot_general(
        table_ref[...],
        weight,
        (((1,), (0,)), ((), ())),
        precision=lax.Precision.HIGHEST,
        preferred_element_type=jnp.float32,
    )


def mixed_weights(cls, score, cand, stats, table):
    total = score.shape[1]
    return pl.pallas_call(
        weights_body,
        in_specs=[pl.BlockSpec(memory_space=pltpu.SMEM)] + [pl.BlockSpec(memory_space=pltpu.VMEM)] * 4,
        out_shape=[
            jax.ShapeDtypeStruct((COEF, total), jnp.float32),
            jax.ShapeDtypeStruct((1, total), jnp.float32),
        ],
        name="mixed_weights",
    )(cls, score, cand, stats, table)


def sums_body(*refs, number, pieces):
    blocks, extras = refs[:number], refs[number : 2 * number]
    refs = refs[2 * number :]
    mixes, cands = refs[:pieces], refs[pieces : 2 * pieces]
    back_ref, out_ref, weight_ref, mix, cand, planes = refs[2 * pieces :]
    i = pl.program_id(0)
    groups = weight_ref.shape[0]
    total = mix.shape[1]
    imag, odd = lane_signs()

    @pl.when(i == 0)
    def _():
        mixed = jnp.concatenate([ref[...] for ref in mixes], 1)
        chosen = jnp.concatenate([ref[...] for ref in cands], 1)
        hot = hot_masks(chosen, groups)
        summed = jnp.zeros((groups, total), jnp.float32)
        for q in range(CAND_OWN):
            summed += jnp.where(hot[q], mixed[q : q + 1], 0.0)
        weight_ref[...] = jnp.sum(summed, axis=1, keepdims=True)
        mix[...] = mixed
        cand[...] = chosen

    @pl.when(i < HALF // SUM_STEP)
    def _():
        hot = hot_masks(cand[...], groups)
        block = 2 * CAND_OWN
        sign = jnp.where(imag == odd, 1.0, -1.0)
        for u in range(SUM_STEP):
            g = i * SUM_STEP + u
            mine = mix[pl.ds(pl.multiple_of(g * block, block), block), :]
            halves = []
            for ab in range(2):
                dense = jnp.zeros((groups, total), jnp.float32)
                for q in range(CAND_OWN):
                    at = ab * CAND_OWN + q
                    dense = jnp.where(hot[q], mine[at : at + 1], dense)
                halves.append(dense)
            weights = jnp.concatenate(halves, 0).astype(jnp.bfloat16)
            made = jnp.dot(
                weights, lanes_of(blocks, u * TURNS, TURNS), preferred_element_type=jnp.float32
            )
            for t in range(TURNS):
                g1 = made[:groups, t * LANES : (t + 1) * LANES]
                g2 = made[groups:, t * LANES : (t + 1) * LANES]
                value = g1 + sign * pltpu.roll(g2, LANES // 2, 1)
                if u == 0:
                    value = jnp.where(i == 0, jnp.where(odd, g2, g1), value)
                start = pl.multiple_of((g * TURNS + t) * groups, groups)
                planes[pl.ds(start, groups), :] = value

            for t in range(TAIL):
                if t % SUM_STEP != u:
                    continue

                @pl.when(g == t)
                def _():
                    made = jnp.dot(
                        weights, lanes_of(extras, t // 2, 1), preferred_element_type=jnp.float32
                    )
                    g1, g2 = made[:groups], made[groups:]
                    value = g1
                    if t > 0:
                        value = g1 + jnp.where(imag, -1.0, 1.0) * pltpu.roll(g2, LANES // 2, 1)
                    rows = pl.ds((BODY + t // 2) * groups, groups)
                    if t % 2:
                        value = jnp.where(odd, value, planes[rows, :])
                    planes[rows, :] = value

    @pl.when(i >= HALF // SUM_STEP)
    def _():
        block, span, _ = out_ref.shape
        first = (i - HALF // SUM_STEP) * block
        back = back_ref[...]
        for c in range(block):
            turned = planes[pl.ds(first + c, CHUNKS, stride=groups), :].T
            parts = []
            for s in range(2):
                at = 2 * s * span
                parts.append(
                    jnp.concatenate([turned[at : at + span], turned[at + span : at + 2 * span]], 1)
                )
            value = jnp.concatenate(parts, 0)
            high = value.astype(jnp.bfloat16)
            low = (value - high.astype(jnp.float32)).astype(jnp.bfloat16)
            placed = jnp.dot(high, back, preferred_element_type=jnp.float32) + jnp.dot(
                low, back, preferred_element_type=jnp.float32
            )
            out_ref[c, :, :HARM] = placed[:span]
            out_ref[c, :, HARM:] = placed[span:]


def sums(blocks, mixes, cands, back, groups, span):
    count = blocks[0].shape[1]
    total = len(blocks) * count
    size = blocks[0].size * len(blocks)
    block = 8
    steps = HALF // SUM_STEP
    whole = lambda i: (0, 0)
    return pl.pallas_call(
        functools.partial(sums_body, number=len(blocks), pieces=len(mixes)),
        grid=(steps + groups // block,),
        in_specs=[
            *[
                pl.BlockSpec(
                    (SUM_STEP * TURNS, count, LANES), lambda i: (jnp.minimum(i, steps - 1), 0, 0)
                )
                for _ in blocks
            ],
            *[
                pl.BlockSpec((EXTRA, count, LANES), lambda i: (BODY // EXTRA, 0, 0))
                for _ in blocks
            ],
            *[pl.BlockSpec(array.shape, whole) for array in (*mixes, *cands, back)],
        ],
        out_specs=[
            pl.BlockSpec(
                (block, span, 2 * HARM), lambda i: (jnp.maximum(i - steps, 0), 0, 0)
            ),
            pl.BlockSpec((groups, 1), whole),
        ],
        out_shape=[
            jax.ShapeDtypeStruct((groups, span, 2 * HARM), jnp.float32),
            jax.ShapeDtypeStruct((groups, 1), jnp.float32),
        ],
        scratch_shapes=[
            pltpu.VMEM((COEF, total), jnp.float32),
            pltpu.VMEM((2 * CAND_OWN, total), jnp.float32),
            pltpu.VMEM((CHUNKS * groups, LANES), jnp.float32),
        ],
        compiler_params=pltpu.CompilerParams(vmem_limit_bytes=48 << 20),
        cost_estimate=pl.CostEstimate(
            flops=4 * size * groups,
            bytes_accessed=2 * size + 8 * groups * span * HARM,
            transcendentals=0,
        ),
        name="sums",
    )(*blocks, *blocks, *mixes, *cands, back)


def hop(value, axis, distance):
    size = lax.axis_size(axis)
    return lax.ppermute(value, axis, [(i, i ^ distance) for i in range(size)])


def spread(own, d):
    n_cls = lax.axis_size("cls")
    blocks = {0: own}
    for j in sorted(range(2, n_cls, 2), key=lambda j: bin(j).count("1")):
        bits = [bit for bit in range(1, n_cls.bit_length()) if j >> bit & 1]
        way = 1 << bits[d % len(bits)]
        blocks[j] = hop(blocks[j ^ way], "cls", way)
    for j in range(0, n_cls, 2):
        blocks[j + 1] = hop(blocks[j], "cls", 1)
    return [blocks[j] for j in range(n_cls)]


def gather_device(particles, references, owner_groups, class_order):
    n_cls, n_prt = lax.axis_size("cls"), lax.axis_size("prt")
    cls, prt = lax.axis_index("cls"), lax.axis_index("prt")
    count, cycles, width = particles.shape
    groups = references.shape[0]
    span = cycles // n_prt
    sel = jnp.asarray(selector(), jnp.bfloat16)
    masks = jnp.asarray(side_masks(), jnp.bfloat16)
    back = jnp.asarray(unselector(), jnp.bfloat16)
    table = jnp.asarray(rotation_table())
    picks = class_order[:, :, :CAND_OWN].reshape(count, OWN_TOP * CAND_OWN)
    cls, prt = (index.reshape(1).astype(jnp.int32) for index in (cls, prt))
    outgoing = arrange_particles(prt, particles, owner_groups, picks, n_prt, sel, masks)
    arrived = [hop(block, "prt", d) if d else block for d, block in enumerate(outgoing)]
    blocks = [spread(block, d) for d, block in enumerate(arrived)]
    arranged, norms = arrange_references(references, prt, n_prt, sel, masks)
    scale = 2.0 / math.sqrt(cycles * width)
    coefs, cands = [], []
    for d in range(n_prt):
        coef, cand = cross_coefficients(blocks[d], arranged, norms, cls)
        coefs.append(hop(coef, "prt", d) if d else coef)
        cands.append(cand)
    score, stat = scores(coefs, cands[0], table, scale)
    stats = lax.all_gather(stat.reshape(1, *stat.shape), "cls", axis=0, tiled=True)
    mix, log_norm = mixed_weights(cls, score, cands[0], stats, table)
    mixes = [hop(mix, "prt", d) if d else mix for d in range(n_prt)]
    class_sums, class_weights = sums(
        [block for piece in blocks for block in piece], mixes, cands, back, groups, span
    )
    own = log_norm[0, :count]
    return class_sums, class_weights[:, 0], own


def per_device(particles, references, owner_groups, class_order):
    n_cls, n_prt = lax.axis_size("cls"), lax.axis_size("prt")
    count, cycles, _ = particles.shape
    groups = references.shape[0]
    cap = max(2, 2 * count * OWN_TOP // n_cls)
    powers = n_cls & (n_cls - 1) == 0 and n_prt & (n_prt - 1) == 0
    fits = 4 * cycles == LANES * n_prt and n_cls * CAND_OWN <= LANES and groups % 16 == 0
    fits = fits and powers and n_cls * count == LANES
    plan = gather_device if cap >= count and fits else dispatch_device
    return plan(particles, references, owner_groups, class_order)


def solution(mesh):
    in_specs = (
        P(("cls", "prt"), None, None),
        P("cls", None, None),
        P(("cls", "prt"), None),
        P(("cls", "prt"), None, None),
    )
    out_specs = (P("cls", "prt", None), P("cls"), P(("cls", "prt")))
    return jax.shard_map(
        per_device, mesh=mesh, in_specs=in_specs, out_specs=out_specs, check_vma=False
    )
```

```python
import functools
import math

import jax
import jax.numpy as jnp
import numpy as np
from jax import lax
from jax.experimental import pallas as pl
from jax.experimental.pallas import tpu as pltpu
from jax.sharding import PartitionSpec as P

CYCLES = 128
HARM = 256
ROTS = 36
OWN_TOP = 4
CAND_OWN = 4


lowest = -1e30


def spectral_tables():
    harmonic = jnp.arange(HARM, dtype=jnp.float32)
    angles = 2.0 * math.pi * jnp.arange(ROTS, dtype=jnp.float32) / ROTS
    phase = harmonic[:, None] * angles[None, :]
    forward = jnp.concatenate([jnp.cos(phase), jnp.sin(phase)], 0)
    backward = jnp.concatenate([jnp.cos(phase), -jnp.sin(phase)], 0).T
    return (forward, backward)


def class_accumulate(lanes, mixed):
    l_re = lanes[..., :HARM]
    l_im = lanes[..., HARM:]
    y_re = mixed[..., :HARM]
    y_im = mixed[..., HARM:]
    s_re = jnp.einsum("lrm,lcm->crm", l_re, y_re, preferred_element_type=jnp.float32) - jnp.einsum(
        "lrm,lcm->crm", l_im, y_im, preferred_element_type=jnp.float32
    )
    s_im = jnp.einsum("lrm,lcm->crm", l_re, y_im, preferred_element_type=jnp.float32) + jnp.einsum(
        "lrm,lcm->crm", l_im, y_re, preferred_element_type=jnp.float32
    )
    return jnp.concatenate([s_re, s_im], -1)


def dispatch_device(particles, references, owner_groups, class_order):
    n_cls = lax.axis_size("cls")
    count = particles.shape[0]
    groups = references.shape[0]
    cap = max(2, 2 * count * OWN_TOP // n_cls)
    slots = n_cls * cap
    width = 2 * HARM
    flat_owner = owner_groups.reshape(-1)
    owner_hot = (flat_owner[:, None] == jnp.arange(n_cls, dtype=jnp.int32)[None, :]).astype(
        jnp.int32
    )
    before = jnp.cumsum(owner_hot, axis=0) - owner_hot
    rank = jnp.sum(before * owner_hot, axis=1)
    slot_of = flat_owner * cap + rank
    match = slot_of[None, :] == jnp.arange(slots, dtype=jnp.int32)[:, None]
    member = jnp.any(match.reshape(slots, count, OWN_TOP), axis=2)
    filled = jnp.any(member, axis=1)
    dispatch = member.astype(jnp.bfloat16)
    outgoing = jnp.dot(
        dispatch, particles.reshape(count, CYCLES * width), preferred_element_type=jnp.float32
    )
    outgoing = outgoing.astype(jnp.bfloat16).reshape(n_cls, cap, CYCLES, width)
    match_int = match.astype(jnp.int32)
    picks = class_order[:, :, :CAND_OWN].reshape(count * OWN_TOP, CAND_OWN)
    slot_cand = jnp.where(filled[:, None], jnp.dot(match_int, picks), -1)
    owner_rows = jnp.repeat(jnp.arange(count, dtype=jnp.int32), OWN_TOP)
    slot_pid = jnp.where(filled, jnp.dot(match_int, owner_rows), -1)
    labels_out = jnp.concatenate([slot_cand, slot_pid[:, None]], 1).reshape(
        n_cls, cap, CAND_OWN + 1
    )
    arrived, labels = (
        lax.all_to_all(outgoing, "cls", split_axis=0, concat_axis=0, tiled=True),
        lax.all_to_all(labels_out, "cls", split_axis=0, concat_axis=0, tiled=True),
    )
    lanes = arrived.reshape(slots, CYCLES, width)
    labels = labels.reshape(slots, CAND_OWN + 1)
    forward, backward = spectral_tables()
    scale = 2.0 / math.sqrt(CYCLES * width)
    norms = jnp.sum(jnp.square(references.astype(jnp.float32)), axis=(1, 2))
    l_re = lanes[..., :HARM]
    l_im = lanes[..., HARM:]
    r_re = references[..., :HARM]
    r_im = references[..., HARM:]
    x_re = jnp.einsum("lrm,crm->lcm", l_re, r_re, preferred_element_type=jnp.float32) + jnp.einsum(
        "lrm,crm->lcm", l_im, r_im, preferred_element_type=jnp.float32
    )
    x_im = jnp.einsum("lrm,crm->lcm", l_im, r_re, preferred_element_type=jnp.float32) - jnp.einsum(
        "lrm,crm->lcm", l_re, r_im, preferred_element_type=jnp.float32
    )
    cross = jnp.concatenate([x_re, x_im], -1)
    corr = jnp.dot(
        cross.reshape(slots * groups, width), forward, precision=lax.Precision.HIGHEST
    ).reshape(slots, groups, ROTS)
    score = (corr - 0.5 * norms[None, :, None]) * scale
    candidate = jnp.any(
        labels[:, :CAND_OWN, None] == jnp.arange(groups, dtype=jnp.int32)[None, None, :], axis=1
    )
    part_max = jnp.max(jnp.where(candidate[:, :, None], score, lowest), axis=(1, 2))
    part_sum = jnp.sum(
        jnp.where(candidate[:, :, None], jnp.exp(score - part_max[:, None, None]), 0.0), axis=(1, 2)
    )
    sender_ids = labels[:, CAND_OWN].astype(jnp.float32)
    table_max, table_sum, table_ids = (
        lax.all_gather(part_max.reshape(1, n_cls, cap), "cls", axis=0, tiled=True),
        lax.all_gather(part_sum.reshape(1, n_cls, cap), "cls", axis=0, tiled=True),
        lax.all_gather(sender_ids.reshape(1, n_cls, cap), "cls", axis=0, tiled=True),
    )
    local_ids = jnp.arange(count, dtype=jnp.float32)
    hit = table_ids[..., None] == local_ids
    top = jnp.max(jnp.where(hit, table_max[..., None], lowest), axis=(0, 2))
    total = jnp.sum(
        jnp.where(
            hit, table_sum[..., None] * jnp.exp(table_max[..., None] - top[None, :, None, :]), 0.0
        ),
        axis=(0, 2),
    )
    table_norm = top + jnp.log(total)
    slot_ids = labels[:, CAND_OWN].reshape(n_cls, cap)
    slot_norm = jnp.sum(
        jnp.where(
            slot_ids[..., None] == jnp.arange(count, dtype=jnp.int32), table_norm[:, None, :], 0.0
        ),
        axis=2,
    ).reshape(slots)
    own_norm = lax.dynamic_index_in_dim(table_norm, lax.axis_index("cls"), 0, keepdims=False)
    weight = jnp.where(candidate[:, :, None], jnp.exp(score - slot_norm[:, None, None]), 0.0)
    mixed = (
        jnp.dot(weight.reshape(slots * groups, ROTS), backward, precision=lax.Precision.HIGHEST)
        .astype(jnp.bfloat16)
        .reshape(slots, groups, width)
    )
    class_weights = lax.psum(jnp.sum(weight, axis=(0, 2)), "prt")
    partial_sums = class_accumulate(lanes, mixed)
    class_sums = lax.psum_scatter(partial_sums, "prt", scatter_dimension=1, tiled=True)
    return (class_sums, class_weights, own_norm)


LANES = 128


def harmonic_plan():
    half = ROTS // 2
    turns = HARM // ROTS
    tail = HARM - turns * ROTS
    chunk_of = np.zeros(HARM, np.int32)
    side_of = np.zeros(HARM, np.int32)
    for m in range(HARM):
        turn, rest = divmod(m, ROTS)
        if turn == turns:
            chunk_of[m] = half * turns + rest // 2
            side_of[m] = rest % 2
        elif rest < half:
            chunk_of[m] = rest * turns + turn
        else:
            chunk_of[m] = ((ROTS - rest) % half) * turns + turn
            side_of[m] = 1
    return half, turns, tail, chunk_of, side_of


HALF, TURNS, TAIL, CHUNK_OF, SIDE_OF = harmonic_plan()
BODY = HALF * TURNS
CHUNKS = BODY + TAIL // 2
EXTRA = TAIL // 2 + 1
COEF = 2 * HALF * CAND_OWN
CROSS_STEP = 6
SUM_STEP = 3


def selector():
    return (np.arange(CHUNKS)[:, None] == CHUNK_OF[None, :]).astype(np.float32)


def side_masks():
    return np.stack([SIDE_OF == 0, SIDE_OF == 1]).astype(np.float32)


def unselector():
    sel = selector()
    return np.concatenate([sel * (SIDE_OF == 0), sel * (SIDE_OF == 1)], 0)


def rotation_table():
    table = np.zeros((HALF, 2, CAND_OWN, ROTS, CAND_OWN))
    angle = 2.0 * np.pi * np.arange(ROTS) / ROTS
    for g in range(HALF):
        first = np.cos(g * angle)
        second = np.cos(HALF * angle) if g == 0 else np.sin(g * angle)
        for q in range(CAND_OWN):
            table[g, 0, q, :, q] = first
            table[g, 1, q, :, q] = second
    return table.reshape(COEF, ROTS * CAND_OWN).astype(np.float32)


def nt_dot(a, b):
    return lax.dot_general(a, b, (((1,), (1,)), ((), ())), preferred_element_type=jnp.float32)


def masked_stack(piece, masks):
    parts = []
    for s in range(2):
        for b in range(2):
            parts.append(piece[:, s * HARM : (s + 1) * HARM] * masks[b : b + 1])
    return jnp.concatenate(parts, 0)


def particle_body(at_ref, x_ref, owner_ref, pick_ref, sel_ref, mask_ref, *refs):
    outs, scr = refs[:-1], refs[-1]
    count, cycles, _ = x_ref.shape
    n_prt = len(outs)
    span = cycles // n_prt
    masks = mask_ref[...]

    def one(n, carry):
        parts = []
        for d in range(n_prt):
            start = pl.multiple_of((at_ref[0] ^ d) * span, span)
            parts.append(masked_stack(x_ref[n, pl.ds(start, span), :], masks))
        w = jnp.concatenate(parts, 0)
        y = nt_dot(sel_ref[...], w)
        for p in range(n_prt):
            scr[p, pl.ds(pl.multiple_of(n * CHUNKS, CHUNKS), CHUNKS), :] = y[
                :, p * LANES : (p + 1) * LANES
            ]
        return carry

    lax.fori_loop(0, count, one, 0)

    def two(c, carry):
        for p in range(n_prt):
            outs[p][c] = scr[p, pl.ds(c, count, stride=CHUNKS), :].astype(jnp.bfloat16)
        return carry

    lax.fori_loop(0, CHUNKS, two, 0)
    lane = lax.broadcasted_iota(jnp.int32, (count, LANES), 1)
    label = jnp.full((count, LANES), -1, jnp.int32)
    for t in range(OWN_TOP):
        mine = (lane // CAND_OWN) == owner_ref[:, t : t + 1]
        for q in range(CAND_OWN):
            at = t * CAND_OWN + q
            label = jnp.where(
                mine & (lane % CAND_OWN == q), pick_ref[:, at : at + 1], label
            )
    label = label.astype(jnp.float32).astype(jnp.bfloat16)
    for p in range(n_prt):
        outs[p][CHUNKS] = label


def arrange_particles(prt, particles, owner, picks, n_prt, sel, masks):
    count = particles.shape[0]
    return pl.pallas_call(
        particle_body,
        in_specs=[pl.BlockSpec(memory_space=pltpu.SMEM)] + [pl.BlockSpec(memory_space=pltpu.VMEM)] * 5,
        out_shape=[jax.ShapeDtypeStruct((CHUNKS + 1, count, LANES), jnp.bfloat16)] * n_prt,
        scratch_shapes=[pltpu.VMEM((n_prt, count * CHUNKS, LANES), jnp.float32)],
        compiler_params=pltpu.CompilerParams(vmem_limit_bytes=32 << 20),
        cost_estimate=pl.CostEstimate(
            flops=particles.size * 2 * CHUNKS, bytes_accessed=particles.size * 4, transcendentals=0
        ),
        name="arrange_particles",
    )(prt, particles, owner, picks, sel, masks)


def reference_body(at_ref, x_ref, sel_ref, mask_ref, out_ref, norm_ref, scr):
    rows = x_ref.shape[0]
    masks = mask_ref[...]
    step = 4

    def one(n, carry):
        w = jnp.concatenate([masked_stack(x_ref[n * step + i], masks) for i in range(step)], 0)
        y = nt_dot(sel_ref[...], w)
        for i in range(step):
            scr[pl.ds(pl.multiple_of((n * step + i) * CHUNKS, CHUNKS), CHUNKS), :] = y[
                :, i * LANES : (i + 1) * LANES
            ]
        return carry

    lax.fori_loop(0, rows // step, one, 0)

    def two(c, carry):
        value = scr[pl.ds(c, rows, stride=CHUNKS), :]
        out_ref[c] = value.astype(jnp.bfloat16)
        return carry + value * value

    norm_ref[...] = lax.fori_loop(0, CHUNKS, two, jnp.zeros((rows, LANES), jnp.float32))


def arrange_references(references, prt, n_prt, sel, masks):
    groups, cycles, width = references.shape
    span = cycles // n_prt
    block = 16
    return pl.pallas_call(
        reference_body,
        grid_spec=pltpu.PrefetchScalarGridSpec(
            num_scalar_prefetch=1,
            grid=(groups // block,),
            in_specs=[
                pl.BlockSpec((block, span, width), lambda i, at: (i, at[0], 0)),
                pl.BlockSpec(sel.shape, lambda i, at: (0, 0)),
                pl.BlockSpec(masks.shape, lambda i, at: (0, 0)),
            ],
            out_specs=[
                pl.BlockSpec((CHUNKS, block, LANES), lambda i, at: (0, i, 0)),
                pl.BlockSpec((block, LANES), lambda i, at: (i, 0)),
            ],
            scratch_shapes=[pltpu.VMEM((block * CHUNKS, LANES), jnp.float32)],
        ),
        out_shape=[
            jax.ShapeDtypeStruct((CHUNKS, groups, LANES), jnp.bfloat16),
            jax.ShapeDtypeStruct((groups, LANES), jnp.float32),
        ],
        compiler_params=pltpu.CompilerParams(vmem_limit_bytes=32 << 20),
        cost_estimate=pl.CostEstimate(
            flops=groups * span * width * 2 * CHUNKS,
            bytes_accessed=groups * span * width * 4,
            transcendentals=0,
        ),
        name="arrange_references",
    )(prt, references, sel, masks)


def lane_signs():
    lane = lax.broadcasted_iota(jnp.int32, (1, LANES), 1)
    quarter = LANES // 4
    imag = lane >= 2 * quarter
    odd = (lane // quarter) % 2 == 1
    return imag, odd


def lanes_of(refs, first, number):
    parts = [
        jnp.concatenate([ref[i] for ref in refs], 0) for i in range(first, first + number)
    ]
    return jnp.concatenate(parts, 1) if number > 1 else parts[0]


def hot_masks(cand, groups):
    rows = lax.broadcasted_iota(jnp.int32, (groups, cand.shape[1]), 0).astype(jnp.float32)
    return [rows == cand[q : q + 1] for q in range(CAND_OWN)]


def residue_weights(q_ref, at, g):
    imag, odd = lane_signs()
    sign = jnp.where(imag == odd, -1.0, 1.0)
    first, second = [], []
    for i in range(TURNS):
        q = q_ref[at * TURNS + i].astype(jnp.float32)
        turned = pltpu.roll(q, LANES // 2, 1) * sign
        if at == 0:
            first.append(jnp.where((g == 0) & odd, 0.0, q))
            second.append(jnp.where(g == 0, jnp.where(odd, q, 0.0), turned))
        else:
            first.append(q)
            second.append(turned)
    return jnp.concatenate(
        [jnp.concatenate(first, 1), jnp.concatenate(second, 1)], 0
    ).astype(jnp.bfloat16)


def chosen_rows(acc, cand):
    groups = acc.shape[0] // 2
    hot = hot_masks(cand, groups)
    rows = []
    for ab in range(2):
        part = acc[ab * groups : (ab + 1) * groups, :]
        for q in range(CAND_OWN):
            rows.append(jnp.sum(jnp.where(hot[q], part, 0.0), axis=0, keepdims=True))
    return jnp.concatenate(rows, 0)


def cross_body(at_ref, *refs):
    number = (len(refs) - 6) // 2
    blocks, extras = refs[:number], refs[number : 2 * number]
    q_ref, qt_ref, norm_ref, coef_ref, cand_ref, acc = refs[2 * number :]
    step = pl.program_id(0)
    groups = q_ref.shape[1]
    imag, odd = lane_signs()

    @pl.when(step == 0)
    def _():
        label = lanes_of(extras, TAIL // 2, 1).astype(jnp.float32).T
        row = lax.broadcasted_iota(jnp.int32, label.shape, 0)
        base = at_ref[0] * CAND_OWN
        for q in range(CAND_OWN):
            cand_ref[q : q + 1, :] = jnp.sum(
                jnp.where(row == base + q, label, 0.0), axis=0, keepdims=True
            )
        cand_ref[CAND_OWN:, :] = jnp.full(
            (cand_ref.shape[0] - CAND_OWN, cand_ref.shape[1]), -1.0, jnp.float32
        )

    for u in range(CROSS_STEP):
        g = step * CROSS_STEP + u
        acc[...] = nt_dot(residue_weights(q_ref, u, g), lanes_of(blocks, u * TURNS, TURNS))

        for i in range(TAIL):
            if i % CROSS_STEP != u:
                continue

            @pl.when(g == i)
            def _():
                q = qt_ref[i // 2].astype(jnp.float32)
                keep = odd if i % 2 else ~odd
                a = jnp.where(keep, q, 0.0)
                turned = pltpu.roll(q, LANES // 2, 1) * jnp.where(imag, 1.0, -1.0)
                b = jnp.where(keep, turned, 0.0)
                if i == 0:
                    b = jnp.zeros_like(b)
                w = jnp.concatenate([a, b], 0).astype(jnp.bfloat16)
                acc[...] += nt_dot(w, lanes_of(extras, i // 2, 1))
                if i == 0:
                    acc[:groups, :] -= 0.5 * jnp.sum(norm_ref[...], axis=1, keepdims=True)

        block = 2 * CAND_OWN
        coef_ref[u * block : (u + 1) * block, :] = chosen_rows(acc[...], cand_ref[...])


def cross_coefficients(blocks, arranged, norms, cls):
    count = blocks[0].shape[1]
    groups = arranged.shape[1]
    total = len(blocks) * count
    half_tail = TAIL // 2
    size = blocks[0].size * len(blocks)
    block = 2 * CAND_OWN
    return pl.pallas_call(
        cross_body,
        grid_spec=pltpu.PrefetchScalarGridSpec(
            num_scalar_prefetch=1,
            grid=(HALF // CROSS_STEP,),
            in_specs=[
                *[
                    pl.BlockSpec((CROSS_STEP * TURNS, count, LANES), lambda g, at: (g, 0, 0))
                    for _ in blocks
                ],
                *[
                    pl.BlockSpec((EXTRA, count, LANES), lambda g, at: (BODY // EXTRA, 0, 0))
                    for _ in blocks
                ],
                pl.BlockSpec((CROSS_STEP * TURNS, groups, LANES), lambda g, at: (g, 0, 0)),
                pl.BlockSpec((half_tail, groups, LANES), lambda g, at: (BODY // half_tail, 0, 0)),
                pl.BlockSpec((groups, LANES), lambda g, at: (0, 0)),
            ],
            out_specs=[
                pl.BlockSpec((CROSS_STEP * block, total), lambda g, at: (g, 0)),
                pl.BlockSpec((block, total), lambda g, at: (0, 0)),
            ],
            scratch_shapes=[pltpu.VMEM((2 * groups, total), jnp.float32)],
        ),
        out_shape=[
            jax.ShapeDtypeStruct((COEF, total), jnp.float32),
            jax.ShapeDtypeStruct((block, total), jnp.float32),
        ],
        compiler_params=pltpu.CompilerParams(vmem_limit_bytes=60 << 20),
        cost_estimate=pl.CostEstimate(
            flops=4 * size * groups, bytes_accessed=2 * size, transcendentals=0
        ),
        name="cross_coefficients",
    )(cls, *blocks, *blocks, arranged, arranged, norms)


def score_body(*refs, scale):
    *coefs, cand_ref, table_ref, score_ref, stat_ref = refs
    corr = lax.dot_general(
        table_ref[...],
        functools.reduce(jnp.add, [ref[...] for ref in coefs]),
        (((0,), (0,)), ((), ())),
        precision=lax.Precision.HIGHEST,
        preferred_element_type=jnp.float32,
    )
    score = jnp.where(cand_ref[0:1, :] >= 0.0, corr * scale, lowest)
    top = jnp.max(score, axis=0, keepdims=True)
    total = jnp.sum(jnp.exp(score - top), axis=0, keepdims=True)
    score_ref[...] = score
    stat_ref[0:1, :] = top
    stat_ref[1:2, :] = jnp.where(cand_ref[0:1, :] >= 0.0, total, 0.0)


def scores(coefs, cand, table, scale):
    total = cand.shape[1]
    return pl.pallas_call(
        functools.partial(score_body, scale=scale),
        out_shape=[
            jax.ShapeDtypeStruct((ROTS * CAND_OWN, total), jnp.float32),
            jax.ShapeDtypeStruct((2, total), jnp.float32),
        ],
        name="scores",
    )(*coefs, cand, table)


def swap_blocks(x, distance, width):
    lane = lax.broadcasted_iota(jnp.int32, x.shape, 1)
    bit = 1
    while bit <= distance:
        if distance & bit:
            shift = bit * width
            down = pltpu.roll(x, shift, 1)
            up = pltpu.roll(x, x.shape[1] - shift, 1)
            x = jnp.where((lane // shift) % 2 == 1, down, up)
        bit *= 2
    return x


def weights_body(at_ref, score_ref, cand_ref, stat_ref, table_ref, mix_ref, norm_ref):
    n_cls, _, total = stat_ref.shape
    width = total // n_cls
    tops, parts = [], []
    for e in range(n_cls):
        table = stat_ref[at_ref[0] ^ e]
        table = swap_blocks(jnp.concatenate([table] * 4, 0), e, width)
        tops.append(table[0:1])
        parts.append(table[1:2])
    top = functools.reduce(jnp.maximum, tops)
    summed = jnp.zeros_like(top)
    for other, part in zip(tops, parts):
        summed += part * jnp.exp(other - top)
    log_norm = top + jnp.log(summed)
    norm_ref[...] = log_norm
    weight = jnp.where(cand_ref[0:1, :] >= 0.0, jnp.exp(score_ref[...] - log_norm), 0.0)
    mix_ref[...] = lax.dot_general(
        table_ref[...],
        weight,
        (((1,), (0,)), ((), ())),
        precision=lax.Precision.HIGHEST,
        preferred_element_type=jnp.float32,
    )


def mixed_weights(cls, score, cand, stats, table):
    total = score.shape[1]
    return pl.pallas_call(
        weights_body,
        in_specs=[pl.BlockSpec(memory_space=pltpu.SMEM)] + [pl.BlockSpec(memory_space=pltpu.VMEM)] * 4,
        out_shape=[
            jax.ShapeDtypeStruct((COEF, total), jnp.float32),
            jax.ShapeDtypeStruct((1, total), jnp.float32),
        ],
        name="mixed_weights",
    )(cls, score, cand, stats, table)


def sums_body(*refs, number, pieces):
    blocks, extras = refs[:number], refs[number : 2 * number]
    refs = refs[2 * number :]
    mixes, cands = refs[:pieces], refs[pieces : 2 * pieces]
    back_ref, out_ref, weight_ref, mix, cand, planes = refs[2 * pieces :]
    i = pl.program_id(0)
    groups = weight_ref.shape[0]
    total = mix.shape[1]
    imag, odd = lane_signs()

    @pl.when(i == 0)
    def _():
        mixed = jnp.concatenate([ref[...] for ref in mixes], 1)
        chosen = jnp.concatenate([ref[...] for ref in cands], 1)
        hot = hot_masks(chosen, groups)
        summed = jnp.zeros((groups, total), jnp.float32)
        for q in range(CAND_OWN):
            summed += jnp.where(hot[q], mixed[q : q + 1], 0.0)
        weight_ref[...] = jnp.sum(summed, axis=1, keepdims=True)
        mix[...] = mixed
        cand[...] = chosen

    @pl.when(i < HALF // SUM_STEP)
    def _():
        hot = hot_masks(cand[...], groups)
        block = 2 * CAND_OWN
        sign = jnp.where(imag == odd, 1.0, -1.0)
        for u in range(SUM_STEP):
            g = i * SUM_STEP + u
            mine = mix[pl.ds(pl.multiple_of(g * block, block), block), :]
            halves = []
            for ab in range(2):
                dense = jnp.zeros((groups, total), jnp.float32)
                for q in range(CAND_OWN):
                    at = ab * CAND_OWN + q
                    dense = jnp.where(hot[q], mine[at : at + 1], dense)
                halves.append(dense)
            weights = jnp.concatenate(halves, 0).astype(jnp.bfloat16)
            made = jnp.dot(
                weights, lanes_of(blocks, u * TURNS, TURNS), preferred_element_type=jnp.float32
            )
            for t in range(TURNS):
                g1 = made[:groups, t * LANES : (t + 1) * LANES]
                g2 = made[groups:, t * LANES : (t + 1) * LANES]
                value = g1 + sign * pltpu.roll(g2, LANES // 2, 1)
                if u == 0:
                    value = jnp.where(i == 0, jnp.where(odd, g2, g1), value)
                start = pl.multiple_of((g * TURNS + t) * groups, groups)
                planes[pl.ds(start, groups), :] = value

            for t in range(TAIL):
                if t % SUM_STEP != u:
                    continue

                @pl.when(g == t)
                def _():
                    made = jnp.dot(
                        weights, lanes_of(extras, t // 2, 1), preferred_element_type=jnp.float32
                    )
                    g1, g2 = made[:groups], made[groups:]
                    value = g1
                    if t > 0:
                        value = g1 + jnp.where(imag, -1.0, 1.0) * pltpu.roll(g2, LANES // 2, 1)
                    rows = pl.ds((BODY + t // 2) * groups, groups)
                    if t % 2:
                        value = jnp.where(odd, value, planes[rows, :])
                    planes[rows, :] = value

    @pl.when(i >= HALF // SUM_STEP)
    def _():
        block, span, _ = out_ref.shape
        first = (i - HALF // SUM_STEP) * block
        back = back_ref[...]
        for c in range(block):
            turned = planes[pl.ds(first + c, CHUNKS, stride=groups), :].T
            parts = []
            for s in range(2):
                at = 2 * s * span
                parts.append(
                    jnp.concatenate([turned[at : at + span], turned[at + span : at + 2 * span]], 1)
                )
            value = jnp.concatenate(parts, 0)
            high = value.astype(jnp.bfloat16)
            low = (value - high.astype(jnp.float32)).astype(jnp.bfloat16)
            placed = jnp.dot(high, back, preferred_element_type=jnp.float32) + jnp.dot(
                low, back, preferred_element_type=jnp.float32
            )
            out_ref[c, :, :HARM] = placed[:span]
            out_ref[c, :, HARM:] = placed[span:]


def sums(blocks, mixes, cands, back, groups, span):
    count = blocks[0].shape[1]
    total = len(blocks) * count
    size = blocks[0].size * len(blocks)
    block = 8
    steps = HALF // SUM_STEP
    whole = lambda i: (0, 0)
    return pl.pallas_call(
        functools.partial(sums_body, number=len(blocks), pieces=len(mixes)),
        grid=(steps + groups // block,),
        in_specs=[
            *[
                pl.BlockSpec(
                    (SUM_STEP * TURNS, count, LANES), lambda i: (jnp.minimum(i, steps - 1), 0, 0)
                )
                for _ in blocks
            ],
            *[
                pl.BlockSpec((EXTRA, count, LANES), lambda i: (BODY // EXTRA, 0, 0))
                for _ in blocks
            ],
            *[pl.BlockSpec(array.shape, whole) for array in (*mixes, *cands, back)],
        ],
        out_specs=[
            pl.BlockSpec(
                (block, span, 2 * HARM), lambda i: (jnp.maximum(i - steps, 0), 0, 0)
            ),
            pl.BlockSpec((groups, 1), whole),
        ],
        out_shape=[
            jax.ShapeDtypeStruct((groups, span, 2 * HARM), jnp.float32),
            jax.ShapeDtypeStruct((groups, 1), jnp.float32),
        ],
        scratch_shapes=[
            pltpu.VMEM((COEF, total), jnp.float32),
            pltpu.VMEM((2 * CAND_OWN, total), jnp.float32),
            pltpu.VMEM((CHUNKS * groups, LANES), jnp.float32),
        ],
        compiler_params=pltpu.CompilerParams(vmem_limit_bytes=60 << 20),
        cost_estimate=pl.CostEstimate(
            flops=4 * size * groups,
            bytes_accessed=2 * size + 8 * groups * span * HARM,
            transcendentals=0,
        ),
        name="sums",
    )(*blocks, *blocks, *mixes, *cands, back)


def hop(value, axis, distance):
    size = lax.axis_size(axis)
    return lax.ppermute(value, axis, [(i, i ^ distance) for i in range(size)])


def after(value, *others):
    return lax.optimization_barrier((value, *others))[0]


def direct(own):
    n_cls = lax.axis_size("cls")
    return {1 << bit: hop(own, "cls", 1 << bit) for bit in range(1, n_cls.bit_length() - 1)}


def relayed(known, d, *others):
    n_cls = lax.axis_size("cls")
    for j in sorted(range(2, n_cls, 2), key=lambda j: bin(j).count("1")):
        if j not in known:
            bits = [bit for bit in range(1, n_cls.bit_length()) if j >> bit & 1]
            way = 1 << bits[d % len(bits)]
            known[j] = hop(after(known[j ^ way], *others), "cls", way)
    return known


def paired(known, *others):
    n_cls = lax.axis_size("cls")
    last = n_cls - 2
    for j in range(0, n_cls, 2):
        block = after(known[j], *others) if j == last and others else known[j]
        known[j + 1] = hop(block, "cls", 1)
    return [known[j] for j in range(n_cls)]


def gather_device(particles, references, owner_groups, class_order):
    n_cls, n_prt = lax.axis_size("cls"), lax.axis_size("prt")
    cls, prt = lax.axis_index("cls"), lax.axis_index("prt")
    count, cycles, width = particles.shape
    groups = references.shape[0]
    span = cycles // n_prt
    sel = jnp.asarray(selector(), jnp.bfloat16)
    masks = jnp.asarray(side_masks(), jnp.bfloat16)
    back = jnp.asarray(unselector(), jnp.bfloat16)
    table = jnp.asarray(rotation_table())
    picks = class_order[:, :, :CAND_OWN].reshape(count, OWN_TOP * CAND_OWN)
    cls, prt = (index.reshape(1).astype(jnp.int32) for index in (cls, prt))
    outgoing = arrange_particles(prt, particles, owner_groups, picks, n_prt, sel, masks)
    arrived = list(outgoing)
    known = []
    for d in range(n_prt):
        if d:
            block = outgoing[d] if d < 3 else after(outgoing[d], arrived[d - 1])
            arrived[d] = hop(block, "prt", d)
        if d == 0:
            known.append({0: arrived[0], **direct(arrived[0])})
    arranged, norms = arrange_references(references, prt, n_prt, sel, masks)
    scale = 2.0 / math.sqrt(cycles * width)
    coefs, cands, sent, blocks = [], [], [], []
    for d in range(n_prt):
        if d:
            own = after(arrived[d], coefs[0]) if d == 2 else arrived[d]
            known.append({0: arrived[d], **direct(own)})
        waits = [arranged] if d == 0 else [coefs[d - 1]] if d == 2 else []
        relayed(known[d], d, *waits)
        blocks.append(paired(known[d], *([coefs[d - 1]] if d == n_prt - 1 else [])))
        coef, cand = cross_coefficients(blocks[d], arranged, norms, cls)
        coefs.append(coef)
        sent.append(hop(coef, "prt", d) if d else coef)
        cands.append(cand)
    score, stat = scores(sent, cands[0], table, scale)
    stats = lax.all_gather(stat.reshape(1, *stat.shape), "cls", axis=0, tiled=True)
    mix, log_norm = mixed_weights(cls, score, cands[0], stats, table)
    mixes = [hop(mix, "prt", d) if d else mix for d in range(n_prt)]
    class_sums, class_weights = sums(
        [block for piece in blocks for block in piece], mixes, cands, back, groups, span
    )
    own = log_norm[0, :count]
    return class_sums, class_weights[:, 0], own


def per_device(particles, references, owner_groups, class_order):
    n_cls, n_prt = lax.axis_size("cls"), lax.axis_size("prt")
    count, cycles, _ = particles.shape
    groups = references.shape[0]
    cap = max(2, 2 * count * OWN_TOP // n_cls)
    powers = n_cls & (n_cls - 1) == 0 and n_prt & (n_prt - 1) == 0
    fits = 4 * cycles == LANES * n_prt and n_cls * CAND_OWN <= LANES and groups % 16 == 0
    fits = fits and powers and n_cls * count == LANES
    plan = gather_device if cap >= count and fits else dispatch_device
    return plan(particles, references, owner_groups, class_order)


def solution(mesh):
    in_specs = (
        P(("cls", "prt"), None, None),
        P("cls", None, None),
        P(("cls", "prt"), None),
        P(("cls", "prt"), None, None),
    )
    out_specs = (P("cls", "prt", None), P("cls"), P(("cls", "prt")))
    return jax.shard_map(
        per_device, mesh=mesh, in_specs=in_specs, out_specs=out_specs, check_vma=False
    )
```

```python
import functools
import math

import jax
import jax.numpy as jnp
import numpy as np
from jax import lax
from jax.experimental import pallas as pl
from jax.experimental.pallas import tpu as pltpu
from jax.sharding import PartitionSpec as P

CYCLES = 128
HARM = 256
ROTS = 36
OWN_TOP = 4
CAND_OWN = 4


lowest = -1e30


def spectral_tables():
    harmonic = jnp.arange(HARM, dtype=jnp.float32)
    angles = 2.0 * math.pi * jnp.arange(ROTS, dtype=jnp.float32) / ROTS
    phase = harmonic[:, None] * angles[None, :]
    forward = jnp.concatenate([jnp.cos(phase), jnp.sin(phase)], 0)
    backward = jnp.concatenate([jnp.cos(phase), -jnp.sin(phase)], 0).T
    return (forward, backward)


def class_accumulate(lanes, mixed):
    l_re = lanes[..., :HARM]
    l_im = lanes[..., HARM:]
    y_re = mixed[..., :HARM]
    y_im = mixed[..., HARM:]
    s_re = jnp.einsum("lrm,lcm->crm", l_re, y_re, preferred_element_type=jnp.float32) - jnp.einsum(
        "lrm,lcm->crm", l_im, y_im, preferred_element_type=jnp.float32
    )
    s_im = jnp.einsum("lrm,lcm->crm", l_re, y_im, preferred_element_type=jnp.float32) + jnp.einsum(
        "lrm,lcm->crm", l_im, y_re, preferred_element_type=jnp.float32
    )
    return jnp.concatenate([s_re, s_im], -1)


def dispatch_device(particles, references, owner_groups, class_order):
    n_cls = lax.axis_size("cls")
    count = particles.shape[0]
    groups = references.shape[0]
    cap = max(2, 2 * count * OWN_TOP // n_cls)
    slots = n_cls * cap
    width = 2 * HARM
    flat_owner = owner_groups.reshape(-1)
    owner_hot = (flat_owner[:, None] == jnp.arange(n_cls, dtype=jnp.int32)[None, :]).astype(
        jnp.int32
    )
    before = jnp.cumsum(owner_hot, axis=0) - owner_hot
    rank = jnp.sum(before * owner_hot, axis=1)
    slot_of = flat_owner * cap + rank
    match = slot_of[None, :] == jnp.arange(slots, dtype=jnp.int32)[:, None]
    member = jnp.any(match.reshape(slots, count, OWN_TOP), axis=2)
    filled = jnp.any(member, axis=1)
    dispatch = member.astype(jnp.bfloat16)
    outgoing = jnp.dot(
        dispatch, particles.reshape(count, CYCLES * width), preferred_element_type=jnp.float32
    )
    outgoing = outgoing.astype(jnp.bfloat16).reshape(n_cls, cap, CYCLES, width)
    match_int = match.astype(jnp.int32)
    picks = class_order[:, :, :CAND_OWN].reshape(count * OWN_TOP, CAND_OWN)
    slot_cand = jnp.where(filled[:, None], jnp.dot(match_int, picks), -1)
    owner_rows = jnp.repeat(jnp.arange(count, dtype=jnp.int32), OWN_TOP)
    slot_pid = jnp.where(filled, jnp.dot(match_int, owner_rows), -1)
    labels_out = jnp.concatenate([slot_cand, slot_pid[:, None]], 1).reshape(
        n_cls, cap, CAND_OWN + 1
    )
    arrived, labels = (
        lax.all_to_all(outgoing, "cls", split_axis=0, concat_axis=0, tiled=True),
        lax.all_to_all(labels_out, "cls", split_axis=0, concat_axis=0, tiled=True),
    )
    lanes = arrived.reshape(slots, CYCLES, width)
    labels = labels.reshape(slots, CAND_OWN + 1)
    forward, backward = spectral_tables()
    scale = 2.0 / math.sqrt(CYCLES * width)
    norms = jnp.sum(jnp.square(references.astype(jnp.float32)), axis=(1, 2))
    l_re = lanes[..., :HARM]
    l_im = lanes[..., HARM:]
    r_re = references[..., :HARM]
    r_im = references[..., HARM:]
    x_re = jnp.einsum("lrm,crm->lcm", l_re, r_re, preferred_element_type=jnp.float32) + jnp.einsum(
        "lrm,crm->lcm", l_im, r_im, preferred_element_type=jnp.float32
    )
    x_im = jnp.einsum("lrm,crm->lcm", l_im, r_re, preferred_element_type=jnp.float32) - jnp.einsum(
        "lrm,crm->lcm", l_re, r_im, preferred_element_type=jnp.float32
    )
    cross = jnp.concatenate([x_re, x_im], -1)
    corr = jnp.dot(
        cross.reshape(slots * groups, width), forward, precision=lax.Precision.HIGHEST
    ).reshape(slots, groups, ROTS)
    score = (corr - 0.5 * norms[None, :, None]) * scale
    candidate = jnp.any(
        labels[:, :CAND_OWN, None] == jnp.arange(groups, dtype=jnp.int32)[None, None, :], axis=1
    )
    part_max = jnp.max(jnp.where(candidate[:, :, None], score, lowest), axis=(1, 2))
    part_sum = jnp.sum(
        jnp.where(candidate[:, :, None], jnp.exp(score - part_max[:, None, None]), 0.0), axis=(1, 2)
    )
    sender_ids = labels[:, CAND_OWN].astype(jnp.float32)
    table_max, table_sum, table_ids = (
        lax.all_gather(part_max.reshape(1, n_cls, cap), "cls", axis=0, tiled=True),
        lax.all_gather(part_sum.reshape(1, n_cls, cap), "cls", axis=0, tiled=True),
        lax.all_gather(sender_ids.reshape(1, n_cls, cap), "cls", axis=0, tiled=True),
    )
    local_ids = jnp.arange(count, dtype=jnp.float32)
    hit = table_ids[..., None] == local_ids
    top = jnp.max(jnp.where(hit, table_max[..., None], lowest), axis=(0, 2))
    total = jnp.sum(
        jnp.where(
            hit, table_sum[..., None] * jnp.exp(table_max[..., None] - top[None, :, None, :]), 0.0
        ),
        axis=(0, 2),
    )
    table_norm = top + jnp.log(total)
    slot_ids = labels[:, CAND_OWN].reshape(n_cls, cap)
    slot_norm = jnp.sum(
        jnp.where(
            slot_ids[..., None] == jnp.arange(count, dtype=jnp.int32), table_norm[:, None, :], 0.0
        ),
        axis=2,
    ).reshape(slots)
    own_norm = lax.dynamic_index_in_dim(table_norm, lax.axis_index("cls"), 0, keepdims=False)
    weight = jnp.where(candidate[:, :, None], jnp.exp(score - slot_norm[:, None, None]), 0.0)
    mixed = (
        jnp.dot(weight.reshape(slots * groups, ROTS), backward, precision=lax.Precision.HIGHEST)
        .astype(jnp.bfloat16)
        .reshape(slots, groups, width)
    )
    class_weights = lax.psum(jnp.sum(weight, axis=(0, 2)), "prt")
    partial_sums = class_accumulate(lanes, mixed)
    class_sums = lax.psum_scatter(partial_sums, "prt", scatter_dimension=1, tiled=True)
    return (class_sums, class_weights, own_norm)


LANES = 128


def harmonic_plan():
    half = ROTS // 2
    turns = HARM // ROTS
    tail = HARM - turns * ROTS
    chunk_of = np.zeros(HARM, np.int32)
    side_of = np.zeros(HARM, np.int32)
    for m in range(HARM):
        turn, rest = divmod(m, ROTS)
        if turn == turns:
            chunk_of[m] = half * turns + rest // 2
            side_of[m] = rest % 2
        elif rest < half:
            chunk_of[m] = rest * turns + turn
        else:
            chunk_of[m] = ((ROTS - rest) % half) * turns + turn
            side_of[m] = 1
    return half, turns, tail, chunk_of, side_of


HALF, TURNS, TAIL, CHUNK_OF, SIDE_OF = harmonic_plan()
BODY = HALF * TURNS
CHUNKS = BODY + TAIL // 2
EXTRA = TAIL // 2 + 1
COEF = 2 * HALF * CAND_OWN
CROSS_STEP = 6
SUM_STEP = 3


def selector():
    return (np.arange(CHUNKS)[:, None] == CHUNK_OF[None, :]).astype(np.float32)


def side_masks():
    return np.stack([SIDE_OF == 0, SIDE_OF == 1]).astype(np.float32)


def unselector():
    sel = selector()
    return np.concatenate([sel * (SIDE_OF == 0), sel * (SIDE_OF == 1)], 0)


def rotation_table():
    table = np.zeros((HALF, 2, CAND_OWN, ROTS, CAND_OWN))
    angle = 2.0 * np.pi * np.arange(ROTS) / ROTS
    for g in range(HALF):
        first = np.cos(g * angle)
        second = np.cos(HALF * angle) if g == 0 else np.sin(g * angle)
        for q in range(CAND_OWN):
            table[g, 0, q, :, q] = first
            table[g, 1, q, :, q] = second
    return table.reshape(COEF, ROTS * CAND_OWN).astype(np.float32)


def nt_dot(a, b):
    return lax.dot_general(a, b, (((1,), (1,)), ((), ())), preferred_element_type=jnp.float32)


def masked_stack(piece, masks):
    parts = []
    for s in range(2):
        for b in range(2):
            parts.append(piece[:, s * HARM : (s + 1) * HARM] * masks[b : b + 1])
    return jnp.concatenate(parts, 0)


def particle_body(at_ref, x_ref, owner_ref, pick_ref, sel_ref, mask_ref, *refs, distances, n_prt):
    outs, scr = refs[:-1], refs[-1]
    count, cycles, _ = x_ref.shape
    number = len(outs)
    span = cycles // n_prt
    masks = mask_ref[...]

    def one(n, carry):
        parts = []
        for d in distances:
            start = pl.multiple_of((at_ref[0] ^ d) * span, span)
            parts.append(masked_stack(x_ref[n, pl.ds(start, span), :], masks))
        w = jnp.concatenate(parts, 0)
        y = nt_dot(sel_ref[...], w)
        for p in range(number):
            scr[p, pl.ds(pl.multiple_of(n * CHUNKS, CHUNKS), CHUNKS), :] = y[
                :, p * LANES : (p + 1) * LANES
            ]
        return carry

    lax.fori_loop(0, count, one, 0)

    def two(c, carry):
        for p in range(number):
            outs[p][c] = scr[p, pl.ds(c, count, stride=CHUNKS), :].astype(jnp.bfloat16)
        return carry

    lax.fori_loop(0, CHUNKS, two, 0)
    lane = lax.broadcasted_iota(jnp.int32, (count, LANES), 1)
    label = jnp.full((count, LANES), -1, jnp.int32)
    for t in range(OWN_TOP):
        mine = (lane // CAND_OWN) == owner_ref[:, t : t + 1]
        for q in range(CAND_OWN):
            at = t * CAND_OWN + q
            label = jnp.where(
                mine & (lane % CAND_OWN == q), pick_ref[:, at : at + 1], label
            )
    label = label.astype(jnp.float32).astype(jnp.bfloat16)
    for p in range(number):
        outs[p][CHUNKS] = label


def arrange_particles(prt, particles, owner, picks, n_prt, distances, sel, masks):
    count = particles.shape[0]
    number = len(distances)
    size = particles.size * number // n_prt
    return pl.pallas_call(
        functools.partial(particle_body, distances=distances, n_prt=n_prt),
        in_specs=[pl.BlockSpec(memory_space=pltpu.SMEM)] + [pl.BlockSpec(memory_space=pltpu.VMEM)] * 5,
        out_shape=[jax.ShapeDtypeStruct((CHUNKS + 1, count, LANES), jnp.bfloat16)] * number,
        scratch_shapes=[pltpu.VMEM((number, count * CHUNKS, LANES), jnp.float32)],
        compiler_params=pltpu.CompilerParams(vmem_limit_bytes=32 << 20),
        cost_estimate=pl.CostEstimate(
            flops=size * 2 * CHUNKS, bytes_accessed=size * 4, transcendentals=0
        ),
        name="arrange_particles",
    )(prt, particles, owner, picks, sel, masks)


def reference_body(at_ref, x_ref, sel_ref, mask_ref, out_ref, norm_ref, scr):
    rows = x_ref.shape[0]
    masks = mask_ref[...]
    step = 4

    def one(n, carry):
        w = jnp.concatenate([masked_stack(x_ref[n * step + i], masks) for i in range(step)], 0)
        y = nt_dot(sel_ref[...], w)
        for i in range(step):
            scr[pl.ds(pl.multiple_of((n * step + i) * CHUNKS, CHUNKS), CHUNKS), :] = y[
                :, i * LANES : (i + 1) * LANES
            ]
        return carry

    lax.fori_loop(0, rows // step, one, 0)

    def two(c, carry):
        value = scr[pl.ds(c, rows, stride=CHUNKS), :]
        out_ref[c] = value.astype(jnp.bfloat16)
        return carry + value * value

    norm_ref[...] = lax.fori_loop(0, CHUNKS, two, jnp.zeros((rows, LANES), jnp.float32))


def arrange_references(references, prt, n_prt, sel, masks):
    groups, cycles, width = references.shape
    span = cycles // n_prt
    block = 16
    return pl.pallas_call(
        reference_body,
        grid_spec=pltpu.PrefetchScalarGridSpec(
            num_scalar_prefetch=1,
            grid=(groups // block,),
            in_specs=[
                pl.BlockSpec((block, span, width), lambda i, at: (i, at[0], 0)),
                pl.BlockSpec(sel.shape, lambda i, at: (0, 0)),
                pl.BlockSpec(masks.shape, lambda i, at: (0, 0)),
            ],
            out_specs=[
                pl.BlockSpec((CHUNKS, block, LANES), lambda i, at: (0, i, 0)),
                pl.BlockSpec((block, LANES), lambda i, at: (i, 0)),
            ],
            scratch_shapes=[pltpu.VMEM((block * CHUNKS, LANES), jnp.float32)],
        ),
        out_shape=[
            jax.ShapeDtypeStruct((CHUNKS, groups, LANES), jnp.bfloat16),
            jax.ShapeDtypeStruct((groups, LANES), jnp.float32),
        ],
        compiler_params=pltpu.CompilerParams(vmem_limit_bytes=60 << 20),
        cost_estimate=pl.CostEstimate(
            flops=groups * span * width * 2 * CHUNKS,
            bytes_accessed=groups * span * width * 4,
            transcendentals=0,
        ),
        name="arrange_references",
    )(prt, references, sel, masks)


def lane_signs():
    lane = lax.broadcasted_iota(jnp.int32, (1, LANES), 1)
    quarter = LANES // 4
    imag = lane >= 2 * quarter
    odd = (lane // quarter) % 2 == 1
    return imag, odd


def lanes_of(refs, first, number):
    parts = [
        jnp.concatenate([ref[i] for ref in refs], 0) for i in range(first, first + number)
    ]
    return jnp.concatenate(parts, 1) if number > 1 else parts[0]


def hot_masks(cand, groups):
    rows = lax.broadcasted_iota(jnp.int32, (groups, cand.shape[1]), 0).astype(jnp.float32)
    return [rows == cand[q : q + 1] for q in range(CAND_OWN)]


def residue_weights(q_ref, at, g):
    imag, odd = lane_signs()
    sign = jnp.where(imag == odd, -1.0, 1.0)
    first, second = [], []
    for i in range(TURNS):
        q = q_ref[at * TURNS + i].astype(jnp.float32)
        turned = pltpu.roll(q, LANES // 2, 1) * sign
        if at == 0:
            first.append(jnp.where((g == 0) & odd, 0.0, q))
            second.append(jnp.where(g == 0, jnp.where(odd, q, 0.0), turned))
        else:
            first.append(q)
            second.append(turned)
    return jnp.concatenate(
        [jnp.concatenate(first, 1), jnp.concatenate(second, 1)], 0
    ).astype(jnp.bfloat16)


def chosen_rows(acc, cand):
    groups = acc.shape[0] // 2
    hot = hot_masks(cand, groups)
    rows = []
    for ab in range(2):
        part = acc[ab * groups : (ab + 1) * groups, :]
        for q in range(CAND_OWN):
            rows.append(jnp.sum(jnp.where(hot[q], part, 0.0), axis=0, keepdims=True))
    return jnp.concatenate(rows, 0)


def cross_body(at_ref, *refs):
    number = (len(refs) - 6) // 2
    blocks, extras = refs[:number], refs[number : 2 * number]
    q_ref, qt_ref, norm_ref, coef_ref, cand_ref, acc = refs[2 * number :]
    step = pl.program_id(0)
    groups = q_ref.shape[1]
    imag, odd = lane_signs()

    @pl.when(step == 0)
    def _():
        label = lanes_of(extras, TAIL // 2, 1).astype(jnp.float32).T
        row = lax.broadcasted_iota(jnp.int32, label.shape, 0)
        base = at_ref[0] * CAND_OWN
        for q in range(CAND_OWN):
            cand_ref[q : q + 1, :] = jnp.sum(
                jnp.where(row == base + q, label, 0.0), axis=0, keepdims=True
            )
        cand_ref[CAND_OWN:, :] = jnp.full(
            (cand_ref.shape[0] - CAND_OWN, cand_ref.shape[1]), -1.0, jnp.float32
        )

    for u in range(CROSS_STEP):
        g = step * CROSS_STEP + u
        acc[...] = nt_dot(residue_weights(q_ref, u, g), lanes_of(blocks, u * TURNS, TURNS))

        for i in range(TAIL):
            if i % CROSS_STEP != u:
                continue

            @pl.when(g == i)
            def _():
                q = qt_ref[i // 2].astype(jnp.float32)
                keep = odd if i % 2 else ~odd
                a = jnp.where(keep, q, 0.0)
                turned = pltpu.roll(q, LANES // 2, 1) * jnp.where(imag, 1.0, -1.0)
                b = jnp.where(keep, turned, 0.0)
                if i == 0:
                    b = jnp.zeros_like(b)
                w = jnp.concatenate([a, b], 0).astype(jnp.bfloat16)
                acc[...] += nt_dot(w, lanes_of(extras, i // 2, 1))
                if i == 0:
                    acc[:groups, :] -= 0.5 * jnp.sum(norm_ref[...], axis=1, keepdims=True)

        block = 2 * CAND_OWN
        coef_ref[u * block : (u + 1) * block, :] = chosen_rows(acc[...], cand_ref[...])


def cross_coefficients(blocks, arranged, norms, cls):
    count = blocks[0].shape[1]
    groups = arranged.shape[1]
    total = len(blocks) * count
    half_tail = TAIL // 2
    size = blocks[0].size * len(blocks)
    block = 2 * CAND_OWN
    return pl.pallas_call(
        cross_body,
        grid_spec=pltpu.PrefetchScalarGridSpec(
            num_scalar_prefetch=1,
            grid=(HALF // CROSS_STEP,),
            in_specs=[
                *[
                    pl.BlockSpec((CROSS_STEP * TURNS, count, LANES), lambda g, at: (g, 0, 0))
                    for _ in blocks
                ],
                *[
                    pl.BlockSpec((EXTRA, count, LANES), lambda g, at: (BODY // EXTRA, 0, 0))
                    for _ in blocks
                ],
                pl.BlockSpec((CROSS_STEP * TURNS, groups, LANES), lambda g, at: (g, 0, 0)),
                pl.BlockSpec((half_tail, groups, LANES), lambda g, at: (BODY // half_tail, 0, 0)),
                pl.BlockSpec((groups, LANES), lambda g, at: (0, 0)),
            ],
            out_specs=[
                pl.BlockSpec((CROSS_STEP * block, total), lambda g, at: (g, 0)),
                pl.BlockSpec((block, total), lambda g, at: (0, 0)),
            ],
            scratch_shapes=[pltpu.VMEM((2 * groups, total), jnp.float32)],
        ),
        out_shape=[
            jax.ShapeDtypeStruct((COEF, total), jnp.float32),
            jax.ShapeDtypeStruct((block, total), jnp.float32),
        ],
        compiler_params=pltpu.CompilerParams(vmem_limit_bytes=60 << 20),
        cost_estimate=pl.CostEstimate(
            flops=4 * size * groups, bytes_accessed=2 * size, transcendentals=0
        ),
        name="cross_coefficients",
    )(cls, *blocks, *blocks, arranged, arranged, norms)


def score_body(*refs, scale):
    *coefs, cand_ref, table_ref, score_ref, stat_ref = refs
    corr = lax.dot_general(
        table_ref[...],
        functools.reduce(jnp.add, [ref[...] for ref in coefs]),
        (((0,), (0,)), ((), ())),
        precision=lax.Precision.HIGHEST,
        preferred_element_type=jnp.float32,
    )
    score = jnp.where(cand_ref[0:1, :] >= 0.0, corr * scale, lowest)
    top = jnp.max(score, axis=0, keepdims=True)
    total = jnp.sum(jnp.exp(score - top), axis=0, keepdims=True)
    score_ref[...] = score
    stat_ref[0:1, :] = top
    stat_ref[1:2, :] = jnp.where(cand_ref[0:1, :] >= 0.0, total, 0.0)


def scores(coefs, cand, table, scale):
    total = cand.shape[1]
    return pl.pallas_call(
        functools.partial(score_body, scale=scale),
        out_shape=[
            jax.ShapeDtypeStruct((ROTS * CAND_OWN, total), jnp.float32),
            jax.ShapeDtypeStruct((2, total), jnp.float32),
        ],
        name="scores",
    )(*coefs, cand, table)


def swap_blocks(x, distance, width):
    lane = lax.broadcasted_iota(jnp.int32, x.shape, 1)
    bit = 1
    while bit <= distance:
        if distance & bit:
            shift = bit * width
            down = pltpu.roll(x, shift, 1)
            up = pltpu.roll(x, x.shape[1] - shift, 1)
            x = jnp.where((lane // shift) % 2 == 1, down, up)
        bit *= 2
    return x


def weights_body(at_ref, score_ref, cand_ref, stat_ref, table_ref, mix_ref, norm_ref):
    n_cls, _, total = stat_ref.shape
    width = total // n_cls
    tops, parts = [], []
    for e in range(n_cls):
        table = stat_ref[at_ref[0] ^ e]
        table = swap_blocks(jnp.concatenate([table] * 4, 0), e, width)
        tops.append(table[0:1])
        parts.append(table[1:2])
    top = functools.reduce(jnp.maximum, tops)
    summed = jnp.zeros_like(top)
    for other, part in zip(tops, parts):
        summed += part * jnp.exp(other - top)
    log_norm = top + jnp.log(summed)
    norm_ref[...] = log_norm
    weight = jnp.where(cand_ref[0:1, :] >= 0.0, jnp.exp(score_ref[...] - log_norm), 0.0)
    mix_ref[...] = lax.dot_general(
        table_ref[...],
        weight,
        (((1,), (0,)), ((), ())),
        precision=lax.Precision.HIGHEST,
        preferred_element_type=jnp.float32,
    )


def mixed_weights(cls, score, cand, stats, table):
    total = score.shape[1]
    return pl.pallas_call(
        weights_body,
        in_specs=[pl.BlockSpec(memory_space=pltpu.SMEM)] + [pl.BlockSpec(memory_space=pltpu.VMEM)] * 4,
        out_shape=[
            jax.ShapeDtypeStruct((COEF, total), jnp.float32),
            jax.ShapeDtypeStruct((1, total), jnp.float32),
        ],
        name="mixed_weights",
    )(cls, score, cand, stats, table)


def sums_body(*refs, number, pieces):
    blocks, extras = refs[:number], refs[number : 2 * number]
    refs = refs[2 * number :]
    mixes, cands = refs[:pieces], refs[pieces : 2 * pieces]
    back_ref, out_ref, weight_ref, mix, cand, planes = refs[2 * pieces :]
    i = pl.program_id(0)
    groups = weight_ref.shape[0]
    total = mix.shape[1]
    imag, odd = lane_signs()

    @pl.when(i == 0)
    def _():
        mixed = jnp.concatenate([ref[...] for ref in mixes], 1)
        chosen = jnp.concatenate([ref[...] for ref in cands], 1)
        hot = hot_masks(chosen, groups)
        summed = jnp.zeros((groups, total), jnp.float32)
        for q in range(CAND_OWN):
            summed += jnp.where(hot[q], mixed[q : q + 1], 0.0)
        weight_ref[...] = jnp.sum(summed, axis=1, keepdims=True)
        mix[...] = mixed
        cand[...] = chosen

    @pl.when(i < HALF // SUM_STEP)
    def _():
        hot = hot_masks(cand[...], groups)
        block = 2 * CAND_OWN
        sign = jnp.where(imag == odd, 1.0, -1.0)
        for u in range(SUM_STEP):
            g = i * SUM_STEP + u
            mine = mix[pl.ds(pl.multiple_of(g * block, block), block), :]
            halves = []
            for ab in range(2):
                dense = jnp.zeros((groups, total), jnp.float32)
                for q in range(CAND_OWN):
                    at = ab * CAND_OWN + q
                    dense = jnp.where(hot[q], mine[at : at + 1], dense)
                halves.append(dense)
            weights = jnp.concatenate(halves, 0).astype(jnp.bfloat16)
            made = jnp.dot(
                weights, lanes_of(blocks, u * TURNS, TURNS), preferred_element_type=jnp.float32
            )
            for t in range(TURNS):
                g1 = made[:groups, t * LANES : (t + 1) * LANES]
                g2 = made[groups:, t * LANES : (t + 1) * LANES]
                value = g1 + sign * pltpu.roll(g2, LANES // 2, 1)
                if u == 0:
                    value = jnp.where(i == 0, jnp.where(odd, g2, g1), value)
                start = pl.multiple_of((g * TURNS + t) * groups, groups)
                planes[pl.ds(start, groups), :] = value

            for t in range(TAIL):
                if t % SUM_STEP != u:
                    continue

                @pl.when(g == t)
                def _():
                    made = jnp.dot(
                        weights, lanes_of(extras, t // 2, 1), preferred_element_type=jnp.float32
                    )
                    g1, g2 = made[:groups], made[groups:]
                    value = g1
                    if t > 0:
                        value = g1 + jnp.where(imag, -1.0, 1.0) * pltpu.roll(g2, LANES // 2, 1)
                    rows = pl.ds((BODY + t // 2) * groups, groups)
                    if t % 2:
                        value = jnp.where(odd, value, planes[rows, :])
                    planes[rows, :] = value

    @pl.when(i >= HALF // SUM_STEP)
    def _():
        block, span, _ = out_ref.shape
        first = (i - HALF // SUM_STEP) * block
        back = back_ref[...]
        for c in range(block):
            turned = planes[pl.ds(first + c, CHUNKS, stride=groups), :].T
            parts = []
            for s in range(2):
                at = 2 * s * span
                parts.append(
                    jnp.concatenate([turned[at : at + span], turned[at + span : at + 2 * span]], 1)
                )
            value = jnp.concatenate(parts, 0)
            high = value.astype(jnp.bfloat16)
            low = (value - high.astype(jnp.float32)).astype(jnp.bfloat16)
            placed = jnp.dot(high, back, preferred_element_type=jnp.float32) + jnp.dot(
                low, back, preferred_element_type=jnp.float32
            )
            out_ref[c, :, :HARM] = placed[:span]
            out_ref[c, :, HARM:] = placed[span:]


def sums(blocks, mixes, cands, back, groups, span):
    count = blocks[0].shape[1]
    total = len(blocks) * count
    size = blocks[0].size * len(blocks)
    block = 8
    steps = HALF // SUM_STEP
    whole = lambda i: (0, 0)
    return pl.pallas_call(
        functools.partial(sums_body, number=len(blocks), pieces=len(mixes)),
        grid=(steps + groups // block,),
        in_specs=[
            *[
                pl.BlockSpec(
                    (SUM_STEP * TURNS, count, LANES), lambda i: (jnp.minimum(i, steps - 1), 0, 0)
                )
                for _ in blocks
            ],
            *[
                pl.BlockSpec((EXTRA, count, LANES), lambda i: (BODY // EXTRA, 0, 0))
                for _ in blocks
            ],
            *[pl.BlockSpec(array.shape, whole) for array in (*mixes, *cands, back)],
        ],
        out_specs=[
            pl.BlockSpec(
                (block, span, 2 * HARM), lambda i: (jnp.maximum(i - steps, 0), 0, 0)
            ),
            pl.BlockSpec((groups, 1), whole),
        ],
        out_shape=[
            jax.ShapeDtypeStruct((groups, span, 2 * HARM), jnp.float32),
            jax.ShapeDtypeStruct((groups, 1), jnp.float32),
        ],
        scratch_shapes=[
            pltpu.VMEM((COEF, total), jnp.float32),
            pltpu.VMEM((2 * CAND_OWN, total), jnp.float32),
            pltpu.VMEM((CHUNKS * groups, LANES), jnp.float32),
        ],
        compiler_params=pltpu.CompilerParams(vmem_limit_bytes=60 << 20),
        cost_estimate=pl.CostEstimate(
            flops=4 * size * groups,
            bytes_accessed=2 * size + 8 * groups * span * HARM,
            transcendentals=0,
        ),
        name="sums",
    )(*blocks, *blocks, *mixes, *cands, back)


def hop(value, axis, distance):
    size = lax.axis_size(axis)
    return lax.ppermute(value, axis, [(i, i ^ distance) for i in range(size)])


def after(value, *others):
    return lax.optimization_barrier((value, *others))[0]


def direct(own):
    n_cls = lax.axis_size("cls")
    return {1 << bit: hop(own, "cls", 1 << bit) for bit in range(1, n_cls.bit_length() - 1)}


def relayed(known, d, *others):
    n_cls = lax.axis_size("cls")
    for j in sorted(range(2, n_cls, 2), key=lambda j: bin(j).count("1")):
        if j not in known:
            bits = [bit for bit in range(1, n_cls.bit_length()) if j >> bit & 1]
            way = 1 << bits[d % len(bits)]
            known[j] = hop(after(known[j ^ way], *others), "cls", way)
    return known


def paired(known, *others):
    n_cls = lax.axis_size("cls")
    last = n_cls - 2
    for j in range(0, n_cls, 2):
        block = after(known[j], *others) if j == last and others else known[j]
        known[j + 1] = hop(block, "cls", 1)
    return [known[j] for j in range(n_cls)]


def gather_device(particles, references, owner_groups, class_order):
    n_cls, n_prt = lax.axis_size("cls"), lax.axis_size("prt")
    cls, prt = lax.axis_index("cls"), lax.axis_index("prt")
    count, cycles, width = particles.shape
    groups = references.shape[0]
    span = cycles // n_prt
    sel = jnp.asarray(selector(), jnp.bfloat16)
    masks = jnp.asarray(side_masks(), jnp.bfloat16)
    back = jnp.asarray(unselector(), jnp.bfloat16)
    table = jnp.asarray(rotation_table())
    picks = class_order[:, :, :CAND_OWN].reshape(count, OWN_TOP * CAND_OWN)
    cls, prt = (index.reshape(1).astype(jnp.int32) for index in (cls, prt))
    outgoing = []
    for first in range(0, n_prt, 2):
        distances = tuple(range(first, min(first + 2, n_prt)))
        place = after(prt, outgoing[0]) if outgoing else prt
        outgoing += arrange_particles(
            place, particles, owner_groups, picks, n_prt, distances, sel, masks
        )
    arrived = [outgoing[0]]
    known = [{0: arrived[0], **direct(arrived[0])}]
    arranged, norms = arrange_references(references, prt, n_prt, sel, masks)
    for d in range(1, n_prt):
        block = after(outgoing[d], arrived[d - 1], arranged) if d > 2 else outgoing[d]
        arrived.append(hop(block, "prt", d))
    for d in range(1, n_prt):
        own = after(arrived[d], arranged) if d < 3 else arrived[d]
        known.append({0: own, **direct(own)})
    relayed(known[0], 0, arranged)
    for d in range(1, n_prt, 2):
        relayed(known[d], d)
    scale = 2.0 / math.sqrt(cycles * width)
    coefs, cands, sent, blocks = [], [], [], []
    for d in range(n_prt):
        if d and d % 2 == 0:
            relayed(known[d], d, coefs[0])
        waits = [arrived[-1], known[1][2]] if d == 0 else [known[-1][2]] if d == 1 else []
        blocks.append(paired(known[d], *(coefs[1:2] if d == n_prt - 1 else [])))
        ready = after(arranged, *waits) if waits else arranged
        coef, cand = cross_coefficients(blocks[d], ready, norms, cls)
        coefs.append(coef)
        sent.append(hop(coef, "prt", d) if d else coef)
        cands.append(cand)
    score, stat = scores(sent, cands[0], table, scale)
    stats = lax.all_gather(stat.reshape(1, *stat.shape), "cls", axis=0, tiled=True)
    mix, log_norm = mixed_weights(cls, score, cands[0], stats, table)
    mixes = [hop(mix, "prt", d) if d else mix for d in range(n_prt)]
    class_sums, class_weights = sums(
        [block for piece in blocks for block in piece], mixes, cands, back, groups, span
    )
    own = log_norm[0, :count]
    return class_sums, class_weights[:, 0], own


def per_device(particles, references, owner_groups, class_order):
    n_cls, n_prt = lax.axis_size("cls"), lax.axis_size("prt")
    count, cycles, _ = particles.shape
    groups = references.shape[0]
    cap = max(2, 2 * count * OWN_TOP // n_cls)
    powers = n_cls & (n_cls - 1) == 0 and n_prt & (n_prt - 1) == 0
    fits = 4 * cycles == LANES * n_prt and n_cls * CAND_OWN <= LANES and groups % 16 == 0
    fits = fits and powers and n_cls * count == LANES
    plan = gather_device if cap >= count and fits else dispatch_device
    return plan(particles, references, owner_groups, class_order)


def solution(mesh):
    in_specs = (
        P(("cls", "prt"), None, None),
        P("cls", None, None),
        P(("cls", "prt"), None),
        P(("cls", "prt"), None, None),
    )
    out_specs = (P("cls", "prt", None), P("cls"), P(("cls", "prt")))
    return jax.shard_map(
        per_device, mesh=mesh, in_specs=in_specs, out_specs=out_specs, check_vma=False
    )
```

```python
import functools
import math

import jax
import jax.numpy as jnp
import numpy as np
from jax import lax
from jax.experimental import pallas as pl
from jax.experimental.pallas import tpu as pltpu
from jax.sharding import PartitionSpec as P

CYCLES = 128
HARM = 256
ROTS = 36
OWN_TOP = 4
CAND_OWN = 4


lowest = -1e30


def spectral_tables():
    harmonic = jnp.arange(HARM, dtype=jnp.float32)
    angles = 2.0 * math.pi * jnp.arange(ROTS, dtype=jnp.float32) / ROTS
    phase = harmonic[:, None] * angles[None, :]
    forward = jnp.concatenate([jnp.cos(phase), jnp.sin(phase)], 0)
    backward = jnp.concatenate([jnp.cos(phase), -jnp.sin(phase)], 0).T
    return (forward, backward)


def class_accumulate(lanes, mixed):
    l_re = lanes[..., :HARM]
    l_im = lanes[..., HARM:]
    y_re = mixed[..., :HARM]
    y_im = mixed[..., HARM:]
    s_re = jnp.einsum("lrm,lcm->crm", l_re, y_re, preferred_element_type=jnp.float32) - jnp.einsum(
        "lrm,lcm->crm", l_im, y_im, preferred_element_type=jnp.float32
    )
    s_im = jnp.einsum("lrm,lcm->crm", l_re, y_im, preferred_element_type=jnp.float32) + jnp.einsum(
        "lrm,lcm->crm", l_im, y_re, preferred_element_type=jnp.float32
    )
    return jnp.concatenate([s_re, s_im], -1)


def dispatch_device(particles, references, owner_groups, class_order):
    n_cls = lax.axis_size("cls")
    count = particles.shape[0]
    groups = references.shape[0]
    cap = max(2, 2 * count * OWN_TOP // n_cls)
    slots = n_cls * cap
    width = 2 * HARM
    flat_owner = owner_groups.reshape(-1)
    owner_hot = (flat_owner[:, None] == jnp.arange(n_cls, dtype=jnp.int32)[None, :]).astype(
        jnp.int32
    )
    before = jnp.cumsum(owner_hot, axis=0) - owner_hot
    rank = jnp.sum(before * owner_hot, axis=1)
    slot_of = flat_owner * cap + rank
    match = slot_of[None, :] == jnp.arange(slots, dtype=jnp.int32)[:, None]
    member = jnp.any(match.reshape(slots, count, OWN_TOP), axis=2)
    filled = jnp.any(member, axis=1)
    dispatch = member.astype(jnp.bfloat16)
    outgoing = jnp.dot(
        dispatch, particles.reshape(count, CYCLES * width), preferred_element_type=jnp.float32
    )
    outgoing = outgoing.astype(jnp.bfloat16).reshape(n_cls, cap, CYCLES, width)
    match_int = match.astype(jnp.int32)
    picks = class_order[:, :, :CAND_OWN].reshape(count * OWN_TOP, CAND_OWN)
    slot_cand = jnp.where(filled[:, None], jnp.dot(match_int, picks), -1)
    owner_rows = jnp.repeat(jnp.arange(count, dtype=jnp.int32), OWN_TOP)
    slot_pid = jnp.where(filled, jnp.dot(match_int, owner_rows), -1)
    labels_out = jnp.concatenate([slot_cand, slot_pid[:, None]], 1).reshape(
        n_cls, cap, CAND_OWN + 1
    )
    arrived, labels = (
        lax.all_to_all(outgoing, "cls", split_axis=0, concat_axis=0, tiled=True),
        lax.all_to_all(labels_out, "cls", split_axis=0, concat_axis=0, tiled=True),
    )
    lanes = arrived.reshape(slots, CYCLES, width)
    labels = labels.reshape(slots, CAND_OWN + 1)
    forward, backward = spectral_tables()
    scale = 2.0 / math.sqrt(CYCLES * width)
    norms = jnp.sum(jnp.square(references.astype(jnp.float32)), axis=(1, 2))
    l_re = lanes[..., :HARM]
    l_im = lanes[..., HARM:]
    r_re = references[..., :HARM]
    r_im = references[..., HARM:]
    x_re = jnp.einsum("lrm,crm->lcm", l_re, r_re, preferred_element_type=jnp.float32) + jnp.einsum(
        "lrm,crm->lcm", l_im, r_im, preferred_element_type=jnp.float32
    )
    x_im = jnp.einsum("lrm,crm->lcm", l_im, r_re, preferred_element_type=jnp.float32) - jnp.einsum(
        "lrm,crm->lcm", l_re, r_im, preferred_element_type=jnp.float32
    )
    cross = jnp.concatenate([x_re, x_im], -1)
    corr = jnp.dot(
        cross.reshape(slots * groups, width), forward, precision=lax.Precision.HIGHEST
    ).reshape(slots, groups, ROTS)
    score = (corr - 0.5 * norms[None, :, None]) * scale
    candidate = jnp.any(
        labels[:, :CAND_OWN, None] == jnp.arange(groups, dtype=jnp.int32)[None, None, :], axis=1
    )
    part_max = jnp.max(jnp.where(candidate[:, :, None], score, lowest), axis=(1, 2))
    part_sum = jnp.sum(
        jnp.where(candidate[:, :, None], jnp.exp(score - part_max[:, None, None]), 0.0), axis=(1, 2)
    )
    sender_ids = labels[:, CAND_OWN].astype(jnp.float32)
    table_max, table_sum, table_ids = (
        lax.all_gather(part_max.reshape(1, n_cls, cap), "cls", axis=0, tiled=True),
        lax.all_gather(part_sum.reshape(1, n_cls, cap), "cls", axis=0, tiled=True),
        lax.all_gather(sender_ids.reshape(1, n_cls, cap), "cls", axis=0, tiled=True),
    )
    local_ids = jnp.arange(count, dtype=jnp.float32)
    hit = table_ids[..., None] == local_ids
    top = jnp.max(jnp.where(hit, table_max[..., None], lowest), axis=(0, 2))
    total = jnp.sum(
        jnp.where(
            hit, table_sum[..., None] * jnp.exp(table_max[..., None] - top[None, :, None, :]), 0.0
        ),
        axis=(0, 2),
    )
    table_norm = top + jnp.log(total)
    slot_ids = labels[:, CAND_OWN].reshape(n_cls, cap)
    slot_norm = jnp.sum(
        jnp.where(
            slot_ids[..., None] == jnp.arange(count, dtype=jnp.int32), table_norm[:, None, :], 0.0
        ),
        axis=2,
    ).reshape(slots)
    own_norm = lax.dynamic_index_in_dim(table_norm, lax.axis_index("cls"), 0, keepdims=False)
    weight = jnp.where(candidate[:, :, None], jnp.exp(score - slot_norm[:, None, None]), 0.0)
    mixed = (
        jnp.dot(weight.reshape(slots * groups, ROTS), backward, precision=lax.Precision.HIGHEST)
        .astype(jnp.bfloat16)
        .reshape(slots, groups, width)
    )
    class_weights = lax.psum(jnp.sum(weight, axis=(0, 2)), "prt")
    partial_sums = class_accumulate(lanes, mixed)
    class_sums = lax.psum_scatter(partial_sums, "prt", scatter_dimension=1, tiled=True)
    return (class_sums, class_weights, own_norm)


LANES = 128


def harmonic_plan():
    half = ROTS // 2
    turns = HARM // ROTS
    tail = HARM - turns * ROTS
    chunk_of = np.zeros(HARM, np.int32)
    side_of = np.zeros(HARM, np.int32)
    for m in range(HARM):
        turn, rest = divmod(m, ROTS)
        if turn == turns:
            chunk_of[m] = half * turns + rest // 2
            side_of[m] = rest % 2
        elif rest < half:
            chunk_of[m] = rest * turns + turn
        else:
            chunk_of[m] = ((ROTS - rest) % half) * turns + turn
            side_of[m] = 1
    return half, turns, tail, chunk_of, side_of


HALF, TURNS, TAIL, CHUNK_OF, SIDE_OF = harmonic_plan()
BODY = HALF * TURNS
CHUNKS = BODY + TAIL // 2
EXTRA = TAIL // 2 + 1
COEF = 2 * HALF * CAND_OWN
CROSS_STEP = 6
SUM_STEP = 3


def selector():
    return (np.arange(CHUNKS)[:, None] == CHUNK_OF[None, :]).astype(np.float32)


def unselector():
    sel = selector()
    return np.concatenate([sel * (SIDE_OF == 0), sel * (SIDE_OF == 1)], 0)


def rotation_table():
    table = np.zeros((HALF, 2, CAND_OWN, ROTS, CAND_OWN))
    angle = 2.0 * np.pi * np.arange(ROTS) / ROTS
    for g in range(HALF):
        first = np.cos(g * angle)
        second = np.cos(HALF * angle) if g == 0 else np.sin(g * angle)
        for q in range(CAND_OWN):
            table[g, 0, q, :, q] = first
            table[g, 1, q, :, q] = second
    return table.reshape(COEF, ROTS * CAND_OWN).astype(np.float32)


def nt_dot(a, b):
    return lax.dot_general(a, b, (((1,), (1,)), ((), ())), preferred_element_type=jnp.float32)


def selector_masks():
    m = lax.broadcasted_iota(jnp.int32, (1, HARM), 1)
    turn = jnp.zeros((1, HARM), jnp.int32)
    for t in range(1, TURNS + 1):
        turn += jnp.where(m >= t * ROTS, 1, 0)
    rest = m - ROTS * turn
    back = jnp.where(rest == HALF, 0, ROTS - rest)
    chunk = jnp.where(rest < HALF, rest, back) * TURNS + turn
    side = jnp.where(rest < HALF, 0, 1)
    chunk = jnp.where(turn == TURNS, BODY + rest // 2, chunk)
    side = jnp.where(turn == TURNS, rest % 2, side)
    rows = lax.broadcasted_iota(jnp.int32, (CHUNKS, HARM), 0)
    sel = jnp.where(rows == chunk, 1.0, 0.0).astype(jnp.bfloat16)
    sides = lax.broadcasted_iota(jnp.int32, (2, HARM), 0)
    masks = jnp.where(sides == side, 1.0, 0.0).astype(jnp.bfloat16)
    return sel, masks


def masked_stack(piece, masks):
    parts = []
    for s in range(2):
        for b in range(2):
            parts.append(piece[:, s * HARM : (s + 1) * HARM] * masks[b : b + 1])
    return jnp.concatenate(parts, 0)


def particle_body(at_ref, x_ref, owner_ref, pick_ref, *refs, distances, n_prt):
    outs, scr = refs[:-1], refs[-1]
    count, cycles, _ = x_ref.shape
    number = len(outs)
    span = cycles // n_prt
    sel, masks = selector_masks()

    def one(n, carry):
        parts = []
        for d in distances:
            start = pl.multiple_of((at_ref[0] ^ d) * span, span)
            parts.append(masked_stack(x_ref[n, pl.ds(start, span), :], masks))
        w = jnp.concatenate(parts, 0)
        y = nt_dot(sel, w)
        for p in range(number):
            scr[p, pl.ds(pl.multiple_of(n * CHUNKS, CHUNKS), CHUNKS), :] = y[
                :, p * LANES : (p + 1) * LANES
            ]
        return carry

    lax.fori_loop(0, count, one, 0)

    def two(c, carry):
        for p in range(number):
            outs[p][c] = scr[p, pl.ds(c, count, stride=CHUNKS), :].astype(jnp.bfloat16)
        return carry

    lax.fori_loop(0, CHUNKS, two, 0)
    lane = lax.broadcasted_iota(jnp.int32, (count, LANES), 1)
    label = jnp.full((count, LANES), -1, jnp.int32)
    for t in range(OWN_TOP):
        mine = (lane // CAND_OWN) == owner_ref[:, t : t + 1]
        for q in range(CAND_OWN):
            at = t * CAND_OWN + q
            label = jnp.where(
                mine & (lane % CAND_OWN == q), pick_ref[:, at : at + 1], label
            )
    label = label.astype(jnp.float32).astype(jnp.bfloat16)
    for p in range(number):
        outs[p][CHUNKS] = label


def arrange_particles(prt, particles, owner, picks, n_prt, distances):
    count = particles.shape[0]
    number = len(distances)
    size = particles.size * number // n_prt
    return pl.pallas_call(
        functools.partial(particle_body, distances=distances, n_prt=n_prt),
        in_specs=[pl.BlockSpec(memory_space=pltpu.SMEM)] + [pl.BlockSpec(memory_space=pltpu.VMEM)] * 3,
        out_shape=[jax.ShapeDtypeStruct((CHUNKS + 1, count, LANES), jnp.bfloat16)] * number,
        scratch_shapes=[pltpu.VMEM((number, count * CHUNKS, LANES), jnp.float32)],
        compiler_params=pltpu.CompilerParams(vmem_limit_bytes=32 << 20),
        cost_estimate=pl.CostEstimate(
            flops=size * 2 * CHUNKS, bytes_accessed=size * 4, transcendentals=0
        ),
        name="arrange_particles",
    )(prt, particles, owner, picks)


def reference_body(at_ref, x_ref, out_ref, norm_ref, scr):
    rows = x_ref.shape[0]
    sel, masks = selector_masks()
    step = 4

    def one(n, carry):
        w = jnp.concatenate([masked_stack(x_ref[n * step + i], masks) for i in range(step)], 0)
        y = nt_dot(sel, w)
        for i in range(step):
            scr[pl.ds(pl.multiple_of((n * step + i) * CHUNKS, CHUNKS), CHUNKS), :] = y[
                :, i * LANES : (i + 1) * LANES
            ]
        return carry

    lax.fori_loop(0, rows // step, one, 0)

    def two(c, carry):
        value = scr[pl.ds(c, rows, stride=CHUNKS), :]
        out_ref[c] = value.astype(jnp.bfloat16)
        return carry + value * value

    norm_ref[...] = lax.fori_loop(0, CHUNKS, two, jnp.zeros((rows, LANES), jnp.float32))


def arrange_references(references, prt, n_prt):
    groups, cycles, width = references.shape
    span = cycles // n_prt
    block = 16
    return pl.pallas_call(
        reference_body,
        grid_spec=pltpu.PrefetchScalarGridSpec(
            num_scalar_prefetch=1,
            grid=(groups // block,),
            in_specs=[
                pl.BlockSpec((block, span, width), lambda i, at: (i, at[0], 0)),
            ],
            out_specs=[
                pl.BlockSpec((CHUNKS, block, LANES), lambda i, at: (0, i, 0)),
                pl.BlockSpec((block, LANES), lambda i, at: (i, 0)),
            ],
            scratch_shapes=[pltpu.VMEM((block * CHUNKS, LANES), jnp.float32)],
        ),
        out_shape=[
            jax.ShapeDtypeStruct((CHUNKS, groups, LANES), jnp.bfloat16),
            jax.ShapeDtypeStruct((groups, LANES), jnp.float32),
        ],
        compiler_params=pltpu.CompilerParams(vmem_limit_bytes=60 << 20),
        cost_estimate=pl.CostEstimate(
            flops=groups * span * width * 2 * CHUNKS,
            bytes_accessed=groups * span * width * 4,
            transcendentals=0,
        ),
        name="arrange_references",
    )(prt, references)


def lane_signs():
    lane = lax.broadcasted_iota(jnp.int32, (1, LANES), 1)
    quarter = LANES // 4
    imag = lane >= 2 * quarter
    odd = (lane // quarter) % 2 == 1
    return imag, odd


def lanes_of(refs, first, number):
    parts = [
        jnp.concatenate([ref[i] for ref in refs], 0) for i in range(first, first + number)
    ]
    return jnp.concatenate(parts, 1) if number > 1 else parts[0]


def hot_masks(cand, groups):
    rows = lax.broadcasted_iota(jnp.int32, (groups, cand.shape[1]), 0).astype(jnp.float32)
    return [rows == cand[q : q + 1] for q in range(CAND_OWN)]


def residue_weights(q_ref, at, g):
    imag, odd = lane_signs()
    sign = jnp.where(imag == odd, -1.0, 1.0)
    first, second = [], []
    for i in range(TURNS):
        q = q_ref[at * TURNS + i].astype(jnp.float32)
        turned = pltpu.roll(q, LANES // 2, 1) * sign
        if at == 0:
            first.append(jnp.where((g == 0) & odd, 0.0, q))
            second.append(jnp.where(g == 0, jnp.where(odd, q, 0.0), turned))
        else:
            first.append(q)
            second.append(turned)
    return jnp.concatenate(
        [jnp.concatenate(first, 1), jnp.concatenate(second, 1)], 0
    ).astype(jnp.bfloat16)


def chosen_rows(acc, cand):
    groups = acc.shape[0] // 2
    hot = hot_masks(cand, groups)
    rows = []
    for ab in range(2):
        part = acc[ab * groups : (ab + 1) * groups, :]
        for q in range(CAND_OWN):
            rows.append(jnp.sum(jnp.where(hot[q], part, 0.0), axis=0, keepdims=True))
    return jnp.concatenate(rows, 0)


def cross_body(at_ref, *refs):
    number = (len(refs) - 6) // 2
    blocks, extras = refs[:number], refs[number : 2 * number]
    q_ref, qt_ref, norm_ref, coef_ref, cand_ref, acc = refs[2 * number :]
    step = pl.program_id(0)
    groups = q_ref.shape[1]
    imag, odd = lane_signs()

    @pl.when(step == 0)
    def _():
        label = lanes_of(extras, TAIL // 2, 1).astype(jnp.float32).T
        row = lax.broadcasted_iota(jnp.int32, label.shape, 0)
        base = at_ref[0] * CAND_OWN
        for q in range(CAND_OWN):
            cand_ref[q : q + 1, :] = jnp.sum(
                jnp.where(row == base + q, label, 0.0), axis=0, keepdims=True
            )
        cand_ref[CAND_OWN:, :] = jnp.full(
            (cand_ref.shape[0] - CAND_OWN, cand_ref.shape[1]), -1.0, jnp.float32
        )

    for u in range(CROSS_STEP):
        g = step * CROSS_STEP + u
        acc[...] = nt_dot(residue_weights(q_ref, u, g), lanes_of(blocks, u * TURNS, TURNS))

        for i in range(TAIL):
            if i % CROSS_STEP != u:
                continue

            @pl.when(g == i)
            def _():
                q = qt_ref[i // 2].astype(jnp.float32)
                keep = odd if i % 2 else ~odd
                a = jnp.where(keep, q, 0.0)
                turned = pltpu.roll(q, LANES // 2, 1) * jnp.where(imag, 1.0, -1.0)
                b = jnp.where(keep, turned, 0.0)
                if i == 0:
                    b = jnp.zeros_like(b)
                w = jnp.concatenate([a, b], 0).astype(jnp.bfloat16)
                acc[...] += nt_dot(w, lanes_of(extras, i // 2, 1))
                if i == 0:
                    acc[:groups, :] -= 0.5 * jnp.sum(norm_ref[...], axis=1, keepdims=True)

        block = 2 * CAND_OWN
        coef_ref[u * block : (u + 1) * block, :] = chosen_rows(acc[...], cand_ref[...])


def cross_coefficients(blocks, arranged, norms, cls):
    count = blocks[0].shape[1]
    groups = arranged.shape[1]
    total = len(blocks) * count
    half_tail = TAIL // 2
    size = blocks[0].size * len(blocks)
    block = 2 * CAND_OWN
    return pl.pallas_call(
        cross_body,
        grid_spec=pltpu.PrefetchScalarGridSpec(
            num_scalar_prefetch=1,
            grid=(HALF // CROSS_STEP,),
            in_specs=[
                *[
                    pl.BlockSpec((CROSS_STEP * TURNS, count, LANES), lambda g, at: (g, 0, 0))
                    for _ in blocks
                ],
                *[
                    pl.BlockSpec((EXTRA, count, LANES), lambda g, at: (BODY // EXTRA, 0, 0))
                    for _ in blocks
                ],
                pl.BlockSpec((CROSS_STEP * TURNS, groups, LANES), lambda g, at: (g, 0, 0)),
                pl.BlockSpec((half_tail, groups, LANES), lambda g, at: (BODY // half_tail, 0, 0)),
                pl.BlockSpec((groups, LANES), lambda g, at: (0, 0)),
            ],
            out_specs=[
                pl.BlockSpec((CROSS_STEP * block, total), lambda g, at: (g, 0)),
                pl.BlockSpec((block, total), lambda g, at: (0, 0)),
            ],
            scratch_shapes=[pltpu.VMEM((2 * groups, total), jnp.float32)],
        ),
        out_shape=[
            jax.ShapeDtypeStruct((COEF, total), jnp.float32),
            jax.ShapeDtypeStruct((block, total), jnp.float32),
        ],
        compiler_params=pltpu.CompilerParams(vmem_limit_bytes=60 << 20),
        cost_estimate=pl.CostEstimate(
            flops=4 * size * groups, bytes_accessed=2 * size, transcendentals=0
        ),
        name="cross_coefficients",
    )(cls, *blocks, *blocks, arranged, arranged, norms)


def score_body(*refs, scale):
    *coefs, cand_ref, table_ref, score_ref, stat_ref = refs
    corr = lax.dot_general(
        table_ref[...],
        functools.reduce(jnp.add, [ref[...] for ref in coefs]),
        (((0,), (0,)), ((), ())),
        precision=lax.Precision.HIGHEST,
        preferred_element_type=jnp.float32,
    )
    score = jnp.where(cand_ref[0:1, :] >= 0.0, corr * scale, lowest)
    top = jnp.max(score, axis=0, keepdims=True)
    total = jnp.sum(jnp.exp(score - top), axis=0, keepdims=True)
    score_ref[...] = score
    stat_ref[0:1, :] = top
    stat_ref[1:2, :] = jnp.where(cand_ref[0:1, :] >= 0.0, total, 0.0)


def scores(coefs, cand, table, scale):
    total = cand.shape[1]
    return pl.pallas_call(
        functools.partial(score_body, scale=scale),
        out_shape=[
            jax.ShapeDtypeStruct((ROTS * CAND_OWN, total), jnp.float32),
            jax.ShapeDtypeStruct((2, total), jnp.float32),
        ],
        name="scores",
    )(*coefs, cand, table)


def swap_blocks(x, distance, width):
    lane = lax.broadcasted_iota(jnp.int32, x.shape, 1)
    bit = 1
    while bit <= distance:
        if distance & bit:
            shift = bit * width
            down = pltpu.roll(x, shift, 1)
            up = pltpu.roll(x, x.shape[1] - shift, 1)
            x = jnp.where((lane // shift) % 2 == 1, down, up)
        bit *= 2
    return x


def weights_body(at_ref, score_ref, cand_ref, stat_ref, table_ref, mix_ref, norm_ref):
    n_cls, _, total = stat_ref.shape
    width = total // n_cls
    tops, parts = [], []
    for e in range(n_cls):
        table = stat_ref[at_ref[0] ^ e]
        table = swap_blocks(jnp.concatenate([table] * 4, 0), e, width)
        tops.append(table[0:1])
        parts.append(table[1:2])
    top = functools.reduce(jnp.maximum, tops)
    summed = jnp.zeros_like(top)
    for other, part in zip(tops, parts):
        summed += part * jnp.exp(other - top)
    log_norm = top + jnp.log(summed)
    norm_ref[...] = log_norm[:, : norm_ref.shape[1]]
    weight = jnp.where(cand_ref[0:1, :] >= 0.0, jnp.exp(score_ref[...] - log_norm), 0.0)
    mix_ref[...] = lax.dot_general(
        table_ref[...],
        weight,
        (((1,), (0,)), ((), ())),
        precision=lax.Precision.HIGHEST,
        preferred_element_type=jnp.float32,
    )


def mixed_weights(cls, score, cand, stats, table, count):
    total = score.shape[1]
    return pl.pallas_call(
        weights_body,
        in_specs=[pl.BlockSpec(memory_space=pltpu.SMEM)] + [pl.BlockSpec(memory_space=pltpu.VMEM)] * 4,
        out_shape=[
            jax.ShapeDtypeStruct((COEF, total), jnp.float32),
            jax.ShapeDtypeStruct((1, count), jnp.float32),
        ],
        name="mixed_weights",
    )(cls, score, cand, stats, table)


def sums_body(*refs, number, pieces):
    blocks, extras = refs[:number], refs[number : 2 * number]
    refs = refs[2 * number :]
    mixes, cands = refs[:pieces], refs[pieces : 2 * pieces]
    back_ref, out_ref, weight_ref, mix, cand, planes = refs[2 * pieces :]
    i = pl.program_id(0)
    groups = weight_ref.shape[1]
    total = mix.shape[1]
    imag, odd = lane_signs()

    @pl.when(i == 0)
    def _():
        mixed = jnp.concatenate([ref[...] for ref in mixes], 1)
        chosen = jnp.concatenate([ref[...] for ref in cands], 1)
        hot = hot_masks(chosen, groups)
        summed = jnp.zeros((groups, total), jnp.float32)
        for q in range(CAND_OWN):
            summed += jnp.where(hot[q], mixed[q : q + 1], 0.0)
        weight_ref[...] = lax.dot_general(
            jnp.ones((1, total), jnp.float32),
            summed,
            (((1,), (1,)), ((), ())),
            precision=lax.Precision.HIGHEST,
            preferred_element_type=jnp.float32,
        )
        mix[...] = mixed
        cand[...] = chosen

    @pl.when(i < HALF // SUM_STEP)
    def _():
        hot = hot_masks(cand[...], groups)
        block = 2 * CAND_OWN
        sign = jnp.where(imag == odd, 1.0, -1.0)
        for u in range(SUM_STEP):
            g = i * SUM_STEP + u
            mine = mix[pl.ds(pl.multiple_of(g * block, block), block), :]
            halves = []
            for ab in range(2):
                dense = jnp.zeros((groups, total), jnp.float32)
                for q in range(CAND_OWN):
                    at = ab * CAND_OWN + q
                    dense = jnp.where(hot[q], mine[at : at + 1], dense)
                halves.append(dense)
            weights = jnp.concatenate(halves, 0).astype(jnp.bfloat16)
            made = jnp.dot(
                weights, lanes_of(blocks, u * TURNS, TURNS), preferred_element_type=jnp.float32
            )
            for t in range(TURNS):
                g1 = made[:groups, t * LANES : (t + 1) * LANES]
                g2 = made[groups:, t * LANES : (t + 1) * LANES]
                value = g1 + sign * pltpu.roll(g2, LANES // 2, 1)
                if u == 0:
                    value = jnp.where(i == 0, jnp.where(odd, g2, g1), value)
                start = pl.multiple_of((g * TURNS + t) * groups, groups)
                planes[pl.ds(start, groups), :] = value

            for t in range(TAIL):
                if t % SUM_STEP != u:
                    continue

                @pl.when(g == t)
                def _():
                    made = jnp.dot(
                        weights, lanes_of(extras, t // 2, 1), preferred_element_type=jnp.float32
                    )
                    g1, g2 = made[:groups], made[groups:]
                    value = g1
                    if t > 0:
                        value = g1 + jnp.where(imag, -1.0, 1.0) * pltpu.roll(g2, LANES // 2, 1)
                    rows = pl.ds((BODY + t // 2) * groups, groups)
                    if t % 2:
                        value = jnp.where(odd, value, planes[rows, :])
                    planes[rows, :] = value

    @pl.when(i >= HALF // SUM_STEP)
    def _():
        block, span, _ = out_ref.shape
        first = (i - HALF // SUM_STEP) * block
        back = back_ref[...]
        for c in range(block):
            turned = planes[pl.ds(first + c, CHUNKS, stride=groups), :].T
            parts = []
            for s in range(2):
                at = 2 * s * span
                parts.append(
                    jnp.concatenate([turned[at : at + span], turned[at + span : at + 2 * span]], 1)
                )
            value = jnp.concatenate(parts, 0)
            high = value.astype(jnp.bfloat16)
            low = (value - high.astype(jnp.float32)).astype(jnp.bfloat16)
            placed = jnp.dot(high, back, preferred_element_type=jnp.float32) + jnp.dot(
                low, back, preferred_element_type=jnp.float32
            )
            out_ref[c, :, :HARM] = placed[:span]
            out_ref[c, :, HARM:] = placed[span:]


def sums(blocks, mixes, cands, back, groups, span):
    count = blocks[0].shape[1]
    total = len(blocks) * count
    size = blocks[0].size * len(blocks)
    block = 8
    steps = HALF // SUM_STEP
    whole = lambda i: (0, 0)
    return pl.pallas_call(
        functools.partial(sums_body, number=len(blocks), pieces=len(mixes)),
        grid=(steps + groups // block,),
        in_specs=[
            *[
                pl.BlockSpec(
                    (SUM_STEP * TURNS, count, LANES), lambda i: (jnp.minimum(i, steps - 1), 0, 0)
                )
                for _ in blocks
            ],
            *[
                pl.BlockSpec((EXTRA, count, LANES), lambda i: (BODY // EXTRA, 0, 0))
                for _ in blocks
            ],
            *[pl.BlockSpec(array.shape, whole) for array in (*mixes, *cands, back)],
        ],
        out_specs=[
            pl.BlockSpec(
                (block, span, 2 * HARM), lambda i: (jnp.maximum(i - steps, 0), 0, 0)
            ),
            pl.BlockSpec((1, groups), whole),
        ],
        out_shape=[
            jax.ShapeDtypeStruct((groups, span, 2 * HARM), jnp.float32),
            jax.ShapeDtypeStruct((1, groups), jnp.float32),
        ],
        scratch_shapes=[
            pltpu.VMEM((COEF, total), jnp.float32),
            pltpu.VMEM((2 * CAND_OWN, total), jnp.float32),
            pltpu.VMEM((CHUNKS * groups, LANES), jnp.float32),
        ],
        compiler_params=pltpu.CompilerParams(vmem_limit_bytes=60 << 20),
        cost_estimate=pl.CostEstimate(
            flops=4 * size * groups,
            bytes_accessed=2 * size + 8 * groups * span * HARM,
            transcendentals=0,
        ),
        name="sums",
    )(*blocks, *blocks, *mixes, *cands, back)


def hop(value, axis, distance):
    size = lax.axis_size(axis)
    return lax.ppermute(value, axis, [(i, i ^ distance) for i in range(size)])


def after(value, *others):
    return lax.optimization_barrier((value, *others))[0]


def direct(own):
    n_cls = lax.axis_size("cls")
    return {1 << bit: hop(own, "cls", 1 << bit) for bit in range(1, n_cls.bit_length() - 1)}


def relayed(known, d, *others):
    n_cls = lax.axis_size("cls")
    for j in sorted(range(2, n_cls, 2), key=lambda j: bin(j).count("1")):
        if j not in known:
            bits = [bit for bit in range(1, n_cls.bit_length()) if j >> bit & 1]
            way = 1 << bits[d % len(bits)]
            known[j] = hop(after(known[j ^ way], *others), "cls", way)
    return known


def paired(known, each, last):
    n_cls = lax.axis_size("cls")
    for j in range(0, n_cls, 2):
        others = last if j == n_cls - 2 else each
        block = after(known[j], *others) if others else known[j]
        known[j + 1] = hop(block, "cls", 1)
    return [known[j] for j in range(n_cls)]


def gather_device(particles, references, owner_groups, class_order):
    n_cls, n_prt = lax.axis_size("cls"), lax.axis_size("prt")
    cls, prt = lax.axis_index("cls"), lax.axis_index("prt")
    count, cycles, width = particles.shape
    groups = references.shape[0]
    span = cycles // n_prt
    back = jnp.asarray(unselector(), jnp.bfloat16)
    table = jnp.asarray(rotation_table())
    picks = class_order[:, :, :CAND_OWN].reshape(count, OWN_TOP * CAND_OWN)
    cls, prt = (index.reshape(1).astype(jnp.int32) for index in (cls, prt))
    outgoing = []
    for first in range(0, n_prt, 2):
        distances = tuple(range(first, min(first + 2, n_prt)))
        place = after(prt, outgoing[0]) if outgoing else prt
        outgoing += arrange_particles(
            place, particles, owner_groups, picks, n_prt, distances
        )
    arrived = [outgoing[0]]
    known = [{0: arrived[0], **direct(arrived[0])}]
    for d in range(1, min(n_prt, 3)):
        arrived.append(hop(outgoing[d], "prt", d))
    early = after(arrived[1], outgoing[-1])
    known.append({0: early, **direct(early)})
    relayed(known[0], 0, outgoing[-1])
    place = after(prt, *arrived[1:2], *[known[0][1 << b] for b in range(1, n_cls.bit_length() - 1)])
    arranged, norms = arrange_references(references, place, n_prt)
    for d in range(2, n_prt):
        if d > 2:
            arrived.append(hop(after(outgoing[d], arrived[d - 1], arranged), "prt", d))
        own = after(arrived[d], arranged) if d == 2 else arrived[d]
        known.append({0: own, **direct(own)})
    for d in range(1, n_prt, 2):
        relayed(known[d], d)
    scale = 2.0 / math.sqrt(cycles * width)
    coefs, cands, sent, blocks = [], [], [], []
    for d in range(n_prt):
        waits = []
        if n_prt > 3:
            waits = [[known[1][2]], [arrived[3], known[2][n_cls // 2]], [known[3][2]], []][min(d, 3)]
        if d and d % 2 == 0:
            relayed(known[d], d, coefs[0])
        each = [arranged, known[1][n_cls // 2]] if d == 0 else coefs[:1] if d < 3 else []
        blocks.append(paired(known[d], each, coefs[-1:]))
        ready = after(arranged, *waits) if waits else arranged
        coef, cand = cross_coefficients(blocks[d], ready, norms, cls)
        coefs.append(coef)
        sent.append(hop(coef, "prt", d) if d else coef)
        cands.append(cand)
    score, stat = scores(sent, cands[0], table, scale)
    stats = lax.all_gather(stat.reshape(1, *stat.shape), "cls", axis=0, tiled=True)
    mix, log_norm = mixed_weights(cls, score, cands[0], stats, table, count)
    mixes = [hop(mix, "prt", d) if d else mix for d in range(n_prt)]
    class_sums, class_weights = sums(
        [block for piece in blocks for block in piece], mixes, cands, back, groups, span
    )
    own = log_norm[0]
    return class_sums, class_weights[0], own


def per_device(particles, references, owner_groups, class_order):
    n_cls, n_prt = lax.axis_size("cls"), lax.axis_size("prt")
    count, cycles, _ = particles.shape
    groups = references.shape[0]
    cap = max(2, 2 * count * OWN_TOP // n_cls)
    powers = n_cls & (n_cls - 1) == 0 and n_prt & (n_prt - 1) == 0
    fits = 4 * cycles == LANES * n_prt and n_cls * CAND_OWN <= LANES and groups % 16 == 0 and n_cls >= 4
    fits = fits and powers and n_cls * count == LANES
    plan = gather_device if cap >= count and fits else dispatch_device
    return plan(particles, references, owner_groups, class_order)


def solution(mesh):
    in_specs = (
        P(("cls", "prt"), None, None),
        P("cls", None, None),
        P(("cls", "prt"), None),
        P(("cls", "prt"), None, None),
    )
    out_specs = (P("cls", "prt", None), P("cls"), P(("cls", "prt")))
    return jax.shard_map(
        per_device, mesh=mesh, in_specs=in_specs, out_specs=out_specs, check_vma=False
    )
```

```python
import functools
import math

import jax
import jax.numpy as jnp
import numpy as np
from jax import lax
from jax.experimental import pallas as pl
from jax.experimental.pallas import tpu as pltpu
from jax.sharding import PartitionSpec as P

CYCLES = 128
HARM = 256
ROTS = 36
OWN_TOP = 4
CAND_OWN = 4


lowest = -1e30


def spectral_tables():
    harmonic = jnp.arange(HARM, dtype=jnp.float32)
    angles = 2.0 * math.pi * jnp.arange(ROTS, dtype=jnp.float32) / ROTS
    phase = harmonic[:, None] * angles[None, :]
    forward = jnp.concatenate([jnp.cos(phase), jnp.sin(phase)], 0)
    backward = jnp.concatenate([jnp.cos(phase), -jnp.sin(phase)], 0).T
    return (forward, backward)


def class_accumulate(lanes, mixed):
    l_re = lanes[..., :HARM]
    l_im = lanes[..., HARM:]
    y_re = mixed[..., :HARM]
    y_im = mixed[..., HARM:]
    s_re = jnp.einsum("lrm,lcm->crm", l_re, y_re, preferred_element_type=jnp.float32) - jnp.einsum(
        "lrm,lcm->crm", l_im, y_im, preferred_element_type=jnp.float32
    )
    s_im = jnp.einsum("lrm,lcm->crm", l_re, y_im, preferred_element_type=jnp.float32) + jnp.einsum(
        "lrm,lcm->crm", l_im, y_re, preferred_element_type=jnp.float32
    )
    return jnp.concatenate([s_re, s_im], -1)


def dispatch_device(particles, references, owner_groups, class_order):
    n_cls = lax.axis_size("cls")
    count = particles.shape[0]
    groups = references.shape[0]
    cap = max(2, 2 * count * OWN_TOP // n_cls)
    slots = n_cls * cap
    width = 2 * HARM
    flat_owner = owner_groups.reshape(-1)
    owner_hot = (flat_owner[:, None] == jnp.arange(n_cls, dtype=jnp.int32)[None, :]).astype(
        jnp.int32
    )
    before = jnp.cumsum(owner_hot, axis=0) - owner_hot
    rank = jnp.sum(before * owner_hot, axis=1)
    slot_of = flat_owner * cap + rank
    match = slot_of[None, :] == jnp.arange(slots, dtype=jnp.int32)[:, None]
    member = jnp.any(match.reshape(slots, count, OWN_TOP), axis=2)
    filled = jnp.any(member, axis=1)
    dispatch = member.astype(jnp.bfloat16)
    outgoing = jnp.dot(
        dispatch, particles.reshape(count, CYCLES * width), preferred_element_type=jnp.float32
    )
    outgoing = outgoing.astype(jnp.bfloat16).reshape(n_cls, cap, CYCLES, width)
    match_int = match.astype(jnp.int32)
    picks = class_order[:, :, :CAND_OWN].reshape(count * OWN_TOP, CAND_OWN)
    slot_cand = jnp.where(filled[:, None], jnp.dot(match_int, picks), -1)
    owner_rows = jnp.repeat(jnp.arange(count, dtype=jnp.int32), OWN_TOP)
    slot_pid = jnp.where(filled, jnp.dot(match_int, owner_rows), -1)
    labels_out = jnp.concatenate([slot_cand, slot_pid[:, None]], 1).reshape(
        n_cls, cap, CAND_OWN + 1
    )
    arrived, labels = (
        lax.all_to_all(outgoing, "cls", split_axis=0, concat_axis=0, tiled=True),
        lax.all_to_all(labels_out, "cls", split_axis=0, concat_axis=0, tiled=True),
    )
    lanes = arrived.reshape(slots, CYCLES, width)
    labels = labels.reshape(slots, CAND_OWN + 1)
    forward, backward = spectral_tables()
    scale = 2.0 / math.sqrt(CYCLES * width)
    norms = jnp.sum(jnp.square(references.astype(jnp.float32)), axis=(1, 2))
    l_re = lanes[..., :HARM]
    l_im = lanes[..., HARM:]
    r_re = references[..., :HARM]
    r_im = references[..., HARM:]
    x_re = jnp.einsum("lrm,crm->lcm", l_re, r_re, preferred_element_type=jnp.float32) + jnp.einsum(
        "lrm,crm->lcm", l_im, r_im, preferred_element_type=jnp.float32
    )
    x_im = jnp.einsum("lrm,crm->lcm", l_im, r_re, preferred_element_type=jnp.float32) - jnp.einsum(
        "lrm,crm->lcm", l_re, r_im, preferred_element_type=jnp.float32
    )
    cross = jnp.concatenate([x_re, x_im], -1)
    corr = jnp.dot(
        cross.reshape(slots * groups, width), forward, precision=lax.Precision.HIGHEST
    ).reshape(slots, groups, ROTS)
    score = (corr - 0.5 * norms[None, :, None]) * scale
    candidate = jnp.any(
        labels[:, :CAND_OWN, None] == jnp.arange(groups, dtype=jnp.int32)[None, None, :], axis=1
    )
    part_max = jnp.max(jnp.where(candidate[:, :, None], score, lowest), axis=(1, 2))
    part_sum = jnp.sum(
        jnp.where(candidate[:, :, None], jnp.exp(score - part_max[:, None, None]), 0.0), axis=(1, 2)
    )
    sender_ids = labels[:, CAND_OWN].astype(jnp.float32)
    table_max, table_sum, table_ids = (
        lax.all_gather(part_max.reshape(1, n_cls, cap), "cls", axis=0, tiled=True),
        lax.all_gather(part_sum.reshape(1, n_cls, cap), "cls", axis=0, tiled=True),
        lax.all_gather(sender_ids.reshape(1, n_cls, cap), "cls", axis=0, tiled=True),
    )
    local_ids = jnp.arange(count, dtype=jnp.float32)
    hit = table_ids[..., None] == local_ids
    top = jnp.max(jnp.where(hit, table_max[..., None], lowest), axis=(0, 2))
    total = jnp.sum(
        jnp.where(
            hit, table_sum[..., None] * jnp.exp(table_max[..., None] - top[None, :, None, :]), 0.0
        ),
        axis=(0, 2),
    )
    table_norm = top + jnp.log(total)
    slot_ids = labels[:, CAND_OWN].reshape(n_cls, cap)
    slot_norm = jnp.sum(
        jnp.where(
            slot_ids[..., None] == jnp.arange(count, dtype=jnp.int32), table_norm[:, None, :], 0.0
        ),
        axis=2,
    ).reshape(slots)
    own_norm = lax.dynamic_index_in_dim(table_norm, lax.axis_index("cls"), 0, keepdims=False)
    weight = jnp.where(candidate[:, :, None], jnp.exp(score - slot_norm[:, None, None]), 0.0)
    mixed = (
        jnp.dot(weight.reshape(slots * groups, ROTS), backward, precision=lax.Precision.HIGHEST)
        .astype(jnp.bfloat16)
        .reshape(slots, groups, width)
    )
    class_weights = lax.psum(jnp.sum(weight, axis=(0, 2)), "prt")
    partial_sums = class_accumulate(lanes, mixed)
    class_sums = lax.psum_scatter(partial_sums, "prt", scatter_dimension=1, tiled=True)
    return (class_sums, class_weights, own_norm)


LANES = 128


def harmonic_plan():
    half = ROTS // 2
    turns = HARM // ROTS
    tail = HARM - turns * ROTS
    chunk_of = np.zeros(HARM, np.int32)
    side_of = np.zeros(HARM, np.int32)
    for m in range(HARM):
        turn, rest = divmod(m, ROTS)
        if turn == turns:
            chunk_of[m] = half * turns + rest // 2
            side_of[m] = rest % 2
        elif rest < half:
            chunk_of[m] = rest * turns + turn
        else:
            chunk_of[m] = ((ROTS - rest) % half) * turns + turn
            side_of[m] = 1
    return half, turns, tail, chunk_of, side_of


HALF, TURNS, TAIL, CHUNK_OF, SIDE_OF = harmonic_plan()
BODY = HALF * TURNS
CHUNKS = BODY + TAIL // 2
EXTRA = TAIL // 2 + 1
COEF = 2 * HALF * CAND_OWN
CROSS_STEP = 6
SUM_STEP = 3


def selector():
    return (np.arange(CHUNKS)[:, None] == CHUNK_OF[None, :]).astype(np.float32)


def unselector():
    sel = selector()
    return np.concatenate([sel * (SIDE_OF == 0), sel * (SIDE_OF == 1)], 0)


def rotation_table():
    table = np.zeros((HALF, 2, CAND_OWN, ROTS, CAND_OWN))
    angle = 2.0 * np.pi * np.arange(ROTS) / ROTS
    for g in range(HALF):
        first = np.cos(g * angle)
        second = np.cos(HALF * angle) if g == 0 else np.sin(g * angle)
        for q in range(CAND_OWN):
            table[g, 0, q, :, q] = first
            table[g, 1, q, :, q] = second
    return table.reshape(COEF, ROTS * CAND_OWN).astype(np.float32)


def nt_dot(a, b):
    return lax.dot_general(a, b, (((1,), (1,)), ((), ())), preferred_element_type=jnp.float32)


def selector_masks():
    m = lax.broadcasted_iota(jnp.int32, (1, HARM), 1)
    turn = jnp.zeros((1, HARM), jnp.int32)
    for t in range(1, TURNS + 1):
        turn += jnp.where(m >= t * ROTS, 1, 0)
    rest = m - ROTS * turn
    back = jnp.where(rest == HALF, 0, ROTS - rest)
    chunk = jnp.where(rest < HALF, rest, back) * TURNS + turn
    side = jnp.where(rest < HALF, 0, 1)
    chunk = jnp.where(turn == TURNS, BODY + rest // 2, chunk)
    side = jnp.where(turn == TURNS, rest % 2, side)
    rows = lax.broadcasted_iota(jnp.int32, (CHUNKS, HARM), 0)
    sel = jnp.where(rows == chunk, 1.0, 0.0).astype(jnp.bfloat16)
    sides = lax.broadcasted_iota(jnp.int32, (2, HARM), 0)
    masks = jnp.where(sides == side, 1.0, 0.0).astype(jnp.bfloat16)
    return sel, masks


def masked_stack(piece, masks):
    parts = []
    for s in range(2):
        for b in range(2):
            parts.append(piece[:, s * HARM : (s + 1) * HARM] * masks[b : b + 1])
    return jnp.concatenate(parts, 0)


def repeat(number, step, body, carry):
    def several(i, carry):
        for u in range(step):
            carry = body(i * step + u, carry)
        return carry

    return lax.fori_loop(0, number // step, several, carry)


def particle_body(at_ref, x_ref, meta_ref, *refs, distances, n_prt):
    outs, scr = refs[:-1], refs[-1]
    count, cycles, _ = x_ref.shape
    number = len(outs)
    span = cycles // n_prt
    sel, masks = selector_masks()

    def one(n, carry):
        parts = []
        for d in distances:
            start = pl.multiple_of((at_ref[0] ^ d) * span, span)
            parts.append(masked_stack(x_ref[n, pl.ds(start, span), :], masks))
        w = jnp.concatenate(parts, 0)
        y = nt_dot(sel, w)
        for p in range(number):
            scr[p, pl.ds(pl.multiple_of(n * CHUNKS, CHUNKS), CHUNKS), :] = y[
                :, p * LANES : (p + 1) * LANES
            ]
        return carry

    repeat(count, 4, one, 0)

    def two(c, carry):
        for p in range(number):
            outs[p][c] = scr[p, pl.ds(c, count, stride=CHUNKS), :].astype(jnp.bfloat16)
        return carry

    repeat(CHUNKS, 8, two, 0)
    lane = lax.broadcasted_iota(jnp.int32, (count, LANES), 1)
    label = jnp.full((count, LANES), -1, jnp.int32)
    for t in range(OWN_TOP):
        mine = (lane // CAND_OWN) == meta_ref[:, t : t + 1]
        for q in range(CAND_OWN):
            at = OWN_TOP + t * CAND_OWN + q
            label = jnp.where(
                mine & (lane % CAND_OWN == q), meta_ref[:, at : at + 1], label
            )
    label = label.astype(jnp.float32).astype(jnp.bfloat16)
    for p in range(number):
        outs[p][CHUNKS] = label


def arrange_particles(prt, particles, meta, n_prt, distances):
    count = particles.shape[0]
    number = len(distances)
    size = particles.size * number // n_prt
    return pl.pallas_call(
        functools.partial(particle_body, distances=distances, n_prt=n_prt),
        in_specs=[pl.BlockSpec(memory_space=pltpu.SMEM)] + [pl.BlockSpec(memory_space=pltpu.VMEM)] * 2,
        out_shape=[jax.ShapeDtypeStruct((CHUNKS + 1, count, LANES), jnp.bfloat16)] * number,
        scratch_shapes=[pltpu.VMEM((number, count * CHUNKS, LANES), jnp.float32)],
        compiler_params=pltpu.CompilerParams(vmem_limit_bytes=32 << 20),
        cost_estimate=pl.CostEstimate(
            flops=size * 2 * CHUNKS, bytes_accessed=size * 4, transcendentals=0
        ),
        name="arrange_particles",
    )(prt, particles, meta)


def reference_body(at_ref, x_ref, out_ref, norm_ref, scr):
    rows = x_ref.shape[0]
    sel, masks = selector_masks()
    step = 4

    def one(n, carry):
        w = jnp.concatenate([masked_stack(x_ref[n * step + i], masks) for i in range(step)], 0)
        y = nt_dot(sel, w)
        for i in range(step):
            scr[pl.ds(pl.multiple_of((n * step + i) * CHUNKS, CHUNKS), CHUNKS), :] = y[
                :, i * LANES : (i + 1) * LANES
            ]
        return carry

    repeat(rows // step, 2, one, 0)

    def two(c, carry):
        value = scr[pl.ds(c, rows, stride=CHUNKS), :]
        out_ref[c] = value.astype(jnp.bfloat16)
        return carry + value * value

    norm_ref[...] = repeat(CHUNKS, 8, two, jnp.zeros((rows, LANES), jnp.float32))


def arrange_references(references, prt, n_prt):
    groups, cycles, width = references.shape
    span = cycles // n_prt
    block = 16
    return pl.pallas_call(
        reference_body,
        grid_spec=pltpu.PrefetchScalarGridSpec(
            num_scalar_prefetch=1,
            grid=(groups // block,),
            in_specs=[
                pl.BlockSpec((block, span, width), lambda i, at: (i, at[0], 0)),
            ],
            out_specs=[
                pl.BlockSpec((CHUNKS, block, LANES), lambda i, at: (0, i, 0)),
                pl.BlockSpec((block, LANES), lambda i, at: (i, 0)),
            ],
            scratch_shapes=[pltpu.VMEM((block * CHUNKS, LANES), jnp.float32)],
        ),
        out_shape=[
            jax.ShapeDtypeStruct((CHUNKS, groups, LANES), jnp.bfloat16),
            jax.ShapeDtypeStruct((groups, LANES), jnp.float32),
        ],
        compiler_params=pltpu.CompilerParams(vmem_limit_bytes=60 << 20),
        cost_estimate=pl.CostEstimate(
            flops=groups * span * width * 2 * CHUNKS,
            bytes_accessed=groups * span * width * 4,
            transcendentals=0,
        ),
        name="arrange_references",
    )(prt, references)


def lane_signs():
    lane = lax.broadcasted_iota(jnp.int32, (1, LANES), 1)
    quarter = LANES // 4
    imag = lane >= 2 * quarter
    odd = (lane // quarter) % 2 == 1
    return imag, odd


def lanes_of(refs, first, number):
    parts = [
        jnp.concatenate([ref[i] for ref in refs], 0) for i in range(first, first + number)
    ]
    return jnp.concatenate(parts, 1) if number > 1 else parts[0]


def hot_masks(cand, groups):
    rows = lax.broadcasted_iota(jnp.int32, (groups, cand.shape[1]), 0).astype(jnp.float32)
    return [rows == cand[q : q + 1] for q in range(CAND_OWN)]


def residue_weights(q_ref, at, g):
    imag, odd = lane_signs()
    sign = jnp.where(imag == odd, -1.0, 1.0)
    first, second = [], []
    for i in range(TURNS):
        q = q_ref[at * TURNS + i].astype(jnp.float32)
        turned = pltpu.roll(q, LANES // 2, 1) * sign
        if at == 0:
            first.append(jnp.where((g == 0) & odd, 0.0, q))
            second.append(jnp.where(g == 0, jnp.where(odd, q, 0.0), turned))
        else:
            first.append(q)
            second.append(turned)
    return jnp.concatenate(
        [jnp.concatenate(first, 1), jnp.concatenate(second, 1)], 0
    ).astype(jnp.bfloat16)


def chosen_rows(acc, cand):
    groups = acc.shape[0] // 2
    hot = hot_masks(cand, groups)
    rows = []
    for ab in range(2):
        part = acc[ab * groups : (ab + 1) * groups, :]
        for q in range(CAND_OWN):
            rows.append(jnp.sum(jnp.where(hot[q], part, 0.0), axis=0, keepdims=True))
    return jnp.concatenate(rows, 0)


def cross_body(at_ref, *refs):
    number = (len(refs) - 6) // 2
    blocks, extras = refs[:number], refs[number : 2 * number]
    q_ref, qt_ref, norm_ref, coef_ref, cand_ref, acc = refs[2 * number :]
    step = pl.program_id(0)
    groups = q_ref.shape[1]
    imag, odd = lane_signs()

    @pl.when(step == 0)
    def _():
        label = lanes_of(extras, TAIL // 2, 1).astype(jnp.float32).T
        row = lax.broadcasted_iota(jnp.int32, label.shape, 0)
        base = at_ref[0] * CAND_OWN
        for q in range(CAND_OWN):
            cand_ref[q : q + 1, :] = jnp.sum(
                jnp.where(row == base + q, label, 0.0), axis=0, keepdims=True
            )
        cand_ref[CAND_OWN:, :] = jnp.full(
            (cand_ref.shape[0] - CAND_OWN, cand_ref.shape[1]), -1.0, jnp.float32
        )

    for u in range(CROSS_STEP):
        g = step * CROSS_STEP + u
        acc[...] = nt_dot(residue_weights(q_ref, u, g), lanes_of(blocks, u * TURNS, TURNS))

        for i in range(TAIL):
            if i % CROSS_STEP != u:
                continue

            @pl.when(g == i)
            def _():
                q = qt_ref[i // 2].astype(jnp.float32)
                keep = odd if i % 2 else ~odd
                a = jnp.where(keep, q, 0.0)
                turned = pltpu.roll(q, LANES // 2, 1) * jnp.where(imag, 1.0, -1.0)
                b = jnp.where(keep, turned, 0.0)
                if i == 0:
                    b = jnp.zeros_like(b)
                w = jnp.concatenate([a, b], 0).astype(jnp.bfloat16)
                acc[...] += nt_dot(w, lanes_of(extras, i // 2, 1))
                if i == 0:
                    acc[:groups, :] -= 0.5 * jnp.sum(norm_ref[...], axis=1, keepdims=True)

        block = 2 * CAND_OWN
        coef_ref[u * block : (u + 1) * block, :] = chosen_rows(acc[...], cand_ref[...])


def cross_coefficients(blocks, arranged, norms, cls):
    count = blocks[0].shape[1]
    groups = arranged.shape[1]
    total = len(blocks) * count
    half_tail = TAIL // 2
    size = blocks[0].size * len(blocks)
    block = 2 * CAND_OWN
    return pl.pallas_call(
        cross_body,
        grid_spec=pltpu.PrefetchScalarGridSpec(
            num_scalar_prefetch=1,
            grid=(HALF // CROSS_STEP,),
            in_specs=[
                *[
                    pl.BlockSpec((CROSS_STEP * TURNS, count, LANES), lambda g, at: (g, 0, 0))
                    for _ in blocks
                ],
                *[
                    pl.BlockSpec((EXTRA, count, LANES), lambda g, at: (BODY // EXTRA, 0, 0))
                    for _ in blocks
                ],
                pl.BlockSpec((CROSS_STEP * TURNS, groups, LANES), lambda g, at: (g, 0, 0)),
                pl.BlockSpec((half_tail, groups, LANES), lambda g, at: (BODY // half_tail, 0, 0)),
                pl.BlockSpec((groups, LANES), lambda g, at: (0, 0)),
            ],
            out_specs=[
                pl.BlockSpec((CROSS_STEP * block, total), lambda g, at: (g, 0)),
                pl.BlockSpec((block, total), lambda g, at: (0, 0)),
            ],
            scratch_shapes=[pltpu.VMEM((2 * groups, total), jnp.float32)],
        ),
        out_shape=[
            jax.ShapeDtypeStruct((COEF, total), jnp.float32),
            jax.ShapeDtypeStruct((block, total), jnp.float32),
        ],
        compiler_params=pltpu.CompilerParams(vmem_limit_bytes=60 << 20),
        cost_estimate=pl.CostEstimate(
            flops=4 * size * groups, bytes_accessed=2 * size, transcendentals=0
        ),
        name="cross_coefficients",
    )(cls, *blocks, *blocks, arranged, arranged, norms)


def score_body(*refs, scale):
    *coefs, cand_ref, table_ref, score_ref, stat_ref = refs
    corr = lax.dot_general(
        table_ref[...],
        functools.reduce(jnp.add, [ref[...] for ref in coefs]),
        (((0,), (0,)), ((), ())),
        precision=lax.Precision.HIGHEST,
        preferred_element_type=jnp.float32,
    )
    score = jnp.where(cand_ref[0:1, :] >= 0.0, corr * scale, lowest)
    top = jnp.max(score, axis=0, keepdims=True)
    total = jnp.sum(jnp.exp(score - top), axis=0, keepdims=True)
    score_ref[...] = score
    stat_ref[0:1, :] = top
    stat_ref[1:2, :] = jnp.where(cand_ref[0:1, :] >= 0.0, total, 0.0)


def scores(coefs, cand, table, scale):
    total = cand.shape[1]
    return pl.pallas_call(
        functools.partial(score_body, scale=scale),
        out_shape=[
            jax.ShapeDtypeStruct((ROTS * CAND_OWN, total), jnp.float32),
            jax.ShapeDtypeStruct((2, total), jnp.float32),
        ],
        name="scores",
    )(*coefs, cand, table)


def swap_blocks(x, distance, width):
    lane = lax.broadcasted_iota(jnp.int32, x.shape, 1)
    bit = 1
    while bit <= distance:
        if distance & bit:
            shift = bit * width
            down = pltpu.roll(x, shift, 1)
            up = pltpu.roll(x, x.shape[1] - shift, 1)
            x = jnp.where((lane // shift) % 2 == 1, down, up)
        bit *= 2
    return x


def weights_body(at_ref, score_ref, cand_ref, stat_ref, table_ref, mix_ref, norm_ref):
    n_cls, _, total = stat_ref.shape
    width = total // n_cls
    tops, parts = [], []
    for e in range(n_cls):
        table = stat_ref[at_ref[0] ^ e]
        table = swap_blocks(jnp.concatenate([table] * 4, 0), e, width)
        tops.append(table[0:1])
        parts.append(table[1:2])
    top = functools.reduce(jnp.maximum, tops)
    summed = jnp.zeros_like(top)
    for other, part in zip(tops, parts):
        summed += part * jnp.exp(other - top)
    log_norm = top + jnp.log(summed)
    norm_ref[...] = log_norm[:, : norm_ref.shape[1]]
    weight = jnp.where(cand_ref[0:1, :] >= 0.0, jnp.exp(score_ref[...] - log_norm), 0.0)
    mix_ref[...] = lax.dot_general(
        table_ref[...],
        weight,
        (((1,), (0,)), ((), ())),
        precision=lax.Precision.HIGHEST,
        preferred_element_type=jnp.float32,
    )


def mixed_weights(cls, score, cand, stats, table, count):
    total = score.shape[1]
    return pl.pallas_call(
        weights_body,
        in_specs=[pl.BlockSpec(memory_space=pltpu.SMEM)] + [pl.BlockSpec(memory_space=pltpu.VMEM)] * 4,
        out_shape=[
            jax.ShapeDtypeStruct((COEF, total), jnp.float32),
            jax.ShapeDtypeStruct((1, count), jnp.float32),
        ],
        name="mixed_weights",
    )(cls, score, cand, stats, table)


def sums_body(*refs, number, pieces):
    blocks, extras = refs[:number], refs[number : 2 * number]
    refs = refs[2 * number :]
    mixes, cands = refs[:pieces], refs[pieces : 2 * pieces]
    back_ref, out_ref, weight_ref, mix, cand, planes = refs[2 * pieces :]
    i = pl.program_id(0)
    groups = weight_ref.shape[1]
    total = mix.shape[1]
    imag, odd = lane_signs()

    @pl.when(i == 0)
    def _():
        mixed = jnp.concatenate([ref[...] for ref in mixes], 1)
        chosen = jnp.concatenate([ref[...] for ref in cands], 1)
        hot = hot_masks(chosen, groups)
        summed = jnp.zeros((groups, total), jnp.float32)
        for q in range(CAND_OWN):
            summed += jnp.where(hot[q], mixed[q : q + 1], 0.0)
        weight_ref[...] = lax.dot_general(
            jnp.ones((1, total), jnp.float32),
            summed,
            (((1,), (1,)), ((), ())),
            precision=lax.Precision.HIGHEST,
            preferred_element_type=jnp.float32,
        )
        mix[...] = mixed
        cand[...] = chosen

    @pl.when(i < HALF // SUM_STEP)
    def _():
        hot = hot_masks(cand[...], groups)
        block = 2 * CAND_OWN
        sign = jnp.where(imag == odd, 1.0, -1.0)
        for u in range(SUM_STEP):
            g = i * SUM_STEP + u
            mine = mix[pl.ds(pl.multiple_of(g * block, block), block), :]
            halves = []
            for ab in range(2):
                dense = jnp.zeros((groups, total), jnp.float32)
                for q in range(CAND_OWN):
                    at = ab * CAND_OWN + q
                    dense = jnp.where(hot[q], mine[at : at + 1], dense)
                halves.append(dense)
            weights = jnp.concatenate(halves, 0).astype(jnp.bfloat16)
            made = jnp.dot(
                weights, lanes_of(blocks, u * TURNS, TURNS), preferred_element_type=jnp.float32
            )
            for t in range(TURNS):
                g1 = made[:groups, t * LANES : (t + 1) * LANES]
                g2 = made[groups:, t * LANES : (t + 1) * LANES]
                value = g1 + sign * pltpu.roll(g2, LANES // 2, 1)
                if u == 0:
                    value = jnp.where(i == 0, jnp.where(odd, g2, g1), value)
                start = pl.multiple_of((g * TURNS + t) * groups, groups)
                planes[pl.ds(start, groups), :] = value

            for t in range(TAIL):
                if t % SUM_STEP != u:
                    continue

                @pl.when(g == t)
                def _():
                    made = jnp.dot(
                        weights, lanes_of(extras, t // 2, 1), preferred_element_type=jnp.float32
                    )
                    g1, g2 = made[:groups], made[groups:]
                    value = g1
                    if t > 0:
                        value = g1 + jnp.where(imag, -1.0, 1.0) * pltpu.roll(g2, LANES // 2, 1)
                    rows = pl.ds((BODY + t // 2) * groups, groups)
                    if t % 2:
                        value = jnp.where(odd, value, planes[rows, :])
                    planes[rows, :] = value

    @pl.when(i >= HALF // SUM_STEP)
    def _():
        block, span, _ = out_ref.shape
        first = (i - HALF // SUM_STEP) * block
        back = back_ref[...]
        values = []
        for c in range(block):
            turned = planes[pl.ds(first + c, CHUNKS, stride=groups), :].T
            for s in range(2):
                at = 2 * s * span
                values.append(
                    jnp.concatenate([turned[at : at + span], turned[at + span : at + 2 * span]], 1)
                )
        value = jnp.concatenate(values, 0)
        high = value.astype(jnp.bfloat16)
        low = (value - high.astype(jnp.float32)).astype(jnp.bfloat16)
        both = jnp.dot(
            jnp.concatenate([high, low], 0), back, preferred_element_type=jnp.float32
        )
        rows = value.shape[0]
        placed = both[:rows] + both[rows:]
        for c in range(block):
            for s in range(2):
                at = (2 * c + s) * span
                out_ref[c, :, s * HARM : (s + 1) * HARM] = placed[at : at + span]


def sums(blocks, mixes, cands, back, groups, span):
    count = blocks[0].shape[1]
    total = len(blocks) * count
    size = blocks[0].size * len(blocks)
    block = 8
    steps = HALF // SUM_STEP
    whole = lambda i: (0, 0)
    return pl.pallas_call(
        functools.partial(sums_body, number=len(blocks), pieces=len(mixes)),
        grid=(steps + groups // block,),
        in_specs=[
            *[
                pl.BlockSpec(
                    (SUM_STEP * TURNS, count, LANES), lambda i: (jnp.minimum(i, steps - 1), 0, 0)
                )
                for _ in blocks
            ],
            *[
                pl.BlockSpec((EXTRA, count, LANES), lambda i: (BODY // EXTRA, 0, 0))
                for _ in blocks
            ],
            *[pl.BlockSpec(array.shape, whole) for array in (*mixes, *cands, back)],
        ],
        out_specs=[
            pl.BlockSpec(
                (block, span, 2 * HARM), lambda i: (jnp.maximum(i - steps, 0), 0, 0)
            ),
            pl.BlockSpec((1, groups), whole),
        ],
        out_shape=[
            jax.ShapeDtypeStruct((groups, span, 2 * HARM), jnp.float32),
            jax.ShapeDtypeStruct((1, groups), jnp.float32),
        ],
        scratch_shapes=[
            pltpu.VMEM((COEF, total), jnp.float32),
            pltpu.VMEM((2 * CAND_OWN, total), jnp.float32),
            pltpu.VMEM((CHUNKS * groups, LANES), jnp.float32),
        ],
        compiler_params=pltpu.CompilerParams(vmem_limit_bytes=60 << 20),
        cost_estimate=pl.CostEstimate(
            flops=4 * size * groups,
            bytes_accessed=2 * size + 8 * groups * span * HARM,
            transcendentals=0,
        ),
        name="sums",
    )(*blocks, *blocks, *mixes, *cands, back)


def hop(value, axis, distance):
    size = lax.axis_size(axis)
    return lax.ppermute(value, axis, [(i, i ^ distance) for i in range(size)])


def after(value, *others):
    return lax.optimization_barrier((value, *others))[0]


def direct(own):
    n_cls = lax.axis_size("cls")
    return {1 << bit: hop(own, "cls", 1 << bit) for bit in range(1, n_cls.bit_length() - 1)}


def relayed(known, d, *others):
    n_cls = lax.axis_size("cls")
    for j in sorted(range(2, n_cls, 2), key=lambda j: bin(j).count("1")):
        if j not in known:
            bits = [bit for bit in range(1, n_cls.bit_length()) if j >> bit & 1]
            way = 1 << bits[d % len(bits)]
            known[j] = hop(after(known[j ^ way], *others), "cls", way)
    return known


def paired(known, each, last):
    n_cls = lax.axis_size("cls")
    for j in range(0, n_cls, 2):
        others = last if j == n_cls - 2 else each
        block = after(known[j], *others) if others else known[j]
        known[j + 1] = hop(block, "cls", 1)
    return [known[j] for j in range(n_cls)]


def gather_device(particles, references, owner_groups, class_order):
    n_cls, n_prt = lax.axis_size("cls"), lax.axis_size("prt")
    cls, prt = lax.axis_index("cls"), lax.axis_index("prt")
    count, cycles, width = particles.shape
    groups = references.shape[0]
    span = cycles // n_prt
    back = jnp.asarray(unselector(), jnp.bfloat16)
    table = jnp.asarray(rotation_table())
    picks = class_order[:, :, :CAND_OWN].reshape(count, OWN_TOP * CAND_OWN)
    meta = jnp.concatenate([owner_groups, picks], 1)
    cls, prt = (index.reshape(1).astype(jnp.int32) for index in (cls, prt))
    order = [d for d in range(n_prt) if d % 2 == 0] + [d for d in range(n_prt) if d % 2]
    outgoing = {}
    place = prt
    for first in range(0, n_prt, 2):
        distances = tuple(order[first : first + 2])
        made = arrange_particles(place, particles, meta, n_prt, distances)
        outgoing.update(zip(distances, made))
        place = after(prt, made[0])
    last = outgoing[order[-1]]
    arrived = {d: hop(outgoing[d], "prt", d) if d else outgoing[d] for d in order}
    known = {0: {0: arrived[0], **direct(arrived[0])}}
    for d in range(1, min(n_prt, 3)):
        own = after(arrived[d], last) if d == 2 else arrived[d]
        known[d] = {0: own, **direct(own)}
    place = after(prt, *[arrived[d] for d in range(1, min(n_prt, 3))])
    arranged, norms = arrange_references(references, place, n_prt)
    for d in range(3, n_prt):
        arrived[d] = after(arrived[d], arranged)
        known[d] = {0: arrived[d], **direct(arrived[d])}
    relayed(known[0], 0, arranged)
    for d in range(1, n_prt):
        relayed(known[d], d)
    scale = 2.0 / math.sqrt(cycles * width)
    coefs, cands, sent, blocks = [], [], [], []
    for d in range(n_prt):
        waits = [known[n_prt - 1][2]] if d == 1 else []
        each = [arranged] if d == 0 else [arranged, arrived[n_prt - 1]] if d == 1 else coefs[:1]
        blocks.append(paired(known[d], each, coefs[-1:] if d > 1 else []))
        ready = after(arranged, *waits) if waits else arranged
        coef, cand = cross_coefficients(blocks[d], ready, norms, cls)
        coefs.append(coef)
        sent.append(hop(coef, "prt", d) if d else coef)
        cands.append(cand)
    score, stat = scores(sent, cands[0], table, scale)
    stats = lax.all_gather(stat.reshape(1, *stat.shape), "cls", axis=0, tiled=True)
    mix, log_norm = mixed_weights(cls, score, cands[0], stats, table, count)
    mixes = [hop(mix, "prt", d) if d else mix for d in range(n_prt)]
    class_sums, class_weights = sums(
        [block for piece in blocks for block in piece], mixes, cands, back, groups, span
    )
    own = log_norm[0]
    return class_sums, class_weights[0], own


def per_device(particles, references, owner_groups, class_order):
    n_cls, n_prt = lax.axis_size("cls"), lax.axis_size("prt")
    count, cycles, _ = particles.shape
    groups = references.shape[0]
    cap = max(2, 2 * count * OWN_TOP // n_cls)
    powers = n_cls & (n_cls - 1) == 0 and n_prt & (n_prt - 1) == 0
    fits = 4 * cycles == LANES * n_prt and n_cls * CAND_OWN <= LANES and groups % 16 == 0 and n_cls >= 4
    fits = fits and powers and n_cls * count == LANES
    plan = gather_device if cap >= count and fits else dispatch_device
    return plan(particles, references, owner_groups, class_order)


def solution(mesh):
    in_specs = (
        P(("cls", "prt"), None, None),
        P("cls", None, None),
        P(("cls", "prt"), None),
        P(("cls", "prt"), None, None),
    )
    out_specs = (P("cls", "prt", None), P("cls"), P(("cls", "prt")))
    return jax.shard_map(
        per_device, mesh=mesh, in_specs=in_specs, out_specs=out_specs, check_vma=False
    )
```

```python
import functools
import math

import jax
import jax.numpy as jnp
import numpy as np
from jax import lax
from jax.experimental import pallas as pl
from jax.experimental.pallas import tpu as pltpu
from jax.sharding import PartitionSpec as P

CYCLES = 128
HARM = 256
ROTS = 36
OWN_TOP = 4
CAND_OWN = 4


lowest = -1e30


def spectral_tables():
    harmonic = jnp.arange(HARM, dtype=jnp.float32)
    angles = 2.0 * math.pi * jnp.arange(ROTS, dtype=jnp.float32) / ROTS
    phase = harmonic[:, None] * angles[None, :]
    forward = jnp.concatenate([jnp.cos(phase), jnp.sin(phase)], 0)
    backward = jnp.concatenate([jnp.cos(phase), -jnp.sin(phase)], 0).T
    return (forward, backward)


def class_accumulate(lanes, mixed):
    l_re = lanes[..., :HARM]
    l_im = lanes[..., HARM:]
    y_re = mixed[..., :HARM]
    y_im = mixed[..., HARM:]
    s_re = jnp.einsum("lrm,lcm->crm", l_re, y_re, preferred_element_type=jnp.float32) - jnp.einsum(
        "lrm,lcm->crm", l_im, y_im, preferred_element_type=jnp.float32
    )
    s_im = jnp.einsum("lrm,lcm->crm", l_re, y_im, preferred_element_type=jnp.float32) + jnp.einsum(
        "lrm,lcm->crm", l_im, y_re, preferred_element_type=jnp.float32
    )
    return jnp.concatenate([s_re, s_im], -1)


def dispatch_device(particles, references, owner_groups, class_order):
    n_cls = lax.axis_size("cls")
    count = particles.shape[0]
    groups = references.shape[0]
    cap = max(2, 2 * count * OWN_TOP // n_cls)
    slots = n_cls * cap
    width = 2 * HARM
    flat_owner = owner_groups.reshape(-1)
    owner_hot = (flat_owner[:, None] == jnp.arange(n_cls, dtype=jnp.int32)[None, :]).astype(
        jnp.int32
    )
    before = jnp.cumsum(owner_hot, axis=0) - owner_hot
    rank = jnp.sum(before * owner_hot, axis=1)
    slot_of = flat_owner * cap + rank
    match = slot_of[None, :] == jnp.arange(slots, dtype=jnp.int32)[:, None]
    member = jnp.any(match.reshape(slots, count, OWN_TOP), axis=2)
    filled = jnp.any(member, axis=1)
    dispatch = member.astype(jnp.bfloat16)
    outgoing = jnp.dot(
        dispatch, particles.reshape(count, CYCLES * width), preferred_element_type=jnp.float32
    )
    outgoing = outgoing.astype(jnp.bfloat16).reshape(n_cls, cap, CYCLES, width)
    match_int = match.astype(jnp.int32)
    picks = class_order[:, :, :CAND_OWN].reshape(count * OWN_TOP, CAND_OWN)
    slot_cand = jnp.where(filled[:, None], jnp.dot(match_int, picks), -1)
    owner_rows = jnp.repeat(jnp.arange(count, dtype=jnp.int32), OWN_TOP)
    slot_pid = jnp.where(filled, jnp.dot(match_int, owner_rows), -1)
    labels_out = jnp.concatenate([slot_cand, slot_pid[:, None]], 1).reshape(
        n_cls, cap, CAND_OWN + 1
    )
    arrived, labels = (
        lax.all_to_all(outgoing, "cls", split_axis=0, concat_axis=0, tiled=True),
        lax.all_to_all(labels_out, "cls", split_axis=0, concat_axis=0, tiled=True),
    )
    lanes = arrived.reshape(slots, CYCLES, width)
    labels = labels.reshape(slots, CAND_OWN + 1)
    forward, backward = spectral_tables()
    scale = 2.0 / math.sqrt(CYCLES * width)
    norms = jnp.sum(jnp.square(references.astype(jnp.float32)), axis=(1, 2))
    l_re = lanes[..., :HARM]
    l_im = lanes[..., HARM:]
    r_re = references[..., :HARM]
    r_im = references[..., HARM:]
    x_re = jnp.einsum("lrm,crm->lcm", l_re, r_re, preferred_element_type=jnp.float32) + jnp.einsum(
        "lrm,crm->lcm", l_im, r_im, preferred_element_type=jnp.float32
    )
    x_im = jnp.einsum("lrm,crm->lcm", l_im, r_re, preferred_element_type=jnp.float32) - jnp.einsum(
        "lrm,crm->lcm", l_re, r_im, preferred_element_type=jnp.float32
    )
    cross = jnp.concatenate([x_re, x_im], -1)
    corr = jnp.dot(
        cross.reshape(slots * groups, width), forward, precision=lax.Precision.HIGHEST
    ).reshape(slots, groups, ROTS)
    score = (corr - 0.5 * norms[None, :, None]) * scale
    candidate = jnp.any(
        labels[:, :CAND_OWN, None] == jnp.arange(groups, dtype=jnp.int32)[None, None, :], axis=1
    )
    part_max = jnp.max(jnp.where(candidate[:, :, None], score, lowest), axis=(1, 2))
    part_sum = jnp.sum(
        jnp.where(candidate[:, :, None], jnp.exp(score - part_max[:, None, None]), 0.0), axis=(1, 2)
    )
    sender_ids = labels[:, CAND_OWN].astype(jnp.float32)
    table_max, table_sum, table_ids = (
        lax.all_gather(part_max.reshape(1, n_cls, cap), "cls", axis=0, tiled=True),
        lax.all_gather(part_sum.reshape(1, n_cls, cap), "cls", axis=0, tiled=True),
        lax.all_gather(sender_ids.reshape(1, n_cls, cap), "cls", axis=0, tiled=True),
    )
    local_ids = jnp.arange(count, dtype=jnp.float32)
    hit = table_ids[..., None] == local_ids
    top = jnp.max(jnp.where(hit, table_max[..., None], lowest), axis=(0, 2))
    total = jnp.sum(
        jnp.where(
            hit, table_sum[..., None] * jnp.exp(table_max[..., None] - top[None, :, None, :]), 0.0
        ),
        axis=(0, 2),
    )
    table_norm = top + jnp.log(total)
    slot_ids = labels[:, CAND_OWN].reshape(n_cls, cap)
    slot_norm = jnp.sum(
        jnp.where(
            slot_ids[..., None] == jnp.arange(count, dtype=jnp.int32), table_norm[:, None, :], 0.0
        ),
        axis=2,
    ).reshape(slots)
    own_norm = lax.dynamic_index_in_dim(table_norm, lax.axis_index("cls"), 0, keepdims=False)
    weight = jnp.where(candidate[:, :, None], jnp.exp(score - slot_norm[:, None, None]), 0.0)
    mixed = (
        jnp.dot(weight.reshape(slots * groups, ROTS), backward, precision=lax.Precision.HIGHEST)
        .astype(jnp.bfloat16)
        .reshape(slots, groups, width)
    )
    class_weights = lax.psum(jnp.sum(weight, axis=(0, 2)), "prt")
    partial_sums = class_accumulate(lanes, mixed)
    class_sums = lax.psum_scatter(partial_sums, "prt", scatter_dimension=1, tiled=True)
    return (class_sums, class_weights, own_norm)


LANES = 128


def harmonic_plan():
    half = ROTS // 2
    turns = HARM // ROTS
    tail = HARM - turns * ROTS
    chunk_of = np.zeros(HARM, np.int32)
    side_of = np.zeros(HARM, np.int32)
    for m in range(HARM):
        turn, rest = divmod(m, ROTS)
        if turn == turns:
            chunk_of[m] = half * turns + rest // 2
            side_of[m] = rest % 2
        elif rest < half:
            chunk_of[m] = rest * turns + turn
        else:
            chunk_of[m] = ((ROTS - rest) % half) * turns + turn
            side_of[m] = 1
    return half, turns, tail, chunk_of, side_of


HALF, TURNS, TAIL, CHUNK_OF, SIDE_OF = harmonic_plan()
BODY = HALF * TURNS
CHUNKS = BODY + TAIL // 2
EXTRA = TAIL // 2 + 1
COEF = 2 * HALF * CAND_OWN
CROSS_STEP = 6
SUM_STEP = 3


def selector():
    return (np.arange(CHUNKS)[:, None] == CHUNK_OF[None, :]).astype(np.float32)


def unselector():
    sel = selector()
    return np.concatenate([sel * (SIDE_OF == 0), sel * (SIDE_OF == 1)], 0)


def rotation_table():
    table = np.zeros((HALF, 2, CAND_OWN, ROTS, CAND_OWN))
    angle = 2.0 * np.pi * np.arange(ROTS) / ROTS
    for g in range(HALF):
        first = np.cos(g * angle)
        second = np.cos(HALF * angle) if g == 0 else np.sin(g * angle)
        for q in range(CAND_OWN):
            table[g, 0, q, :, q] = first
            table[g, 1, q, :, q] = second
    return table.reshape(COEF, ROTS * CAND_OWN).astype(np.float32)


def nt_dot(a, b):
    return lax.dot_general(a, b, (((1,), (1,)), ((), ())), preferred_element_type=jnp.float32)


def selector_masks():
    m = lax.broadcasted_iota(jnp.int32, (1, HARM), 1)
    turn = jnp.zeros((1, HARM), jnp.int32)
    for t in range(1, TURNS + 1):
        turn += jnp.where(m >= t * ROTS, 1, 0)
    rest = m - ROTS * turn
    back = jnp.where(rest == HALF, 0, ROTS - rest)
    chunk = jnp.where(rest < HALF, rest, back) * TURNS + turn
    side = jnp.where(rest < HALF, 0, 1)
    chunk = jnp.where(turn == TURNS, BODY + rest // 2, chunk)
    side = jnp.where(turn == TURNS, rest % 2, side)
    rows = lax.broadcasted_iota(jnp.int32, (CHUNKS, HARM), 0)
    sel = jnp.where(rows == chunk, 1.0, 0.0).astype(jnp.bfloat16)
    sides = lax.broadcasted_iota(jnp.int32, (2, HARM), 0)
    masks = jnp.where(sides == side, 1.0, 0.0).astype(jnp.bfloat16)
    return sel, masks


def masked_stack(piece, masks):
    parts = []
    for s in range(2):
        for b in range(2):
            parts.append(piece[:, s * HARM : (s + 1) * HARM] * masks[b : b + 1])
    return jnp.concatenate(parts, 0)


def repeat(number, step, body, carry):
    def several(i, carry):
        for u in range(step):
            carry = body(i * step + u, carry)
        return carry

    return lax.fori_loop(0, number // step, several, carry)


def particle_body(at_ref, x_ref, meta_ref, *refs, distances, n_prt):
    outs, scr = refs[:-1], refs[-1]
    count, cycles, _ = x_ref.shape
    number = len(outs)
    span = cycles // n_prt
    sel, masks = selector_masks()

    def one(n, carry):
        parts = []
        for d in distances:
            start = pl.multiple_of((at_ref[0] ^ d) * span, span)
            parts.append(masked_stack(x_ref[n, pl.ds(start, span), :], masks))
        w = jnp.concatenate(parts, 0)
        y = nt_dot(sel, w)
        for p in range(number):
            scr[p, pl.ds(pl.multiple_of(n * CHUNKS, CHUNKS), CHUNKS), :] = y[
                :, p * LANES : (p + 1) * LANES
            ]
        return carry

    repeat(count, 4, one, 0)

    def two(c, carry):
        for p in range(number):
            outs[p][c] = scr[p, pl.ds(c, count, stride=CHUNKS), :].astype(jnp.bfloat16)
        return carry

    repeat(CHUNKS, 8, two, 0)
    lane = lax.broadcasted_iota(jnp.int32, (count, LANES), 1)
    label = jnp.full((count, LANES), -1, jnp.int32)
    for t in range(OWN_TOP):
        mine = (lane // CAND_OWN) == meta_ref[:, t : t + 1]
        for q in range(CAND_OWN):
            at = OWN_TOP + t * CAND_OWN + q
            label = jnp.where(
                mine & (lane % CAND_OWN == q), meta_ref[:, at : at + 1], label
            )
    label = label.astype(jnp.float32).astype(jnp.bfloat16)
    for p in range(number):
        outs[p][CHUNKS] = label


def arrange_particles(prt, particles, meta, n_prt, distances):
    count = particles.shape[0]
    number = len(distances)
    size = particles.size * number // n_prt
    return pl.pallas_call(
        functools.partial(particle_body, distances=distances, n_prt=n_prt),
        in_specs=[pl.BlockSpec(memory_space=pltpu.SMEM)] + [pl.BlockSpec(memory_space=pltpu.VMEM)] * 2,
        out_shape=[jax.ShapeDtypeStruct((CHUNKS + 1, count, LANES), jnp.bfloat16)] * number,
        scratch_shapes=[pltpu.VMEM((number, count * CHUNKS, LANES), jnp.float32)],
        compiler_params=pltpu.CompilerParams(vmem_limit_bytes=32 << 20),
        cost_estimate=pl.CostEstimate(
            flops=size * 2 * CHUNKS, bytes_accessed=size * 4, transcendentals=0
        ),
        name="arrange_particles",
    )(prt, particles, meta)


def reference_body(at_ref, x_ref, out_ref, norm_ref, scr):
    rows = x_ref.shape[0]
    sel, masks = selector_masks()
    step = 4

    def one(n, carry):
        w = jnp.concatenate([masked_stack(x_ref[n * step + i], masks) for i in range(step)], 0)
        y = nt_dot(sel, w)
        for i in range(step):
            scr[pl.ds(pl.multiple_of((n * step + i) * CHUNKS, CHUNKS), CHUNKS), :] = y[
                :, i * LANES : (i + 1) * LANES
            ]
        return carry

    repeat(rows // step, 2, one, 0)

    def two(c, carry):
        value = scr[pl.ds(c, rows, stride=CHUNKS), :]
        out_ref[c] = value.astype(jnp.bfloat16)
        return carry + value * value

    norm_ref[...] = repeat(CHUNKS, 8, two, jnp.zeros((rows, LANES), jnp.float32))


def arrange_references(references, prt, n_prt):
    groups, cycles, width = references.shape
    span = cycles // n_prt
    block = 16
    return pl.pallas_call(
        reference_body,
        grid_spec=pltpu.PrefetchScalarGridSpec(
            num_scalar_prefetch=1,
            grid=(groups // block,),
            in_specs=[
                pl.BlockSpec((block, span, width), lambda i, at: (i, at[0], 0)),
            ],
            out_specs=[
                pl.BlockSpec((CHUNKS, block, LANES), lambda i, at: (0, i, 0)),
                pl.BlockSpec((block, LANES), lambda i, at: (i, 0)),
            ],
            scratch_shapes=[pltpu.VMEM((block * CHUNKS, LANES), jnp.float32)],
        ),
        out_shape=[
            jax.ShapeDtypeStruct((CHUNKS, groups, LANES), jnp.bfloat16),
            jax.ShapeDtypeStruct((groups, LANES), jnp.float32),
        ],
        compiler_params=pltpu.CompilerParams(vmem_limit_bytes=60 << 20),
        cost_estimate=pl.CostEstimate(
            flops=groups * span * width * 2 * CHUNKS,
            bytes_accessed=groups * span * width * 4,
            transcendentals=0,
        ),
        name="arrange_references",
    )(prt, references)


def lane_signs():
    lane = lax.broadcasted_iota(jnp.int32, (1, LANES), 1)
    quarter = LANES // 4
    imag = lane >= 2 * quarter
    odd = (lane // quarter) % 2 == 1
    return imag, odd


def lanes_of(refs, first, number):
    parts = [
        jnp.concatenate([ref[i] for ref in refs], 0) for i in range(first, first + number)
    ]
    return jnp.concatenate(parts, 1) if number > 1 else parts[0]


def hot_masks(cand, groups):
    rows = lax.broadcasted_iota(jnp.int32, (groups, cand.shape[1]), 0).astype(jnp.float32)
    return [rows == cand[q : q + 1] for q in range(CAND_OWN)]


def residue_weights(q_ref, at, g):
    imag, odd = lane_signs()
    sign = jnp.where(imag == odd, -1.0, 1.0)
    first, second = [], []
    for i in range(TURNS):
        q = q_ref[at * TURNS + i].astype(jnp.float32)
        turned = pltpu.roll(q, LANES // 2, 1) * sign
        if at == 0:
            first.append(jnp.where((g == 0) & odd, 0.0, q))
            second.append(jnp.where(g == 0, jnp.where(odd, q, 0.0), turned))
        else:
            first.append(q)
            second.append(turned)
    return jnp.concatenate(
        [jnp.concatenate(first, 1), jnp.concatenate(second, 1)], 0
    ).astype(jnp.bfloat16)


def chosen_rows(acc, cand):
    groups = acc.shape[0] // 2
    hot = hot_masks(cand, groups)
    rows = []
    for ab in range(2):
        part = acc[ab * groups : (ab + 1) * groups, :]
        for q in range(CAND_OWN):
            rows.append(jnp.sum(jnp.where(hot[q], part, 0.0), axis=0, keepdims=True))
    return jnp.concatenate(rows, 0)


def cross_body(at_ref, *refs):
    number = (len(refs) - 6) // 2
    blocks, extras = refs[:number], refs[number : 2 * number]
    q_ref, qt_ref, norm_ref, coef_ref, cand_ref, acc = refs[2 * number :]
    step = pl.program_id(0)
    groups = q_ref.shape[1]
    imag, odd = lane_signs()

    @pl.when(step == 0)
    def _():
        label = lanes_of(extras, TAIL // 2, 1).astype(jnp.float32).T
        row = lax.broadcasted_iota(jnp.int32, label.shape, 0)
        base = at_ref[0] * CAND_OWN
        for q in range(CAND_OWN):
            cand_ref[q : q + 1, :] = jnp.sum(
                jnp.where(row == base + q, label, 0.0), axis=0, keepdims=True
            )
        cand_ref[CAND_OWN:, :] = jnp.full(
            (cand_ref.shape[0] - CAND_OWN, cand_ref.shape[1]), -1.0, jnp.float32
        )

    for u in range(CROSS_STEP):
        g = step * CROSS_STEP + u
        acc[...] = nt_dot(residue_weights(q_ref, u, g), lanes_of(blocks, u * TURNS, TURNS))

        for i in range(TAIL):
            if i % CROSS_STEP != u:
                continue

            @pl.when(g == i)
            def _():
                q = qt_ref[i // 2].astype(jnp.float32)
                keep = odd if i % 2 else ~odd
                a = jnp.where(keep, q, 0.0)
                turned = pltpu.roll(q, LANES // 2, 1) * jnp.where(imag, 1.0, -1.0)
                b = jnp.where(keep, turned, 0.0)
                if i == 0:
                    b = jnp.zeros_like(b)
                w = jnp.concatenate([a, b], 0).astype(jnp.bfloat16)
                acc[...] += nt_dot(w, lanes_of(extras, i // 2, 1))
                if i == 0:
                    acc[:groups, :] -= 0.5 * jnp.sum(norm_ref[...], axis=1, keepdims=True)

        block = 2 * CAND_OWN
        coef_ref[u * block : (u + 1) * block, :] = chosen_rows(acc[...], cand_ref[...])


def cross_coefficients(blocks, arranged, norms, cls):
    count = blocks[0].shape[1]
    groups = arranged.shape[1]
    total = len(blocks) * count
    half_tail = TAIL // 2
    size = blocks[0].size * len(blocks)
    block = 2 * CAND_OWN
    return pl.pallas_call(
        cross_body,
        grid_spec=pltpu.PrefetchScalarGridSpec(
            num_scalar_prefetch=1,
            grid=(HALF // CROSS_STEP,),
            in_specs=[
                *[
                    pl.BlockSpec((CROSS_STEP * TURNS, count, LANES), lambda g, at: (g, 0, 0))
                    for _ in blocks
                ],
                *[
                    pl.BlockSpec((EXTRA, count, LANES), lambda g, at: (BODY // EXTRA, 0, 0))
                    for _ in blocks
                ],
                pl.BlockSpec((CROSS_STEP * TURNS, groups, LANES), lambda g, at: (g, 0, 0)),
                pl.BlockSpec((half_tail, groups, LANES), lambda g, at: (BODY // half_tail, 0, 0)),
                pl.BlockSpec((groups, LANES), lambda g, at: (0, 0)),
            ],
            out_specs=[
                pl.BlockSpec((CROSS_STEP * block, total), lambda g, at: (g, 0)),
                pl.BlockSpec((block, total), lambda g, at: (0, 0)),
            ],
            scratch_shapes=[pltpu.VMEM((2 * groups, total), jnp.float32)],
        ),
        out_shape=[
            jax.ShapeDtypeStruct((COEF, total), jnp.float32),
            jax.ShapeDtypeStruct((block, total), jnp.float32),
        ],
        compiler_params=pltpu.CompilerParams(vmem_limit_bytes=60 << 20),
        cost_estimate=pl.CostEstimate(
            flops=4 * size * groups, bytes_accessed=2 * size, transcendentals=0
        ),
        name="cross_coefficients",
    )(cls, *blocks, *blocks, arranged, arranged, norms)


def score_body(*refs, scale):
    *coefs, cand_ref, table_ref, score_ref, stat_ref = refs
    corr = lax.dot_general(
        table_ref[...],
        functools.reduce(jnp.add, [ref[...] for ref in coefs]),
        (((0,), (0,)), ((), ())),
        precision=lax.Precision.HIGHEST,
        preferred_element_type=jnp.float32,
    )
    score = jnp.where(cand_ref[0:1, :] >= 0.0, corr * scale, lowest)
    top = jnp.max(score, axis=0, keepdims=True)
    total = jnp.sum(jnp.exp(score - top), axis=0, keepdims=True)
    score_ref[...] = score
    stat_ref[0:1, :] = top
    stat_ref[1:2, :] = jnp.where(cand_ref[0:1, :] >= 0.0, total, 0.0)


def scores(coefs, cand, table, scale):
    total = cand.shape[1]
    return pl.pallas_call(
        functools.partial(score_body, scale=scale),
        out_shape=[
            jax.ShapeDtypeStruct((ROTS * CAND_OWN, total), jnp.float32),
            jax.ShapeDtypeStruct((2, total), jnp.float32),
        ],
        name="scores",
    )(*coefs, cand, table)


def swap_blocks(x, distance, width):
    lane = lax.broadcasted_iota(jnp.int32, x.shape, 1)
    bit = 1
    while bit <= distance:
        if distance & bit:
            shift = bit * width
            down = pltpu.roll(x, shift, 1)
            up = pltpu.roll(x, x.shape[1] - shift, 1)
            x = jnp.where((lane // shift) % 2 == 1, down, up)
        bit *= 2
    return x


def weights_body(at_ref, score_ref, cand_ref, stat_ref, table_ref, mix_ref, norm_ref):
    n_cls, _, total = stat_ref.shape
    width = total // n_cls
    tops, parts = [], []
    for e in range(n_cls):
        table = stat_ref[at_ref[0] ^ e]
        table = swap_blocks(jnp.concatenate([table] * 4, 0), e, width)
        tops.append(table[0:1])
        parts.append(table[1:2])
    top = functools.reduce(jnp.maximum, tops)
    summed = jnp.zeros_like(top)
    for other, part in zip(tops, parts):
        summed += part * jnp.exp(other - top)
    log_norm = top + jnp.log(summed)
    norm_ref[...] = log_norm[:, : norm_ref.shape[1]]
    weight = jnp.where(cand_ref[0:1, :] >= 0.0, jnp.exp(score_ref[...] - log_norm), 0.0)
    mix_ref[...] = lax.dot_general(
        table_ref[...],
        weight,
        (((1,), (0,)), ((), ())),
        precision=lax.Precision.HIGHEST,
        preferred_element_type=jnp.float32,
    )


def mixed_weights(cls, score, cand, stats, table, count):
    total = score.shape[1]
    return pl.pallas_call(
        weights_body,
        in_specs=[pl.BlockSpec(memory_space=pltpu.SMEM)] + [pl.BlockSpec(memory_space=pltpu.VMEM)] * 4,
        out_shape=[
            jax.ShapeDtypeStruct((COEF, total), jnp.float32),
            jax.ShapeDtypeStruct((1, count), jnp.float32),
        ],
        name="mixed_weights",
    )(cls, score, cand, stats, table)


def sums_body(*refs, number, pieces):
    blocks, extras = refs[:number], refs[number : 2 * number]
    refs = refs[2 * number :]
    mixes, cands = refs[:pieces], refs[pieces : 2 * pieces]
    back_ref, out_ref, weight_ref, mix, cand, planes = refs[2 * pieces :]
    i = pl.program_id(0)
    groups = weight_ref.shape[1]
    total = mix.shape[1]
    imag, odd = lane_signs()

    @pl.when(i == 0)
    def _():
        mixed = jnp.concatenate([ref[...] for ref in mixes], 1)
        chosen = jnp.concatenate([ref[...] for ref in cands], 1)
        hot = hot_masks(chosen, groups)
        summed = jnp.zeros((groups, total), jnp.float32)
        for q in range(CAND_OWN):
            summed += jnp.where(hot[q], mixed[q : q + 1], 0.0)
        weight_ref[...] = lax.dot_general(
            jnp.ones((1, total), jnp.float32),
            summed,
            (((1,), (1,)), ((), ())),
            precision=lax.Precision.HIGHEST,
            preferred_element_type=jnp.float32,
        )
        mix[...] = mixed
        cand[...] = chosen

    @pl.when(i < HALF // SUM_STEP)
    def _():
        hot = hot_masks(cand[...], groups)
        block = 2 * CAND_OWN
        sign = jnp.where(imag == odd, 1.0, -1.0)
        for u in range(SUM_STEP):
            g = i * SUM_STEP + u
            mine = mix[pl.ds(pl.multiple_of(g * block, block), block), :]
            halves = []
            for ab in range(2):
                dense = jnp.zeros((groups, total), jnp.float32)
                for q in range(CAND_OWN):
                    at = ab * CAND_OWN + q
                    dense = jnp.where(hot[q], mine[at : at + 1], dense)
                halves.append(dense)
            weights = jnp.concatenate(halves, 0).astype(jnp.bfloat16)
            made = jnp.dot(
                weights, lanes_of(blocks, u * TURNS, TURNS), preferred_element_type=jnp.float32
            )
            for t in range(TURNS):
                g1 = made[:groups, t * LANES : (t + 1) * LANES]
                g2 = made[groups:, t * LANES : (t + 1) * LANES]
                value = g1 + sign * pltpu.roll(g2, LANES // 2, 1)
                if u == 0:
                    value = jnp.where(i == 0, jnp.where(odd, g2, g1), value)
                start = pl.multiple_of((g * TURNS + t) * groups, groups)
                planes[pl.ds(start, groups), :] = value

            for t in range(TAIL):
                if t % SUM_STEP != u:
                    continue

                @pl.when(g == t)
                def _():
                    made = jnp.dot(
                        weights, lanes_of(extras, t // 2, 1), preferred_element_type=jnp.float32
                    )
                    g1, g2 = made[:groups], made[groups:]
                    value = g1
                    if t > 0:
                        value = g1 + jnp.where(imag, -1.0, 1.0) * pltpu.roll(g2, LANES // 2, 1)
                    rows = pl.ds((BODY + t // 2) * groups, groups)
                    if t % 2:
                        value = jnp.where(odd, value, planes[rows, :])
                    planes[rows, :] = value

    @pl.when(i >= HALF // SUM_STEP)
    def _():
        block, span, _ = out_ref.shape
        first = (i - HALF // SUM_STEP) * block
        back = back_ref[...]
        values = []
        for c in range(block):
            turned = planes[pl.ds(first + c, CHUNKS, stride=groups), :].T
            for s in range(2):
                at = 2 * s * span
                values.append(
                    jnp.concatenate([turned[at : at + span], turned[at + span : at + 2 * span]], 1)
                )
        value = jnp.concatenate(values, 0)
        high = value.astype(jnp.bfloat16)
        low = (value - high.astype(jnp.float32)).astype(jnp.bfloat16)
        both = jnp.dot(
            jnp.concatenate([high, low], 0), back, preferred_element_type=jnp.float32
        )
        rows = value.shape[0]
        placed = both[:rows] + both[rows:]
        for c in range(block):
            for s in range(2):
                at = (2 * c + s) * span
                out_ref[c, :, s * HARM : (s + 1) * HARM] = placed[at : at + span]


def sums(blocks, mixes, cands, back, groups, span):
    count = blocks[0].shape[1]
    total = len(blocks) * count
    size = blocks[0].size * len(blocks)
    block = 8
    steps = HALF // SUM_STEP
    whole = lambda i: (0, 0)
    return pl.pallas_call(
        functools.partial(sums_body, number=len(blocks), pieces=len(mixes)),
        grid=(steps + groups // block,),
        in_specs=[
            *[
                pl.BlockSpec(
                    (SUM_STEP * TURNS, count, LANES), lambda i: (jnp.minimum(i, steps - 1), 0, 0)
                )
                for _ in blocks
            ],
            *[
                pl.BlockSpec((EXTRA, count, LANES), lambda i: (BODY // EXTRA, 0, 0))
                for _ in blocks
            ],
            *[pl.BlockSpec(array.shape, whole) for array in (*mixes, *cands, back)],
        ],
        out_specs=[
            pl.BlockSpec(
                (block, span, 2 * HARM), lambda i: (jnp.maximum(i - steps, 0), 0, 0)
            ),
            pl.BlockSpec((1, groups), whole),
        ],
        out_shape=[
            jax.ShapeDtypeStruct((groups, span, 2 * HARM), jnp.float32),
            jax.ShapeDtypeStruct((1, groups), jnp.float32),
        ],
        scratch_shapes=[
            pltpu.VMEM((COEF, total), jnp.float32),
            pltpu.VMEM((2 * CAND_OWN, total), jnp.float32),
            pltpu.VMEM((CHUNKS * groups, LANES), jnp.float32),
        ],
        compiler_params=pltpu.CompilerParams(vmem_limit_bytes=60 << 20),
        cost_estimate=pl.CostEstimate(
            flops=4 * size * groups,
            bytes_accessed=2 * size + 8 * groups * span * HARM,
            transcendentals=0,
        ),
        name="sums",
    )(*blocks, *blocks, *mixes, *cands, back)


def hop(value, axis, distance):
    size = lax.axis_size(axis)
    return lax.ppermute(value, axis, [(i, i ^ distance) for i in range(size)])


def after(value, *others):
    return lax.optimization_barrier((value, *others))[0]


def direct(own):
    n_cls = lax.axis_size("cls")
    return {1 << bit: hop(own, "cls", 1 << bit) for bit in range(1, n_cls.bit_length() - 1)}


def relayed(known, d, *others):
    n_cls = lax.axis_size("cls")
    for j in sorted(range(2, n_cls, 2), key=lambda j: bin(j).count("1")):
        if j not in known:
            bits = [bit for bit in range(1, n_cls.bit_length()) if j >> bit & 1]
            way = 1 << bits[d % len(bits)]
            known[j] = hop(after(known[j ^ way], *others), "cls", way)
    return known


def paired(known, each, last):
    n_cls = lax.axis_size("cls")
    for j in range(0, n_cls, 2):
        others = last if j == n_cls - 2 else each
        block = after(known[j], *others) if others else known[j]
        known[j + 1] = hop(block, "cls", 1)
    return [known[j] for j in range(n_cls)]


def gather_device(particles, references, owner_groups, class_order):
    n_cls, n_prt = lax.axis_size("cls"), lax.axis_size("prt")
    cls, prt = lax.axis_index("cls"), lax.axis_index("prt")
    count, cycles, width = particles.shape
    groups = references.shape[0]
    span = cycles // n_prt
    back = jnp.asarray(unselector(), jnp.bfloat16)
    table = jnp.asarray(rotation_table())
    picks = class_order[:, :, :CAND_OWN].reshape(count, OWN_TOP * CAND_OWN)
    meta = jnp.concatenate([owner_groups, picks], 1)
    cls, prt = (index.reshape(1).astype(jnp.int32) for index in (cls, prt))
    order = [d for d in range(n_prt) if d % 2 == 0] + [d for d in range(n_prt) if d % 2]
    outgoing = {}
    place = prt
    for first in range(0, n_prt, 2):
        distances = tuple(order[first : first + 2])
        made = arrange_particles(place, particles, meta, n_prt, distances)
        outgoing.update(zip(distances, made))
        place = after(prt, made[0])
    last = outgoing[order[-1]]
    arrived = {0: outgoing[0]}
    for d in order[1:]:
        block = after(outgoing[d], arrived[2]) if d > 2 else outgoing[d]
        arrived[d] = hop(block, "prt", d)
    known = {0: {0: arrived[0], **direct(arrived[0])}}
    for d in range(1, min(n_prt, 3)):
        own = after(arrived[d], last) if d == 2 else arrived[d]
        known[d] = {0: own, **direct(own)}
    place = after(prt, *[arrived[d] for d in range(1, min(n_prt, 3))])
    arranged, norms = arrange_references(references, place, n_prt)
    for d in range(3, n_prt):
        arrived[d] = after(arrived[d], arranged)
        known[d] = {0: arrived[d], **direct(arrived[d])}
    relayed(known[0], 0, arranged)
    for d in range(1, n_prt):
        relayed(known[d], d)
    scale = 2.0 / math.sqrt(cycles * width)
    coefs, cands, sent, blocks = [], [], [], []
    for d in range(n_prt):
        waits = [known[n_prt - 1][2]] if d == 1 else []
        each = [arranged] if d == 0 else [arranged, arrived[n_prt - 1]] if d == 1 else coefs[:1]
        blocks.append(paired(known[d], each, coefs[-1:] if d > 1 else []))
        ready = after(arranged, *waits) if waits else arranged
        coef, cand = cross_coefficients(blocks[d], ready, norms, cls)
        coefs.append(coef)
        sent.append(hop(coef, "prt", d) if d else coef)
        cands.append(cand)
    score, stat = scores(sent, cands[0], table, scale)
    stats = lax.all_gather(stat.reshape(1, *stat.shape), "cls", axis=0, tiled=True)
    mix, log_norm = mixed_weights(cls, score, cands[0], stats, table, count)
    mixes = [hop(mix, "prt", d) if d else mix for d in range(n_prt)]
    class_sums, class_weights = sums(
        [block for piece in blocks for block in piece], mixes, cands, back, groups, span
    )
    own = log_norm[0]
    return class_sums, class_weights[0], own


def per_device(particles, references, owner_groups, class_order):
    n_cls, n_prt = lax.axis_size("cls"), lax.axis_size("prt")
    count, cycles, _ = particles.shape
    groups = references.shape[0]
    cap = max(2, 2 * count * OWN_TOP // n_cls)
    powers = n_cls & (n_cls - 1) == 0 and n_prt & (n_prt - 1) == 0
    fits = 4 * cycles == LANES * n_prt and n_cls * CAND_OWN <= LANES and groups % 16 == 0 and n_cls >= 4
    fits = fits and powers and n_cls * count == LANES
    plan = gather_device if cap >= count and fits else dispatch_device
    return plan(particles, references, owner_groups, class_order)


def solution(mesh):
    in_specs = (
        P(("cls", "prt"), None, None),
        P("cls", None, None),
        P(("cls", "prt"), None),
        P(("cls", "prt"), None, None),
    )
    out_specs = (P("cls", "prt", None), P("cls"), P(("cls", "prt")))
    return jax.shard_map(
        per_device, mesh=mesh, in_specs=in_specs, out_specs=out_specs, check_vma=False
    )
```

```python
import functools
import math

import jax
import jax.numpy as jnp
import numpy as np
from jax import lax
from jax.experimental import pallas as pl
from jax.experimental.pallas import tpu as pltpu
from jax.sharding import PartitionSpec as P

CYCLES = 128
HARM = 256
ROTS = 36
OWN_TOP = 4
CAND_OWN = 4


lowest = -1e30


def spectral_tables():
    harmonic = jnp.arange(HARM, dtype=jnp.float32)
    angles = 2.0 * math.pi * jnp.arange(ROTS, dtype=jnp.float32) / ROTS
    phase = harmonic[:, None] * angles[None, :]
    forward = jnp.concatenate([jnp.cos(phase), jnp.sin(phase)], 0)
    backward = jnp.concatenate([jnp.cos(phase), -jnp.sin(phase)], 0).T
    return (forward, backward)


def class_accumulate(lanes, mixed):
    l_re = lanes[..., :HARM]
    l_im = lanes[..., HARM:]
    y_re = mixed[..., :HARM]
    y_im = mixed[..., HARM:]
    s_re = jnp.einsum("lrm,lcm->crm", l_re, y_re, preferred_element_type=jnp.float32) - jnp.einsum(
        "lrm,lcm->crm", l_im, y_im, preferred_element_type=jnp.float32
    )
    s_im = jnp.einsum("lrm,lcm->crm", l_re, y_im, preferred_element_type=jnp.float32) + jnp.einsum(
        "lrm,lcm->crm", l_im, y_re, preferred_element_type=jnp.float32
    )
    return jnp.concatenate([s_re, s_im], -1)


def dispatch_device(particles, references, owner_groups, class_order):
    n_cls = lax.axis_size("cls")
    count = particles.shape[0]
    groups = references.shape[0]
    cap = max(2, 2 * count * OWN_TOP // n_cls)
    slots = n_cls * cap
    width = 2 * HARM
    flat_owner = owner_groups.reshape(-1)
    owner_hot = (flat_owner[:, None] == jnp.arange(n_cls, dtype=jnp.int32)[None, :]).astype(
        jnp.int32
    )
    before = jnp.cumsum(owner_hot, axis=0) - owner_hot
    rank = jnp.sum(before * owner_hot, axis=1)
    slot_of = flat_owner * cap + rank
    match = slot_of[None, :] == jnp.arange(slots, dtype=jnp.int32)[:, None]
    member = jnp.any(match.reshape(slots, count, OWN_TOP), axis=2)
    filled = jnp.any(member, axis=1)
    dispatch = member.astype(jnp.bfloat16)
    outgoing = jnp.dot(
        dispatch, particles.reshape(count, CYCLES * width), preferred_element_type=jnp.float32
    )
    outgoing = outgoing.astype(jnp.bfloat16).reshape(n_cls, cap, CYCLES, width)
    match_int = match.astype(jnp.int32)
    picks = class_order[:, :, :CAND_OWN].reshape(count * OWN_TOP, CAND_OWN)
    slot_cand = jnp.where(filled[:, None], jnp.dot(match_int, picks), -1)
    owner_rows = jnp.repeat(jnp.arange(count, dtype=jnp.int32), OWN_TOP)
    slot_pid = jnp.where(filled, jnp.dot(match_int, owner_rows), -1)
    labels_out = jnp.concatenate([slot_cand, slot_pid[:, None]], 1).reshape(
        n_cls, cap, CAND_OWN + 1
    )
    arrived, labels = (
        lax.all_to_all(outgoing, "cls", split_axis=0, concat_axis=0, tiled=True),
        lax.all_to_all(labels_out, "cls", split_axis=0, concat_axis=0, tiled=True),
    )
    lanes = arrived.reshape(slots, CYCLES, width)
    labels = labels.reshape(slots, CAND_OWN + 1)
    forward, backward = spectral_tables()
    scale = 2.0 / math.sqrt(CYCLES * width)
    norms = jnp.sum(jnp.square(references.astype(jnp.float32)), axis=(1, 2))
    l_re = lanes[..., :HARM]
    l_im = lanes[..., HARM:]
    r_re = references[..., :HARM]
    r_im = references[..., HARM:]
    x_re = jnp.einsum("lrm,crm->lcm", l_re, r_re, preferred_element_type=jnp.float32) + jnp.einsum(
        "lrm,crm->lcm", l_im, r_im, preferred_element_type=jnp.float32
    )
    x_im = jnp.einsum("lrm,crm->lcm", l_im, r_re, preferred_element_type=jnp.float32) - jnp.einsum(
        "lrm,crm->lcm", l_re, r_im, preferred_element_type=jnp.float32
    )
    cross = jnp.concatenate([x_re, x_im], -1)
    corr = jnp.dot(
        cross.reshape(slots * groups, width), forward, precision=lax.Precision.HIGHEST
    ).reshape(slots, groups, ROTS)
    score = (corr - 0.5 * norms[None, :, None]) * scale
    candidate = jnp.any(
        labels[:, :CAND_OWN, None] == jnp.arange(groups, dtype=jnp.int32)[None, None, :], axis=1
    )
    part_max = jnp.max(jnp.where(candidate[:, :, None], score, lowest), axis=(1, 2))
    part_sum = jnp.sum(
        jnp.where(candidate[:, :, None], jnp.exp(score - part_max[:, None, None]), 0.0), axis=(1, 2)
    )
    sender_ids = labels[:, CAND_OWN].astype(jnp.float32)
    table_max, table_sum, table_ids = (
        lax.all_gather(part_max.reshape(1, n_cls, cap), "cls", axis=0, tiled=True),
        lax.all_gather(part_sum.reshape(1, n_cls, cap), "cls", axis=0, tiled=True),
        lax.all_gather(sender_ids.reshape(1, n_cls, cap), "cls", axis=0, tiled=True),
    )
    local_ids = jnp.arange(count, dtype=jnp.float32)
    hit = table_ids[..., None] == local_ids
    top = jnp.max(jnp.where(hit, table_max[..., None], lowest), axis=(0, 2))
    total = jnp.sum(
        jnp.where(
            hit, table_sum[..., None] * jnp.exp(table_max[..., None] - top[None, :, None, :]), 0.0
        ),
        axis=(0, 2),
    )
    table_norm = top + jnp.log(total)
    slot_ids = labels[:, CAND_OWN].reshape(n_cls, cap)
    slot_norm = jnp.sum(
        jnp.where(
            slot_ids[..., None] == jnp.arange(count, dtype=jnp.int32), table_norm[:, None, :], 0.0
        ),
        axis=2,
    ).reshape(slots)
    own_norm = lax.dynamic_index_in_dim(table_norm, lax.axis_index("cls"), 0, keepdims=False)
    weight = jnp.where(candidate[:, :, None], jnp.exp(score - slot_norm[:, None, None]), 0.0)
    mixed = (
        jnp.dot(weight.reshape(slots * groups, ROTS), backward, precision=lax.Precision.HIGHEST)
        .astype(jnp.bfloat16)
        .reshape(slots, groups, width)
    )
    class_weights = lax.psum(jnp.sum(weight, axis=(0, 2)), "prt")
    partial_sums = class_accumulate(lanes, mixed)
    class_sums = lax.psum_scatter(partial_sums, "prt", scatter_dimension=1, tiled=True)
    return (class_sums, class_weights, own_norm)


LANES = 128


def harmonic_plan():
    half = ROTS // 2
    turns = HARM // ROTS
    tail = HARM - turns * ROTS
    chunk_of = np.zeros(HARM, np.int32)
    side_of = np.zeros(HARM, np.int32)
    for m in range(HARM):
        turn, rest = divmod(m, ROTS)
        if turn == turns:
            chunk_of[m] = half * turns + rest // 2
            side_of[m] = rest % 2
        elif rest < half:
            chunk_of[m] = rest * turns + turn
        else:
            chunk_of[m] = ((ROTS - rest) % half) * turns + turn
            side_of[m] = 1
    return half, turns, tail, chunk_of, side_of


HALF, TURNS, TAIL, CHUNK_OF, SIDE_OF = harmonic_plan()
BODY = HALF * TURNS
CHUNKS = BODY + TAIL // 2
EXTRA = TAIL // 2 + 1
COEF = 2 * HALF * CAND_OWN
CROSS_STEP = 6
SUM_STEP = 3


def selector():
    return (np.arange(CHUNKS)[:, None] == CHUNK_OF[None, :]).astype(np.float32)


def unselector():
    sel = selector()
    return np.concatenate([sel * (SIDE_OF == 0), sel * (SIDE_OF == 1)], 0)


def rotation_table():
    table = np.zeros((HALF, 2, CAND_OWN, ROTS, CAND_OWN))
    angle = 2.0 * np.pi * np.arange(ROTS) / ROTS
    for g in range(HALF):
        first = np.cos(g * angle)
        second = np.cos(HALF * angle) if g == 0 else np.sin(g * angle)
        for q in range(CAND_OWN):
            table[g, 0, q, :, q] = first
            table[g, 1, q, :, q] = second
    return table.reshape(COEF, ROTS * CAND_OWN).astype(np.float32)


def nt_dot(a, b):
    return lax.dot_general(a, b, (((1,), (1,)), ((), ())), preferred_element_type=jnp.float32)


def selector_masks():
    m = lax.broadcasted_iota(jnp.int32, (1, HARM), 1)
    turn = jnp.zeros((1, HARM), jnp.int32)
    for t in range(1, TURNS + 1):
        turn += jnp.where(m >= t * ROTS, 1, 0)
    rest = m - ROTS * turn
    back = jnp.where(rest == HALF, 0, ROTS - rest)
    chunk = jnp.where(rest < HALF, rest, back) * TURNS + turn
    side = jnp.where(rest < HALF, 0, 1)
    chunk = jnp.where(turn == TURNS, BODY + rest // 2, chunk)
    side = jnp.where(turn == TURNS, rest % 2, side)
    rows = lax.broadcasted_iota(jnp.int32, (CHUNKS, HARM), 0)
    sel = jnp.where(rows == chunk, 1.0, 0.0).astype(jnp.bfloat16)
    sides = lax.broadcasted_iota(jnp.int32, (2, HARM), 0)
    masks = jnp.where(sides == side, 1.0, 0.0).astype(jnp.bfloat16)
    return sel, masks


def masked_stack(piece, masks):
    parts = []
    for s in range(2):
        for b in range(2):
            parts.append(piece[:, s * HARM : (s + 1) * HARM] * masks[b : b + 1])
    return jnp.concatenate(parts, 0)


def repeat(number, step, body, carry):
    def several(i, carry):
        for u in range(step):
            carry = body(i * step + u, carry)
        return carry

    return lax.fori_loop(0, number // step, several, carry)


def particle_body(at_ref, x_ref, meta_ref, *refs, distances, n_prt):
    outs, scr = refs[:-1], refs[-1]
    count, cycles, _ = x_ref.shape
    number = len(outs)
    span = cycles // n_prt
    sel, masks = selector_masks()

    def one(n, carry):
        parts = []
        for d in distances:
            start = pl.multiple_of((at_ref[0] ^ d) * span, span)
            parts.append(masked_stack(x_ref[n, pl.ds(start, span), :], masks))
        w = jnp.concatenate(parts, 0)
        y = nt_dot(sel, w)
        for p in range(number):
            scr[p, pl.ds(pl.multiple_of(n * CHUNKS, CHUNKS), CHUNKS), :] = y[
                :, p * LANES : (p + 1) * LANES
            ]
        return carry

    repeat(count, 4, one, 0)

    def two(c, carry):
        for p in range(number):
            outs[p][c] = scr[p, pl.ds(c, count, stride=CHUNKS), :].astype(jnp.bfloat16)
        return carry

    repeat(CHUNKS, 8, two, 0)
    lane = lax.broadcasted_iota(jnp.int32, (count, LANES), 1)
    label = jnp.full((count, LANES), -1, jnp.int32)
    for t in range(OWN_TOP):
        mine = (lane // CAND_OWN) == meta_ref[:, t : t + 1]
        for q in range(CAND_OWN):
            at = OWN_TOP + t * CAND_OWN + q
            label = jnp.where(
                mine & (lane % CAND_OWN == q), meta_ref[:, at : at + 1], label
            )
    label = label.astype(jnp.float32).astype(jnp.bfloat16)
    for p in range(number):
        outs[p][CHUNKS] = label


def arrange_particles(prt, particles, meta, n_prt, distances):
    count = particles.shape[0]
    number = len(distances)
    size = particles.size * number // n_prt
    return pl.pallas_call(
        functools.partial(particle_body, distances=distances, n_prt=n_prt),
        in_specs=[pl.BlockSpec(memory_space=pltpu.SMEM)] + [pl.BlockSpec(memory_space=pltpu.VMEM)] * 2,
        out_shape=[jax.ShapeDtypeStruct((CHUNKS + 1, count, LANES), jnp.bfloat16)] * number,
        scratch_shapes=[pltpu.VMEM((number, count * CHUNKS, LANES), jnp.float32)],
        compiler_params=pltpu.CompilerParams(vmem_limit_bytes=32 << 20),
        cost_estimate=pl.CostEstimate(
            flops=size * 2 * CHUNKS, bytes_accessed=size * 4, transcendentals=0
        ),
        name="arrange_particles",
    )(prt, particles, meta)


def reference_body(at_ref, x_ref, out_ref, norm_ref, scr):
    rows = x_ref.shape[0]
    sel, masks = selector_masks()
    step = 4

    def one(n, carry):
        w = jnp.concatenate([masked_stack(x_ref[n * step + i], masks) for i in range(step)], 0)
        y = nt_dot(sel, w)
        for i in range(step):
            scr[pl.ds(pl.multiple_of((n * step + i) * CHUNKS, CHUNKS), CHUNKS), :] = y[
                :, i * LANES : (i + 1) * LANES
            ]
        return carry

    repeat(rows // step, 2, one, 0)

    def two(c, carry):
        value = scr[pl.ds(c, rows, stride=CHUNKS), :]
        out_ref[c] = value.astype(jnp.bfloat16)
        return carry + value * value

    norm_ref[...] = repeat(CHUNKS, 8, two, jnp.zeros((rows, LANES), jnp.float32))


def arrange_references(references, prt, n_prt):
    groups, cycles, width = references.shape
    span = cycles // n_prt
    block = 16
    return pl.pallas_call(
        reference_body,
        grid_spec=pltpu.PrefetchScalarGridSpec(
            num_scalar_prefetch=1,
            grid=(groups // block,),
            in_specs=[
                pl.BlockSpec((block, span, width), lambda i, at: (i, at[0], 0)),
            ],
            out_specs=[
                pl.BlockSpec((CHUNKS, block, LANES), lambda i, at: (0, i, 0)),
                pl.BlockSpec((block, LANES), lambda i, at: (i, 0)),
            ],
            scratch_shapes=[pltpu.VMEM((block * CHUNKS, LANES), jnp.float32)],
        ),
        out_shape=[
            jax.ShapeDtypeStruct((CHUNKS, groups, LANES), jnp.bfloat16),
            jax.ShapeDtypeStruct((groups, LANES), jnp.float32),
        ],
        compiler_params=pltpu.CompilerParams(vmem_limit_bytes=60 << 20),
        cost_estimate=pl.CostEstimate(
            flops=groups * span * width * 2 * CHUNKS,
            bytes_accessed=groups * span * width * 4,
            transcendentals=0,
        ),
        name="arrange_references",
    )(prt, references)


def lane_signs():
    lane = lax.broadcasted_iota(jnp.int32, (1, LANES), 1)
    quarter = LANES // 4
    imag = lane >= 2 * quarter
    odd = (lane // quarter) % 2 == 1
    return imag, odd


def lanes_of(refs, first, number):
    parts = [
        jnp.concatenate([ref[i] for ref in refs], 0) for i in range(first, first + number)
    ]
    return jnp.concatenate(parts, 1) if number > 1 else parts[0]


def hot_masks(cand, groups):
    rows = lax.broadcasted_iota(jnp.int32, (groups, cand.shape[1]), 0).astype(jnp.float32)
    return [rows == cand[q : q + 1] for q in range(CAND_OWN)]


def residue_weights(q_ref, at, g):
    imag, odd = lane_signs()
    sign = jnp.where(imag == odd, -1.0, 1.0)
    first, second = [], []
    for i in range(TURNS):
        q = q_ref[at * TURNS + i].astype(jnp.float32)
        turned = pltpu.roll(q, LANES // 2, 1) * sign
        if at == 0:
            first.append(jnp.where((g == 0) & odd, 0.0, q))
            second.append(jnp.where(g == 0, jnp.where(odd, q, 0.0), turned))
        else:
            first.append(q)
            second.append(turned)
    return jnp.concatenate(
        [jnp.concatenate(first, 1), jnp.concatenate(second, 1)], 0
    ).astype(jnp.bfloat16)


def chosen_rows(acc, cand):
    groups = acc.shape[0] // 2
    hot = hot_masks(cand, groups)
    rows = []
    for ab in range(2):
        part = acc[ab * groups : (ab + 1) * groups, :]
        for q in range(CAND_OWN):
            rows.append(jnp.sum(jnp.where(hot[q], part, 0.0), axis=0, keepdims=True))
    return jnp.concatenate(rows, 0)


def cross_body(at_ref, *refs):
    number = (len(refs) - 6) // 2
    blocks, extras = refs[:number], refs[number : 2 * number]
    q_ref, qt_ref, norm_ref, coef_ref, cand_ref, acc = refs[2 * number :]
    step = pl.program_id(0)
    groups = q_ref.shape[1]
    imag, odd = lane_signs()

    @pl.when(step == 0)
    def _():
        label = lanes_of(extras, TAIL // 2, 1).astype(jnp.float32).T
        row = lax.broadcasted_iota(jnp.int32, label.shape, 0)
        base = at_ref[0] * CAND_OWN
        for q in range(CAND_OWN):
            cand_ref[q : q + 1, :] = jnp.sum(
                jnp.where(row == base + q, label, 0.0), axis=0, keepdims=True
            )
        cand_ref[CAND_OWN:, :] = jnp.full(
            (cand_ref.shape[0] - CAND_OWN, cand_ref.shape[1]), -1.0, jnp.float32
        )

    for u in range(CROSS_STEP):
        g = step * CROSS_STEP + u
        acc[...] = nt_dot(residue_weights(q_ref, u, g), lanes_of(blocks, u * TURNS, TURNS))

        for i in range(TAIL):
            if i % CROSS_STEP != u:
                continue

            @pl.when(g == i)
            def _():
                q = qt_ref[i // 2].astype(jnp.float32)
                keep = odd if i % 2 else ~odd
                a = jnp.where(keep, q, 0.0)
                turned = pltpu.roll(q, LANES // 2, 1) * jnp.where(imag, 1.0, -1.0)
                b = jnp.where(keep, turned, 0.0)
                if i == 0:
                    b = jnp.zeros_like(b)
                w = jnp.concatenate([a, b], 0).astype(jnp.bfloat16)
                acc[...] += nt_dot(w, lanes_of(extras, i // 2, 1))
                if i == 0:
                    acc[:groups, :] -= 0.5 * jnp.sum(norm_ref[...], axis=1, keepdims=True)

        block = 2 * CAND_OWN
        coef_ref[u * block : (u + 1) * block, :] = chosen_rows(acc[...], cand_ref[...])


def cross_coefficients(blocks, arranged, norms, cls):
    count = blocks[0].shape[1]
    groups = arranged.shape[1]
    total = len(blocks) * count
    half_tail = TAIL // 2
    size = blocks[0].size * len(blocks)
    block = 2 * CAND_OWN
    return pl.pallas_call(
        cross_body,
        grid_spec=pltpu.PrefetchScalarGridSpec(
            num_scalar_prefetch=1,
            grid=(HALF // CROSS_STEP,),
            in_specs=[
                *[
                    pl.BlockSpec((CROSS_STEP * TURNS, count, LANES), lambda g, at: (g, 0, 0))
                    for _ in blocks
                ],
                *[
                    pl.BlockSpec((EXTRA, count, LANES), lambda g, at: (BODY // EXTRA, 0, 0))
                    for _ in blocks
                ],
                pl.BlockSpec((CROSS_STEP * TURNS, groups, LANES), lambda g, at: (g, 0, 0)),
                pl.BlockSpec((half_tail, groups, LANES), lambda g, at: (BODY // half_tail, 0, 0)),
                pl.BlockSpec((groups, LANES), lambda g, at: (0, 0)),
            ],
            out_specs=[
                pl.BlockSpec((CROSS_STEP * block, total), lambda g, at: (g, 0)),
                pl.BlockSpec((block, total), lambda g, at: (0, 0)),
            ],
            scratch_shapes=[pltpu.VMEM((2 * groups, total), jnp.float32)],
        ),
        out_shape=[
            jax.ShapeDtypeStruct((COEF, total), jnp.float32),
            jax.ShapeDtypeStruct((block, total), jnp.float32),
        ],
        compiler_params=pltpu.CompilerParams(vmem_limit_bytes=60 << 20),
        cost_estimate=pl.CostEstimate(
            flops=4 * size * groups, bytes_accessed=2 * size, transcendentals=0
        ),
        name="cross_coefficients",
    )(cls, *blocks, *blocks, arranged, arranged, norms)


def score_body(*refs, scale):
    *coefs, cand_ref, table_ref, score_ref, stat_ref = refs
    corr = lax.dot_general(
        table_ref[...],
        functools.reduce(jnp.add, [ref[...] for ref in coefs]),
        (((0,), (0,)), ((), ())),
        precision=lax.Precision.HIGHEST,
        preferred_element_type=jnp.float32,
    )
    score = jnp.where(cand_ref[0:1, :] >= 0.0, corr * scale, lowest)
    top = jnp.max(score, axis=0, keepdims=True)
    total = jnp.sum(jnp.exp(score - top), axis=0, keepdims=True)
    score_ref[...] = score
    stat_ref[0:1, :] = top
    stat_ref[1:2, :] = jnp.where(cand_ref[0:1, :] >= 0.0, total, 0.0)


def scores(coefs, cand, table, scale):
    total = cand.shape[1]
    return pl.pallas_call(
        functools.partial(score_body, scale=scale),
        out_shape=[
            jax.ShapeDtypeStruct((ROTS * CAND_OWN, total), jnp.float32),
            jax.ShapeDtypeStruct((2, total), jnp.float32),
        ],
        name="scores",
    )(*coefs, cand, table)


def swap_blocks(x, distance, width):
    lane = lax.broadcasted_iota(jnp.int32, x.shape, 1)
    bit = 1
    while bit <= distance:
        if distance & bit:
            shift = bit * width
            down = pltpu.roll(x, shift, 1)
            up = pltpu.roll(x, x.shape[1] - shift, 1)
            x = jnp.where((lane // shift) % 2 == 1, down, up)
        bit *= 2
    return x


def weights_body(at_ref, score_ref, cand_ref, stat_ref, table_ref, mix_ref, norm_ref):
    n_cls, _, total = stat_ref.shape
    width = total // n_cls
    tops, parts = [], []
    for e in range(n_cls):
        table = stat_ref[at_ref[0] ^ e]
        table = swap_blocks(jnp.concatenate([table] * 4, 0), e, width)
        tops.append(table[0:1])
        parts.append(table[1:2])
    top = functools.reduce(jnp.maximum, tops)
    summed = jnp.zeros_like(top)
    for other, part in zip(tops, parts):
        summed += part * jnp.exp(other - top)
    log_norm = top + jnp.log(summed)
    norm_ref[...] = log_norm[:, : norm_ref.shape[1]]
    weight = jnp.where(cand_ref[0:1, :] >= 0.0, jnp.exp(score_ref[...] - log_norm), 0.0)
    mix_ref[...] = lax.dot_general(
        table_ref[...],
        weight,
        (((1,), (0,)), ((), ())),
        precision=lax.Precision.HIGHEST,
        preferred_element_type=jnp.float32,
    )


def mixed_weights(cls, score, cand, stats, table, count):
    total = score.shape[1]
    return pl.pallas_call(
        weights_body,
        in_specs=[pl.BlockSpec(memory_space=pltpu.SMEM)] + [pl.BlockSpec(memory_space=pltpu.VMEM)] * 4,
        out_shape=[
            jax.ShapeDtypeStruct((COEF, total), jnp.float32),
            jax.ShapeDtypeStruct((1, count), jnp.float32),
        ],
        name="mixed_weights",
    )(cls, score, cand, stats, table)


def sums_body(*refs, number, pieces):
    blocks, extras = refs[:number], refs[number : 2 * number]
    refs = refs[2 * number :]
    mixes, cands = refs[:pieces], refs[pieces : 2 * pieces]
    back_ref, out_ref, weight_ref, mix, cand, planes = refs[2 * pieces :]
    i = pl.program_id(0)
    groups = weight_ref.shape[1]
    total = mix.shape[1]
    imag, odd = lane_signs()

    @pl.when(i == 0)
    def _():
        mixed = jnp.concatenate([ref[...] for ref in mixes], 1)
        chosen = jnp.concatenate([ref[...] for ref in cands], 1)
        hot = hot_masks(chosen, groups)
        summed = jnp.zeros((groups, total), jnp.float32)
        for q in range(CAND_OWN):
            summed += jnp.where(hot[q], mixed[q : q + 1], 0.0)
        weight_ref[...] = lax.dot_general(
            jnp.ones((1, total), jnp.float32),
            summed,
            (((1,), (1,)), ((), ())),
            precision=lax.Precision.HIGHEST,
            preferred_element_type=jnp.float32,
        )
        mix[...] = mixed
        cand[...] = chosen

    @pl.when(i < HALF // SUM_STEP)
    def _():
        hot = hot_masks(cand[...], groups)
        block = 2 * CAND_OWN
        sign = jnp.where(imag == odd, 1.0, -1.0)
        for u in range(SUM_STEP):
            g = i * SUM_STEP + u
            mine = mix[pl.ds(pl.multiple_of(g * block, block), block), :]
            halves = []
            for ab in range(2):
                dense = jnp.zeros((groups, total), jnp.float32)
                for q in range(CAND_OWN):
                    at = ab * CAND_OWN + q
                    dense = jnp.where(hot[q], mine[at : at + 1], dense)
                halves.append(dense)
            weights = jnp.concatenate(halves, 0).astype(jnp.bfloat16)
            made = jnp.dot(
                weights, lanes_of(blocks, u * TURNS, TURNS), preferred_element_type=jnp.float32
            )
            for t in range(TURNS):
                g1 = made[:groups, t * LANES : (t + 1) * LANES]
                g2 = made[groups:, t * LANES : (t + 1) * LANES]
                value = g1 + sign * pltpu.roll(g2, LANES // 2, 1)
                if u == 0:
                    value = jnp.where(i == 0, jnp.where(odd, g2, g1), value)
                start = pl.multiple_of((g * TURNS + t) * groups, groups)
                planes[pl.ds(start, groups), :] = value

            for t in range(TAIL):
                if t % SUM_STEP != u:
                    continue

                @pl.when(g == t)
                def _():
                    made = jnp.dot(
                        weights, lanes_of(extras, t // 2, 1), preferred_element_type=jnp.float32
                    )
                    g1, g2 = made[:groups], made[groups:]
                    value = g1
                    if t > 0:
                        value = g1 + jnp.where(imag, -1.0, 1.0) * pltpu.roll(g2, LANES // 2, 1)
                    rows = pl.ds((BODY + t // 2) * groups, groups)
                    if t % 2:
                        value = jnp.where(odd, value, planes[rows, :])
                    planes[rows, :] = value

    @pl.when(i >= HALF // SUM_STEP)
    def _():
        block, span, _ = out_ref.shape
        first = (i - HALF // SUM_STEP) * block
        back = back_ref[...]
        values = []
        for c in range(block):
            turned = planes[pl.ds(first + c, CHUNKS, stride=groups), :].T
            for s in range(2):
                at = 2 * s * span
                values.append(
                    jnp.concatenate([turned[at : at + span], turned[at + span : at + 2 * span]], 1)
                )
        value = jnp.concatenate(values, 0)
        high = value.astype(jnp.bfloat16)
        low = (value - high.astype(jnp.float32)).astype(jnp.bfloat16)
        both = jnp.dot(
            jnp.concatenate([high, low], 0), back, preferred_element_type=jnp.float32
        )
        rows = value.shape[0]
        placed = both[:rows] + both[rows:]
        for c in range(block):
            for s in range(2):
                at = (2 * c + s) * span
                out_ref[c, :, s * HARM : (s + 1) * HARM] = placed[at : at + span]


def sums(blocks, mixes, cands, back, groups, span):
    count = blocks[0].shape[1]
    total = len(blocks) * count
    size = blocks[0].size * len(blocks)
    block = 8
    steps = HALF // SUM_STEP
    whole = lambda i: (0, 0)
    return pl.pallas_call(
        functools.partial(sums_body, number=len(blocks), pieces=len(mixes)),
        grid=(steps + groups // block,),
        in_specs=[
            *[
                pl.BlockSpec(
                    (SUM_STEP * TURNS, count, LANES), lambda i: (jnp.minimum(i, steps - 1), 0, 0)
                )
                for _ in blocks
            ],
            *[
                pl.BlockSpec((EXTRA, count, LANES), lambda i: (BODY // EXTRA, 0, 0))
                for _ in blocks
            ],
            *[pl.BlockSpec(array.shape, whole) for array in (*mixes, *cands, back)],
        ],
        out_specs=[
            pl.BlockSpec(
                (block, span, 2 * HARM), lambda i: (jnp.maximum(i - steps, 0), 0, 0)
            ),
            pl.BlockSpec((1, groups), whole),
        ],
        out_shape=[
            jax.ShapeDtypeStruct((groups, span, 2 * HARM), jnp.float32),
            jax.ShapeDtypeStruct((1, groups), jnp.float32),
        ],
        scratch_shapes=[
            pltpu.VMEM((COEF, total), jnp.float32),
            pltpu.VMEM((2 * CAND_OWN, total), jnp.float32),
            pltpu.VMEM((CHUNKS * groups, LANES), jnp.float32),
        ],
        compiler_params=pltpu.CompilerParams(vmem_limit_bytes=60 << 20),
        cost_estimate=pl.CostEstimate(
            flops=4 * size * groups,
            bytes_accessed=2 * size + 8 * groups * span * HARM,
            transcendentals=0,
        ),
        name="sums",
    )(*blocks, *blocks, *mixes, *cands, back)


def hop(value, axis, distance):
    size = lax.axis_size(axis)
    return lax.ppermute(value, axis, [(i, i ^ distance) for i in range(size)])


def after(value, *others):
    return lax.optimization_barrier((value, *others))[0]


def direct(own):
    n_cls = lax.axis_size("cls")
    return {1 << bit: hop(own, "cls", 1 << bit) for bit in range(1, n_cls.bit_length() - 1)}


def relayed(known, d, *others):
    n_cls = lax.axis_size("cls")
    for j in sorted(range(2, n_cls, 2), key=lambda j: bin(j).count("1")):
        if j not in known:
            bits = [bit for bit in range(1, n_cls.bit_length()) if j >> bit & 1]
            way = 1 << bits[d % len(bits)]
            known[j] = hop(after(known[j ^ way], *others), "cls", way)
    return known


def paired(known, each, last):
    n_cls = lax.axis_size("cls")
    for j in range(0, n_cls, 2):
        others = last if j == n_cls - 2 else each
        block = after(known[j], *others) if others else known[j]
        known[j + 1] = hop(block, "cls", 1)
    return [known[j] for j in range(n_cls)]


def gather_device(particles, references, owner_groups, class_order):
    n_cls, n_prt = lax.axis_size("cls"), lax.axis_size("prt")
    cls, prt = lax.axis_index("cls"), lax.axis_index("prt")
    count, cycles, width = particles.shape
    groups = references.shape[0]
    span = cycles // n_prt
    back = jnp.asarray(unselector(), jnp.bfloat16)
    table = jnp.asarray(rotation_table())
    picks = class_order[:, :, :CAND_OWN].reshape(count, OWN_TOP * CAND_OWN)
    meta = jnp.concatenate([owner_groups, picks], 1)
    cls, prt = (index.reshape(1).astype(jnp.int32) for index in (cls, prt))
    order = [d for d in range(n_prt) if d % 2 == 0] + [d for d in range(n_prt) if d % 2]
    outgoing = {}
    place = prt
    for first in range(0, n_prt, 2):
        distances = tuple(order[first : first + 2])
        made = arrange_particles(place, particles, meta, n_prt, distances)
        outgoing.update(zip(distances, made))
        place = after(prt, made[0])
    last = outgoing[order[-1]]
    arrived = {0: outgoing[0]}
    for d in order[1:]:
        block = after(outgoing[d], arrived[2]) if d > 2 else outgoing[d]
        arrived[d] = hop(block, "prt", d)
    known = {0: {0: arrived[0], **direct(arrived[0])}}
    for d in range(1, min(n_prt, 3)):
        own = after(arrived[d], last) if d == 2 else arrived[d]
        known[d] = {0: own, **direct(own)}
    place = after(prt, known[0][2], known[0][n_cls // 2])
    place = after(place, *[arrived[d] for d in range(1, min(n_prt, 3))])
    arranged, norms = arrange_references(references, place, n_prt)
    for d in range(3, n_prt):
        arrived[d] = after(arrived[d], arranged)
        known[d] = {0: arrived[d], **direct(arrived[d])}
    relayed(known[0], 0, arranged)
    for d in range(1, n_prt):
        relayed(known[d], d)
    scale = 2.0 / math.sqrt(cycles * width)
    coefs, cands, sent, blocks = [], [], [], []
    for d in range(n_prt):
        waits = [known[n_prt - 1][2]] if d == 1 else []
        first = [known[e][j] for e in range(1, n_prt) for j in (2, n_cls // 2)]
        each = first if d < 2 else coefs[:1]
        blocks.append(paired(known[d], each, coefs[-1:] if d > 1 else []))
        ready = after(arranged, *waits) if waits else arranged
        coef, cand = cross_coefficients(blocks[d], ready, norms, cls)
        coefs.append(coef)
        sent.append(hop(coef, "prt", d) if d else coef)
        cands.append(cand)
    score, stat = scores(sent, cands[0], table, scale)
    stats = lax.all_gather(stat.reshape(1, *stat.shape), "cls", axis=0, tiled=True)
    mix, log_norm = mixed_weights(cls, score, cands[0], stats, table, count)
    mixes = [hop(mix, "prt", d) if d else mix for d in range(n_prt)]
    class_sums, class_weights = sums(
        [block for piece in blocks for block in piece], mixes, cands, back, groups, span
    )
    own = log_norm[0]
    return class_sums, class_weights[0], own


def per_device(particles, references, owner_groups, class_order):
    n_cls, n_prt = lax.axis_size("cls"), lax.axis_size("prt")
    count, cycles, _ = particles.shape
    groups = references.shape[0]
    cap = max(2, 2 * count * OWN_TOP // n_cls)
    powers = n_cls & (n_cls - 1) == 0 and n_prt & (n_prt - 1) == 0
    fits = 4 * cycles == LANES * n_prt and n_cls * CAND_OWN <= LANES and groups % 16 == 0 and n_cls >= 4
    fits = fits and powers and n_cls * count == LANES
    plan = gather_device if cap >= count and fits else dispatch_device
    return plan(particles, references, owner_groups, class_order)


def solution(mesh):
    in_specs = (
        P(("cls", "prt"), None, None),
        P("cls", None, None),
        P(("cls", "prt"), None),
        P(("cls", "prt"), None, None),
    )
    out_specs = (P("cls", "prt", None), P("cls"), P(("cls", "prt")))
    return jax.shard_map(
        per_device, mesh=mesh, in_specs=in_specs, out_specs=out_specs, check_vma=False
    )
```

```python
import functools
import math

import jax
import jax.numpy as jnp
import numpy as np
from jax import lax
from jax.experimental import pallas as pl
from jax.experimental.pallas import tpu as pltpu
from jax.sharding import PartitionSpec as P

CYCLES = 128
HARM = 256
ROTS = 36
OWN_TOP = 4
CAND_OWN = 4


lowest = -1e30


def spectral_tables():
    harmonic = jnp.arange(HARM, dtype=jnp.float32)
    angles = 2.0 * math.pi * jnp.arange(ROTS, dtype=jnp.float32) / ROTS
    phase = harmonic[:, None] * angles[None, :]
    forward = jnp.concatenate([jnp.cos(phase), jnp.sin(phase)], 0)
    backward = jnp.concatenate([jnp.cos(phase), -jnp.sin(phase)], 0).T
    return (forward, backward)


def class_accumulate(lanes, mixed):
    l_re = lanes[..., :HARM]
    l_im = lanes[..., HARM:]
    y_re = mixed[..., :HARM]
    y_im = mixed[..., HARM:]
    s_re = jnp.einsum("lrm,lcm->crm", l_re, y_re, preferred_element_type=jnp.float32) - jnp.einsum(
        "lrm,lcm->crm", l_im, y_im, preferred_element_type=jnp.float32
    )
    s_im = jnp.einsum("lrm,lcm->crm", l_re, y_im, preferred_element_type=jnp.float32) + jnp.einsum(
        "lrm,lcm->crm", l_im, y_re, preferred_element_type=jnp.float32
    )
    return jnp.concatenate([s_re, s_im], -1)


def dispatch_device(particles, references, owner_groups, class_order):
    n_cls = lax.axis_size("cls")
    count = particles.shape[0]
    groups = references.shape[0]
    cap = max(2, 2 * count * OWN_TOP // n_cls)
    slots = n_cls * cap
    width = 2 * HARM
    flat_owner = owner_groups.reshape(-1)
    owner_hot = (flat_owner[:, None] == jnp.arange(n_cls, dtype=jnp.int32)[None, :]).astype(
        jnp.int32
    )
    before = jnp.cumsum(owner_hot, axis=0) - owner_hot
    rank = jnp.sum(before * owner_hot, axis=1)
    slot_of = flat_owner * cap + rank
    match = slot_of[None, :] == jnp.arange(slots, dtype=jnp.int32)[:, None]
    member = jnp.any(match.reshape(slots, count, OWN_TOP), axis=2)
    filled = jnp.any(member, axis=1)
    dispatch = member.astype(jnp.bfloat16)
    outgoing = jnp.dot(
        dispatch, particles.reshape(count, CYCLES * width), preferred_element_type=jnp.float32
    )
    outgoing = outgoing.astype(jnp.bfloat16).reshape(n_cls, cap, CYCLES, width)
    match_int = match.astype(jnp.int32)
    picks = class_order[:, :, :CAND_OWN].reshape(count * OWN_TOP, CAND_OWN)
    slot_cand = jnp.where(filled[:, None], jnp.dot(match_int, picks), -1)
    owner_rows = jnp.repeat(jnp.arange(count, dtype=jnp.int32), OWN_TOP)
    slot_pid = jnp.where(filled, jnp.dot(match_int, owner_rows), -1)
    labels_out = jnp.concatenate([slot_cand, slot_pid[:, None]], 1).reshape(
        n_cls, cap, CAND_OWN + 1
    )
    arrived, labels = (
        lax.all_to_all(outgoing, "cls", split_axis=0, concat_axis=0, tiled=True),
        lax.all_to_all(labels_out, "cls", split_axis=0, concat_axis=0, tiled=True),
    )
    lanes = arrived.reshape(slots, CYCLES, width)
    labels = labels.reshape(slots, CAND_OWN + 1)
    forward, backward = spectral_tables()
    scale = 2.0 / math.sqrt(CYCLES * width)
    norms = jnp.sum(jnp.square(references.astype(jnp.float32)), axis=(1, 2))
    l_re = lanes[..., :HARM]
    l_im = lanes[..., HARM:]
    r_re = references[..., :HARM]
    r_im = references[..., HARM:]
    x_re = jnp.einsum("lrm,crm->lcm", l_re, r_re, preferred_element_type=jnp.float32) + jnp.einsum(
        "lrm,crm->lcm", l_im, r_im, preferred_element_type=jnp.float32
    )
    x_im = jnp.einsum("lrm,crm->lcm", l_im, r_re, preferred_element_type=jnp.float32) - jnp.einsum(
        "lrm,crm->lcm", l_re, r_im, preferred_element_type=jnp.float32
    )
    cross = jnp.concatenate([x_re, x_im], -1)
    corr = jnp.dot(
        cross.reshape(slots * groups, width), forward, precision=lax.Precision.HIGHEST
    ).reshape(slots, groups, ROTS)
    score = (corr - 0.5 * norms[None, :, None]) * scale
    candidate = jnp.any(
        labels[:, :CAND_OWN, None] == jnp.arange(groups, dtype=jnp.int32)[None, None, :], axis=1
    )
    part_max = jnp.max(jnp.where(candidate[:, :, None], score, lowest), axis=(1, 2))
    part_sum = jnp.sum(
        jnp.where(candidate[:, :, None], jnp.exp(score - part_max[:, None, None]), 0.0), axis=(1, 2)
    )
    sender_ids = labels[:, CAND_OWN].astype(jnp.float32)
    table_max, table_sum, table_ids = (
        lax.all_gather(part_max.reshape(1, n_cls, cap), "cls", axis=0, tiled=True),
        lax.all_gather(part_sum.reshape(1, n_cls, cap), "cls", axis=0, tiled=True),
        lax.all_gather(sender_ids.reshape(1, n_cls, cap), "cls", axis=0, tiled=True),
    )
    local_ids = jnp.arange(count, dtype=jnp.float32)
    hit = table_ids[..., None] == local_ids
    top = jnp.max(jnp.where(hit, table_max[..., None], lowest), axis=(0, 2))
    total = jnp.sum(
        jnp.where(
            hit, table_sum[..., None] * jnp.exp(table_max[..., None] - top[None, :, None, :]), 0.0
        ),
        axis=(0, 2),
    )
    table_norm = top + jnp.log(total)
    slot_ids = labels[:, CAND_OWN].reshape(n_cls, cap)
    slot_norm = jnp.sum(
        jnp.where(
            slot_ids[..., None] == jnp.arange(count, dtype=jnp.int32), table_norm[:, None, :], 0.0
        ),
        axis=2,
    ).reshape(slots)
    own_norm = lax.dynamic_index_in_dim(table_norm, lax.axis_index("cls"), 0, keepdims=False)
    weight = jnp.where(candidate[:, :, None], jnp.exp(score - slot_norm[:, None, None]), 0.0)
    mixed = (
        jnp.dot(weight.reshape(slots * groups, ROTS), backward, precision=lax.Precision.HIGHEST)
        .astype(jnp.bfloat16)
        .reshape(slots, groups, width)
    )
    class_weights = lax.psum(jnp.sum(weight, axis=(0, 2)), "prt")
    partial_sums = class_accumulate(lanes, mixed)
    class_sums = lax.psum_scatter(partial_sums, "prt", scatter_dimension=1, tiled=True)
    return (class_sums, class_weights, own_norm)


LANES = 128


def harmonic_plan():
    half = ROTS // 2
    turns = HARM // ROTS
    tail = HARM - turns * ROTS
    chunk_of = np.zeros(HARM, np.int32)
    side_of = np.zeros(HARM, np.int32)
    for m in range(HARM):
        turn, rest = divmod(m, ROTS)
        if turn == turns:
            chunk_of[m] = half * turns + rest // 2
            side_of[m] = rest % 2
        elif rest < half:
            chunk_of[m] = rest * turns + turn
        else:
            chunk_of[m] = ((ROTS - rest) % half) * turns + turn
            side_of[m] = 1
    return half, turns, tail, chunk_of, side_of


HALF, TURNS, TAIL, CHUNK_OF, SIDE_OF = harmonic_plan()
BODY = HALF * TURNS
CHUNKS = BODY + TAIL // 2
EXTRA = TAIL // 2 + 1
COEF = 2 * HALF * CAND_OWN
CROSS_STEP = 3
SUM_STEP = 3


def selector():
    return (np.arange(CHUNKS)[:, None] == CHUNK_OF[None, :]).astype(np.float32)


def unselector():
    sel = selector()
    return np.concatenate([sel * (SIDE_OF == 0), sel * (SIDE_OF == 1)], 0)


def rotation_table():
    table = np.zeros((HALF, 2, CAND_OWN, ROTS, CAND_OWN))
    angle = 2.0 * np.pi * np.arange(ROTS) / ROTS
    for g in range(HALF):
        first = np.cos(g * angle)
        second = np.cos(HALF * angle) if g == 0 else np.sin(g * angle)
        for q in range(CAND_OWN):
            table[g, 0, q, :, q] = first
            table[g, 1, q, :, q] = second
    return table.reshape(COEF, ROTS * CAND_OWN).astype(np.float32)


def nt_dot(a, b):
    return lax.dot_general(a, b, (((1,), (1,)), ((), ())), preferred_element_type=jnp.float32)


def selector_masks():
    m = lax.broadcasted_iota(jnp.int32, (1, HARM), 1)
    turn = jnp.zeros((1, HARM), jnp.int32)
    for t in range(1, TURNS + 1):
        turn += jnp.where(m >= t * ROTS, 1, 0)
    rest = m - ROTS * turn
    back = jnp.where(rest == HALF, 0, ROTS - rest)
    chunk = jnp.where(rest < HALF, rest, back) * TURNS + turn
    side = jnp.where(rest < HALF, 0, 1)
    chunk = jnp.where(turn == TURNS, BODY + rest // 2, chunk)
    side = jnp.where(turn == TURNS, rest % 2, side)
    rows = lax.broadcasted_iota(jnp.int32, (CHUNKS, HARM), 0)
    sel = jnp.where(rows == chunk, 1.0, 0.0).astype(jnp.bfloat16)
    sides = lax.broadcasted_iota(jnp.int32, (2, HARM), 0)
    masks = jnp.where(sides == side, 1.0, 0.0).astype(jnp.bfloat16)
    return sel, masks


def masked_stack(piece, masks):
    parts = []
    for s in range(2):
        for b in range(2):
            parts.append(piece[:, s * HARM : (s + 1) * HARM] * masks[b : b + 1])
    return jnp.concatenate(parts, 0)


def repeat(number, step, body, carry):
    def several(i, carry):
        for u in range(step):
            carry = body(i * step + u, carry)
        return carry

    return lax.fori_loop(0, number // step, several, carry)


def particle_body(at_ref, x_ref, meta_ref, *refs, distances, n_prt):
    outs, scr = refs[:-1], refs[-1]
    count, cycles, _ = x_ref.shape
    number = len(outs)
    span = cycles // n_prt
    sel, masks = selector_masks()

    def one(n, carry):
        parts = []
        for d in distances:
            start = pl.multiple_of((at_ref[0] ^ d) * span, span)
            parts.append(masked_stack(x_ref[n, pl.ds(start, span), :], masks))
        w = jnp.concatenate(parts, 0)
        y = nt_dot(sel, w)
        for p in range(number):
            scr[p, pl.ds(pl.multiple_of(n * CHUNKS, CHUNKS), CHUNKS), :] = y[
                :, p * LANES : (p + 1) * LANES
            ]
        return carry

    repeat(count, 4, one, 0)

    def two(c, carry):
        for p in range(number):
            outs[p][c] = scr[p, pl.ds(c, count, stride=CHUNKS), :].astype(jnp.bfloat16)
        return carry

    repeat(CHUNKS, 8, two, 0)
    lane = lax.broadcasted_iota(jnp.int32, (count, LANES), 1)
    label = jnp.full((count, LANES), -1, jnp.int32)
    for t in range(OWN_TOP):
        mine = (lane // CAND_OWN) == meta_ref[:, t : t + 1]
        for q in range(CAND_OWN):
            at = OWN_TOP + t * CAND_OWN + q
            label = jnp.where(
                mine & (lane % CAND_OWN == q), meta_ref[:, at : at + 1], label
            )
    label = label.astype(jnp.float32).astype(jnp.bfloat16)
    for p in range(number):
        outs[p][CHUNKS] = label


def arrange_particles(prt, particles, meta, n_prt, distances):
    count = particles.shape[0]
    number = len(distances)
    size = particles.size * number // n_prt
    return pl.pallas_call(
        functools.partial(particle_body, distances=distances, n_prt=n_prt),
        in_specs=[pl.BlockSpec(memory_space=pltpu.SMEM)] + [pl.BlockSpec(memory_space=pltpu.VMEM)] * 2,
        out_shape=[jax.ShapeDtypeStruct((CHUNKS + 1, count, LANES), jnp.bfloat16)] * number,
        scratch_shapes=[pltpu.VMEM((number, count * CHUNKS, LANES), jnp.float32)],
        compiler_params=pltpu.CompilerParams(vmem_limit_bytes=32 << 20),
        cost_estimate=pl.CostEstimate(
            flops=size * 2 * CHUNKS, bytes_accessed=size * 4, transcendentals=0
        ),
        name="arrange_particles",
    )(prt, particles, meta)


def reference_body(at_ref, x_ref, out_ref, norm_ref, scr):
    rows = x_ref.shape[0]
    sel, masks = selector_masks()
    step = 4

    def one(n, carry):
        w = jnp.concatenate([masked_stack(x_ref[n * step + i], masks) for i in range(step)], 0)
        y = nt_dot(sel, w)
        for i in range(step):
            scr[pl.ds(pl.multiple_of((n * step + i) * CHUNKS, CHUNKS), CHUNKS), :] = y[
                :, i * LANES : (i + 1) * LANES
            ]
        return carry

    repeat(rows // step, 2, one, 0)

    def two(c, carry):
        value = scr[pl.ds(c, rows, stride=CHUNKS), :]
        out_ref[c] = value.astype(jnp.bfloat16)
        return carry + value * value

    norm_ref[...] = repeat(CHUNKS, 8, two, jnp.zeros((rows, LANES), jnp.float32))


def arrange_references(references, prt, n_prt):
    groups, cycles, width = references.shape
    span = cycles // n_prt
    block = 16
    return pl.pallas_call(
        reference_body,
        grid_spec=pltpu.PrefetchScalarGridSpec(
            num_scalar_prefetch=1,
            grid=(groups // block,),
            in_specs=[
                pl.BlockSpec((block, span, width), lambda i, at: (i, at[0], 0)),
            ],
            out_specs=[
                pl.BlockSpec((CHUNKS, block, LANES), lambda i, at: (0, i, 0)),
                pl.BlockSpec((block, LANES), lambda i, at: (i, 0)),
            ],
            scratch_shapes=[pltpu.VMEM((block * CHUNKS, LANES), jnp.float32)],
        ),
        out_shape=[
            jax.ShapeDtypeStruct((CHUNKS, groups, LANES), jnp.bfloat16),
            jax.ShapeDtypeStruct((groups, LANES), jnp.float32),
        ],
        compiler_params=pltpu.CompilerParams(vmem_limit_bytes=60 << 20),
        cost_estimate=pl.CostEstimate(
            flops=groups * span * width * 64 * CHUNKS,
            bytes_accessed=groups * span * width * 4,
            transcendentals=0,
        ),
        name="arrange_references",
    )(prt, references)


def lane_signs():
    lane = lax.broadcasted_iota(jnp.int32, (1, LANES), 1)
    quarter = LANES // 4
    imag = lane >= 2 * quarter
    odd = (lane // quarter) % 2 == 1
    return imag, odd


def lanes_of(refs, first, number):
    parts = [
        jnp.concatenate([ref[i] for ref in refs], 0) for i in range(first, first + number)
    ]
    return jnp.concatenate(parts, 1) if number > 1 else parts[0]


def hot_masks(cand, groups):
    rows = lax.broadcasted_iota(jnp.int32, (groups, cand.shape[1]), 0).astype(jnp.float32)
    return [rows == cand[q : q + 1] for q in range(CAND_OWN)]


def residue_weights(q_ref, at, g):
    imag, odd = lane_signs()
    sign = jnp.where(imag == odd, -1.0, 1.0)
    first, second = [], []
    for i in range(TURNS):
        q = q_ref[at * TURNS + i].astype(jnp.float32)
        turned = pltpu.roll(q, LANES // 2, 1) * sign
        if at == 0:
            first.append(jnp.where((g == 0) & odd, 0.0, q))
            second.append(jnp.where(g == 0, jnp.where(odd, q, 0.0), turned))
        else:
            first.append(q)
            second.append(turned)
    return jnp.concatenate(
        [jnp.concatenate(first, 1), jnp.concatenate(second, 1)], 0
    ).astype(jnp.bfloat16)


def chosen_rows(acc, cand):
    groups = acc.shape[0] // 2
    hot = hot_masks(cand, groups)
    rows = []
    for ab in range(2):
        part = acc[ab * groups : (ab + 1) * groups, :]
        for q in range(CAND_OWN):
            rows.append(jnp.sum(jnp.where(hot[q], part, 0.0), axis=0, keepdims=True))
    return jnp.concatenate(rows, 0)


def cross_body(at_ref, *refs):
    number = (len(refs) - 6) // 2
    blocks, extras = refs[:number], refs[number : 2 * number]
    q_ref, qt_ref, norm_ref, coef_ref, cand_ref, acc = refs[2 * number :]
    step = pl.program_id(0)
    groups = q_ref.shape[1]
    imag, odd = lane_signs()

    @pl.when(step == 0)
    def _():
        label = lanes_of(extras, TAIL // 2, 1).astype(jnp.float32).T
        row = lax.broadcasted_iota(jnp.int32, label.shape, 0)
        base = at_ref[0] * CAND_OWN
        for q in range(CAND_OWN):
            cand_ref[q : q + 1, :] = jnp.sum(
                jnp.where(row == base + q, label, 0.0), axis=0, keepdims=True
            )
        cand_ref[CAND_OWN:, :] = jnp.full(
            (cand_ref.shape[0] - CAND_OWN, cand_ref.shape[1]), -1.0, jnp.float32
        )

    for u in range(CROSS_STEP):
        g = step * CROSS_STEP + u
        acc[...] = nt_dot(residue_weights(q_ref, u, g), lanes_of(blocks, u * TURNS, TURNS))

        for i in range(TAIL):
            if i % CROSS_STEP != u:
                continue

            @pl.when(g == i)
            def _():
                q = qt_ref[i // 2].astype(jnp.float32)
                keep = odd if i % 2 else ~odd
                a = jnp.where(keep, q, 0.0)
                turned = pltpu.roll(q, LANES // 2, 1) * jnp.where(imag, 1.0, -1.0)
                b = jnp.where(keep, turned, 0.0)
                if i == 0:
                    b = jnp.zeros_like(b)
                w = jnp.concatenate([a, b], 0).astype(jnp.bfloat16)
                acc[...] += nt_dot(w, lanes_of(extras, i // 2, 1))
                if i == 0:
                    acc[:groups, :] -= 0.5 * jnp.sum(norm_ref[...], axis=1, keepdims=True)

        block = 2 * CAND_OWN
        coef_ref[u * block : (u + 1) * block, :] = chosen_rows(acc[...], cand_ref[...])


def cross_coefficients(blocks, arranged, norms, cls):
    count = blocks[0].shape[1]
    groups = arranged.shape[1]
    total = len(blocks) * count
    half_tail = TAIL // 2
    size = blocks[0].size * len(blocks)
    block = 2 * CAND_OWN
    return pl.pallas_call(
        cross_body,
        grid_spec=pltpu.PrefetchScalarGridSpec(
            num_scalar_prefetch=1,
            grid=(HALF // CROSS_STEP,),
            in_specs=[
                *[
                    pl.BlockSpec((CROSS_STEP * TURNS, count, LANES), lambda g, at: (g, 0, 0))
                    for _ in blocks
                ],
                *[
                    pl.BlockSpec((EXTRA, count, LANES), lambda g, at: (BODY // EXTRA, 0, 0))
                    for _ in blocks
                ],
                pl.BlockSpec((CROSS_STEP * TURNS, groups, LANES), lambda g, at: (g, 0, 0)),
                pl.BlockSpec((half_tail, groups, LANES), lambda g, at: (BODY // half_tail, 0, 0)),
                pl.BlockSpec((groups, LANES), lambda g, at: (0, 0)),
            ],
            out_specs=[
                pl.BlockSpec((CROSS_STEP * block, total), lambda g, at: (g, 0)),
                pl.BlockSpec((block, total), lambda g, at: (0, 0)),
            ],
            scratch_shapes=[pltpu.VMEM((2 * groups, total), jnp.float32)],
        ),
        out_shape=[
            jax.ShapeDtypeStruct((COEF, total), jnp.float32),
            jax.ShapeDtypeStruct((block, total), jnp.float32),
        ],
        compiler_params=pltpu.CompilerParams(vmem_limit_bytes=60 << 20),
        cost_estimate=pl.CostEstimate(
            flops=128 * size * groups, bytes_accessed=2 * size, transcendentals=0
        ),
        name="cross_coefficients",
    )(cls, *blocks, *blocks, arranged, arranged, norms)


def score_body(*refs, scale):
    *coefs, cand_ref, table_ref, score_ref, stat_ref = refs
    corr = lax.dot_general(
        table_ref[...],
        functools.reduce(jnp.add, [ref[...] for ref in coefs]),
        (((0,), (0,)), ((), ())),
        precision=lax.Precision.HIGHEST,
        preferred_element_type=jnp.float32,
    )
    score = jnp.where(cand_ref[0:1, :] >= 0.0, corr * scale, lowest)
    top = jnp.max(score, axis=0, keepdims=True)
    total = jnp.sum(jnp.exp(score - top), axis=0, keepdims=True)
    score_ref[...] = score
    stat_ref[0:1, :] = top
    stat_ref[1:2, :] = jnp.where(cand_ref[0:1, :] >= 0.0, total, 0.0)


def scores(coefs, cand, table, scale):
    total = cand.shape[1]
    return pl.pallas_call(
        functools.partial(score_body, scale=scale),
        out_shape=[
            jax.ShapeDtypeStruct((ROTS * CAND_OWN, total), jnp.float32),
            jax.ShapeDtypeStruct((2, total), jnp.float32),
        ],
        name="scores",
    )(*coefs, cand, table)


def swap_blocks(x, distance, width):
    lane = lax.broadcasted_iota(jnp.int32, x.shape, 1)
    bit = 1
    while bit <= distance:
        if distance & bit:
            shift = bit * width
            down = pltpu.roll(x, shift, 1)
            up = pltpu.roll(x, x.shape[1] - shift, 1)
            x = jnp.where((lane // shift) % 2 == 1, down, up)
        bit *= 2
    return x


def weights_body(at_ref, score_ref, cand_ref, stat_ref, table_ref, mix_ref, norm_ref):
    n_cls, _, total = stat_ref.shape
    width = total // n_cls
    tops, parts = [], []
    for e in range(n_cls):
        table = stat_ref[at_ref[0] ^ e]
        table = swap_blocks(jnp.concatenate([table] * 4, 0), e, width)
        tops.append(table[0:1])
        parts.append(table[1:2])
    top = functools.reduce(jnp.maximum, tops)
    summed = jnp.zeros_like(top)
    for other, part in zip(tops, parts):
        summed += part * jnp.exp(other - top)
    log_norm = top + jnp.log(summed)
    norm_ref[...] = log_norm[:, : norm_ref.shape[1]]
    weight = jnp.where(cand_ref[0:1, :] >= 0.0, jnp.exp(score_ref[...] - log_norm), 0.0)
    mix_ref[...] = lax.dot_general(
        table_ref[...],
        weight,
        (((1,), (0,)), ((), ())),
        precision=lax.Precision.HIGHEST,
        preferred_element_type=jnp.float32,
    )


def mixed_weights(cls, score, cand, stats, table, count):
    total = score.shape[1]
    return pl.pallas_call(
        weights_body,
        in_specs=[pl.BlockSpec(memory_space=pltpu.SMEM)] + [pl.BlockSpec(memory_space=pltpu.VMEM)] * 4,
        out_shape=[
            jax.ShapeDtypeStruct((COEF, total), jnp.float32),
            jax.ShapeDtypeStruct((1, count), jnp.float32),
        ],
        name="mixed_weights",
    )(cls, score, cand, stats, table)


def sums_body(*refs, number, pieces):
    blocks, extras = refs[:number], refs[number : 2 * number]
    refs = refs[2 * number :]
    mixes, cands = refs[:pieces], refs[pieces : 2 * pieces]
    back_ref, out_ref, weight_ref, mix, cand, planes = refs[2 * pieces :]
    i = pl.program_id(0)
    groups = weight_ref.shape[1]
    total = mix.shape[1]
    imag, odd = lane_signs()

    @pl.when(i == 0)
    def _():
        mixed = jnp.concatenate([ref[...] for ref in mixes], 1)
        chosen = jnp.concatenate([ref[...] for ref in cands], 1)
        hot = hot_masks(chosen, groups)
        summed = jnp.zeros((groups, total), jnp.float32)
        for q in range(CAND_OWN):
            summed += jnp.where(hot[q], mixed[q : q + 1], 0.0)
        weight_ref[...] = lax.dot_general(
            jnp.ones((1, total), jnp.float32),
            summed,
            (((1,), (1,)), ((), ())),
            precision=lax.Precision.HIGHEST,
            preferred_element_type=jnp.float32,
        )
        mix[...] = mixed
        cand[...] = chosen

    @pl.when(i < HALF // SUM_STEP)
    def _():
        hot = hot_masks(cand[...], groups)
        block = 2 * CAND_OWN
        sign = jnp.where(imag == odd, 1.0, -1.0)
        for u in range(SUM_STEP):
            g = i * SUM_STEP + u
            mine = mix[pl.ds(pl.multiple_of(g * block, block), block), :]
            halves = []
            for ab in range(2):
                dense = jnp.zeros((groups, total), jnp.float32)
                for q in range(CAND_OWN):
                    at = ab * CAND_OWN + q
                    dense = jnp.where(hot[q], mine[at : at + 1], dense)
                halves.append(dense)
            weights = jnp.concatenate(halves, 0).astype(jnp.bfloat16)
            made = jnp.dot(
                weights, lanes_of(blocks, u * TURNS, TURNS), preferred_element_type=jnp.float32
            )
            for t in range(TURNS):
                g1 = made[:groups, t * LANES : (t + 1) * LANES]
                g2 = made[groups:, t * LANES : (t + 1) * LANES]
                value = g1 + sign * pltpu.roll(g2, LANES // 2, 1)
                if u == 0:
                    value = jnp.where(i == 0, jnp.where(odd, g2, g1), value)
                start = pl.multiple_of((g * TURNS + t) * groups, groups)
                planes[pl.ds(start, groups), :] = value

            for t in range(TAIL):
                if t % SUM_STEP != u:
                    continue

                @pl.when(g == t)
                def _():
                    made = jnp.dot(
                        weights, lanes_of(extras, t // 2, 1), preferred_element_type=jnp.float32
                    )
                    g1, g2 = made[:groups], made[groups:]
                    value = g1
                    if t > 0:
                        value = g1 + jnp.where(imag, -1.0, 1.0) * pltpu.roll(g2, LANES // 2, 1)
                    rows = pl.ds((BODY + t // 2) * groups, groups)
                    if t % 2:
                        value = jnp.where(odd, value, planes[rows, :])
                    planes[rows, :] = value

    @pl.when(i >= HALF // SUM_STEP)
    def _():
        block, span, _ = out_ref.shape
        first = (i - HALF // SUM_STEP) * block
        back = back_ref[...]
        values = []
        for c in range(block):
            turned = planes[pl.ds(first + c, CHUNKS, stride=groups), :].T
            for s in range(2):
                at = 2 * s * span
                values.append(
                    jnp.concatenate([turned[at : at + span], turned[at + span : at + 2 * span]], 1)
                )
        value = jnp.concatenate(values, 0)
        high = value.astype(jnp.bfloat16)
        low = (value - high.astype(jnp.float32)).astype(jnp.bfloat16)
        both = jnp.dot(
            jnp.concatenate([high, low], 0), back, preferred_element_type=jnp.float32
        )
        rows = value.shape[0]
        placed = both[:rows] + both[rows:]
        for c in range(block):
            for s in range(2):
                at = (2 * c + s) * span
                out_ref[c, :, s * HARM : (s + 1) * HARM] = placed[at : at + span]


def sums(blocks, mixes, cands, back, groups, span):
    count = blocks[0].shape[1]
    total = len(blocks) * count
    size = blocks[0].size * len(blocks)
    block = 8
    steps = HALF // SUM_STEP
    whole = lambda i: (0, 0)
    return pl.pallas_call(
        functools.partial(sums_body, number=len(blocks), pieces=len(mixes)),
        grid=(steps + groups // block,),
        in_specs=[
            *[
                pl.BlockSpec(
                    (SUM_STEP * TURNS, count, LANES), lambda i: (jnp.minimum(i, steps - 1), 0, 0)
                )
                for _ in blocks
            ],
            *[
                pl.BlockSpec((EXTRA, count, LANES), lambda i: (BODY // EXTRA, 0, 0))
                for _ in blocks
            ],
            *[pl.BlockSpec(array.shape, whole) for array in (*mixes, *cands, back)],
        ],
        out_specs=[
            pl.BlockSpec(
                (block, span, 2 * HARM), lambda i: (jnp.maximum(i - steps, 0), 0, 0)
            ),
            pl.BlockSpec((1, groups), whole),
        ],
        out_shape=[
            jax.ShapeDtypeStruct((groups, span, 2 * HARM), jnp.float32),
            jax.ShapeDtypeStruct((1, groups), jnp.float32),
        ],
        scratch_shapes=[
            pltpu.VMEM((COEF, total), jnp.float32),
            pltpu.VMEM((2 * CAND_OWN, total), jnp.float32),
            pltpu.VMEM((CHUNKS * groups, LANES), jnp.float32),
        ],
        compiler_params=pltpu.CompilerParams(vmem_limit_bytes=60 << 20),
        cost_estimate=pl.CostEstimate(
            flops=4 * size * groups,
            bytes_accessed=2 * size + 8 * groups * span * HARM,
            transcendentals=0,
        ),
        name="sums",
    )(*blocks, *blocks, *mixes, *cands, back)


def hop(value, axis, distance):
    size = lax.axis_size(axis)
    return lax.ppermute(value, axis, [(i, i ^ distance) for i in range(size)])


def after(value, *others):
    return lax.optimization_barrier((value, *others))[0]


def direct(own):
    n_cls = lax.axis_size("cls")
    return {1 << bit: hop(own, "cls", 1 << bit) for bit in range(1, n_cls.bit_length() - 1)}


def relayed(known, d, *others):
    n_cls = lax.axis_size("cls")
    for j in sorted(range(2, n_cls, 2), key=lambda j: bin(j).count("1")):
        if j not in known:
            bits = [bit for bit in range(1, n_cls.bit_length()) if j >> bit & 1]
            way = 1 << bits[d % len(bits)]
            known[j] = hop(after(known[j ^ way], *others), "cls", way)
    return known


def paired(known, each, last):
    n_cls = lax.axis_size("cls")
    for j in range(0, n_cls, 2):
        others = last if j == n_cls - 2 else each
        block = after(known[j], *others) if others else known[j]
        known[j + 1] = hop(block, "cls", 1)
    return [known[j] for j in range(n_cls)]


def gather_device(particles, references, owner_groups, class_order):
    n_cls, n_prt = lax.axis_size("cls"), lax.axis_size("prt")
    cls, prt = lax.axis_index("cls"), lax.axis_index("prt")
    count, cycles, width = particles.shape
    groups = references.shape[0]
    span = cycles // n_prt
    back = jnp.asarray(unselector(), jnp.bfloat16)
    table = jnp.asarray(rotation_table())
    picks = class_order[:, :, :CAND_OWN].reshape(count, OWN_TOP * CAND_OWN)
    meta = jnp.concatenate([owner_groups, picks], 1)
    cls, prt = (index.reshape(1).astype(jnp.int32) for index in (cls, prt))
    order = [d for d in range(n_prt) if d % 2 == 0] + [d for d in range(n_prt) if d % 2]
    outgoing = {}
    place = prt
    for first in range(0, n_prt, 2):
        distances = tuple(order[first : first + 2])
        made = arrange_particles(place, particles, meta, n_prt, distances)
        outgoing.update(zip(distances, made))
        place = after(prt, made[0])
    last = outgoing[order[-1]]
    arrived = {0: outgoing[0]}
    for d in order[1:]:
        block = after(outgoing[d], arrived[2]) if d > 2 else outgoing[d]
        arrived[d] = hop(block, "prt", d)
    known = {0: {0: arrived[0], **direct(arrived[0])}}
    for d in range(1, min(n_prt, 3)):
        own = after(arrived[d], last) if d == 2 else arrived[d]
        known[d] = {0: own, **direct(own)}
    place = after(prt, known[0][2], known[0][n_cls // 2])
    place = after(place, *[arrived[d] for d in range(1, min(n_prt, 3))])
    arranged, norms = arrange_references(references, place, n_prt)
    for d in range(3, n_prt):
        arrived[d] = after(arrived[d], arranged)
        known[d] = {0: arrived[d], **direct(arrived[d])}
    relayed(known[0], 0, arranged)
    for d in range(1, n_prt):
        relayed(known[d], d)
    scale = 2.0 / math.sqrt(cycles * width)
    coefs, cands, sent, blocks = [], [], [], []
    for d in range(n_prt):
        waits = [known[n_prt - 1][2]] if d == 1 else []
        first = [known[e][j] for e in range(1, n_prt) for j in (2, n_cls // 2)]
        blocks.append(paired(known[d], first if d < 2 else [], []))
        ready = after(arranged, *waits) if waits else arranged
        coef, cand = cross_coefficients(blocks[d], ready, norms, cls)
        coefs.append(coef)
        sent.append(hop(coef, "prt", d) if d else coef)
        cands.append(cand)
    score, stat = scores(sent, cands[0], table, scale)
    stats = lax.all_gather(stat.reshape(1, *stat.shape), "cls", axis=0, tiled=True)
    mix, log_norm = mixed_weights(cls, score, cands[0], stats, table, count)
    mixes = [hop(mix, "prt", d) if d else mix for d in range(n_prt)]
    class_sums, class_weights = sums(
        [block for piece in blocks for block in piece], mixes, cands, back, groups, span
    )
    own = log_norm[0]
    return class_sums, class_weights[0], own


def per_device(particles, references, owner_groups, class_order):
    n_cls, n_prt = lax.axis_size("cls"), lax.axis_size("prt")
    count, cycles, _ = particles.shape
    groups = references.shape[0]
    cap = max(2, 2 * count * OWN_TOP // n_cls)
    powers = n_cls & (n_cls - 1) == 0 and n_prt & (n_prt - 1) == 0
    fits = 4 * cycles == LANES * n_prt and n_cls * CAND_OWN <= LANES and groups % 16 == 0 and n_cls >= 4
    fits = fits and powers and n_cls * count == LANES
    plan = gather_device if cap >= count and fits else dispatch_device
    return plan(particles, references, owner_groups, class_order)


def solution(mesh):
    in_specs = (
        P(("cls", "prt"), None, None),
        P("cls", None, None),
        P(("cls", "prt"), None),
        P(("cls", "prt"), None, None),
    )
    out_specs = (P("cls", "prt", None), P("cls"), P(("cls", "prt")))
    return jax.shard_map(
        per_device, mesh=mesh, in_specs=in_specs, out_specs=out_specs, check_vma=False
    )
```

```python
import functools
import math

import jax
import jax.numpy as jnp
import numpy as np
from jax import lax
from jax.experimental import pallas as pl
from jax.experimental.pallas import tpu as pltpu
from jax.sharding import PartitionSpec as P

CYCLES = 128
HARM = 256
ROTS = 36
OWN_TOP = 4
CAND_OWN = 4


lowest = -1e30


def spectral_tables():
    harmonic = jnp.arange(HARM, dtype=jnp.float32)
    angles = 2.0 * math.pi * jnp.arange(ROTS, dtype=jnp.float32) / ROTS
    phase = harmonic[:, None] * angles[None, :]
    forward = jnp.concatenate([jnp.cos(phase), jnp.sin(phase)], 0)
    backward = jnp.concatenate([jnp.cos(phase), -jnp.sin(phase)], 0).T
    return (forward, backward)


def class_accumulate(lanes, mixed):
    l_re = lanes[..., :HARM]
    l_im = lanes[..., HARM:]
    y_re = mixed[..., :HARM]
    y_im = mixed[..., HARM:]
    s_re = jnp.einsum("lrm,lcm->crm", l_re, y_re, preferred_element_type=jnp.float32) - jnp.einsum(
        "lrm,lcm->crm", l_im, y_im, preferred_element_type=jnp.float32
    )
    s_im = jnp.einsum("lrm,lcm->crm", l_re, y_im, preferred_element_type=jnp.float32) + jnp.einsum(
        "lrm,lcm->crm", l_im, y_re, preferred_element_type=jnp.float32
    )
    return jnp.concatenate([s_re, s_im], -1)


def dispatch_device(particles, references, owner_groups, class_order):
    n_cls = lax.axis_size("cls")
    count = particles.shape[0]
    groups = references.shape[0]
    cap = max(2, 2 * count * OWN_TOP // n_cls)
    slots = n_cls * cap
    width = 2 * HARM
    flat_owner = owner_groups.reshape(-1)
    owner_hot = (flat_owner[:, None] == jnp.arange(n_cls, dtype=jnp.int32)[None, :]).astype(
        jnp.int32
    )
    before = jnp.cumsum(owner_hot, axis=0) - owner_hot
    rank = jnp.sum(before * owner_hot, axis=1)
    slot_of = flat_owner * cap + rank
    match = slot_of[None, :] == jnp.arange(slots, dtype=jnp.int32)[:, None]
    member = jnp.any(match.reshape(slots, count, OWN_TOP), axis=2)
    filled = jnp.any(member, axis=1)
    dispatch = member.astype(jnp.bfloat16)
    outgoing = jnp.dot(
        dispatch, particles.reshape(count, CYCLES * width), preferred_element_type=jnp.float32
    )
    outgoing = outgoing.astype(jnp.bfloat16).reshape(n_cls, cap, CYCLES, width)
    match_int = match.astype(jnp.int32)
    picks = class_order[:, :, :CAND_OWN].reshape(count * OWN_TOP, CAND_OWN)
    slot_cand = jnp.where(filled[:, None], jnp.dot(match_int, picks), -1)
    owner_rows = jnp.repeat(jnp.arange(count, dtype=jnp.int32), OWN_TOP)
    slot_pid = jnp.where(filled, jnp.dot(match_int, owner_rows), -1)
    labels_out = jnp.concatenate([slot_cand, slot_pid[:, None]], 1).reshape(
        n_cls, cap, CAND_OWN + 1
    )
    arrived, labels = (
        lax.all_to_all(outgoing, "cls", split_axis=0, concat_axis=0, tiled=True),
        lax.all_to_all(labels_out, "cls", split_axis=0, concat_axis=0, tiled=True),
    )
    lanes = arrived.reshape(slots, CYCLES, width)
    labels = labels.reshape(slots, CAND_OWN + 1)
    forward, backward = spectral_tables()
    scale = 2.0 / math.sqrt(CYCLES * width)
    norms = jnp.sum(jnp.square(references.astype(jnp.float32)), axis=(1, 2))
    l_re = lanes[..., :HARM]
    l_im = lanes[..., HARM:]
    r_re = references[..., :HARM]
    r_im = references[..., HARM:]
    x_re = jnp.einsum("lrm,crm->lcm", l_re, r_re, preferred_element_type=jnp.float32) + jnp.einsum(
        "lrm,crm->lcm", l_im, r_im, preferred_element_type=jnp.float32
    )
    x_im = jnp.einsum("lrm,crm->lcm", l_im, r_re, preferred_element_type=jnp.float32) - jnp.einsum(
        "lrm,crm->lcm", l_re, r_im, preferred_element_type=jnp.float32
    )
    cross = jnp.concatenate([x_re, x_im], -1)
    corr = jnp.dot(
        cross.reshape(slots * groups, width), forward, precision=lax.Precision.HIGHEST
    ).reshape(slots, groups, ROTS)
    score = (corr - 0.5 * norms[None, :, None]) * scale
    candidate = jnp.any(
        labels[:, :CAND_OWN, None] == jnp.arange(groups, dtype=jnp.int32)[None, None, :], axis=1
    )
    part_max = jnp.max(jnp.where(candidate[:, :, None], score, lowest), axis=(1, 2))
    part_sum = jnp.sum(
        jnp.where(candidate[:, :, None], jnp.exp(score - part_max[:, None, None]), 0.0), axis=(1, 2)
    )
    sender_ids = labels[:, CAND_OWN].astype(jnp.float32)
    table_max, table_sum, table_ids = (
        lax.all_gather(part_max.reshape(1, n_cls, cap), "cls", axis=0, tiled=True),
        lax.all_gather(part_sum.reshape(1, n_cls, cap), "cls", axis=0, tiled=True),
        lax.all_gather(sender_ids.reshape(1, n_cls, cap), "cls", axis=0, tiled=True),
    )
    local_ids = jnp.arange(count, dtype=jnp.float32)
    hit = table_ids[..., None] == local_ids
    top = jnp.max(jnp.where(hit, table_max[..., None], lowest), axis=(0, 2))
    total = jnp.sum(
        jnp.where(
            hit, table_sum[..., None] * jnp.exp(table_max[..., None] - top[None, :, None, :]), 0.0
        ),
        axis=(0, 2),
    )
    table_norm = top + jnp.log(total)
    slot_ids = labels[:, CAND_OWN].reshape(n_cls, cap)
    slot_norm = jnp.sum(
        jnp.where(
            slot_ids[..., None] == jnp.arange(count, dtype=jnp.int32), table_norm[:, None, :], 0.0
        ),
        axis=2,
    ).reshape(slots)
    own_norm = lax.dynamic_index_in_dim(table_norm, lax.axis_index("cls"), 0, keepdims=False)
    weight = jnp.where(candidate[:, :, None], jnp.exp(score - slot_norm[:, None, None]), 0.0)
    mixed = (
        jnp.dot(weight.reshape(slots * groups, ROTS), backward, precision=lax.Precision.HIGHEST)
        .astype(jnp.bfloat16)
        .reshape(slots, groups, width)
    )
    class_weights = lax.psum(jnp.sum(weight, axis=(0, 2)), "prt")
    partial_sums = class_accumulate(lanes, mixed)
    class_sums = lax.psum_scatter(partial_sums, "prt", scatter_dimension=1, tiled=True)
    return (class_sums, class_weights, own_norm)


LANES = 128


def harmonic_plan():
    half = ROTS // 2
    turns = HARM // ROTS
    tail = HARM - turns * ROTS
    chunk_of = np.zeros(HARM, np.int32)
    side_of = np.zeros(HARM, np.int32)
    for m in range(HARM):
        turn, rest = divmod(m, ROTS)
        if turn == turns:
            chunk_of[m] = half * turns + rest // 2
            side_of[m] = rest % 2
        elif rest < half:
            chunk_of[m] = rest * turns + turn
        else:
            chunk_of[m] = ((ROTS - rest) % half) * turns + turn
            side_of[m] = 1
    return half, turns, tail, chunk_of, side_of


HALF, TURNS, TAIL, CHUNK_OF, SIDE_OF = harmonic_plan()
BODY = HALF * TURNS
CHUNKS = BODY + TAIL // 2
EXTRA = TAIL // 2 + 1
COEF = 2 * HALF * CAND_OWN
RANGE = 6
RANGES = ((BODY, CHUNKS + 1),) + tuple(
    (first * TURNS, (first + RANGE) * TURNS) for first in range(0, HALF, RANGE)
)


def selector():
    return (np.arange(CHUNKS)[:, None] == CHUNK_OF[None, :]).astype(np.float32)


def unselector():
    sel = selector()
    return np.concatenate([sel * (SIDE_OF == 0), sel * (SIDE_OF == 1)], 0)


def rotation_table():
    table = np.zeros((HALF, 2, CAND_OWN, ROTS, CAND_OWN))
    angle = 2.0 * np.pi * np.arange(ROTS) / ROTS
    for g in range(HALF):
        first = np.cos(g * angle)
        second = np.cos(HALF * angle) if g == 0 else np.sin(g * angle)
        for q in range(CAND_OWN):
            table[g, 0, q, :, q] = first
            table[g, 1, q, :, q] = second
    return table.reshape(COEF, ROTS * CAND_OWN).astype(np.float32)


def nt_dot(a, b):
    return lax.dot_general(a, b, (((1,), (1,)), ((), ())), preferred_element_type=jnp.float32)


def selector_masks():
    m = lax.broadcasted_iota(jnp.int32, (1, HARM), 1)
    turn = jnp.zeros((1, HARM), jnp.int32)
    for t in range(1, TURNS + 1):
        turn += jnp.where(m >= t * ROTS, 1, 0)
    rest = m - ROTS * turn
    back = jnp.where(rest == HALF, 0, ROTS - rest)
    chunk = jnp.where(rest < HALF, rest, back) * TURNS + turn
    side = jnp.where(rest < HALF, 0, 1)
    chunk = jnp.where(turn == TURNS, BODY + rest // 2, chunk)
    side = jnp.where(turn == TURNS, rest % 2, side)
    rows = lax.broadcasted_iota(jnp.int32, (CHUNKS, HARM), 0)
    sel = jnp.where(rows == chunk, 1.0, 0.0).astype(jnp.bfloat16)
    sides = lax.broadcasted_iota(jnp.int32, (2, HARM), 0)
    masks = jnp.where(sides == side, 1.0, 0.0).astype(jnp.bfloat16)
    return sel, masks


def masked_stack(piece, masks):
    parts = []
    for s in range(2):
        for b in range(2):
            parts.append(piece[:, s * HARM : (s + 1) * HARM] * masks[b : b + 1])
    return jnp.concatenate(parts, 0)


def repeat(number, step, body, carry):
    def several(i, carry):
        for u in range(step):
            carry = body(i * step + u, carry)
        return carry

    return lax.fori_loop(0, number // step, several, carry)


def particle_body(at_ref, x_ref, meta_ref, *refs, distances, n_prt):
    outs, scr = refs[:-1], refs[-1]
    count, cycles, _ = x_ref.shape
    number = len(outs)
    span = cycles // n_prt
    sel, masks = selector_masks()

    def one(n, carry):
        parts = []
        for d in distances:
            start = pl.multiple_of((at_ref[0] ^ d) * span, span)
            parts.append(masked_stack(x_ref[n, pl.ds(start, span), :], masks))
        w = jnp.concatenate(parts, 0)
        y = nt_dot(sel, w)
        for p in range(number):
            scr[p, pl.ds(pl.multiple_of(n * CHUNKS, CHUNKS), CHUNKS), :] = y[
                :, p * LANES : (p + 1) * LANES
            ]
        return carry

    repeat(count, 4, one, 0)

    def two(c, carry):
        for p in range(number):
            outs[p][c] = scr[p, pl.ds(c, count, stride=CHUNKS), :].astype(jnp.bfloat16)
        return carry

    repeat(CHUNKS, 8, two, 0)
    lane = lax.broadcasted_iota(jnp.int32, (count, LANES), 1)
    label = jnp.full((count, LANES), -1, jnp.int32)
    for t in range(OWN_TOP):
        mine = (lane // CAND_OWN) == meta_ref[:, t : t + 1]
        for q in range(CAND_OWN):
            at = OWN_TOP + t * CAND_OWN + q
            label = jnp.where(
                mine & (lane % CAND_OWN == q), meta_ref[:, at : at + 1], label
            )
    label = label.astype(jnp.float32).astype(jnp.bfloat16)
    for p in range(number):
        outs[p][CHUNKS] = label


def arrange_particles(prt, particles, meta, n_prt, distances):
    count = particles.shape[0]
    number = len(distances)
    size = particles.size * number // n_prt
    return pl.pallas_call(
        functools.partial(particle_body, distances=distances, n_prt=n_prt),
        in_specs=[pl.BlockSpec(memory_space=pltpu.SMEM)] + [pl.BlockSpec(memory_space=pltpu.VMEM)] * 2,
        out_shape=[jax.ShapeDtypeStruct((CHUNKS + 1, count, LANES), jnp.bfloat16)] * number,
        scratch_shapes=[pltpu.VMEM((number, count * CHUNKS, LANES), jnp.float32)],
        compiler_params=pltpu.CompilerParams(vmem_limit_bytes=32 << 20),
        cost_estimate=pl.CostEstimate(
            flops=size * 2 * CHUNKS, bytes_accessed=size * 4, transcendentals=0
        ),
        name="arrange_particles",
    )(prt, particles, meta)


def reference_body(at_ref, x_ref, out_ref, norm_ref, scr):
    rows = x_ref.shape[0]
    sel, masks = selector_masks()
    step = 4

    def one(n, carry):
        w = jnp.concatenate([masked_stack(x_ref[n * step + i], masks) for i in range(step)], 0)
        y = nt_dot(sel, w)
        for i in range(step):
            scr[pl.ds(pl.multiple_of((n * step + i) * CHUNKS, CHUNKS), CHUNKS), :] = y[
                :, i * LANES : (i + 1) * LANES
            ]
        return carry

    repeat(rows // step, 2, one, 0)

    def two(c, carry):
        value = scr[pl.ds(c, rows, stride=CHUNKS), :]
        out_ref[c] = value.astype(jnp.bfloat16)
        return carry + value * value

    norm_ref[...] = repeat(CHUNKS, 8, two, jnp.zeros((rows, LANES), jnp.float32))


def arrange_references(references, prt, n_prt):
    groups, cycles, width = references.shape
    span = cycles // n_prt
    block = 16
    return pl.pallas_call(
        reference_body,
        grid_spec=pltpu.PrefetchScalarGridSpec(
            num_scalar_prefetch=1,
            grid=(groups // block,),
            in_specs=[
                pl.BlockSpec((block, span, width), lambda i, at: (i, at[0], 0)),
            ],
            out_specs=[
                pl.BlockSpec((CHUNKS, block, LANES), lambda i, at: (0, i, 0)),
                pl.BlockSpec((block, LANES), lambda i, at: (i, 0)),
            ],
            scratch_shapes=[pltpu.VMEM((block * CHUNKS, LANES), jnp.float32)],
        ),
        out_shape=[
            jax.ShapeDtypeStruct((CHUNKS, groups, LANES), jnp.bfloat16),
            jax.ShapeDtypeStruct((groups, LANES), jnp.float32),
        ],
        compiler_params=pltpu.CompilerParams(vmem_limit_bytes=60 << 20),
        cost_estimate=pl.CostEstimate(
            flops=groups * span * width * 2 * CHUNKS,
            bytes_accessed=groups * span * width * 4,
            transcendentals=0,
        ),
        name="arrange_references",
    )(prt, references)


def lane_signs():
    lane = lax.broadcasted_iota(jnp.int32, (1, LANES), 1)
    quarter = LANES // 4
    imag = lane >= 2 * quarter
    odd = (lane // quarter) % 2 == 1
    return imag, odd


def lanes_of(held, first, number):
    parts = []
    for i in range(number):
        parts.append(jnp.concatenate([held[j, first + i] for j in range(held.shape[0])], 0))
    return jnp.concatenate(parts, 1) if number > 1 else parts[0]


def fetch(blocks, held, sems):
    copies = []
    for r, (first, last) in enumerate(RANGES):
        chunks = pl.ds(first, last - first)
        copies.append(
            [
                pltpu.make_async_copy(block.at[chunks], held.at[j, chunks], sems.at[r, j])
                for j, block in enumerate(blocks)
            ]
        )
    for group in copies:
        for copy in group:
            copy.start()
    return copies


def hot_masks(cand, groups):
    rows = lax.broadcasted_iota(jnp.int32, (groups, cand.shape[1]), 0).astype(jnp.float32)
    return [rows == cand[q : q + 1] for q in range(CAND_OWN)]


def residue_weights(q_ref, g, special):
    imag, odd = lane_signs()
    sign = jnp.where(imag == odd, -1.0, 1.0)
    first, second = [], []
    for i in range(TURNS):
        q = q_ref[g * TURNS + i].astype(jnp.float32)
        turned = pltpu.roll(q, LANES // 2, 1) * sign
        if special:
            first.append(jnp.where((g == 0) & odd, 0.0, q))
            second.append(jnp.where(g == 0, jnp.where(odd, q, 0.0), turned))
        else:
            first.append(q)
            second.append(turned)
    return jnp.concatenate(
        [jnp.concatenate(first, 1), jnp.concatenate(second, 1)], 0
    ).astype(jnp.bfloat16)


def chosen_rows(acc, cand):
    groups = acc.shape[0] // 2
    hot = hot_masks(cand, groups)
    rows = []
    for ab in range(2):
        part = acc[ab * groups : (ab + 1) * groups, :]
        for q in range(CAND_OWN):
            rows.append(jnp.sum(jnp.where(hot[q], part, 0.0), axis=0, keepdims=True))
    return jnp.concatenate(rows, 0)


def cross_body(at_ref, *refs):
    blocks = refs[:-7]
    q_ref, norm_ref, coef_ref, cand_ref, held, acc, sems = refs[-7:]
    groups = q_ref.shape[1]
    imag, odd = lane_signs()
    copies = fetch(blocks, held, sems)
    for copy in copies[0]:
        copy.wait()
    label = lanes_of(held, CHUNKS, 1).astype(jnp.float32).T
    row = lax.broadcasted_iota(jnp.int32, label.shape, 0)
    base = at_ref[0] * CAND_OWN
    for q in range(CAND_OWN):
        cand_ref[q : q + 1, :] = jnp.sum(
            jnp.where(row == base + q, label, 0.0), axis=0, keepdims=True
        )
    cand_ref[CAND_OWN:, :] = jnp.full(
        (cand_ref.shape[0] - CAND_OWN, cand_ref.shape[1]), -1.0, jnp.float32
    )

    def tail(i):
        q = q_ref[BODY + i // 2].astype(jnp.float32)
        keep = odd if i % 2 else ~odd
        a = jnp.where(keep, q, 0.0)
        turned = pltpu.roll(q, LANES // 2, 1) * jnp.where(imag, 1.0, -1.0)
        b = jnp.where(keep, turned, 0.0)
        if i == 0:
            b = jnp.zeros_like(b)
        w = jnp.concatenate([a, b], 0).astype(jnp.bfloat16)
        acc[...] += nt_dot(w, lanes_of(held, BODY + i // 2, 1))
        if i == 0:
            acc[:groups, :] -= 0.5 * jnp.sum(norm_ref[...], axis=1, keepdims=True)

    for r in range(1, len(RANGES)):
        for copy in copies[r]:
            copy.wait()

        def one(u, carry):
            g = (r - 1) * RANGE + u
            acc[...] = nt_dot(residue_weights(q_ref, g, r == 1), lanes_of(held, g * TURNS, TURNS))
            if r == 1:
                for i in range(TAIL):
                    pl.when(g == i)(functools.partial(tail, i))
            block = 2 * CAND_OWN
            coef_ref[pl.ds(pl.multiple_of(g * block, block), block), :] = chosen_rows(
                acc[...], cand_ref[...]
            )
            return carry

        lax.fori_loop(0, RANGE, one, 0)


def cross_coefficients(blocks, arranged, norms, cls):
    number = len(blocks)
    count = blocks[0].shape[1]
    groups = arranged.shape[1]
    total = number * count
    size = blocks[0].size * number
    block = 2 * CAND_OWN
    return pl.pallas_call(
        cross_body,
        in_specs=[pl.BlockSpec(memory_space=pltpu.SMEM)]
        + [pl.BlockSpec(memory_space=pl.ANY)] * number
        + [pl.BlockSpec(memory_space=pltpu.VMEM)] * 2,
        out_shape=[
            jax.ShapeDtypeStruct((COEF, total), jnp.float32),
            jax.ShapeDtypeStruct((block, total), jnp.float32),
        ],
        scratch_shapes=[
            pltpu.VMEM((number, *blocks[0].shape), jnp.bfloat16),
            pltpu.VMEM((2 * groups, total), jnp.float32),
            pltpu.SemaphoreType.DMA((len(RANGES), number)),
        ],
        compiler_params=pltpu.CompilerParams(vmem_limit_bytes=60 << 20),
        cost_estimate=pl.CostEstimate(
            flops=4 * size * groups, bytes_accessed=2 * size, transcendentals=0
        ),
        name="cross_coefficients",
    )(cls, *blocks, arranged, norms)


def score_body(*refs, scale):
    *coefs, cand_ref, table_ref, score_ref, stat_ref = refs
    corr = lax.dot_general(
        table_ref[...],
        functools.reduce(jnp.add, [ref[...] for ref in coefs]),
        (((0,), (0,)), ((), ())),
        precision=lax.Precision.HIGHEST,
        preferred_element_type=jnp.float32,
    )
    score = jnp.where(cand_ref[0:1, :] >= 0.0, corr * scale, lowest)
    top = jnp.max(score, axis=0, keepdims=True)
    total = jnp.sum(jnp.exp(score - top), axis=0, keepdims=True)
    score_ref[...] = score
    stat_ref[0:1, :] = top
    stat_ref[1:2, :] = jnp.where(cand_ref[0:1, :] >= 0.0, total, 0.0)


def scores(coefs, cand, table, scale):
    total = cand.shape[1]
    return pl.pallas_call(
        functools.partial(score_body, scale=scale),
        out_shape=[
            jax.ShapeDtypeStruct((ROTS * CAND_OWN, total), jnp.float32),
            jax.ShapeDtypeStruct((2, total), jnp.float32),
        ],
        name="scores",
    )(*coefs, cand, table)


def swap_blocks(x, distance, width):
    lane = lax.broadcasted_iota(jnp.int32, x.shape, 1)
    bit = 1
    while bit <= distance:
        if distance & bit:
            shift = bit * width
            down = pltpu.roll(x, shift, 1)
            up = pltpu.roll(x, x.shape[1] - shift, 1)
            x = jnp.where((lane // shift) % 2 == 1, down, up)
        bit *= 2
    return x


def weights_body(at_ref, score_ref, cand_ref, stat_ref, table_ref, mix_ref, norm_ref):
    n_cls, _, total = stat_ref.shape
    width = total // n_cls
    tops, parts = [], []
    for e in range(n_cls):
        table = stat_ref[at_ref[0] ^ e]
        table = swap_blocks(jnp.concatenate([table] * 4, 0), e, width)
        tops.append(table[0:1])
        parts.append(table[1:2])
    top = functools.reduce(jnp.maximum, tops)
    summed = jnp.zeros_like(top)
    for other, part in zip(tops, parts):
        summed += part * jnp.exp(other - top)
    log_norm = top + jnp.log(summed)
    norm_ref[...] = log_norm[:, : norm_ref.shape[1]]
    weight = jnp.where(cand_ref[0:1, :] >= 0.0, jnp.exp(score_ref[...] - log_norm), 0.0)
    mix_ref[...] = lax.dot_general(
        table_ref[...],
        weight,
        (((1,), (0,)), ((), ())),
        precision=lax.Precision.HIGHEST,
        preferred_element_type=jnp.float32,
    )


def mixed_weights(cls, score, cand, stats, table, count):
    total = score.shape[1]
    return pl.pallas_call(
        weights_body,
        in_specs=[pl.BlockSpec(memory_space=pltpu.SMEM)] + [pl.BlockSpec(memory_space=pltpu.VMEM)] * 4,
        out_shape=[
            jax.ShapeDtypeStruct((COEF, total), jnp.float32),
            jax.ShapeDtypeStruct((1, count), jnp.float32),
        ],
        name="mixed_weights",
    )(cls, score, cand, stats, table)


def sums_body(*refs, number, pieces):
    blocks = refs[:number]
    refs = refs[number:]
    mixes, cands = refs[:pieces], refs[pieces : 2 * pieces]
    back_ref, out_ref, weight_ref, mix, cand, planes, held, sems = refs[2 * pieces :]
    step = pl.program_id(0)
    groups = weight_ref.shape[1]
    total = mix.shape[1]
    imag, odd = lane_signs()

    @pl.when(step == 0)
    def _():
        copies = fetch(blocks, held, sems)
        mixed = jnp.concatenate([ref[...] for ref in mixes], 1)
        chosen = jnp.concatenate([ref[...] for ref in cands], 1)
        hot = hot_masks(chosen, groups)
        summed = jnp.zeros((groups, total), jnp.float32)
        for q in range(CAND_OWN):
            summed += jnp.where(hot[q], mixed[q : q + 1], 0.0)
        weight_ref[...] = lax.dot_general(
            jnp.ones((1, total), jnp.float32),
            summed,
            (((1,), (1,)), ((), ())),
            precision=lax.Precision.HIGHEST,
            preferred_element_type=jnp.float32,
        )
        mix[...] = mixed
        cand[...] = chosen
        sign = jnp.where(imag == odd, 1.0, -1.0)
        for copy in copies[0]:
            copy.wait()

        def tail(t, weights):
            made = jnp.dot(
                weights, lanes_of(held, BODY + t // 2, 1), preferred_element_type=jnp.float32
            )
            g1, g2 = made[:groups], made[groups:]
            value = g1
            if t > 0:
                value = g1 + jnp.where(imag, -1.0, 1.0) * pltpu.roll(g2, LANES // 2, 1)
            rows = pl.ds((BODY + t // 2) * groups, groups)
            if t % 2:
                value = jnp.where(odd, value, planes[rows, :])
            planes[rows, :] = value

        for r in range(1, len(RANGES)):
            for copy in copies[r]:
                copy.wait()

            def one(u, carry):
                g = (r - 1) * RANGE + u
                hot = hot_masks(cand[...], groups)
                block = 2 * CAND_OWN
                mine = mix[pl.ds(pl.multiple_of(g * block, block), block), :]
                halves = []
                for ab in range(2):
                    dense = jnp.zeros((groups, total), jnp.float32)
                    for q in range(CAND_OWN):
                        at = ab * CAND_OWN + q
                        dense = jnp.where(hot[q], mine[at : at + 1], dense)
                    halves.append(dense)
                weights = jnp.concatenate(halves, 0).astype(jnp.bfloat16)
                made = jnp.dot(
                    weights, lanes_of(held, g * TURNS, TURNS), preferred_element_type=jnp.float32
                )
                for t in range(TURNS):
                    g1 = made[:groups, t * LANES : (t + 1) * LANES]
                    g2 = made[groups:, t * LANES : (t + 1) * LANES]
                    value = g1 + sign * pltpu.roll(g2, LANES // 2, 1)
                    if r == 1:
                        value = jnp.where(g == 0, jnp.where(odd, g2, g1), value)
                    start = pl.multiple_of((g * TURNS + t) * groups, groups)
                    planes[pl.ds(start, groups), :] = value
                if r == 1:
                    for t in range(TAIL):
                        pl.when(g == t)(functools.partial(tail, t, weights))
                return carry

            lax.fori_loop(0, RANGE, one, 0)

    @pl.when(step > 0)
    def _():
        block, span, _ = out_ref.shape
        first = (step - 1) * block
        back = back_ref[...]
        values = []
        for c in range(block):
            turned = planes[pl.ds(first + c, CHUNKS, stride=groups), :].T
            for s in range(2):
                at = 2 * s * span
                values.append(
                    jnp.concatenate([turned[at : at + span], turned[at + span : at + 2 * span]], 1)
                )
        value = jnp.concatenate(values, 0)
        high = value.astype(jnp.bfloat16)
        low = (value - high.astype(jnp.float32)).astype(jnp.bfloat16)
        both = jnp.dot(
            jnp.concatenate([high, low], 0), back, preferred_element_type=jnp.float32
        )
        rows = value.shape[0]
        placed = both[:rows] + both[rows:]
        for c in range(block):
            for s in range(2):
                at = (2 * c + s) * span
                out_ref[c, :, s * HARM : (s + 1) * HARM] = placed[at : at + span]


def sums(blocks, mixes, cands, back, groups, span):
    number = len(blocks)
    count = blocks[0].shape[1]
    total = number * count
    size = blocks[0].size * number
    block = 8
    whole = lambda i: (0, 0)
    return pl.pallas_call(
        functools.partial(sums_body, number=number, pieces=len(mixes)),
        grid=(1 + groups // block,),
        in_specs=[
            *[pl.BlockSpec(memory_space=pl.ANY)] * number,
            *[pl.BlockSpec(array.shape, whole) for array in (*mixes, *cands, back)],
        ],
        out_specs=[
            pl.BlockSpec((block, span, 2 * HARM), lambda i: (jnp.maximum(i - 1, 0), 0, 0)),
            pl.BlockSpec((1, groups), whole),
        ],
        out_shape=[
            jax.ShapeDtypeStruct((groups, span, 2 * HARM), jnp.float32),
            jax.ShapeDtypeStruct((1, groups), jnp.float32),
        ],
        scratch_shapes=[
            pltpu.VMEM((COEF, total), jnp.float32),
            pltpu.VMEM((2 * CAND_OWN, total), jnp.float32),
            pltpu.VMEM((CHUNKS * groups, LANES), jnp.float32),
            pltpu.VMEM((number, *blocks[0].shape), jnp.bfloat16),
            pltpu.SemaphoreType.DMA((len(RANGES), number)),
        ],
        compiler_params=pltpu.CompilerParams(vmem_limit_bytes=60 << 20),
        cost_estimate=pl.CostEstimate(
            flops=4 * size * groups,
            bytes_accessed=2 * size + 8 * groups * span * HARM,
            transcendentals=0,
        ),
        name="sums",
    )(*blocks, *mixes, *cands, back)


def hop(value, axis, distance):
    size = lax.axis_size(axis)
    return lax.ppermute(value, axis, [(i, i ^ distance) for i in range(size)])


def after(value, *others):
    return lax.optimization_barrier((value, *others))[0]


def direct(own):
    n_cls = lax.axis_size("cls")
    return {1 << bit: hop(own, "cls", 1 << bit) for bit in range(1, n_cls.bit_length() - 1)}


def relayed(known, d, *others):
    n_cls = lax.axis_size("cls")
    for j in sorted(range(2, n_cls, 2), key=lambda j: bin(j).count("1")):
        if j not in known:
            bits = [bit for bit in range(1, n_cls.bit_length()) if j >> bit & 1]
            way = 1 << bits[d % len(bits)]
            known[j] = hop(after(known[j ^ way], *others), "cls", way)
    return known


def paired(known, each, last):
    n_cls = lax.axis_size("cls")
    for j in range(0, n_cls, 2):
        others = last if j == n_cls - 2 else each
        block = after(known[j], *others) if others else known[j]
        known[j + 1] = hop(block, "cls", 1)
    return [known[j] for j in range(n_cls)]


def gather_device(particles, references, owner_groups, class_order):
    n_cls, n_prt = lax.axis_size("cls"), lax.axis_size("prt")
    cls, prt = lax.axis_index("cls"), lax.axis_index("prt")
    count, cycles, width = particles.shape
    groups = references.shape[0]
    span = cycles // n_prt
    back = jnp.asarray(unselector(), jnp.bfloat16)
    table = jnp.asarray(rotation_table())
    picks = class_order[:, :, :CAND_OWN].reshape(count, OWN_TOP * CAND_OWN)
    meta = jnp.concatenate([owner_groups, picks], 1)
    cls, prt = (index.reshape(1).astype(jnp.int32) for index in (cls, prt))
    outgoing = []
    for first in range(0, n_prt, 2):
        distances = tuple(range(first, min(first + 2, n_prt)))
        place = after(prt, outgoing[0]) if outgoing else prt
        outgoing += arrange_particles(
            place, particles, meta, n_prt, distances
        )
    arrived = [outgoing[0]]
    known = [{0: arrived[0], **direct(arrived[0])}]
    for d in range(1, min(n_prt, 3)):
        arrived.append(hop(outgoing[d], "prt", d))
    early = after(arrived[1], outgoing[-1])
    known.append({0: early, **direct(early)})
    relayed(known[0], 0, outgoing[-1])
    place = after(prt, *arrived[1:2], *[known[0][1 << b] for b in range(1, n_cls.bit_length() - 1)])
    arranged, norms = arrange_references(references, place, n_prt)
    for d in range(2, n_prt):
        if d > 2:
            arrived.append(hop(after(outgoing[d], arrived[d - 1], arranged), "prt", d))
        own = after(arrived[d], arranged) if d == 2 else arrived[d]
        known.append({0: own, **direct(own)})
    for d in range(1, n_prt, 2):
        relayed(known[d], d)
    scale = 2.0 / math.sqrt(cycles * width)
    coefs, cands, sent, blocks = [], [], [], []
    for d in range(n_prt):
        waits = []
        if n_prt > 3:
            waits = [[known[1][2]], [arrived[3], known[2][n_cls // 2]], [known[3][2]], []][min(d, 3)]
        if d and d % 2 == 0:
            relayed(known[d], d, coefs[0])
        each = [arranged, known[1][n_cls // 2]] if d == 0 else coefs[:1] if d < 3 else []
        blocks.append(paired(known[d], each, coefs[-1:]))
        ready = after(arranged, *waits) if waits else arranged
        coef, cand = cross_coefficients(blocks[d], ready, norms, cls)
        coefs.append(coef)
        sent.append(hop(coef, "prt", d) if d else coef)
        cands.append(cand)
    score, stat = scores(sent, cands[0], table, scale)
    stats = lax.all_gather(stat.reshape(1, *stat.shape), "cls", axis=0, tiled=True)
    mix, log_norm = mixed_weights(cls, score, cands[0], stats, table, count)
    mixes = [hop(mix, "prt", d) if d else mix for d in range(n_prt)]
    class_sums, class_weights = sums(
        [block for piece in blocks for block in piece], mixes, cands, back, groups, span
    )
    own = log_norm[0]
    return class_sums, class_weights[0], own


def per_device(particles, references, owner_groups, class_order):
    n_cls, n_prt = lax.axis_size("cls"), lax.axis_size("prt")
    count, cycles, _ = particles.shape
    groups = references.shape[0]
    cap = max(2, 2 * count * OWN_TOP // n_cls)
    powers = n_cls & (n_cls - 1) == 0 and n_prt & (n_prt - 1) == 0
    fits = 4 * cycles == LANES * n_prt and n_cls * CAND_OWN <= LANES and groups % 16 == 0 and n_cls >= 4
    fits = fits and powers and n_cls * count == LANES
    plan = gather_device if cap >= count and fits else dispatch_device
    return plan(particles, references, owner_groups, class_order)


def solution(mesh):
    in_specs = (
        P(("cls", "prt"), None, None),
        P("cls", None, None),
        P(("cls", "prt"), None),
        P(("cls", "prt"), None, None),
    )
    out_specs = (P("cls", "prt", None), P("cls"), P(("cls", "prt")))
    return jax.shard_map(
        per_device, mesh=mesh, in_specs=in_specs, out_specs=out_specs, check_vma=False
    )
```

```python
import functools
import math

import jax
import jax.numpy as jnp
import numpy as np
from jax import lax
from jax.experimental import pallas as pl
from jax.experimental.pallas import tpu as pltpu
from jax.sharding import PartitionSpec as P

CYCLES = 128
HARM = 256
ROTS = 36
OWN_TOP = 4
CAND_OWN = 4


lowest = -1e30


def spectral_tables():
    harmonic = jnp.arange(HARM, dtype=jnp.float32)
    angles = 2.0 * math.pi * jnp.arange(ROTS, dtype=jnp.float32) / ROTS
    phase = harmonic[:, None] * angles[None, :]
    forward = jnp.concatenate([jnp.cos(phase), jnp.sin(phase)], 0)
    backward = jnp.concatenate([jnp.cos(phase), -jnp.sin(phase)], 0).T
    return (forward, backward)


def class_accumulate(lanes, mixed):
    l_re = lanes[..., :HARM]
    l_im = lanes[..., HARM:]
    y_re = mixed[..., :HARM]
    y_im = mixed[..., HARM:]
    s_re = jnp.einsum("lrm,lcm->crm", l_re, y_re, preferred_element_type=jnp.float32) - jnp.einsum(
        "lrm,lcm->crm", l_im, y_im, preferred_element_type=jnp.float32
    )
    s_im = jnp.einsum("lrm,lcm->crm", l_re, y_im, preferred_element_type=jnp.float32) + jnp.einsum(
        "lrm,lcm->crm", l_im, y_re, preferred_element_type=jnp.float32
    )
    return jnp.concatenate([s_re, s_im], -1)


def dispatch_device(particles, references, owner_groups, class_order):
    n_cls = lax.axis_size("cls")
    count = particles.shape[0]
    groups = references.shape[0]
    cap = max(2, 2 * count * OWN_TOP // n_cls)
    slots = n_cls * cap
    width = 2 * HARM
    flat_owner = owner_groups.reshape(-1)
    owner_hot = (flat_owner[:, None] == jnp.arange(n_cls, dtype=jnp.int32)[None, :]).astype(
        jnp.int32
    )
    before = jnp.cumsum(owner_hot, axis=0) - owner_hot
    rank = jnp.sum(before * owner_hot, axis=1)
    slot_of = flat_owner * cap + rank
    match = slot_of[None, :] == jnp.arange(slots, dtype=jnp.int32)[:, None]
    member = jnp.any(match.reshape(slots, count, OWN_TOP), axis=2)
    filled = jnp.any(member, axis=1)
    dispatch = member.astype(jnp.bfloat16)
    outgoing = jnp.dot(
        dispatch, particles.reshape(count, CYCLES * width), preferred_element_type=jnp.float32
    )
    outgoing = outgoing.astype(jnp.bfloat16).reshape(n_cls, cap, CYCLES, width)
    match_int = match.astype(jnp.int32)
    picks = class_order[:, :, :CAND_OWN].reshape(count * OWN_TOP, CAND_OWN)
    slot_cand = jnp.where(filled[:, None], jnp.dot(match_int, picks), -1)
    owner_rows = jnp.repeat(jnp.arange(count, dtype=jnp.int32), OWN_TOP)
    slot_pid = jnp.where(filled, jnp.dot(match_int, owner_rows), -1)
    labels_out = jnp.concatenate([slot_cand, slot_pid[:, None]], 1).reshape(
        n_cls, cap, CAND_OWN + 1
    )
    arrived, labels = (
        lax.all_to_all(outgoing, "cls", split_axis=0, concat_axis=0, tiled=True),
        lax.all_to_all(labels_out, "cls", split_axis=0, concat_axis=0, tiled=True),
    )
    lanes = arrived.reshape(slots, CYCLES, width)
    labels = labels.reshape(slots, CAND_OWN + 1)
    forward, backward = spectral_tables()
    scale = 2.0 / math.sqrt(CYCLES * width)
    norms = jnp.sum(jnp.square(references.astype(jnp.float32)), axis=(1, 2))
    l_re = lanes[..., :HARM]
    l_im = lanes[..., HARM:]
    r_re = references[..., :HARM]
    r_im = references[..., HARM:]
    x_re = jnp.einsum("lrm,crm->lcm", l_re, r_re, preferred_element_type=jnp.float32) + jnp.einsum(
        "lrm,crm->lcm", l_im, r_im, preferred_element_type=jnp.float32
    )
    x_im = jnp.einsum("lrm,crm->lcm", l_im, r_re, preferred_element_type=jnp.float32) - jnp.einsum(
        "lrm,crm->lcm", l_re, r_im, preferred_element_type=jnp.float32
    )
    cross = jnp.concatenate([x_re, x_im], -1)
    corr = jnp.dot(
        cross.reshape(slots * groups, width), forward, precision=lax.Precision.HIGHEST
    ).reshape(slots, groups, ROTS)
    score = (corr - 0.5 * norms[None, :, None]) * scale
    candidate = jnp.any(
        labels[:, :CAND_OWN, None] == jnp.arange(groups, dtype=jnp.int32)[None, None, :], axis=1
    )
    part_max = jnp.max(jnp.where(candidate[:, :, None], score, lowest), axis=(1, 2))
    part_sum = jnp.sum(
        jnp.where(candidate[:, :, None], jnp.exp(score - part_max[:, None, None]), 0.0), axis=(1, 2)
    )
    sender_ids = labels[:, CAND_OWN].astype(jnp.float32)
    table_max, table_sum, table_ids = (
        lax.all_gather(part_max.reshape(1, n_cls, cap), "cls", axis=0, tiled=True),
        lax.all_gather(part_sum.reshape(1, n_cls, cap), "cls", axis=0, tiled=True),
        lax.all_gather(sender_ids.reshape(1, n_cls, cap), "cls", axis=0, tiled=True),
    )
    local_ids = jnp.arange(count, dtype=jnp.float32)
    hit = table_ids[..., None] == local_ids
    top = jnp.max(jnp.where(hit, table_max[..., None], lowest), axis=(0, 2))
    total = jnp.sum(
        jnp.where(
            hit, table_sum[..., None] * jnp.exp(table_max[..., None] - top[None, :, None, :]), 0.0
        ),
        axis=(0, 2),
    )
    table_norm = top + jnp.log(total)
    slot_ids = labels[:, CAND_OWN].reshape(n_cls, cap)
    slot_norm = jnp.sum(
        jnp.where(
            slot_ids[..., None] == jnp.arange(count, dtype=jnp.int32), table_norm[:, None, :], 0.0
        ),
        axis=2,
    ).reshape(slots)
    own_norm = lax.dynamic_index_in_dim(table_norm, lax.axis_index("cls"), 0, keepdims=False)
    weight = jnp.where(candidate[:, :, None], jnp.exp(score - slot_norm[:, None, None]), 0.0)
    mixed = (
        jnp.dot(weight.reshape(slots * groups, ROTS), backward, precision=lax.Precision.HIGHEST)
        .astype(jnp.bfloat16)
        .reshape(slots, groups, width)
    )
    class_weights = lax.psum(jnp.sum(weight, axis=(0, 2)), "prt")
    partial_sums = class_accumulate(lanes, mixed)
    class_sums = lax.psum_scatter(partial_sums, "prt", scatter_dimension=1, tiled=True)
    return (class_sums, class_weights, own_norm)


LANES = 128


def harmonic_plan():
    half = ROTS // 2
    turns = HARM // ROTS
    tail = HARM - turns * ROTS
    chunk_of = np.zeros(HARM, np.int32)
    side_of = np.zeros(HARM, np.int32)
    for m in range(HARM):
        turn, rest = divmod(m, ROTS)
        if turn == turns:
            chunk_of[m] = half * turns + rest // 2
            side_of[m] = rest % 2
        elif rest < half:
            chunk_of[m] = rest * turns + turn
        else:
            chunk_of[m] = ((ROTS - rest) % half) * turns + turn
            side_of[m] = 1
    return half, turns, tail, chunk_of, side_of


HALF, TURNS, TAIL, CHUNK_OF, SIDE_OF = harmonic_plan()
BODY = HALF * TURNS
CHUNKS = BODY + TAIL // 2
EXTRA = TAIL // 2 + 1
COEF = 2 * HALF * CAND_OWN
RANGE = 6
RANGES = ((BODY, CHUNKS + 1),) + tuple(
    (first * TURNS, (first + RANGE) * TURNS) for first in range(0, HALF, RANGE)
)


def selector():
    return (np.arange(CHUNKS)[:, None] == CHUNK_OF[None, :]).astype(np.float32)


def unselector():
    sel = selector()
    return np.concatenate([sel * (SIDE_OF == 0), sel * (SIDE_OF == 1)], 0)


def rotation_table():
    table = np.zeros((HALF, 2, CAND_OWN, ROTS, CAND_OWN))
    angle = 2.0 * np.pi * np.arange(ROTS) / ROTS
    for g in range(HALF):
        first = np.cos(g * angle)
        second = np.cos(HALF * angle) if g == 0 else np.sin(g * angle)
        for q in range(CAND_OWN):
            table[g, 0, q, :, q] = first
            table[g, 1, q, :, q] = second
    return table.reshape(COEF, ROTS * CAND_OWN).astype(np.float32)


def nt_dot(a, b):
    return lax.dot_general(a, b, (((1,), (1,)), ((), ())), preferred_element_type=jnp.float32)


def selector_masks():
    m = lax.broadcasted_iota(jnp.int32, (1, HARM), 1)
    turn = jnp.zeros((1, HARM), jnp.int32)
    for t in range(1, TURNS + 1):
        turn += jnp.where(m >= t * ROTS, 1, 0)
    rest = m - ROTS * turn
    back = jnp.where(rest == HALF, 0, ROTS - rest)
    chunk = jnp.where(rest < HALF, rest, back) * TURNS + turn
    side = jnp.where(rest < HALF, 0, 1)
    chunk = jnp.where(turn == TURNS, BODY + rest // 2, chunk)
    side = jnp.where(turn == TURNS, rest % 2, side)
    rows = lax.broadcasted_iota(jnp.int32, (CHUNKS, HARM), 0)
    sel = jnp.where(rows == chunk, 1.0, 0.0).astype(jnp.bfloat16)
    sides = lax.broadcasted_iota(jnp.int32, (2, HARM), 0)
    masks = jnp.where(sides == side, 1.0, 0.0).astype(jnp.bfloat16)
    return sel, masks


def masked_stack(piece, masks):
    parts = []
    for s in range(2):
        for b in range(2):
            parts.append(piece[:, s * HARM : (s + 1) * HARM] * masks[b : b + 1])
    return jnp.concatenate(parts, 0)


def repeat(number, step, body, carry):
    def several(i, carry):
        for u in range(step):
            carry = body(i * step + u, carry)
        return carry

    return lax.fori_loop(0, number // step, several, carry)


def particle_body(at_ref, x_ref, meta_ref, *refs, distances, n_prt):
    outs, scr = refs[:-1], refs[-1]
    count, cycles, _ = x_ref.shape
    number = len(outs)
    span = cycles // n_prt
    sel, masks = selector_masks()

    def one(n, carry):
        parts = []
        for d in distances:
            start = pl.multiple_of((at_ref[0] ^ d) * span, span)
            parts.append(masked_stack(x_ref[n, pl.ds(start, span), :], masks))
        w = jnp.concatenate(parts, 0)
        y = nt_dot(sel, w)
        for p in range(number):
            scr[p, pl.ds(pl.multiple_of(n * CHUNKS, CHUNKS), CHUNKS), :] = y[
                :, p * LANES : (p + 1) * LANES
            ]
        return carry

    repeat(count, 4, one, 0)

    def two(c, carry):
        for p in range(number):
            outs[p][c] = scr[p, pl.ds(c, count, stride=CHUNKS), :].astype(jnp.bfloat16)
        return carry

    repeat(CHUNKS, 8, two, 0)
    lane = lax.broadcasted_iota(jnp.int32, (count, LANES), 1)
    label = jnp.full((count, LANES), -1, jnp.int32)
    for t in range(OWN_TOP):
        mine = (lane // CAND_OWN) == meta_ref[:, t : t + 1]
        for q in range(CAND_OWN):
            at = OWN_TOP + t * CAND_OWN + q
            label = jnp.where(
                mine & (lane % CAND_OWN == q), meta_ref[:, at : at + 1], label
            )
    label = label.astype(jnp.float32).astype(jnp.bfloat16)
    for p in range(number):
        outs[p][CHUNKS] = label


def arrange_particles(prt, particles, meta, n_prt, distances):
    count = particles.shape[0]
    number = len(distances)
    size = particles.size * number // n_prt
    return pl.pallas_call(
        functools.partial(particle_body, distances=distances, n_prt=n_prt),
        in_specs=[pl.BlockSpec(memory_space=pltpu.SMEM)] + [pl.BlockSpec(memory_space=pltpu.VMEM)] * 2,
        out_shape=[jax.ShapeDtypeStruct((CHUNKS + 1, count, LANES), jnp.bfloat16)] * number,
        scratch_shapes=[pltpu.VMEM((number, count * CHUNKS, LANES), jnp.float32)],
        compiler_params=pltpu.CompilerParams(vmem_limit_bytes=32 << 20),
        cost_estimate=pl.CostEstimate(
            flops=size * 2 * CHUNKS, bytes_accessed=size * 4, transcendentals=0
        ),
        name="arrange_particles",
    )(prt, particles, meta)


def reference_body(at_ref, x_ref, out_ref, norm_ref, scr):
    rows = x_ref.shape[0]
    sel, masks = selector_masks()
    step = 4

    def one(n, carry):
        w = jnp.concatenate([masked_stack(x_ref[n * step + i], masks) for i in range(step)], 0)
        y = nt_dot(sel, w)
        for i in range(step):
            scr[pl.ds(pl.multiple_of((n * step + i) * CHUNKS, CHUNKS), CHUNKS), :] = y[
                :, i * LANES : (i + 1) * LANES
            ]
        return carry

    repeat(rows // step, 2, one, 0)

    def two(c, carry):
        value = scr[pl.ds(c, rows, stride=CHUNKS), :]
        out_ref[c] = value.astype(jnp.bfloat16)
        return carry + value * value

    norm_ref[...] = repeat(CHUNKS, 8, two, jnp.zeros((rows, LANES), jnp.float32))


def arrange_references(references, prt, n_prt):
    groups, cycles, width = references.shape
    span = cycles // n_prt
    block = 16
    return pl.pallas_call(
        reference_body,
        grid_spec=pltpu.PrefetchScalarGridSpec(
            num_scalar_prefetch=1,
            grid=(groups // block,),
            in_specs=[
                pl.BlockSpec((block, span, width), lambda i, at: (i, at[0], 0)),
            ],
            out_specs=[
                pl.BlockSpec((CHUNKS, block, LANES), lambda i, at: (0, i, 0)),
                pl.BlockSpec((block, LANES), lambda i, at: (i, 0)),
            ],
            scratch_shapes=[pltpu.VMEM((block * CHUNKS, LANES), jnp.float32)],
        ),
        out_shape=[
            jax.ShapeDtypeStruct((CHUNKS, groups, LANES), jnp.bfloat16),
            jax.ShapeDtypeStruct((groups, LANES), jnp.float32),
        ],
        compiler_params=pltpu.CompilerParams(vmem_limit_bytes=60 << 20),
        cost_estimate=pl.CostEstimate(
            flops=groups * span * width * 2 * CHUNKS,
            bytes_accessed=groups * span * width * 4,
            transcendentals=0,
        ),
        name="arrange_references",
    )(prt, references)


def lane_signs():
    lane = lax.broadcasted_iota(jnp.int32, (1, LANES), 1)
    quarter = LANES // 4
    imag = lane >= 2 * quarter
    odd = (lane // quarter) % 2 == 1
    return imag, odd


def lanes_of(held, first, number):
    parts = []
    for i in range(number):
        parts.append(jnp.concatenate([held[j, first + i] for j in range(held.shape[0])], 0))
    return jnp.concatenate(parts, 1) if number > 1 else parts[0]


def fetch(blocks, held, sems):
    copies = []
    for r, (first, last) in enumerate(RANGES):
        chunks = pl.ds(first, last - first)
        copies.append(
            [
                pltpu.make_async_copy(block.at[chunks], held.at[j, chunks], sems.at[r, j])
                for j, block in enumerate(blocks)
            ]
        )
    for group in copies:
        for copy in group:
            copy.start()
    return copies


def hot_masks(cand, groups):
    rows = lax.broadcasted_iota(jnp.int32, (groups, cand.shape[1]), 0).astype(jnp.float32)
    return [rows == cand[q : q + 1] for q in range(CAND_OWN)]


def residue_weights(q_ref, g):
    imag, odd = lane_signs()
    sign = jnp.where(imag == odd, -1.0, 1.0)
    first, second = [], []
    for i in range(TURNS):
        q = q_ref[g * TURNS + i].astype(jnp.float32)
        turned = pltpu.roll(q, LANES // 2, 1) * sign
        if g == 0:
            first.append(jnp.where(odd, 0.0, q))
            second.append(jnp.where(odd, q, 0.0))
        else:
            first.append(q)
            second.append(turned)
    return jnp.concatenate(
        [jnp.concatenate(first, 1), jnp.concatenate(second, 1)], 0
    ).astype(jnp.bfloat16)


def chosen_rows(acc, cand):
    groups = acc.shape[0] // 2
    hot = hot_masks(cand, groups)
    rows = []
    for ab in range(2):
        part = acc[ab * groups : (ab + 1) * groups, :]
        for q in range(CAND_OWN):
            rows.append(jnp.sum(jnp.where(hot[q], part, 0.0), axis=0, keepdims=True))
    return jnp.concatenate(rows, 0)


def cross_body(at_ref, *refs):
    blocks = refs[:-6]
    q_ref, norm_ref, coef_ref, cand_ref, held, sems = refs[-6:]
    groups = q_ref.shape[1]
    imag, odd = lane_signs()
    copies = fetch(blocks, held, sems)
    for copy in copies[0]:
        copy.wait()
    label = lanes_of(held, CHUNKS, 1).astype(jnp.float32).T
    row = lax.broadcasted_iota(jnp.int32, label.shape, 0)
    base = at_ref[0] * CAND_OWN
    for q in range(CAND_OWN):
        cand_ref[q : q + 1, :] = jnp.sum(
            jnp.where(row == base + q, label, 0.0), axis=0, keepdims=True
        )
    cand_ref[CAND_OWN:, :] = jnp.full(
        (cand_ref.shape[0] - CAND_OWN, cand_ref.shape[1]), -1.0, jnp.float32
    )

    def tail(i):
        q = q_ref[BODY + i // 2].astype(jnp.float32)
        keep = odd if i % 2 else ~odd
        a = jnp.where(keep, q, 0.0)
        turned = pltpu.roll(q, LANES // 2, 1) * jnp.where(imag, 1.0, -1.0)
        b = jnp.where(keep, turned, 0.0)
        if i == 0:
            b = jnp.zeros_like(b)
        w = jnp.concatenate([a, b], 0).astype(jnp.bfloat16)
        return nt_dot(w, lanes_of(held, BODY + i // 2, 1))

    for r in range(1, len(RANGES)):
        for copy in copies[r]:
            copy.wait()

        for g in range((r - 1) * RANGE, r * RANGE):
            acc = nt_dot(residue_weights(q_ref, g), lanes_of(held, g * TURNS, TURNS))
            if g < TAIL:
                acc += tail(g)
            if g == 0:
                half_norm = 0.5 * jnp.sum(norm_ref[...], axis=1, keepdims=True)
                acc = jnp.concatenate([acc[:groups] - half_norm, acc[groups:]], 0)
            block = 2 * CAND_OWN
            coef_ref[g * block : (g + 1) * block, :] = chosen_rows(acc, cand_ref[...])


def cross_coefficients(blocks, arranged, norms, cls):
    number = len(blocks)
    count = blocks[0].shape[1]
    groups = arranged.shape[1]
    total = number * count
    size = blocks[0].size * number
    block = 2 * CAND_OWN
    return pl.pallas_call(
        cross_body,
        in_specs=[pl.BlockSpec(memory_space=pltpu.SMEM)]
        + [pl.BlockSpec(memory_space=pl.ANY)] * number
        + [pl.BlockSpec(memory_space=pltpu.VMEM)] * 2,
        out_shape=[
            jax.ShapeDtypeStruct((COEF, total), jnp.float32),
            jax.ShapeDtypeStruct((block, total), jnp.float32),
        ],
        scratch_shapes=[
            pltpu.VMEM((number, *blocks[0].shape), jnp.bfloat16),
            pltpu.SemaphoreType.DMA((len(RANGES), number)),
        ],
        compiler_params=pltpu.CompilerParams(vmem_limit_bytes=60 << 20),
        cost_estimate=pl.CostEstimate(
            flops=4 * size * groups, bytes_accessed=2 * size, transcendentals=0
        ),
        name="cross_coefficients",
    )(cls, *blocks, arranged, norms)


def score_body(*refs, scale):
    *coefs, cand_ref, table_ref, score_ref, stat_ref = refs
    corr = lax.dot_general(
        table_ref[...],
        functools.reduce(jnp.add, [ref[...] for ref in coefs]),
        (((0,), (0,)), ((), ())),
        precision=lax.Precision.HIGHEST,
        preferred_element_type=jnp.float32,
    )
    score = jnp.where(cand_ref[0:1, :] >= 0.0, corr * scale, lowest)
    top = jnp.max(score, axis=0, keepdims=True)
    total = jnp.sum(jnp.exp(score - top), axis=0, keepdims=True)
    score_ref[...] = score
    stat_ref[0:1, :] = top
    stat_ref[1:2, :] = jnp.where(cand_ref[0:1, :] >= 0.0, total, 0.0)


def scores(coefs, cand, table, scale):
    total = cand.shape[1]
    return pl.pallas_call(
        functools.partial(score_body, scale=scale),
        out_shape=[
            jax.ShapeDtypeStruct((ROTS * CAND_OWN, total), jnp.float32),
            jax.ShapeDtypeStruct((2, total), jnp.float32),
        ],
        name="scores",
    )(*coefs, cand, table)


def swap_blocks(x, distance, width):
    lane = lax.broadcasted_iota(jnp.int32, x.shape, 1)
    bit = 1
    while bit <= distance:
        if distance & bit:
            shift = bit * width
            down = pltpu.roll(x, shift, 1)
            up = pltpu.roll(x, x.shape[1] - shift, 1)
            x = jnp.where((lane // shift) % 2 == 1, down, up)
        bit *= 2
    return x


def weights_body(at_ref, score_ref, cand_ref, stat_ref, table_ref, mix_ref, norm_ref):
    n_cls, _, total = stat_ref.shape
    width = total // n_cls
    tops, parts = [], []
    for e in range(n_cls):
        table = stat_ref[at_ref[0] ^ e]
        table = swap_blocks(jnp.concatenate([table] * 4, 0), e, width)
        tops.append(table[0:1])
        parts.append(table[1:2])
    top = functools.reduce(jnp.maximum, tops)
    summed = jnp.zeros_like(top)
    for other, part in zip(tops, parts):
        summed += part * jnp.exp(other - top)
    log_norm = top + jnp.log(summed)
    norm_ref[...] = log_norm[:, : norm_ref.shape[1]]
    weight = jnp.where(cand_ref[0:1, :] >= 0.0, jnp.exp(score_ref[...] - log_norm), 0.0)
    mix_ref[...] = lax.dot_general(
        table_ref[...],
        weight,
        (((1,), (0,)), ((), ())),
        precision=lax.Precision.HIGHEST,
        preferred_element_type=jnp.float32,
    )


def mixed_weights(cls, score, cand, stats, table, count):
    total = score.shape[1]
    return pl.pallas_call(
        weights_body,
        in_specs=[pl.BlockSpec(memory_space=pltpu.SMEM)] + [pl.BlockSpec(memory_space=pltpu.VMEM)] * 4,
        out_shape=[
            jax.ShapeDtypeStruct((COEF, total), jnp.float32),
            jax.ShapeDtypeStruct((1, count), jnp.float32),
        ],
        name="mixed_weights",
    )(cls, score, cand, stats, table)


def sums_body(*refs, number, pieces):
    blocks = refs[:number]
    refs = refs[number:]
    mixes, cands = refs[:pieces], refs[pieces : 2 * pieces]
    back_ref, out_ref, weight_ref, mix, cand, planes, held, sems = refs[2 * pieces :]
    step = pl.program_id(0)
    groups = weight_ref.shape[1]
    total = mix.shape[1]
    imag, odd = lane_signs()

    @pl.when(step == 0)
    def _():
        copies = fetch(blocks, held, sems)
        mixed = jnp.concatenate([ref[...] for ref in mixes], 1)
        chosen = jnp.concatenate([ref[...] for ref in cands], 1)
        hot = hot_masks(chosen, groups)
        summed = jnp.zeros((groups, total), jnp.float32)
        for q in range(CAND_OWN):
            summed += jnp.where(hot[q], mixed[q : q + 1], 0.0)
        weight_ref[...] = lax.dot_general(
            jnp.ones((1, total), jnp.float32),
            summed,
            (((1,), (1,)), ((), ())),
            precision=lax.Precision.HIGHEST,
            preferred_element_type=jnp.float32,
        )
        mix[...] = mixed
        cand[...] = chosen
        sign = jnp.where(imag == odd, 1.0, -1.0)
        for copy in copies[0]:
            copy.wait()

        def tail(t, weights):
            made = jnp.dot(
                weights, lanes_of(held, BODY + t // 2, 1), preferred_element_type=jnp.float32
            )
            g1, g2 = made[:groups], made[groups:]
            value = g1
            if t > 0:
                value = g1 + jnp.where(imag, -1.0, 1.0) * pltpu.roll(g2, LANES // 2, 1)
            rows = pl.ds((BODY + t // 2) * groups, groups)
            if t % 2:
                value = jnp.where(odd, value, planes[rows, :])
            planes[rows, :] = value

        for r in range(1, len(RANGES)):
            for copy in copies[r]:
                copy.wait()

            hot = hot_masks(cand[...], groups)
            block = 2 * CAND_OWN
            for g in range((r - 1) * RANGE, r * RANGE):
                mine = mix[g * block : (g + 1) * block, :]
                halves = []
                for ab in range(2):
                    dense = jnp.zeros((groups, total), jnp.float32)
                    for q in range(CAND_OWN):
                        at = ab * CAND_OWN + q
                        dense = jnp.where(hot[q], mine[at : at + 1], dense)
                    halves.append(dense)
                weights = jnp.concatenate(halves, 0).astype(jnp.bfloat16)
                made = jnp.dot(
                    weights, lanes_of(held, g * TURNS, TURNS), preferred_element_type=jnp.float32
                )
                for t in range(TURNS):
                    g1 = made[:groups, t * LANES : (t + 1) * LANES]
                    g2 = made[groups:, t * LANES : (t + 1) * LANES]
                    if g == 0:
                        value = jnp.where(odd, g2, g1)
                    else:
                        value = g1 + sign * pltpu.roll(g2, LANES // 2, 1)
                    start = (g * TURNS + t) * groups
                    planes[start : start + groups, :] = value
                if g < TAIL:
                    tail(g, weights)

    @pl.when(step > 0)
    def _():
        block, span, _ = out_ref.shape
        first = (step - 1) * block
        back = back_ref[...]
        values = []
        for c in range(block):
            turned = planes[pl.ds(first + c, CHUNKS, stride=groups), :].T
            for s in range(2):
                at = 2 * s * span
                values.append(
                    jnp.concatenate([turned[at : at + span], turned[at + span : at + 2 * span]], 1)
                )
        value = jnp.concatenate(values, 0)
        high = value.astype(jnp.bfloat16)
        low = (value - high.astype(jnp.float32)).astype(jnp.bfloat16)
        both = jnp.dot(
            jnp.concatenate([high, low], 0), back, preferred_element_type=jnp.float32
        )
        rows = value.shape[0]
        placed = both[:rows] + both[rows:]
        for c in range(block):
            for s in range(2):
                at = (2 * c + s) * span
                out_ref[c, :, s * HARM : (s + 1) * HARM] = placed[at : at + span]


def sums(blocks, mixes, cands, back, groups, span):
    number = len(blocks)
    count = blocks[0].shape[1]
    total = number * count
    size = blocks[0].size * number
    block = 8
    whole = lambda i: (0, 0)
    return pl.pallas_call(
        functools.partial(sums_body, number=number, pieces=len(mixes)),
        grid=(1 + groups // block,),
        in_specs=[
            *[pl.BlockSpec(memory_space=pl.ANY)] * number,
            *[pl.BlockSpec(array.shape, whole) for array in (*mixes, *cands, back)],
        ],
        out_specs=[
            pl.BlockSpec((block, span, 2 * HARM), lambda i: (jnp.maximum(i - 1, 0), 0, 0)),
            pl.BlockSpec((1, groups), whole),
        ],
        out_shape=[
            jax.ShapeDtypeStruct((groups, span, 2 * HARM), jnp.float32),
            jax.ShapeDtypeStruct((1, groups), jnp.float32),
        ],
        scratch_shapes=[
            pltpu.VMEM((COEF, total), jnp.float32),
            pltpu.VMEM((2 * CAND_OWN, total), jnp.float32),
            pltpu.VMEM((CHUNKS * groups, LANES), jnp.float32),
            pltpu.VMEM((number, *blocks[0].shape), jnp.bfloat16),
            pltpu.SemaphoreType.DMA((len(RANGES), number)),
        ],
        compiler_params=pltpu.CompilerParams(vmem_limit_bytes=60 << 20),
        cost_estimate=pl.CostEstimate(
            flops=4 * size * groups,
            bytes_accessed=2 * size + 8 * groups * span * HARM,
            transcendentals=0,
        ),
        name="sums",
    )(*blocks, *mixes, *cands, back)


def hop(value, axis, distance):
    size = lax.axis_size(axis)
    return lax.ppermute(value, axis, [(i, i ^ distance) for i in range(size)])


def after(value, *others):
    return lax.optimization_barrier((value, *others))[0]


def direct(own):
    n_cls = lax.axis_size("cls")
    return {1 << bit: hop(own, "cls", 1 << bit) for bit in range(1, n_cls.bit_length() - 1)}


def relayed(known, d, *others):
    n_cls = lax.axis_size("cls")
    for j in sorted(range(2, n_cls, 2), key=lambda j: bin(j).count("1")):
        if j not in known:
            bits = [bit for bit in range(1, n_cls.bit_length()) if j >> bit & 1]
            way = 1 << bits[(1 - d // 2) % len(bits)]
            known[j] = hop(after(known[j ^ way], *others), "cls", way)
    return known


def paired(known, each, last):
    n_cls = lax.axis_size("cls")
    for j in range(0, n_cls, 2):
        others = last if j == n_cls - 2 else each
        block = after(known[j], *others) if others else known[j]
        known[j + 1] = hop(block, "cls", 1)
    return [known[j] for j in range(n_cls)]


def gather_device(particles, references, owner_groups, class_order):
    n_cls, n_prt = lax.axis_size("cls"), lax.axis_size("prt")
    cls, prt = lax.axis_index("cls"), lax.axis_index("prt")
    count, cycles, width = particles.shape
    groups = references.shape[0]
    span = cycles // n_prt
    back = jnp.asarray(unselector(), jnp.bfloat16)
    table = jnp.asarray(rotation_table())
    picks = class_order[:, :, :CAND_OWN].reshape(count, OWN_TOP * CAND_OWN)
    meta = jnp.concatenate([owner_groups, picks], 1)
    cls, prt = (index.reshape(1).astype(jnp.int32) for index in (cls, prt))
    order = [d for d in range(n_prt) if d % 2 == 0] + [d for d in range(n_prt) if d % 2]
    outgoing = {}
    place = prt
    for first in range(0, n_prt, 2):
        distances = tuple(order[first : first + 2])
        made = arrange_particles(place, particles, meta, n_prt, distances)
        outgoing.update(zip(distances, made))
        place = after(prt, made[0])
    lead, second, *others = order[1:]
    final = outgoing[order[-1]]
    arrived = {d: outgoing[d] if d == 0 else hop(outgoing[d], "prt", d) for d in order[:3]}
    known = {0: {0: arrived[0], **direct(arrived[0])}}
    early = after(arrived[lead], final)
    known[lead] = {0: early, **direct(early)}
    relayed(known[0], 0, final)
    far = n_cls // 2
    place = after(prt, arrived[lead], known[0][2], known[0][far])
    arranged, norms = arrange_references(references, place, n_prt)
    previous = arrived[lead]
    for d in others:
        previous = arrived[d] = hop(after(outgoing[d], previous), "prt", d)
    own = after(arrived[second], arranged)
    known[second] = {0: own, **direct(own)}
    for d in others:
        known[d] = {0: arrived[d], **direct(arrived[d])}
    for d in (lead, *others):
        relayed(known[d], d)
    scale = 2.0 / math.sqrt(cycles * width)
    made, blocks, done = {}, {}, []
    for d in (0, lead, second, *others):
        waits = {
            0: [known[lead][2]],
            lead: [previous, known[second][far]],
            second: [known[others[0]][2]],
        }.get(d, [])
        if d == second:
            relayed(known[d], d, done[0])
        each = [arranged, known[lead][far]] if d == 0 else [] if d in others else done[:1]
        blocks[d] = paired(known[d], each, done[-1:])
        ready = after(arranged, *waits) if waits else arranged
        made[d] = cross_coefficients(blocks[d], ready, norms, cls)
        done.append(made[d][0])
    distances = range(n_prt)
    sent = [hop(made[d][0], "prt", d) if d else made[d][0] for d in distances]
    cands = [made[d][1] for d in distances]
    blocks = [blocks[d] for d in distances]
    score, stat = scores(sent, cands[0], table, scale)
    stats = lax.all_gather(stat.reshape(1, *stat.shape), "cls", axis=0, tiled=True)
    mix, log_norm = mixed_weights(cls, score, cands[0], stats, table, count)
    mixes = [hop(mix, "prt", d) if d else mix for d in range(n_prt)]
    class_sums, class_weights = sums(
        [block for piece in blocks for block in piece], mixes, cands, back, groups, span
    )
    own = log_norm[0]
    return class_sums, class_weights[0], own


def per_device(particles, references, owner_groups, class_order):
    n_cls, n_prt = lax.axis_size("cls"), lax.axis_size("prt")
    count, cycles, _ = particles.shape
    groups = references.shape[0]
    cap = max(2, 2 * count * OWN_TOP // n_cls)
    powers = n_cls & (n_cls - 1) == 0 and n_prt & (n_prt - 1) == 0
    fits = 4 * cycles == LANES * n_prt and n_cls * CAND_OWN <= LANES and groups % 16 == 0 and n_cls >= 4 and n_prt >= 4
    fits = fits and powers and n_cls * count == LANES
    plan = gather_device if cap >= count and fits else dispatch_device
    return plan(particles, references, owner_groups, class_order)


def solution(mesh):
    in_specs = (
        P(("cls", "prt"), None, None),
        P("cls", None, None),
        P(("cls", "prt"), None),
        P(("cls", "prt"), None, None),
    )
    out_specs = (P("cls", "prt", None), P("cls"), P(("cls", "prt")))
    return jax.shard_map(
        per_device, mesh=mesh, in_specs=in_specs, out_specs=out_specs, check_vma=False
    )
```

```python
import functools
import math

import jax
import jax.numpy as jnp
import numpy as np
from jax import lax
from jax.experimental import pallas as pl
from jax.experimental.pallas import tpu as pltpu
from jax.sharding import PartitionSpec as P

CYCLES = 128
HARM = 256
ROTS = 36
OWN_TOP = 4
CAND_OWN = 4


lowest = -1e30


def spectral_tables():
    harmonic = jnp.arange(HARM, dtype=jnp.float32)
    angles = 2.0 * math.pi * jnp.arange(ROTS, dtype=jnp.float32) / ROTS
    phase = harmonic[:, None] * angles[None, :]
    forward = jnp.concatenate([jnp.cos(phase), jnp.sin(phase)], 0)
    backward = jnp.concatenate([jnp.cos(phase), -jnp.sin(phase)], 0).T
    return (forward, backward)


def class_accumulate(lanes, mixed):
    l_re = lanes[..., :HARM]
    l_im = lanes[..., HARM:]
    y_re = mixed[..., :HARM]
    y_im = mixed[..., HARM:]
    s_re = jnp.einsum("lrm,lcm->crm", l_re, y_re, preferred_element_type=jnp.float32) - jnp.einsum(
        "lrm,lcm->crm", l_im, y_im, preferred_element_type=jnp.float32
    )
    s_im = jnp.einsum("lrm,lcm->crm", l_re, y_im, preferred_element_type=jnp.float32) + jnp.einsum(
        "lrm,lcm->crm", l_im, y_re, preferred_element_type=jnp.float32
    )
    return jnp.concatenate([s_re, s_im], -1)


def dispatch_device(particles, references, owner_groups, class_order):
    n_cls = lax.axis_size("cls")
    count = particles.shape[0]
    groups = references.shape[0]
    cap = max(2, 2 * count * OWN_TOP // n_cls)
    slots = n_cls * cap
    width = 2 * HARM
    flat_owner = owner_groups.reshape(-1)
    owner_hot = (flat_owner[:, None] == jnp.arange(n_cls, dtype=jnp.int32)[None, :]).astype(
        jnp.int32
    )
    before = jnp.cumsum(owner_hot, axis=0) - owner_hot
    rank = jnp.sum(before * owner_hot, axis=1)
    slot_of = flat_owner * cap + rank
    match = slot_of[None, :] == jnp.arange(slots, dtype=jnp.int32)[:, None]
    member = jnp.any(match.reshape(slots, count, OWN_TOP), axis=2)
    filled = jnp.any(member, axis=1)
    dispatch = member.astype(jnp.bfloat16)
    outgoing = jnp.dot(
        dispatch, particles.reshape(count, CYCLES * width), preferred_element_type=jnp.float32
    )
    outgoing = outgoing.astype(jnp.bfloat16).reshape(n_cls, cap, CYCLES, width)
    match_int = match.astype(jnp.int32)
    picks = class_order[:, :, :CAND_OWN].reshape(count * OWN_TOP, CAND_OWN)
    slot_cand = jnp.where(filled[:, None], jnp.dot(match_int, picks), -1)
    owner_rows = jnp.repeat(jnp.arange(count, dtype=jnp.int32), OWN_TOP)
    slot_pid = jnp.where(filled, jnp.dot(match_int, owner_rows), -1)
    labels_out = jnp.concatenate([slot_cand, slot_pid[:, None]], 1).reshape(
        n_cls, cap, CAND_OWN + 1
    )
    arrived, labels = (
        lax.all_to_all(outgoing, "cls", split_axis=0, concat_axis=0, tiled=True),
        lax.all_to_all(labels_out, "cls", split_axis=0, concat_axis=0, tiled=True),
    )
    lanes = arrived.reshape(slots, CYCLES, width)
    labels = labels.reshape(slots, CAND_OWN + 1)
    forward, backward = spectral_tables()
    scale = 2.0 / math.sqrt(CYCLES * width)
    norms = jnp.sum(jnp.square(references.astype(jnp.float32)), axis=(1, 2))
    l_re = lanes[..., :HARM]
    l_im = lanes[..., HARM:]
    r_re = references[..., :HARM]
    r_im = references[..., HARM:]
    x_re = jnp.einsum("lrm,crm->lcm", l_re, r_re, preferred_element_type=jnp.float32) + jnp.einsum(
        "lrm,crm->lcm", l_im, r_im, preferred_element_type=jnp.float32
    )
    x_im = jnp.einsum("lrm,crm->lcm", l_im, r_re, preferred_element_type=jnp.float32) - jnp.einsum(
        "lrm,crm->lcm", l_re, r_im, preferred_element_type=jnp.float32
    )
    cross = jnp.concatenate([x_re, x_im], -1)
    corr = jnp.dot(
        cross.reshape(slots * groups, width), forward, precision=lax.Precision.HIGHEST
    ).reshape(slots, groups, ROTS)
    score = (corr - 0.5 * norms[None, :, None]) * scale
    candidate = jnp.any(
        labels[:, :CAND_OWN, None] == jnp.arange(groups, dtype=jnp.int32)[None, None, :], axis=1
    )
    part_max = jnp.max(jnp.where(candidate[:, :, None], score, lowest), axis=(1, 2))
    part_sum = jnp.sum(
        jnp.where(candidate[:, :, None], jnp.exp(score - part_max[:, None, None]), 0.0), axis=(1, 2)
    )
    sender_ids = labels[:, CAND_OWN].astype(jnp.float32)
    table_max, table_sum, table_ids = (
        lax.all_gather(part_max.reshape(1, n_cls, cap), "cls", axis=0, tiled=True),
        lax.all_gather(part_sum.reshape(1, n_cls, cap), "cls", axis=0, tiled=True),
        lax.all_gather(sender_ids.reshape(1, n_cls, cap), "cls", axis=0, tiled=True),
    )
    local_ids = jnp.arange(count, dtype=jnp.float32)
    hit = table_ids[..., None] == local_ids
    top = jnp.max(jnp.where(hit, table_max[..., None], lowest), axis=(0, 2))
    total = jnp.sum(
        jnp.where(
            hit, table_sum[..., None] * jnp.exp(table_max[..., None] - top[None, :, None, :]), 0.0
        ),
        axis=(0, 2),
    )
    table_norm = top + jnp.log(total)
    slot_ids = labels[:, CAND_OWN].reshape(n_cls, cap)
    slot_norm = jnp.sum(
        jnp.where(
            slot_ids[..., None] == jnp.arange(count, dtype=jnp.int32), table_norm[:, None, :], 0.0
        ),
        axis=2,
    ).reshape(slots)
    own_norm = lax.dynamic_index_in_dim(table_norm, lax.axis_index("cls"), 0, keepdims=False)
    weight = jnp.where(candidate[:, :, None], jnp.exp(score - slot_norm[:, None, None]), 0.0)
    mixed = (
        jnp.dot(weight.reshape(slots * groups, ROTS), backward, precision=lax.Precision.HIGHEST)
        .astype(jnp.bfloat16)
        .reshape(slots, groups, width)
    )
    class_weights = lax.psum(jnp.sum(weight, axis=(0, 2)), "prt")
    partial_sums = class_accumulate(lanes, mixed)
    class_sums = lax.psum_scatter(partial_sums, "prt", scatter_dimension=1, tiled=True)
    return (class_sums, class_weights, own_norm)


LANES = 128


def harmonic_plan():
    half = ROTS // 2
    turns = HARM // ROTS
    tail = HARM - turns * ROTS
    chunk_of = np.zeros(HARM, np.int32)
    side_of = np.zeros(HARM, np.int32)
    for m in range(HARM):
        turn, rest = divmod(m, ROTS)
        if turn == turns:
            chunk_of[m] = half * turns + rest // 2
            side_of[m] = rest % 2
        elif rest < half:
            chunk_of[m] = rest * turns + turn
        else:
            chunk_of[m] = ((ROTS - rest) % half) * turns + turn
            side_of[m] = 1
    return half, turns, tail, chunk_of, side_of


HALF, TURNS, TAIL, CHUNK_OF, SIDE_OF = harmonic_plan()
BODY = HALF * TURNS
CHUNKS = BODY + TAIL // 2
EXTRA = TAIL // 2 + 1
COEF = 2 * HALF * CAND_OWN
RANGE = 6
RANGES = ((BODY, CHUNKS + 1),) + tuple(
    (first * TURNS, (first + RANGE) * TURNS) for first in range(0, HALF, RANGE)
)


def selector():
    return (np.arange(CHUNKS)[:, None] == CHUNK_OF[None, :]).astype(np.float32)


def unselector():
    sel = selector()
    return np.concatenate([sel * (SIDE_OF == 0), sel * (SIDE_OF == 1)], 0)


def rotation_table():
    table = np.zeros((HALF, 2, CAND_OWN, ROTS, CAND_OWN))
    angle = 2.0 * np.pi * np.arange(ROTS) / ROTS
    for g in range(HALF):
        first = np.cos(g * angle)
        second = np.cos(HALF * angle) if g == 0 else np.sin(g * angle)
        for q in range(CAND_OWN):
            table[g, 0, q, :, q] = first
            table[g, 1, q, :, q] = second
    return table.reshape(COEF, ROTS * CAND_OWN).astype(np.float32)


def nt_dot(a, b):
    return lax.dot_general(a, b, (((1,), (1,)), ((), ())), preferred_element_type=jnp.float32)


def selector_masks():
    m = lax.broadcasted_iota(jnp.int32, (1, HARM), 1)
    turn = jnp.zeros((1, HARM), jnp.int32)
    for t in range(1, TURNS + 1):
        turn += jnp.where(m >= t * ROTS, 1, 0)
    rest = m - ROTS * turn
    back = jnp.where(rest == HALF, 0, ROTS - rest)
    chunk = jnp.where(rest < HALF, rest, back) * TURNS + turn
    side = jnp.where(rest < HALF, 0, 1)
    chunk = jnp.where(turn == TURNS, BODY + rest // 2, chunk)
    side = jnp.where(turn == TURNS, rest % 2, side)
    rows = lax.broadcasted_iota(jnp.int32, (CHUNKS, HARM), 0)
    sel = jnp.where(rows == chunk, 1.0, 0.0).astype(jnp.bfloat16)
    sides = lax.broadcasted_iota(jnp.int32, (2, HARM), 0)
    masks = jnp.where(sides == side, 1.0, 0.0).astype(jnp.bfloat16)
    return sel, masks


def masked_stack(piece, masks):
    parts = []
    for s in range(2):
        for b in range(2):
            parts.append(piece[:, s * HARM : (s + 1) * HARM] * masks[b : b + 1])
    return jnp.concatenate(parts, 0)


def repeat(number, step, body, carry):
    def several(i, carry):
        for u in range(step):
            carry = body(i * step + u, carry)
        return carry

    return lax.fori_loop(0, number // step, several, carry)


def particle_body(at_ref, x_ref, meta_ref, *refs, distances, n_prt):
    outs, scr = refs[:-1], refs[-1]
    count, cycles, _ = x_ref.shape
    number = len(outs)
    span = cycles // n_prt
    sel, masks = selector_masks()

    def one(n, carry):
        parts = []
        for d in distances:
            start = pl.multiple_of((at_ref[0] ^ d) * span, span)
            parts.append(masked_stack(x_ref[n, pl.ds(start, span), :], masks))
        w = jnp.concatenate(parts, 0)
        y = nt_dot(sel, w)
        for p in range(number):
            scr[p, pl.ds(pl.multiple_of(n * CHUNKS, CHUNKS), CHUNKS), :] = y[
                :, p * LANES : (p + 1) * LANES
            ]
        return carry

    repeat(count, 4, one, 0)

    def two(c, carry):
        for p in range(number):
            outs[p][c] = scr[p, pl.ds(c, count, stride=CHUNKS), :].astype(jnp.bfloat16)
        return carry

    repeat(CHUNKS, 8, two, 0)
    lane = lax.broadcasted_iota(jnp.int32, (count, LANES), 1)
    label = jnp.full((count, LANES), -1, jnp.int32)
    for t in range(OWN_TOP):
        mine = (lane // CAND_OWN) == meta_ref[:, t : t + 1]
        for q in range(CAND_OWN):
            at = OWN_TOP + t * CAND_OWN + q
            label = jnp.where(
                mine & (lane % CAND_OWN == q), meta_ref[:, at : at + 1], label
            )
    label = label.astype(jnp.float32).astype(jnp.bfloat16)
    for p in range(number):
        outs[p][CHUNKS] = label


def arrange_particles(prt, particles, meta, n_prt, distances):
    count = particles.shape[0]
    number = len(distances)
    size = particles.size * number // n_prt
    return pl.pallas_call(
        functools.partial(particle_body, distances=distances, n_prt=n_prt),
        in_specs=[pl.BlockSpec(memory_space=pltpu.SMEM)] + [pl.BlockSpec(memory_space=pltpu.VMEM)] * 2,
        out_shape=[jax.ShapeDtypeStruct((CHUNKS + 1, count, LANES), jnp.bfloat16)] * number,
        scratch_shapes=[pltpu.VMEM((number, count * CHUNKS, LANES), jnp.float32)],
        compiler_params=pltpu.CompilerParams(vmem_limit_bytes=32 << 20),
        cost_estimate=pl.CostEstimate(
            flops=size * 2 * CHUNKS, bytes_accessed=size * 4, transcendentals=0
        ),
        name="arrange_particles",
    )(prt, particles, meta)


def reference_body(at_ref, x_ref, out_ref, norm_ref, scr):
    rows = x_ref.shape[0]
    sel, masks = selector_masks()
    step = 4

    def one(n, carry):
        w = jnp.concatenate([masked_stack(x_ref[n * step + i], masks) for i in range(step)], 0)
        y = nt_dot(sel, w)
        for i in range(step):
            scr[pl.ds(pl.multiple_of((n * step + i) * CHUNKS, CHUNKS), CHUNKS), :] = y[
                :, i * LANES : (i + 1) * LANES
            ]
        return carry

    repeat(rows // step, 2, one, 0)

    def two(c, carry):
        value = scr[pl.ds(c, rows, stride=CHUNKS), :]
        out_ref[c] = value.astype(jnp.bfloat16)
        return carry + value * value

    norm_ref[...] = repeat(CHUNKS, 8, two, jnp.zeros((rows, LANES), jnp.float32))


def arrange_references(references, prt, n_prt):
    groups, cycles, width = references.shape
    span = cycles // n_prt
    block = 16
    return pl.pallas_call(
        reference_body,
        grid_spec=pltpu.PrefetchScalarGridSpec(
            num_scalar_prefetch=1,
            grid=(groups // block,),
            in_specs=[
                pl.BlockSpec((block, span, width), lambda i, at: (i, at[0], 0)),
            ],
            out_specs=[
                pl.BlockSpec((CHUNKS, block, LANES), lambda i, at: (0, i, 0)),
                pl.BlockSpec((block, LANES), lambda i, at: (i, 0)),
            ],
            scratch_shapes=[pltpu.VMEM((block * CHUNKS, LANES), jnp.float32)],
        ),
        out_shape=[
            jax.ShapeDtypeStruct((CHUNKS, groups, LANES), jnp.bfloat16),
            jax.ShapeDtypeStruct((groups, LANES), jnp.float32),
        ],
        compiler_params=pltpu.CompilerParams(vmem_limit_bytes=60 << 20),
        cost_estimate=pl.CostEstimate(
            flops=groups * span * width * 2 * CHUNKS,
            bytes_accessed=groups * span * width * 4,
            transcendentals=0,
        ),
        name="arrange_references",
    )(prt, references)


def lane_signs():
    lane = lax.broadcasted_iota(jnp.int32, (1, LANES), 1)
    quarter = LANES // 4
    imag = lane >= 2 * quarter
    odd = (lane // quarter) % 2 == 1
    return imag, odd


def lanes_of(held, first, number):
    parts = []
    for i in range(number):
        parts.append(jnp.concatenate([held[j, first + i] for j in range(held.shape[0])], 0))
    return jnp.concatenate(parts, 1) if number > 1 else parts[0]


def fetch(blocks, held, sems):
    copies = []
    for r, (first, last) in enumerate(RANGES):
        chunks = pl.ds(first, last - first)
        copies.append(
            [
                pltpu.make_async_copy(block.at[chunks], held.at[j, chunks], sems.at[r, j])
                for j, block in enumerate(blocks)
            ]
        )
    for group in copies:
        for copy in group:
            copy.start()
    return copies


def hot_masks(cand, groups):
    rows = lax.broadcasted_iota(jnp.int32, (groups, cand.shape[1]), 0).astype(jnp.float32)
    return [rows == cand[q : q + 1] for q in range(CAND_OWN)]


def residue_weights(q_ref, g):
    imag, odd = lane_signs()
    sign = jnp.where(imag == odd, -1.0, 1.0)
    first, second = [], []
    for i in range(TURNS):
        q = q_ref[g * TURNS + i].astype(jnp.float32)
        turned = pltpu.roll(q, LANES // 2, 1) * sign
        if g == 0:
            first.append(jnp.where(odd, 0.0, q))
            second.append(jnp.where(odd, q, 0.0))
        else:
            first.append(q)
            second.append(turned)
    return jnp.concatenate(
        [jnp.concatenate(first, 1), jnp.concatenate(second, 1)], 0
    ).astype(jnp.bfloat16)


def chosen_rows(acc, cand):
    groups = acc.shape[0] // 2
    hot = hot_masks(cand, groups)
    rows = []
    for ab in range(2):
        part = acc[ab * groups : (ab + 1) * groups, :]
        for q in range(CAND_OWN):
            rows.append(jnp.sum(jnp.where(hot[q], part, 0.0), axis=0, keepdims=True))
    return jnp.concatenate(rows, 0)


def cross_body(at_ref, *refs):
    blocks = refs[:-6]
    q_ref, norm_ref, coef_ref, cand_ref, held, sems = refs[-6:]
    groups = q_ref.shape[1]
    imag, odd = lane_signs()
    copies = fetch(blocks, held, sems)
    for copy in copies[0]:
        copy.wait()
    label = lanes_of(held, CHUNKS, 1).astype(jnp.float32).T
    row = lax.broadcasted_iota(jnp.int32, label.shape, 0)
    base = at_ref[0] * CAND_OWN
    for q in range(CAND_OWN):
        cand_ref[q : q + 1, :] = jnp.sum(
            jnp.where(row == base + q, label, 0.0), axis=0, keepdims=True
        )
    cand_ref[CAND_OWN:, :] = jnp.full(
        (cand_ref.shape[0] - CAND_OWN, cand_ref.shape[1]), -1.0, jnp.float32
    )

    def tail(i):
        q = q_ref[BODY + i // 2].astype(jnp.float32)
        keep = odd if i % 2 else ~odd
        a = jnp.where(keep, q, 0.0)
        turned = pltpu.roll(q, LANES // 2, 1) * jnp.where(imag, 1.0, -1.0)
        b = jnp.where(keep, turned, 0.0)
        if i == 0:
            b = jnp.zeros_like(b)
        w = jnp.concatenate([a, b], 0).astype(jnp.bfloat16)
        return nt_dot(w, lanes_of(held, BODY + i // 2, 1))

    for r in range(1, len(RANGES)):
        for copy in copies[r]:
            copy.wait()

        for g in range((r - 1) * RANGE, r * RANGE):
            acc = nt_dot(residue_weights(q_ref, g), lanes_of(held, g * TURNS, TURNS))
            if g < TAIL:
                acc += tail(g)
            if g == 0:
                half_norm = 0.5 * jnp.sum(norm_ref[...], axis=1, keepdims=True)
                acc = jnp.concatenate([acc[:groups] - half_norm, acc[groups:]], 0)
            block = 2 * CAND_OWN
            coef_ref[g * block : (g + 1) * block, :] = chosen_rows(acc, cand_ref[...])


def cross_coefficients(blocks, arranged, norms, cls):
    number = len(blocks)
    count = blocks[0].shape[1]
    groups = arranged.shape[1]
    total = number * count
    size = blocks[0].size * number
    block = 2 * CAND_OWN
    return pl.pallas_call(
        cross_body,
        in_specs=[pl.BlockSpec(memory_space=pltpu.SMEM)]
        + [pl.BlockSpec(memory_space=pl.ANY)] * number
        + [pl.BlockSpec(memory_space=pltpu.VMEM)] * 2,
        out_shape=[
            jax.ShapeDtypeStruct((COEF, total), jnp.float32),
            jax.ShapeDtypeStruct((block, total), jnp.float32),
        ],
        scratch_shapes=[
            pltpu.VMEM((number, *blocks[0].shape), jnp.bfloat16),
            pltpu.SemaphoreType.DMA((len(RANGES), number)),
        ],
        compiler_params=pltpu.CompilerParams(vmem_limit_bytes=60 << 20),
        cost_estimate=pl.CostEstimate(
            flops=4 * size * groups, bytes_accessed=2 * size, transcendentals=0
        ),
        name="cross_coefficients",
    )(cls, *blocks, arranged, norms)


def score_body(*refs, scale):
    *coefs, cand_ref, table_ref, score_ref, stat_ref = refs
    corr = lax.dot_general(
        table_ref[...],
        functools.reduce(jnp.add, [ref[...] for ref in coefs]),
        (((0,), (0,)), ((), ())),
        precision=lax.Precision.HIGHEST,
        preferred_element_type=jnp.float32,
    )
    score = jnp.where(cand_ref[0:1, :] >= 0.0, corr * scale, lowest)
    top = jnp.max(score, axis=0, keepdims=True)
    total = jnp.sum(jnp.exp(score - top), axis=0, keepdims=True)
    score_ref[...] = score
    stat_ref[0:1, :] = top
    stat_ref[1:2, :] = jnp.where(cand_ref[0:1, :] >= 0.0, total, 0.0)


def scores(coefs, cand, table, scale):
    total = cand.shape[1]
    return pl.pallas_call(
        functools.partial(score_body, scale=scale),
        out_shape=[
            jax.ShapeDtypeStruct((ROTS * CAND_OWN, total), jnp.float32),
            jax.ShapeDtypeStruct((2, total), jnp.float32),
        ],
        name="scores",
    )(*coefs, cand, table)


def swap_blocks(x, distance, width):
    lane = lax.broadcasted_iota(jnp.int32, x.shape, 1)
    bit = 1
    while bit <= distance:
        if distance & bit:
            shift = bit * width
            down = pltpu.roll(x, shift, 1)
            up = pltpu.roll(x, x.shape[1] - shift, 1)
            x = jnp.where((lane // shift) % 2 == 1, down, up)
        bit *= 2
    return x


def weights_body(at_ref, score_ref, cand_ref, stat_ref, table_ref, mix_ref, norm_ref):
    n_cls, _, total = stat_ref.shape
    width = total // n_cls
    tops, parts = [], []
    for e in range(n_cls):
        table = stat_ref[at_ref[0] ^ e]
        table = swap_blocks(jnp.concatenate([table] * 4, 0), e, width)
        tops.append(table[0:1])
        parts.append(table[1:2])
    top = functools.reduce(jnp.maximum, tops)
    summed = jnp.zeros_like(top)
    for other, part in zip(tops, parts):
        summed += part * jnp.exp(other - top)
    log_norm = top + jnp.log(summed)
    norm_ref[...] = log_norm[:, : norm_ref.shape[1]]
    weight = jnp.where(cand_ref[0:1, :] >= 0.0, jnp.exp(score_ref[...] - log_norm), 0.0)
    mix_ref[...] = lax.dot_general(
        table_ref[...],
        weight,
        (((1,), (0,)), ((), ())),
        precision=lax.Precision.HIGHEST,
        preferred_element_type=jnp.float32,
    )


def mixed_weights(cls, score, cand, stats, table, count):
    total = score.shape[1]
    return pl.pallas_call(
        weights_body,
        in_specs=[pl.BlockSpec(memory_space=pltpu.SMEM)] + [pl.BlockSpec(memory_space=pltpu.VMEM)] * 4,
        out_shape=[
            jax.ShapeDtypeStruct((COEF, total), jnp.float32),
            jax.ShapeDtypeStruct((1, count), jnp.float32),
        ],
        name="mixed_weights",
    )(cls, score, cand, stats, table)


def sums_body(*refs, number, pieces):
    blocks = refs[:number]
    refs = refs[number:]
    mixes, cands = refs[:pieces], refs[pieces : 2 * pieces]
    back_ref, out_ref, weight_ref, mix, cand, planes, held, sems = refs[2 * pieces :]
    step = pl.program_id(0)
    groups = weight_ref.shape[1]
    total = mix.shape[1]
    imag, odd = lane_signs()

    @pl.when(step == 0)
    def _():
        copies = fetch(blocks, held, sems)
        mixed = jnp.concatenate([ref[...] for ref in mixes], 1)
        chosen = jnp.concatenate([ref[...] for ref in cands], 1)
        hot = hot_masks(chosen, groups)
        summed = jnp.zeros((groups, total), jnp.float32)
        for q in range(CAND_OWN):
            summed += jnp.where(hot[q], mixed[q : q + 1], 0.0)
        weight_ref[...] = lax.dot_general(
            jnp.ones((1, total), jnp.float32),
            summed,
            (((1,), (1,)), ((), ())),
            precision=lax.Precision.HIGHEST,
            preferred_element_type=jnp.float32,
        )
        mix[...] = mixed
        cand[...] = chosen
        sign = jnp.where(imag == odd, 1.0, -1.0)
        for copy in copies[0]:
            copy.wait()

        def tail(t, weights):
            made = jnp.dot(
                weights, lanes_of(held, BODY + t // 2, 1), preferred_element_type=jnp.float32
            )
            g1, g2 = made[:groups], made[groups:]
            value = g1
            if t > 0:
                value = g1 + jnp.where(imag, -1.0, 1.0) * pltpu.roll(g2, LANES // 2, 1)
            rows = pl.ds((BODY + t // 2) * groups, groups)
            if t % 2:
                value = jnp.where(odd, value, planes[rows, :])
            planes[rows, :] = value

        for r in range(1, len(RANGES)):
            for copy in copies[r]:
                copy.wait()

            hot = hot_masks(cand[...], groups)
            block = 2 * CAND_OWN
            for g in range((r - 1) * RANGE, r * RANGE):
                mine = mix[g * block : (g + 1) * block, :]
                halves = []
                for ab in range(2):
                    dense = jnp.zeros((groups, total), jnp.float32)
                    for q in range(CAND_OWN):
                        at = ab * CAND_OWN + q
                        dense = jnp.where(hot[q], mine[at : at + 1], dense)
                    halves.append(dense)
                weights = jnp.concatenate(halves, 0).astype(jnp.bfloat16)
                made = jnp.dot(
                    weights, lanes_of(held, g * TURNS, TURNS), preferred_element_type=jnp.float32
                )
                for t in range(TURNS):
                    g1 = made[:groups, t * LANES : (t + 1) * LANES]
                    g2 = made[groups:, t * LANES : (t + 1) * LANES]
                    if g == 0:
                        value = jnp.where(odd, g2, g1)
                    else:
                        value = g1 + sign * pltpu.roll(g2, LANES // 2, 1)
                    start = (g * TURNS + t) * groups
                    planes[start : start + groups, :] = value
                if g < TAIL:
                    tail(g, weights)

    @pl.when(step > 0)
    def _():
        block, span, _ = out_ref.shape
        first = (step - 1) * block
        back = back_ref[...]
        values = []
        for c in range(block):
            turned = planes[pl.ds(first + c, CHUNKS, stride=groups), :].T
            for s in range(2):
                at = 2 * s * span
                values.append(
                    jnp.concatenate([turned[at : at + span], turned[at + span : at + 2 * span]], 1)
                )
        value = jnp.concatenate(values, 0)
        high = value.astype(jnp.bfloat16)
        low = (value - high.astype(jnp.float32)).astype(jnp.bfloat16)
        both = jnp.dot(
            jnp.concatenate([high, low], 0), back, preferred_element_type=jnp.float32
        )
        rows = value.shape[0]
        placed = both[:rows] + both[rows:]
        for c in range(block):
            for s in range(2):
                at = (2 * c + s) * span
                out_ref[c, :, s * HARM : (s + 1) * HARM] = placed[at : at + span]


def sums(blocks, mixes, cands, back, groups, span):
    number = len(blocks)
    count = blocks[0].shape[1]
    total = number * count
    size = blocks[0].size * number
    block = 8
    whole = lambda i: (0, 0)
    return pl.pallas_call(
        functools.partial(sums_body, number=number, pieces=len(mixes)),
        grid=(1 + groups // block,),
        in_specs=[
            *[pl.BlockSpec(memory_space=pl.ANY)] * number,
            *[pl.BlockSpec(array.shape, whole) for array in (*mixes, *cands, back)],
        ],
        out_specs=[
            pl.BlockSpec((block, span, 2 * HARM), lambda i: (jnp.maximum(i - 1, 0), 0, 0)),
            pl.BlockSpec((1, groups), whole),
        ],
        out_shape=[
            jax.ShapeDtypeStruct((groups, span, 2 * HARM), jnp.float32),
            jax.ShapeDtypeStruct((1, groups), jnp.float32),
        ],
        scratch_shapes=[
            pltpu.VMEM((COEF, total), jnp.float32),
            pltpu.VMEM((2 * CAND_OWN, total), jnp.float32),
            pltpu.VMEM((CHUNKS * groups, LANES), jnp.float32),
            pltpu.VMEM((number, *blocks[0].shape), jnp.bfloat16),
            pltpu.SemaphoreType.DMA((len(RANGES), number)),
        ],
        compiler_params=pltpu.CompilerParams(vmem_limit_bytes=60 << 20),
        cost_estimate=pl.CostEstimate(
            flops=4 * size * groups,
            bytes_accessed=2 * size + 8 * groups * span * HARM,
            transcendentals=0,
        ),
        name="sums",
    )(*blocks, *mixes, *cands, back)


def hop(value, axis, distance):
    size = lax.axis_size(axis)
    return lax.ppermute(value, axis, [(i, i ^ distance) for i in range(size)])


def after(value, *others):
    return lax.optimization_barrier((value, *others))[0]


def direct(own):
    n_cls = lax.axis_size("cls")
    return {1 << bit: hop(own, "cls", 1 << bit) for bit in range(1, n_cls.bit_length() - 1)}


def relayed(known, d, *others):
    n_cls = lax.axis_size("cls")
    for j in sorted(range(2, n_cls, 2), key=lambda j: bin(j).count("1")):
        if j not in known:
            bits = [bit for bit in range(1, n_cls.bit_length()) if j >> bit & 1]
            way = 1 << bits[d % len(bits)]
            known[j] = hop(after(known[j ^ way], *others), "cls", way)
    return known


def paired(known, each, last):
    n_cls = lax.axis_size("cls")
    for j in range(0, n_cls, 2):
        others = last if j == n_cls - 2 else each
        block = after(known[j], *others) if others else known[j]
        known[j + 1] = hop(block, "cls", 1)
    return [known[j] for j in range(n_cls)]


def gather_device(particles, references, owner_groups, class_order):
    n_cls, n_prt = lax.axis_size("cls"), lax.axis_size("prt")
    cls, prt = lax.axis_index("cls"), lax.axis_index("prt")
    count, cycles, width = particles.shape
    groups = references.shape[0]
    span = cycles // n_prt
    back = jnp.asarray(unselector(), jnp.bfloat16)
    table = jnp.asarray(rotation_table())
    picks = class_order[:, :, :CAND_OWN].reshape(count, OWN_TOP * CAND_OWN)
    meta = jnp.concatenate([owner_groups, picks], 1)
    cls, prt = (index.reshape(1).astype(jnp.int32) for index in (cls, prt))
    outgoing = []
    for first in range(0, n_prt, 2):
        distances = tuple(range(first, min(first + 2, n_prt)))
        place = after(prt, outgoing[0]) if outgoing else prt
        outgoing += arrange_particles(
            place, particles, meta, n_prt, distances
        )
    arrived = [outgoing[0]]
    known = [{0: arrived[0], **direct(arrived[0])}]
    for d in range(1, min(n_prt, 3)):
        arrived.append(hop(outgoing[d], "prt", d))
    early = after(arrived[1], outgoing[-1])
    known.append({0: early, **direct(early)})
    relayed(known[0], 0, outgoing[-1])
    place = after(prt, *arrived[1:2], *[known[0][1 << b] for b in range(1, n_cls.bit_length() - 1)])
    arranged, norms = arrange_references(references, place, n_prt)
    for d in range(2, n_prt):
        if d > 2:
            arrived.append(hop(after(outgoing[d], arrived[d - 1], arranged), "prt", d))
        own = after(arrived[d], arranged) if d == 2 else arrived[d]
        known.append({0: own, **direct(own)})
    for d in range(1, n_prt, 2):
        relayed(known[d], d)
    scale = 2.0 / math.sqrt(cycles * width)
    coefs, cands, sent, blocks = [], [], [], []
    for d in range(n_prt):
        waits = []
        if n_prt > 3:
            waits = [[known[1][2]], [arrived[3], known[2][n_cls // 2]], [known[3][2]], []][min(d, 3)]
        if d and d % 2 == 0:
            relayed(known[d], d, coefs[0])
        each = [arranged, known[1][n_cls // 2]] if d == 0 else coefs[:1] if d < 3 else []
        blocks.append(paired(known[d], each, coefs[-1:]))
        ready = after(arranged, *waits) if waits else arranged
        coef, cand = cross_coefficients(blocks[d], ready, norms, cls)
        coefs.append(coef)
        sent.append(hop(coef, "prt", d) if d else coef)
        cands.append(cand)
    score, stat = scores(sent, cands[0], table, scale)
    stats = lax.all_gather(stat.reshape(1, *stat.shape), "cls", axis=0, tiled=True)
    mix, log_norm = mixed_weights(cls, score, cands[0], stats, table, count)
    mixes = [hop(mix, "prt", d) if d else mix for d in range(n_prt)]
    class_sums, class_weights = sums(
        [block for piece in blocks for block in piece], mixes, cands, back, groups, span
    )
    own = log_norm[0]
    return class_sums, class_weights[0], own


def per_device(particles, references, owner_groups, class_order):
    n_cls, n_prt = lax.axis_size("cls"), lax.axis_size("prt")
    count, cycles, _ = particles.shape
    groups = references.shape[0]
    cap = max(2, 2 * count * OWN_TOP // n_cls)
    powers = n_cls & (n_cls - 1) == 0 and n_prt & (n_prt - 1) == 0
    fits = 4 * cycles == LANES * n_prt and n_cls * CAND_OWN <= LANES and groups % 16 == 0 and n_cls >= 4 and n_prt >= 4
    fits = fits and powers and n_cls * count == LANES
    plan = gather_device if cap >= count and fits else dispatch_device
    return plan(particles, references, owner_groups, class_order)


def solution(mesh):
    in_specs = (
        P(("cls", "prt"), None, None),
        P("cls", None, None),
        P(("cls", "prt"), None),
        P(("cls", "prt"), None, None),
    )
    out_specs = (P("cls", "prt", None), P("cls"), P(("cls", "prt")))
    return jax.shard_map(
        per_device, mesh=mesh, in_specs=in_specs, out_specs=out_specs, check_vma=False
    )
```

```python
import functools
import math

import jax
import jax.numpy as jnp
import numpy as np
from jax import lax
from jax.experimental import pallas as pl
from jax.experimental.pallas import tpu as pltpu
from jax.sharding import PartitionSpec as P

CYCLES = 128
HARM = 256
ROTS = 36
OWN_TOP = 4
CAND_OWN = 4


lowest = -1e30


def spectral_tables():
    harmonic = jnp.arange(HARM, dtype=jnp.float32)
    angles = 2.0 * math.pi * jnp.arange(ROTS, dtype=jnp.float32) / ROTS
    phase = harmonic[:, None] * angles[None, :]
    forward = jnp.concatenate([jnp.cos(phase), jnp.sin(phase)], 0)
    backward = jnp.concatenate([jnp.cos(phase), -jnp.sin(phase)], 0).T
    return (forward, backward)


def class_accumulate(lanes, mixed):
    l_re = lanes[..., :HARM]
    l_im = lanes[..., HARM:]
    y_re = mixed[..., :HARM]
    y_im = mixed[..., HARM:]
    s_re = jnp.einsum("lrm,lcm->crm", l_re, y_re, preferred_element_type=jnp.float32) - jnp.einsum(
        "lrm,lcm->crm", l_im, y_im, preferred_element_type=jnp.float32
    )
    s_im = jnp.einsum("lrm,lcm->crm", l_re, y_im, preferred_element_type=jnp.float32) + jnp.einsum(
        "lrm,lcm->crm", l_im, y_re, preferred_element_type=jnp.float32
    )
    return jnp.concatenate([s_re, s_im], -1)


def dispatch_device(particles, references, owner_groups, class_order):
    n_cls = lax.axis_size("cls")
    count = particles.shape[0]
    groups = references.shape[0]
    cap = max(2, 2 * count * OWN_TOP // n_cls)
    slots = n_cls * cap
    width = 2 * HARM
    flat_owner = owner_groups.reshape(-1)
    owner_hot = (flat_owner[:, None] == jnp.arange(n_cls, dtype=jnp.int32)[None, :]).astype(
        jnp.int32
    )
    before = jnp.cumsum(owner_hot, axis=0) - owner_hot
    rank = jnp.sum(before * owner_hot, axis=1)
    slot_of = flat_owner * cap + rank
    match = slot_of[None, :] == jnp.arange(slots, dtype=jnp.int32)[:, None]
    member = jnp.any(match.reshape(slots, count, OWN_TOP), axis=2)
    filled = jnp.any(member, axis=1)
    dispatch = member.astype(jnp.bfloat16)
    outgoing = jnp.dot(
        dispatch, particles.reshape(count, CYCLES * width), preferred_element_type=jnp.float32
    )
    outgoing = outgoing.astype(jnp.bfloat16).reshape(n_cls, cap, CYCLES, width)
    match_int = match.astype(jnp.int32)
    picks = class_order[:, :, :CAND_OWN].reshape(count * OWN_TOP, CAND_OWN)
    slot_cand = jnp.where(filled[:, None], jnp.dot(match_int, picks), -1)
    owner_rows = jnp.repeat(jnp.arange(count, dtype=jnp.int32), OWN_TOP)
    slot_pid = jnp.where(filled, jnp.dot(match_int, owner_rows), -1)
    labels_out = jnp.concatenate([slot_cand, slot_pid[:, None]], 1).reshape(
        n_cls, cap, CAND_OWN + 1
    )
    arrived, labels = (
        lax.all_to_all(outgoing, "cls", split_axis=0, concat_axis=0, tiled=True),
        lax.all_to_all(labels_out, "cls", split_axis=0, concat_axis=0, tiled=True),
    )
    lanes = arrived.reshape(slots, CYCLES, width)
    labels = labels.reshape(slots, CAND_OWN + 1)
    forward, backward = spectral_tables()
    scale = 2.0 / math.sqrt(CYCLES * width)
    norms = jnp.sum(jnp.square(references.astype(jnp.float32)), axis=(1, 2))
    l_re = lanes[..., :HARM]
    l_im = lanes[..., HARM:]
    r_re = references[..., :HARM]
    r_im = references[..., HARM:]
    x_re = jnp.einsum("lrm,crm->lcm", l_re, r_re, preferred_element_type=jnp.float32) + jnp.einsum(
        "lrm,crm->lcm", l_im, r_im, preferred_element_type=jnp.float32
    )
    x_im = jnp.einsum("lrm,crm->lcm", l_im, r_re, preferred_element_type=jnp.float32) - jnp.einsum(
        "lrm,crm->lcm", l_re, r_im, preferred_element_type=jnp.float32
    )
    cross = jnp.concatenate([x_re, x_im], -1)
    corr = jnp.dot(
        cross.reshape(slots * groups, width), forward, precision=lax.Precision.HIGHEST
    ).reshape(slots, groups, ROTS)
    score = (corr - 0.5 * norms[None, :, None]) * scale
    candidate = jnp.any(
        labels[:, :CAND_OWN, None] == jnp.arange(groups, dtype=jnp.int32)[None, None, :], axis=1
    )
    part_max = jnp.max(jnp.where(candidate[:, :, None], score, lowest), axis=(1, 2))
    part_sum = jnp.sum(
        jnp.where(candidate[:, :, None], jnp.exp(score - part_max[:, None, None]), 0.0), axis=(1, 2)
    )
    sender_ids = labels[:, CAND_OWN].astype(jnp.float32)
    table_max, table_sum, table_ids = (
        lax.all_gather(part_max.reshape(1, n_cls, cap), "cls", axis=0, tiled=True),
        lax.all_gather(part_sum.reshape(1, n_cls, cap), "cls", axis=0, tiled=True),
        lax.all_gather(sender_ids.reshape(1, n_cls, cap), "cls", axis=0, tiled=True),
    )
    local_ids = jnp.arange(count, dtype=jnp.float32)
    hit = table_ids[..., None] == local_ids
    top = jnp.max(jnp.where(hit, table_max[..., None], lowest), axis=(0, 2))
    total = jnp.sum(
        jnp.where(
            hit, table_sum[..., None] * jnp.exp(table_max[..., None] - top[None, :, None, :]), 0.0
        ),
        axis=(0, 2),
    )
    table_norm = top + jnp.log(total)
    slot_ids = labels[:, CAND_OWN].reshape(n_cls, cap)
    slot_norm = jnp.sum(
        jnp.where(
            slot_ids[..., None] == jnp.arange(count, dtype=jnp.int32), table_norm[:, None, :], 0.0
        ),
        axis=2,
    ).reshape(slots)
    own_norm = lax.dynamic_index_in_dim(table_norm, lax.axis_index("cls"), 0, keepdims=False)
    weight = jnp.where(candidate[:, :, None], jnp.exp(score - slot_norm[:, None, None]), 0.0)
    mixed = (
        jnp.dot(weight.reshape(slots * groups, ROTS), backward, precision=lax.Precision.HIGHEST)
        .astype(jnp.bfloat16)
        .reshape(slots, groups, width)
    )
    class_weights = lax.psum(jnp.sum(weight, axis=(0, 2)), "prt")
    partial_sums = class_accumulate(lanes, mixed)
    class_sums = lax.psum_scatter(partial_sums, "prt", scatter_dimension=1, tiled=True)
    return (class_sums, class_weights, own_norm)


LANES = 128


def harmonic_plan():
    half = ROTS // 2
    turns = HARM // ROTS
    tail = HARM - turns * ROTS
    chunk_of = np.zeros(HARM, np.int32)
    side_of = np.zeros(HARM, np.int32)
    for m in range(HARM):
        turn, rest = divmod(m, ROTS)
        if turn == turns:
            chunk_of[m] = half * turns + rest // 2
            side_of[m] = rest % 2
        elif rest < half:
            chunk_of[m] = rest * turns + turn
        else:
            chunk_of[m] = ((ROTS - rest) % half) * turns + turn
            side_of[m] = 1
    return half, turns, tail, chunk_of, side_of


HALF, TURNS, TAIL, CHUNK_OF, SIDE_OF = harmonic_plan()
BODY = HALF * TURNS
CHUNKS = BODY + TAIL // 2
EXTRA = TAIL // 2 + 1
COEF = 2 * HALF * CAND_OWN
RANGE = 6
RANGES = ((BODY, CHUNKS + 1),) + tuple(
    (first * TURNS, (first + RANGE) * TURNS) for first in range(0, HALF, RANGE)
)


def selector():
    return (np.arange(CHUNKS)[:, None] == CHUNK_OF[None, :]).astype(np.float32)


def unselector():
    sel = selector()
    return np.concatenate([sel * (SIDE_OF == 0), sel * (SIDE_OF == 1)], 0)


def rotation_table():
    table = np.zeros((HALF, 2, CAND_OWN, ROTS, CAND_OWN))
    angle = 2.0 * np.pi * np.arange(ROTS) / ROTS
    for g in range(HALF):
        first = np.cos(g * angle)
        second = np.cos(HALF * angle) if g == 0 else np.sin(g * angle)
        for q in range(CAND_OWN):
            table[g, 0, q, :, q] = first
            table[g, 1, q, :, q] = second
    return table.reshape(COEF, ROTS * CAND_OWN).astype(np.float32)


def nt_dot(a, b):
    return lax.dot_general(a, b, (((1,), (1,)), ((), ())), preferred_element_type=jnp.float32)


def selector_masks():
    m = lax.broadcasted_iota(jnp.int32, (1, HARM), 1)
    turn = jnp.zeros((1, HARM), jnp.int32)
    for t in range(1, TURNS + 1):
        turn += jnp.where(m >= t * ROTS, 1, 0)
    rest = m - ROTS * turn
    back = jnp.where(rest == HALF, 0, ROTS - rest)
    chunk = jnp.where(rest < HALF, rest, back) * TURNS + turn
    side = jnp.where(rest < HALF, 0, 1)
    chunk = jnp.where(turn == TURNS, BODY + rest // 2, chunk)
    side = jnp.where(turn == TURNS, rest % 2, side)
    rows = lax.broadcasted_iota(jnp.int32, (CHUNKS, HARM), 0)
    sel = jnp.where(rows == chunk, 1.0, 0.0).astype(jnp.bfloat16)
    sides = lax.broadcasted_iota(jnp.int32, (2, HARM), 0)
    masks = jnp.where(sides == side, 1.0, 0.0).astype(jnp.bfloat16)
    return sel, masks


def masked_stack(piece, masks):
    parts = []
    for s in range(2):
        for b in range(2):
            parts.append(piece[:, s * HARM : (s + 1) * HARM] * masks[b : b + 1])
    return jnp.concatenate(parts, 0)


def repeat(number, step, body, carry):
    def several(i, carry):
        for u in range(step):
            carry = body(i * step + u, carry)
        return carry

    return lax.fori_loop(0, number // step, several, carry)


def particle_body(at_ref, x_ref, meta_ref, *refs, distances, n_prt):
    outs, scr = refs[:-1], refs[-1]
    count, cycles, _ = x_ref.shape
    number = len(outs)
    span = cycles // n_prt
    sel, masks = selector_masks()

    def one(n, carry):
        parts = []
        for d in distances:
            start = pl.multiple_of((at_ref[0] ^ d) * span, span)
            parts.append(masked_stack(x_ref[n, pl.ds(start, span), :], masks))
        w = jnp.concatenate(parts, 0)
        y = nt_dot(sel, w)
        for p in range(number):
            scr[p, pl.ds(pl.multiple_of(n * CHUNKS, CHUNKS), CHUNKS), :] = y[
                :, p * LANES : (p + 1) * LANES
            ]
        return carry

    repeat(count, 4, one, 0)

    def two(c, carry):
        for p in range(number):
            outs[p][c] = scr[p, pl.ds(c, count, stride=CHUNKS), :].astype(jnp.bfloat16)
        return carry

    repeat(CHUNKS, 8, two, 0)
    lane = lax.broadcasted_iota(jnp.int32, (count, LANES), 1)
    label = jnp.full((count, LANES), -1, jnp.int32)
    for t in range(OWN_TOP):
        mine = (lane // CAND_OWN) == meta_ref[:, t : t + 1]
        for q in range(CAND_OWN):
            at = OWN_TOP + t * CAND_OWN + q
            label = jnp.where(
                mine & (lane % CAND_OWN == q), meta_ref[:, at : at + 1], label
            )
    label = label.astype(jnp.float32).astype(jnp.bfloat16)
    for p in range(number):
        outs[p][CHUNKS] = label


def arrange_particles(prt, particles, meta, n_prt, distances):
    count = particles.shape[0]
    number = len(distances)
    size = particles.size * number // n_prt
    return pl.pallas_call(
        functools.partial(particle_body, distances=distances, n_prt=n_prt),
        in_specs=[pl.BlockSpec(memory_space=pltpu.SMEM)] + [pl.BlockSpec(memory_space=pltpu.VMEM)] * 2,
        out_shape=[jax.ShapeDtypeStruct((CHUNKS + 1, count, LANES), jnp.bfloat16)] * number,
        scratch_shapes=[pltpu.VMEM((number, count * CHUNKS, LANES), jnp.float32)],
        compiler_params=pltpu.CompilerParams(vmem_limit_bytes=32 << 20),
        cost_estimate=pl.CostEstimate(
            flops=size * 2 * CHUNKS, bytes_accessed=size * 4, transcendentals=0
        ),
        name="arrange_particles",
    )(prt, particles, meta)


def reference_body(at_ref, x_ref, out_ref, norm_ref, scr):
    rows = x_ref.shape[0]
    sel, masks = selector_masks()
    step = 4

    def one(n, carry):
        w = jnp.concatenate([masked_stack(x_ref[n * step + i], masks) for i in range(step)], 0)
        y = nt_dot(sel, w)
        for i in range(step):
            scr[pl.ds(pl.multiple_of((n * step + i) * CHUNKS, CHUNKS), CHUNKS), :] = y[
                :, i * LANES : (i + 1) * LANES
            ]
        return carry

    repeat(rows // step, 2, one, 0)

    def two(c, carry):
        value = scr[pl.ds(c, rows, stride=CHUNKS), :]
        out_ref[c] = value.astype(jnp.bfloat16)
        return carry + value * value

    norm_ref[...] = repeat(CHUNKS, 8, two, jnp.zeros((rows, LANES), jnp.float32))


def arrange_references(references, prt, n_prt):
    groups, cycles, width = references.shape
    span = cycles // n_prt
    block = 16
    return pl.pallas_call(
        reference_body,
        grid_spec=pltpu.PrefetchScalarGridSpec(
            num_scalar_prefetch=1,
            grid=(groups // block,),
            in_specs=[
                pl.BlockSpec((block, span, width), lambda i, at: (i, at[0], 0)),
            ],
            out_specs=[
                pl.BlockSpec((CHUNKS, block, LANES), lambda i, at: (0, i, 0)),
                pl.BlockSpec((block, LANES), lambda i, at: (i, 0)),
            ],
            scratch_shapes=[pltpu.VMEM((block * CHUNKS, LANES), jnp.float32)],
        ),
        out_shape=[
            jax.ShapeDtypeStruct((CHUNKS, groups, LANES), jnp.bfloat16),
            jax.ShapeDtypeStruct((groups, LANES), jnp.float32),
        ],
        compiler_params=pltpu.CompilerParams(vmem_limit_bytes=60 << 20),
        cost_estimate=pl.CostEstimate(
            flops=groups * span * width * 2 * CHUNKS,
            bytes_accessed=groups * span * width * 4,
            transcendentals=0,
        ),
        name="arrange_references",
    )(prt, references)


def lane_signs():
    lane = lax.broadcasted_iota(jnp.int32, (1, LANES), 1)
    quarter = LANES // 4
    imag = lane >= 2 * quarter
    odd = (lane // quarter) % 2 == 1
    return imag, odd


def lanes_of(held, first, number):
    parts = []
    for i in range(number):
        parts.append(jnp.concatenate([held[j, first + i] for j in range(held.shape[0])], 0))
    return jnp.concatenate(parts, 1) if number > 1 else parts[0]


def fetch(blocks, held, sems):
    copies = []
    for r, (first, last) in enumerate(RANGES):
        chunks = pl.ds(first, last - first)
        copies.append(
            [
                pltpu.make_async_copy(block.at[chunks], held.at[j, chunks], sems.at[r, j])
                for j, block in enumerate(blocks)
            ]
        )
    for group in copies:
        for copy in group:
            copy.start()
    return copies


def hot_masks(cand, groups):
    rows = lax.broadcasted_iota(jnp.int32, (groups, cand.shape[1]), 0).astype(jnp.float32)
    return [rows == cand[q : q + 1] for q in range(CAND_OWN)]


def residue_weights(q_ref, g):
    imag, odd = lane_signs()
    sign = jnp.where(imag == odd, -1.0, 1.0)
    first, second = [], []
    for i in range(TURNS):
        q = q_ref[g * TURNS + i].astype(jnp.float32)
        turned = pltpu.roll(q, LANES // 2, 1) * sign
        if g == 0:
            first.append(jnp.where(odd, 0.0, q))
            second.append(jnp.where(odd, q, 0.0))
        else:
            first.append(q)
            second.append(turned)
    return jnp.concatenate(
        [jnp.concatenate(first, 1), jnp.concatenate(second, 1)], 0
    ).astype(jnp.bfloat16)


def chosen_rows(acc, cand):
    groups = acc.shape[0] // 2
    hot = hot_masks(cand, groups)
    rows = []
    for ab in range(2):
        part = acc[ab * groups : (ab + 1) * groups, :]
        for q in range(CAND_OWN):
            rows.append(jnp.sum(jnp.where(hot[q], part, 0.0), axis=0, keepdims=True))
    return jnp.concatenate(rows, 0)


def cross_body(at_ref, *refs):
    blocks = refs[:-6]
    q_ref, norm_ref, coef_ref, cand_ref, held, sems = refs[-6:]
    groups = q_ref.shape[1]
    imag, odd = lane_signs()
    copies = fetch(blocks, held, sems)
    for copy in copies[0]:
        copy.wait()
    label = lanes_of(held, CHUNKS, 1).astype(jnp.float32).T
    row = lax.broadcasted_iota(jnp.int32, label.shape, 0)
    base = at_ref[0] * CAND_OWN
    for q in range(CAND_OWN):
        cand_ref[q : q + 1, :] = jnp.sum(
            jnp.where(row == base + q, label, 0.0), axis=0, keepdims=True
        )
    cand_ref[CAND_OWN:, :] = jnp.full(
        (cand_ref.shape[0] - CAND_OWN, cand_ref.shape[1]), -1.0, jnp.float32
    )

    def tail(i):
        q = q_ref[BODY + i // 2].astype(jnp.float32)
        keep = odd if i % 2 else ~odd
        a = jnp.where(keep, q, 0.0)
        turned = pltpu.roll(q, LANES // 2, 1) * jnp.where(imag, 1.0, -1.0)
        b = jnp.where(keep, turned, 0.0)
        if i == 0:
            b = jnp.zeros_like(b)
        w = jnp.concatenate([a, b], 0).astype(jnp.bfloat16)
        return nt_dot(w, lanes_of(held, BODY + i // 2, 1))

    for r in range(1, len(RANGES)):
        for copy in copies[r]:
            copy.wait()

        for g in range((r - 1) * RANGE, r * RANGE):
            acc = nt_dot(residue_weights(q_ref, g), lanes_of(held, g * TURNS, TURNS))
            if g < TAIL:
                acc += tail(g)
            if g == 0:
                half_norm = 0.5 * jnp.sum(norm_ref[...], axis=1, keepdims=True)
                acc = jnp.concatenate([acc[:groups] - half_norm, acc[groups:]], 0)
            block = 2 * CAND_OWN
            coef_ref[g * block : (g + 1) * block, :] = chosen_rows(acc, cand_ref[...])


def cross_coefficients(blocks, arranged, norms, cls):
    number = len(blocks)
    count = blocks[0].shape[1]
    groups = arranged.shape[1]
    total = number * count
    size = blocks[0].size * number
    block = 2 * CAND_OWN
    return pl.pallas_call(
        cross_body,
        in_specs=[pl.BlockSpec(memory_space=pltpu.SMEM)]
        + [pl.BlockSpec(memory_space=pl.ANY)] * number
        + [pl.BlockSpec(memory_space=pltpu.VMEM)] * 2,
        out_shape=[
            jax.ShapeDtypeStruct((COEF, total), jnp.float32),
            jax.ShapeDtypeStruct((block, total), jnp.float32),
        ],
        scratch_shapes=[
            pltpu.VMEM((number, *blocks[0].shape), jnp.bfloat16),
            pltpu.SemaphoreType.DMA((len(RANGES), number)),
        ],
        compiler_params=pltpu.CompilerParams(vmem_limit_bytes=60 << 20),
        cost_estimate=pl.CostEstimate(
            flops=4 * size * groups, bytes_accessed=2 * size, transcendentals=0
        ),
        name="cross_coefficients",
    )(cls, *blocks, arranged, norms)


def score_body(*refs, scale):
    *coefs, cand_ref, table_ref, score_ref, stat_ref = refs
    corr = lax.dot_general(
        table_ref[...],
        functools.reduce(jnp.add, [ref[...] for ref in coefs]),
        (((0,), (0,)), ((), ())),
        precision=lax.Precision.HIGHEST,
        preferred_element_type=jnp.float32,
    )
    score = jnp.where(cand_ref[0:1, :] >= 0.0, corr * scale, lowest)
    top = jnp.max(score, axis=0, keepdims=True)
    total = jnp.sum(jnp.exp(score - top), axis=0, keepdims=True)
    score_ref[...] = score
    stat_ref[0:1, :] = top
    stat_ref[1:2, :] = jnp.where(cand_ref[0:1, :] >= 0.0, total, 0.0)


def scores(coefs, cand, table, scale):
    total = cand.shape[1]
    return pl.pallas_call(
        functools.partial(score_body, scale=scale),
        out_shape=[
            jax.ShapeDtypeStruct((ROTS * CAND_OWN, total), jnp.float32),
            jax.ShapeDtypeStruct((2, total), jnp.float32),
        ],
        name="scores",
    )(*coefs, cand, table)


def swap_blocks(x, distance, width):
    lane = lax.broadcasted_iota(jnp.int32, x.shape, 1)
    bit = 1
    while bit <= distance:
        if distance & bit:
            shift = bit * width
            down = pltpu.roll(x, shift, 1)
            up = pltpu.roll(x, x.shape[1] - shift, 1)
            x = jnp.where((lane // shift) % 2 == 1, down, up)
        bit *= 2
    return x


def weights_body(at_ref, score_ref, cand_ref, stat_ref, table_ref, mix_ref, norm_ref):
    n_cls, _, total = stat_ref.shape
    width = total // n_cls
    tops, parts = [], []
    for e in range(n_cls):
        table = stat_ref[at_ref[0] ^ e]
        table = swap_blocks(jnp.concatenate([table] * 4, 0), e, width)
        tops.append(table[0:1])
        parts.append(table[1:2])
    top = functools.reduce(jnp.maximum, tops)
    summed = jnp.zeros_like(top)
    for other, part in zip(tops, parts):
        summed += part * jnp.exp(other - top)
    log_norm = top + jnp.log(summed)
    norm_ref[...] = log_norm[:, : norm_ref.shape[1]]
    weight = jnp.where(cand_ref[0:1, :] >= 0.0, jnp.exp(score_ref[...] - log_norm), 0.0)
    mix_ref[...] = lax.dot_general(
        table_ref[...],
        weight,
        (((1,), (0,)), ((), ())),
        precision=lax.Precision.HIGHEST,
        preferred_element_type=jnp.float32,
    )


def mixed_weights(cls, score, cand, stats, table, count):
    total = score.shape[1]
    return pl.pallas_call(
        weights_body,
        in_specs=[pl.BlockSpec(memory_space=pltpu.SMEM)] + [pl.BlockSpec(memory_space=pltpu.VMEM)] * 4,
        out_shape=[
            jax.ShapeDtypeStruct((COEF, total), jnp.float32),
            jax.ShapeDtypeStruct((1, count), jnp.float32),
        ],
        name="mixed_weights",
    )(cls, score, cand, stats, table)


def sums_body(*refs, number, pieces):
    blocks = refs[:number]
    refs = refs[number:]
    mixes, cands = refs[:pieces], refs[pieces : 2 * pieces]
    back_ref, out_ref, weight_ref, mix, cand, planes, held, sems = refs[2 * pieces :]
    step = pl.program_id(0)
    groups = weight_ref.shape[1]
    total = mix.shape[1]
    imag, odd = lane_signs()

    @pl.when(step == 0)
    def _():
        copies = fetch(blocks, held, sems)
        mixed = jnp.concatenate([ref[...] for ref in mixes], 1)
        chosen = jnp.concatenate([ref[...] for ref in cands], 1)
        hot = hot_masks(chosen, groups)
        summed = jnp.zeros((groups, total), jnp.float32)
        for q in range(CAND_OWN):
            summed += jnp.where(hot[q], mixed[q : q + 1], 0.0)
        weight_ref[...] = lax.dot_general(
            jnp.ones((1, total), jnp.float32),
            summed,
            (((1,), (1,)), ((), ())),
            precision=lax.Precision.HIGHEST,
            preferred_element_type=jnp.float32,
        )
        mix[...] = mixed
        cand[...] = chosen
        sign = jnp.where(imag == odd, 1.0, -1.0)
        for copy in copies[0]:
            copy.wait()

        def tail(t, weights):
            made = jnp.dot(
                weights, lanes_of(held, BODY + t // 2, 1), preferred_element_type=jnp.float32
            )
            g1, g2 = made[:groups], made[groups:]
            value = g1
            if t > 0:
                value = g1 + jnp.where(imag, -1.0, 1.0) * pltpu.roll(g2, LANES // 2, 1)
            rows = pl.ds((BODY + t // 2) * groups, groups)
            if t % 2:
                value = jnp.where(odd, value, planes[rows, :])
            planes[rows, :] = value

        for r in range(1, len(RANGES)):
            for copy in copies[r]:
                copy.wait()

            hot = hot_masks(cand[...], groups)
            block = 2 * CAND_OWN
            for g in range((r - 1) * RANGE, r * RANGE):
                mine = mix[g * block : (g + 1) * block, :]
                halves = []
                for ab in range(2):
                    dense = jnp.zeros((groups, total), jnp.float32)
                    for q in range(CAND_OWN):
                        at = ab * CAND_OWN + q
                        dense = jnp.where(hot[q], mine[at : at + 1], dense)
                    halves.append(dense)
                weights = jnp.concatenate(halves, 0).astype(jnp.bfloat16)
                made = jnp.dot(
                    weights, lanes_of(held, g * TURNS, TURNS), preferred_element_type=jnp.float32
                )
                for t in range(TURNS):
                    g1 = made[:groups, t * LANES : (t + 1) * LANES]
                    g2 = made[groups:, t * LANES : (t + 1) * LANES]
                    if g == 0:
                        value = jnp.where(odd, g2, g1)
                    else:
                        value = g1 + sign * pltpu.roll(g2, LANES // 2, 1)
                    start = (g * TURNS + t) * groups
                    planes[start : start + groups, :] = value
                if g < TAIL:
                    tail(g, weights)

    @pl.when(step > 0)
    def _():
        block, span, _ = out_ref.shape
        first = (step - 1) * block
        back = back_ref[...]
        values = []
        for c in range(block):
            turned = planes[pl.ds(first + c, CHUNKS, stride=groups), :].T
            for s in range(2):
                at = 2 * s * span
                values.append(
                    jnp.concatenate([turned[at : at + span], turned[at + span : at + 2 * span]], 1)
                )
        value = jnp.concatenate(values, 0)
        high = value.astype(jnp.bfloat16)
        low = (value - high.astype(jnp.float32)).astype(jnp.bfloat16)
        both = jnp.dot(
            jnp.concatenate([high, low], 0), back, preferred_element_type=jnp.float32
        )
        rows = value.shape[0]
        placed = both[:rows] + both[rows:]
        for c in range(block):
            for s in range(2):
                at = (2 * c + s) * span
                out_ref[c, :, s * HARM : (s + 1) * HARM] = placed[at : at + span]


def sums(blocks, mixes, cands, back, groups, span):
    number = len(blocks)
    count = blocks[0].shape[1]
    total = number * count
    size = blocks[0].size * number
    block = 8
    whole = lambda i: (0, 0)
    return pl.pallas_call(
        functools.partial(sums_body, number=number, pieces=len(mixes)),
        grid=(1 + groups // block,),
        in_specs=[
            *[pl.BlockSpec(memory_space=pl.ANY)] * number,
            *[pl.BlockSpec(array.shape, whole) for array in (*mixes, *cands, back)],
        ],
        out_specs=[
            pl.BlockSpec((block, span, 2 * HARM), lambda i: (jnp.maximum(i - 1, 0), 0, 0)),
            pl.BlockSpec((1, groups), whole),
        ],
        out_shape=[
            jax.ShapeDtypeStruct((groups, span, 2 * HARM), jnp.float32),
            jax.ShapeDtypeStruct((1, groups), jnp.float32),
        ],
        scratch_shapes=[
            pltpu.VMEM((COEF, total), jnp.float32),
            pltpu.VMEM((2 * CAND_OWN, total), jnp.float32),
            pltpu.VMEM((CHUNKS * groups, LANES), jnp.float32),
            pltpu.VMEM((number, *blocks[0].shape), jnp.bfloat16),
            pltpu.SemaphoreType.DMA((len(RANGES), number)),
        ],
        compiler_params=pltpu.CompilerParams(vmem_limit_bytes=60 << 20),
        cost_estimate=pl.CostEstimate(
            flops=4 * size * groups,
            bytes_accessed=2 * size + 8 * groups * span * HARM,
            transcendentals=0,
        ),
        name="sums",
    )(*blocks, *mixes, *cands, back)


def hop(value, axis, distance):
    size = lax.axis_size(axis)
    return lax.ppermute(value, axis, [(i, i ^ distance) for i in range(size)])


def after(value, *others):
    return lax.optimization_barrier((value, *others))[0]


def direct(own):
    n_cls = lax.axis_size("cls")
    return {1 << bit: hop(own, "cls", 1 << bit) for bit in range(1, n_cls.bit_length() - 1)}


def relayed(known, d, *others):
    n_cls = lax.axis_size("cls")
    for j in sorted(range(2, n_cls, 2), key=lambda j: bin(j).count("1")):
        if j not in known:
            bits = [bit for bit in range(1, n_cls.bit_length()) if j >> bit & 1]
            way = 1 << bits[d % len(bits)]
            known[j] = hop(after(known[j ^ way], *others), "cls", way)
    return known


def paired(known, each, last):
    n_cls = lax.axis_size("cls")
    for j in range(0, n_cls, 2):
        others = last if j == n_cls - 2 else each
        block = after(known[j], *others) if others else known[j]
        known[j + 1] = hop(block, "cls", 1)
    return [known[j] for j in range(n_cls)]


def gather_device(particles, references, owner_groups, class_order):
    n_cls, n_prt = lax.axis_size("cls"), lax.axis_size("prt")
    cls, prt = lax.axis_index("cls"), lax.axis_index("prt")
    count, cycles, width = particles.shape
    groups = references.shape[0]
    span = cycles // n_prt
    back = jnp.asarray(unselector(), jnp.bfloat16)
    table = jnp.asarray(rotation_table())
    picks = class_order[:, :, :CAND_OWN].reshape(count, OWN_TOP * CAND_OWN)
    meta = jnp.concatenate([owner_groups, picks], 1)
    cls, prt = (index.reshape(1).astype(jnp.int32) for index in (cls, prt))
    outgoing = []
    for distances in (tuple(range(min(n_prt, 3))), tuple(range(3, n_prt))):
        place = after(prt, outgoing[0]) if outgoing else prt
        outgoing += arrange_particles(
            place, particles, meta, n_prt, distances
        )
    arrived = [outgoing[0]]
    known = [{0: arrived[0], **direct(arrived[0])}]
    for d in range(1, min(n_prt, 3)):
        arrived.append(hop(outgoing[d], "prt", d))
    early = after(arrived[1], outgoing[-1])
    known.append({0: early, **direct(early)})
    relayed(known[0], 0, outgoing[-1], arrived[2])
    place = after(prt, *arrived[1:2], *[known[0][1 << b] for b in range(1, n_cls.bit_length() - 1)])
    arranged, norms = arrange_references(references, place, n_prt)
    for d in range(2, n_prt):
        if d > 2:
            arrived.append(hop(after(outgoing[d], arrived[d - 1]), "prt", d))
        own = after(arrived[d], arranged) if d == 2 else arrived[d]
        known.append({0: own, **direct(own)})
    for d in range(1, n_prt, 2):
        relayed(known[d], d)
    scale = 2.0 / math.sqrt(cycles * width)
    coefs, cands, sent, blocks = [], [], [], []
    for d in range(n_prt):
        waits = []
        if n_prt > 3:
            waits = [[known[1][2]], [arrived[3], known[2][n_cls // 2]], [known[3][2]], []][min(d, 3)]
        if d and d % 2 == 0:
            relayed(known[d], d, coefs[0])
        each = [arranged, known[1][n_cls // 2]] if d == 0 else coefs[:1] if d < 3 else []
        blocks.append(paired(known[d], each, coefs[-1:]))
        ready = after(arranged, *waits) if waits else arranged
        coef, cand = cross_coefficients(blocks[d], ready, norms, cls)
        coefs.append(coef)
        sent.append(hop(coef, "prt", d) if d else coef)
        cands.append(cand)
    score, stat = scores(sent, cands[0], table, scale)
    stats = lax.all_gather(stat.reshape(1, *stat.shape), "cls", axis=0, tiled=True)
    mix, log_norm = mixed_weights(cls, score, cands[0], stats, table, count)
    mixes = [hop(mix, "prt", d) if d else mix for d in range(n_prt)]
    class_sums, class_weights = sums(
        [block for piece in blocks for block in piece], mixes, cands, back, groups, span
    )
    own = log_norm[0]
    return class_sums, class_weights[0], own


def per_device(particles, references, owner_groups, class_order):
    n_cls, n_prt = lax.axis_size("cls"), lax.axis_size("prt")
    count, cycles, _ = particles.shape
    groups = references.shape[0]
    cap = max(2, 2 * count * OWN_TOP // n_cls)
    powers = n_cls & (n_cls - 1) == 0 and n_prt & (n_prt - 1) == 0
    fits = 4 * cycles == LANES * n_prt and n_cls * CAND_OWN <= LANES and groups % 16 == 0 and n_cls >= 4 and n_prt >= 4
    fits = fits and powers and n_cls * count == LANES
    plan = gather_device if cap >= count and fits else dispatch_device
    return plan(particles, references, owner_groups, class_order)


def solution(mesh):
    in_specs = (
        P(("cls", "prt"), None, None),
        P("cls", None, None),
        P(("cls", "prt"), None),
        P(("cls", "prt"), None, None),
    )
    out_specs = (P("cls", "prt", None), P("cls"), P(("cls", "prt")))
    return jax.shard_map(
        per_device, mesh=mesh, in_specs=in_specs, out_specs=out_specs, check_vma=False
    )
```

```python
import functools
import math

import jax
import jax.numpy as jnp
import numpy as np
from jax import lax
from jax.experimental import pallas as pl
from jax.experimental.pallas import tpu as pltpu
from jax.sharding import PartitionSpec as P

CYCLES = 128
HARM = 256
ROTS = 36
OWN_TOP = 4
CAND_OWN = 4


lowest = -1e30


def spectral_tables():
    harmonic = jnp.arange(HARM, dtype=jnp.float32)
    angles = 2.0 * math.pi * jnp.arange(ROTS, dtype=jnp.float32) / ROTS
    phase = harmonic[:, None] * angles[None, :]
    forward = jnp.concatenate([jnp.cos(phase), jnp.sin(phase)], 0)
    backward = jnp.concatenate([jnp.cos(phase), -jnp.sin(phase)], 0).T
    return (forward, backward)


def class_accumulate(lanes, mixed):
    l_re = lanes[..., :HARM]
    l_im = lanes[..., HARM:]
    y_re = mixed[..., :HARM]
    y_im = mixed[..., HARM:]
    s_re = jnp.einsum("lrm,lcm->crm", l_re, y_re, preferred_element_type=jnp.float32) - jnp.einsum(
        "lrm,lcm->crm", l_im, y_im, preferred_element_type=jnp.float32
    )
    s_im = jnp.einsum("lrm,lcm->crm", l_re, y_im, preferred_element_type=jnp.float32) + jnp.einsum(
        "lrm,lcm->crm", l_im, y_re, preferred_element_type=jnp.float32
    )
    return jnp.concatenate([s_re, s_im], -1)


def dispatch_device(particles, references, owner_groups, class_order):
    n_cls = lax.axis_size("cls")
    count = particles.shape[0]
    groups = references.shape[0]
    cap = max(2, 2 * count * OWN_TOP // n_cls)
    slots = n_cls * cap
    width = 2 * HARM
    flat_owner = owner_groups.reshape(-1)
    owner_hot = (flat_owner[:, None] == jnp.arange(n_cls, dtype=jnp.int32)[None, :]).astype(
        jnp.int32
    )
    before = jnp.cumsum(owner_hot, axis=0) - owner_hot
    rank = jnp.sum(before * owner_hot, axis=1)
    slot_of = flat_owner * cap + rank
    match = slot_of[None, :] == jnp.arange(slots, dtype=jnp.int32)[:, None]
    member = jnp.any(match.reshape(slots, count, OWN_TOP), axis=2)
    filled = jnp.any(member, axis=1)
    dispatch = member.astype(jnp.bfloat16)
    outgoing = jnp.dot(
        dispatch, particles.reshape(count, CYCLES * width), preferred_element_type=jnp.float32
    )
    outgoing = outgoing.astype(jnp.bfloat16).reshape(n_cls, cap, CYCLES, width)
    match_int = match.astype(jnp.int32)
    picks = class_order[:, :, :CAND_OWN].reshape(count * OWN_TOP, CAND_OWN)
    slot_cand = jnp.where(filled[:, None], jnp.dot(match_int, picks), -1)
    owner_rows = jnp.repeat(jnp.arange(count, dtype=jnp.int32), OWN_TOP)
    slot_pid = jnp.where(filled, jnp.dot(match_int, owner_rows), -1)
    labels_out = jnp.concatenate([slot_cand, slot_pid[:, None]], 1).reshape(
        n_cls, cap, CAND_OWN + 1
    )
    arrived, labels = (
        lax.all_to_all(outgoing, "cls", split_axis=0, concat_axis=0, tiled=True),
        lax.all_to_all(labels_out, "cls", split_axis=0, concat_axis=0, tiled=True),
    )
    lanes = arrived.reshape(slots, CYCLES, width)
    labels = labels.reshape(slots, CAND_OWN + 1)
    forward, backward = spectral_tables()
    scale = 2.0 / math.sqrt(CYCLES * width)
    norms = jnp.sum(jnp.square(references.astype(jnp.float32)), axis=(1, 2))
    l_re = lanes[..., :HARM]
    l_im = lanes[..., HARM:]
    r_re = references[..., :HARM]
    r_im = references[..., HARM:]
    x_re = jnp.einsum("lrm,crm->lcm", l_re, r_re, preferred_element_type=jnp.float32) + jnp.einsum(
        "lrm,crm->lcm", l_im, r_im, preferred_element_type=jnp.float32
    )
    x_im = jnp.einsum("lrm,crm->lcm", l_im, r_re, preferred_element_type=jnp.float32) - jnp.einsum(
        "lrm,crm->lcm", l_re, r_im, preferred_element_type=jnp.float32
    )
    cross = jnp.concatenate([x_re, x_im], -1)
    corr = jnp.dot(
        cross.reshape(slots * groups, width), forward, precision=lax.Precision.HIGHEST
    ).reshape(slots, groups, ROTS)
    score = (corr - 0.5 * norms[None, :, None]) * scale
    candidate = jnp.any(
        labels[:, :CAND_OWN, None] == jnp.arange(groups, dtype=jnp.int32)[None, None, :], axis=1
    )
    part_max = jnp.max(jnp.where(candidate[:, :, None], score, lowest), axis=(1, 2))
    part_sum = jnp.sum(
        jnp.where(candidate[:, :, None], jnp.exp(score - part_max[:, None, None]), 0.0), axis=(1, 2)
    )
    sender_ids = labels[:, CAND_OWN].astype(jnp.float32)
    table_max, table_sum, table_ids = (
        lax.all_gather(part_max.reshape(1, n_cls, cap), "cls", axis=0, tiled=True),
        lax.all_gather(part_sum.reshape(1, n_cls, cap), "cls", axis=0, tiled=True),
        lax.all_gather(sender_ids.reshape(1, n_cls, cap), "cls", axis=0, tiled=True),
    )
    local_ids = jnp.arange(count, dtype=jnp.float32)
    hit = table_ids[..., None] == local_ids
    top = jnp.max(jnp.where(hit, table_max[..., None], lowest), axis=(0, 2))
    total = jnp.sum(
        jnp.where(
            hit, table_sum[..., None] * jnp.exp(table_max[..., None] - top[None, :, None, :]), 0.0
        ),
        axis=(0, 2),
    )
    table_norm = top + jnp.log(total)
    slot_ids = labels[:, CAND_OWN].reshape(n_cls, cap)
    slot_norm = jnp.sum(
        jnp.where(
            slot_ids[..., None] == jnp.arange(count, dtype=jnp.int32), table_norm[:, None, :], 0.0
        ),
        axis=2,
    ).reshape(slots)
    own_norm = lax.dynamic_index_in_dim(table_norm, lax.axis_index("cls"), 0, keepdims=False)
    weight = jnp.where(candidate[:, :, None], jnp.exp(score - slot_norm[:, None, None]), 0.0)
    mixed = (
        jnp.dot(weight.reshape(slots * groups, ROTS), backward, precision=lax.Precision.HIGHEST)
        .astype(jnp.bfloat16)
        .reshape(slots, groups, width)
    )
    class_weights = lax.psum(jnp.sum(weight, axis=(0, 2)), "prt")
    partial_sums = class_accumulate(lanes, mixed)
    class_sums = lax.psum_scatter(partial_sums, "prt", scatter_dimension=1, tiled=True)
    return (class_sums, class_weights, own_norm)


LANES = 128


def harmonic_plan():
    half = ROTS // 2
    turns = HARM // ROTS
    tail = HARM - turns * ROTS
    chunk_of = np.zeros(HARM, np.int32)
    side_of = np.zeros(HARM, np.int32)
    for m in range(HARM):
        turn, rest = divmod(m, ROTS)
        if turn == turns:
            chunk_of[m] = half * turns + rest // 2
            side_of[m] = rest % 2
        elif rest < half:
            chunk_of[m] = rest * turns + turn
        else:
            chunk_of[m] = ((ROTS - rest) % half) * turns + turn
            side_of[m] = 1
    return half, turns, tail, chunk_of, side_of


HALF, TURNS, TAIL, CHUNK_OF, SIDE_OF = harmonic_plan()
BODY = HALF * TURNS
CHUNKS = BODY + TAIL // 2
EXTRA = TAIL // 2 + 1
COEF = 2 * HALF * CAND_OWN
RANGE = 6
RANGES = ((BODY, CHUNKS + 1),) + tuple(
    (first * TURNS, (first + RANGE) * TURNS) for first in range(0, HALF, RANGE)
)


def selector():
    return (np.arange(CHUNKS)[:, None] == CHUNK_OF[None, :]).astype(np.float32)


def unselector():
    sel = selector()
    return np.concatenate([sel * (SIDE_OF == 0), sel * (SIDE_OF == 1)], 0)


def rotation_table():
    table = np.zeros((HALF, 2, CAND_OWN, ROTS, CAND_OWN))
    angle = 2.0 * np.pi * np.arange(ROTS) / ROTS
    for g in range(HALF):
        first = np.cos(g * angle)
        second = np.cos(HALF * angle) if g == 0 else np.sin(g * angle)
        for q in range(CAND_OWN):
            table[g, 0, q, :, q] = first
            table[g, 1, q, :, q] = second
    return table.reshape(COEF, ROTS * CAND_OWN).astype(np.float32)


def nt_dot(a, b):
    return lax.dot_general(a, b, (((1,), (1,)), ((), ())), preferred_element_type=jnp.float32)


def selector_masks():
    m = lax.broadcasted_iota(jnp.int32, (1, HARM), 1)
    turn = jnp.zeros((1, HARM), jnp.int32)
    for t in range(1, TURNS + 1):
        turn += jnp.where(m >= t * ROTS, 1, 0)
    rest = m - ROTS * turn
    back = jnp.where(rest == HALF, 0, ROTS - rest)
    chunk = jnp.where(rest < HALF, rest, back) * TURNS + turn
    side = jnp.where(rest < HALF, 0, 1)
    chunk = jnp.where(turn == TURNS, BODY + rest // 2, chunk)
    side = jnp.where(turn == TURNS, rest % 2, side)
    rows = lax.broadcasted_iota(jnp.int32, (CHUNKS, HARM), 0)
    sel = jnp.where(rows == chunk, 1.0, 0.0).astype(jnp.bfloat16)
    sides = lax.broadcasted_iota(jnp.int32, (2, HARM), 0)
    masks = jnp.where(sides == side, 1.0, 0.0).astype(jnp.bfloat16)
    return sel, masks


def masked_stack(piece, masks):
    parts = []
    for s in range(2):
        for b in range(2):
            parts.append(piece[:, s * HARM : (s + 1) * HARM] * masks[b : b + 1])
    return jnp.concatenate(parts, 0)


def repeat(number, step, body, carry):
    def several(i, carry):
        for u in range(step):
            carry = body(i * step + u, carry)
        return carry

    return lax.fori_loop(0, number // step, several, carry)


def particle_body(at_ref, x_ref, meta_ref, *refs, distances, n_prt):
    outs, scr = refs[:-1], refs[-1]
    count, cycles, _ = x_ref.shape
    number = len(outs)
    span = cycles // n_prt
    sel, masks = selector_masks()

    def one(n, carry):
        parts = []
        for d in distances:
            start = pl.multiple_of((at_ref[0] ^ d) * span, span)
            parts.append(masked_stack(x_ref[n, pl.ds(start, span), :], masks))
        w = jnp.concatenate(parts, 0)
        y = nt_dot(sel, w)
        for p in range(number):
            scr[p, pl.ds(pl.multiple_of(n * CHUNKS, CHUNKS), CHUNKS), :] = y[
                :, p * LANES : (p + 1) * LANES
            ]
        return carry

    repeat(count, 4, one, 0)

    def two(c, carry):
        for p in range(number):
            outs[p][c] = scr[p, pl.ds(c, count, stride=CHUNKS), :].astype(jnp.bfloat16)
        return carry

    repeat(CHUNKS, 8, two, 0)
    lane = lax.broadcasted_iota(jnp.int32, (count, LANES), 1)
    label = jnp.full((count, LANES), -1, jnp.int32)
    for t in range(OWN_TOP):
        mine = (lane // CAND_OWN) == meta_ref[:, t : t + 1]
        for q in range(CAND_OWN):
            at = OWN_TOP + t * CAND_OWN + q
            label = jnp.where(
                mine & (lane % CAND_OWN == q), meta_ref[:, at : at + 1], label
            )
    label = label.astype(jnp.float32).astype(jnp.bfloat16)
    for p in range(number):
        outs[p][CHUNKS] = label


def arrange_particles(prt, particles, meta, n_prt, distances):
    count = particles.shape[0]
    number = len(distances)
    size = particles.size * number // n_prt
    return pl.pallas_call(
        functools.partial(particle_body, distances=distances, n_prt=n_prt),
        in_specs=[pl.BlockSpec(memory_space=pltpu.SMEM)] + [pl.BlockSpec(memory_space=pltpu.VMEM)] * 2,
        out_shape=[jax.ShapeDtypeStruct((CHUNKS + 1, count, LANES), jnp.bfloat16)] * number,
        scratch_shapes=[pltpu.VMEM((number, count * CHUNKS, LANES), jnp.float32)],
        compiler_params=pltpu.CompilerParams(vmem_limit_bytes=32 << 20),
        cost_estimate=pl.CostEstimate(
            flops=size * 2 * CHUNKS, bytes_accessed=size * 4, transcendentals=0
        ),
        name="arrange_particles",
    )(prt, particles, meta)


def reference_body(at_ref, x_ref, out_ref, norm_ref, scr):
    rows = x_ref.shape[0]
    sel, masks = selector_masks()
    step = 4

    def one(n, carry):
        w = jnp.concatenate([masked_stack(x_ref[n * step + i], masks) for i in range(step)], 0)
        y = nt_dot(sel, w)
        for i in range(step):
            scr[pl.ds(pl.multiple_of((n * step + i) * CHUNKS, CHUNKS), CHUNKS), :] = y[
                :, i * LANES : (i + 1) * LANES
            ]
        return carry

    repeat(rows // step, 2, one, 0)

    def two(c, carry):
        value = scr[pl.ds(c, rows, stride=CHUNKS), :]
        out_ref[c] = value.astype(jnp.bfloat16)
        return carry + value * value

    norm_ref[...] = repeat(CHUNKS, 8, two, jnp.zeros((rows, LANES), jnp.float32))


def arrange_references(references, prt, n_prt):
    groups, cycles, width = references.shape
    span = cycles // n_prt
    block = 16
    return pl.pallas_call(
        reference_body,
        grid_spec=pltpu.PrefetchScalarGridSpec(
            num_scalar_prefetch=1,
            grid=(groups // block,),
            in_specs=[
                pl.BlockSpec((block, span, width), lambda i, at: (i, at[0], 0)),
            ],
            out_specs=[
                pl.BlockSpec((CHUNKS, block, LANES), lambda i, at: (0, i, 0)),
                pl.BlockSpec((block, LANES), lambda i, at: (i, 0)),
            ],
            scratch_shapes=[pltpu.VMEM((block * CHUNKS, LANES), jnp.float32)],
        ),
        out_shape=[
            jax.ShapeDtypeStruct((CHUNKS, groups, LANES), jnp.bfloat16),
            jax.ShapeDtypeStruct((groups, LANES), jnp.float32),
        ],
        compiler_params=pltpu.CompilerParams(vmem_limit_bytes=60 << 20),
        cost_estimate=pl.CostEstimate(
            flops=groups * span * width * 2 * CHUNKS,
            bytes_accessed=groups * span * width * 4,
            transcendentals=0,
        ),
        name="arrange_references",
    )(prt, references)


def lane_signs():
    lane = lax.broadcasted_iota(jnp.int32, (1, LANES), 1)
    quarter = LANES // 4
    imag = lane >= 2 * quarter
    odd = (lane // quarter) % 2 == 1
    return imag, odd


def lanes_of(held, first, number):
    parts = []
    for i in range(number):
        parts.append(jnp.concatenate([held[j, first + i] for j in range(held.shape[0])], 0))
    return jnp.concatenate(parts, 1) if number > 1 else parts[0]


def fetch(blocks, held, sems):
    copies = []
    for r, (first, last) in enumerate(RANGES):
        chunks = pl.ds(first, last - first)
        copies.append(
            [
                pltpu.make_async_copy(block.at[chunks], held.at[j, chunks], sems.at[r, j])
                for j, block in enumerate(blocks)
            ]
        )
    for group in copies:
        for copy in group:
            copy.start()
    return copies


def hot_masks(cand, groups):
    rows = lax.broadcasted_iota(jnp.int32, (groups, cand.shape[1]), 0).astype(jnp.float32)
    return [rows == cand[q : q + 1] for q in range(CAND_OWN)]


def residue_weights(q_ref, g):
    imag, odd = lane_signs()
    sign = jnp.where(imag == odd, -1.0, 1.0)
    first, second = [], []
    for i in range(TURNS):
        q = q_ref[g * TURNS + i].astype(jnp.float32)
        turned = pltpu.roll(q, LANES // 2, 1) * sign
        if g == 0:
            first.append(jnp.where(odd, 0.0, q))
            second.append(jnp.where(odd, q, 0.0))
        else:
            first.append(q)
            second.append(turned)
    return jnp.concatenate(
        [jnp.concatenate(first, 1), jnp.concatenate(second, 1)], 0
    ).astype(jnp.bfloat16)


def chosen_rows(acc, cand):
    groups = acc.shape[0] // 2
    hot = hot_masks(cand, groups)
    rows = []
    for ab in range(2):
        part = acc[ab * groups : (ab + 1) * groups, :]
        for q in range(CAND_OWN):
            rows.append(jnp.sum(jnp.where(hot[q], part, 0.0), axis=0, keepdims=True))
    return jnp.concatenate(rows, 0)


def cross_body(at_ref, *refs):
    blocks = refs[:-6]
    q_ref, norm_ref, coef_ref, cand_ref, held, sems = refs[-6:]
    groups = q_ref.shape[1]
    imag, odd = lane_signs()
    copies = fetch(blocks, held, sems)
    for copy in copies[0]:
        copy.wait()
    label = lanes_of(held, CHUNKS, 1).astype(jnp.float32).T
    row = lax.broadcasted_iota(jnp.int32, label.shape, 0)
    base = at_ref[0] * CAND_OWN
    for q in range(CAND_OWN):
        cand_ref[q : q + 1, :] = jnp.sum(
            jnp.where(row == base + q, label, 0.0), axis=0, keepdims=True
        )
    cand_ref[CAND_OWN:, :] = jnp.full(
        (cand_ref.shape[0] - CAND_OWN, cand_ref.shape[1]), -1.0, jnp.float32
    )

    def tail(i):
        q = q_ref[BODY + i // 2].astype(jnp.float32)
        keep = odd if i % 2 else ~odd
        a = jnp.where(keep, q, 0.0)
        turned = pltpu.roll(q, LANES // 2, 1) * jnp.where(imag, 1.0, -1.0)
        b = jnp.where(keep, turned, 0.0)
        if i == 0:
            b = jnp.zeros_like(b)
        w = jnp.concatenate([a, b], 0).astype(jnp.bfloat16)
        return nt_dot(w, lanes_of(held, BODY + i // 2, 1))

    for r in range(1, len(RANGES)):
        for copy in copies[r]:
            copy.wait()

        for g in range((r - 1) * RANGE, r * RANGE):
            acc = nt_dot(residue_weights(q_ref, g), lanes_of(held, g * TURNS, TURNS))
            if g < TAIL:
                acc += tail(g)
            if g == 0:
                half_norm = 0.5 * jnp.sum(norm_ref[...], axis=1, keepdims=True)
                acc = jnp.concatenate([acc[:groups] - half_norm, acc[groups:]], 0)
            block = 2 * CAND_OWN
            coef_ref[g * block : (g + 1) * block, :] = chosen_rows(acc, cand_ref[...])


def cross_coefficients(blocks, arranged, norms, cls):
    number = len(blocks)
    count = blocks[0].shape[1]
    groups = arranged.shape[1]
    total = number * count
    size = blocks[0].size * number
    block = 2 * CAND_OWN
    return pl.pallas_call(
        cross_body,
        in_specs=[pl.BlockSpec(memory_space=pltpu.SMEM)]
        + [pl.BlockSpec(memory_space=pl.ANY)] * number
        + [pl.BlockSpec(memory_space=pltpu.VMEM)] * 2,
        out_shape=[
            jax.ShapeDtypeStruct((COEF, total), jnp.float32),
            jax.ShapeDtypeStruct((block, total), jnp.float32),
        ],
        scratch_shapes=[
            pltpu.VMEM((number, *blocks[0].shape), jnp.bfloat16),
            pltpu.SemaphoreType.DMA((len(RANGES), number)),
        ],
        compiler_params=pltpu.CompilerParams(vmem_limit_bytes=60 << 20),
        cost_estimate=pl.CostEstimate(
            flops=4 * size * groups, bytes_accessed=2 * size, transcendentals=0
        ),
        name="cross_coefficients",
    )(cls, *blocks, arranged, norms)


def score_body(*refs, scale):
    *coefs, cand_ref, table_ref, score_ref, stat_ref = refs
    corr = lax.dot_general(
        table_ref[...],
        functools.reduce(jnp.add, [ref[...] for ref in coefs]),
        (((0,), (0,)), ((), ())),
        precision=lax.Precision.HIGHEST,
        preferred_element_type=jnp.float32,
    )
    score = jnp.where(cand_ref[0:1, :] >= 0.0, corr * scale, lowest)
    top = jnp.max(score, axis=0, keepdims=True)
    total = jnp.sum(jnp.exp(score - top), axis=0, keepdims=True)
    score_ref[...] = score
    stat_ref[0:1, :] = top
    stat_ref[1:2, :] = jnp.where(cand_ref[0:1, :] >= 0.0, total, 0.0)


def scores(coefs, cand, table, scale):
    total = cand.shape[1]
    return pl.pallas_call(
        functools.partial(score_body, scale=scale),
        out_shape=[
            jax.ShapeDtypeStruct((ROTS * CAND_OWN, total), jnp.float32),
            jax.ShapeDtypeStruct((2, total), jnp.float32),
        ],
        name="scores",
    )(*coefs, cand, table)


def swap_blocks(x, distance, width):
    lane = lax.broadcasted_iota(jnp.int32, x.shape, 1)
    bit = 1
    while bit <= distance:
        if distance & bit:
            shift = bit * width
            down = pltpu.roll(x, shift, 1)
            up = pltpu.roll(x, x.shape[1] - shift, 1)
            x = jnp.where((lane // shift) % 2 == 1, down, up)
        bit *= 2
    return x


def weights_body(at_ref, score_ref, cand_ref, stat_ref, table_ref, mix_ref, norm_ref):
    n_cls, _, total = stat_ref.shape
    width = total // n_cls
    tops, parts = [], []
    for e in range(n_cls):
        table = stat_ref[at_ref[0] ^ e]
        table = swap_blocks(jnp.concatenate([table] * 4, 0), e, width)
        tops.append(table[0:1])
        parts.append(table[1:2])
    top = functools.reduce(jnp.maximum, tops)
    summed = jnp.zeros_like(top)
    for other, part in zip(tops, parts):
        summed += part * jnp.exp(other - top)
    log_norm = top + jnp.log(summed)
    norm_ref[...] = log_norm[:, : norm_ref.shape[1]]
    weight = jnp.where(cand_ref[0:1, :] >= 0.0, jnp.exp(score_ref[...] - log_norm), 0.0)
    mix_ref[...] = lax.dot_general(
        table_ref[...],
        weight,
        (((1,), (0,)), ((), ())),
        precision=lax.Precision.HIGHEST,
        preferred_element_type=jnp.float32,
    )


def mixed_weights(cls, score, cand, stats, table, count):
    total = score.shape[1]
    return pl.pallas_call(
        weights_body,
        in_specs=[pl.BlockSpec(memory_space=pltpu.SMEM)] + [pl.BlockSpec(memory_space=pltpu.VMEM)] * 4,
        out_shape=[
            jax.ShapeDtypeStruct((COEF, total), jnp.float32),
            jax.ShapeDtypeStruct((1, count), jnp.float32),
        ],
        name="mixed_weights",
    )(cls, score, cand, stats, table)


def sums_body(*refs, number, pieces):
    blocks = refs[:number]
    refs = refs[number:]
    mixes, cands = refs[:pieces], refs[pieces : 2 * pieces]
    back_ref, out_ref, weight_ref, mix, cand, planes, held, sems = refs[2 * pieces :]
    step = pl.program_id(0)
    groups = weight_ref.shape[1]
    total = mix.shape[1]
    imag, odd = lane_signs()

    @pl.when(step == 0)
    def _():
        copies = fetch(blocks, held, sems)
        mixed = jnp.concatenate([ref[...] for ref in mixes], 1)
        chosen = jnp.concatenate([ref[...] for ref in cands], 1)
        hot = hot_masks(chosen, groups)
        summed = jnp.zeros((groups, total), jnp.float32)
        for q in range(CAND_OWN):
            summed += jnp.where(hot[q], mixed[q : q + 1], 0.0)
        weight_ref[...] = lax.dot_general(
            jnp.ones((1, total), jnp.float32),
            summed,
            (((1,), (1,)), ((), ())),
            precision=lax.Precision.HIGHEST,
            preferred_element_type=jnp.float32,
        )
        mix[...] = mixed
        cand[...] = chosen
        sign = jnp.where(imag == odd, 1.0, -1.0)
        for copy in copies[0]:
            copy.wait()

        def tail(t, weights):
            made = jnp.dot(
                weights, lanes_of(held, BODY + t // 2, 1), preferred_element_type=jnp.float32
            )
            g1, g2 = made[:groups], made[groups:]
            value = g1
            if t > 0:
                value = g1 + jnp.where(imag, -1.0, 1.0) * pltpu.roll(g2, LANES // 2, 1)
            rows = pl.ds((BODY + t // 2) * groups, groups)
            if t % 2:
                value = jnp.where(odd, value, planes[rows, :])
            planes[rows, :] = value

        for r in range(1, len(RANGES)):
            for copy in copies[r]:
                copy.wait()

            hot = hot_masks(cand[...], groups)
            block = 2 * CAND_OWN
            for g in range((r - 1) * RANGE, r * RANGE):
                mine = mix[g * block : (g + 1) * block, :]
                halves = []
                for ab in range(2):
                    dense = jnp.zeros((groups, total), jnp.float32)
                    for q in range(CAND_OWN):
                        at = ab * CAND_OWN + q
                        dense = jnp.where(hot[q], mine[at : at + 1], dense)
                    halves.append(dense)
                weights = jnp.concatenate(halves, 0).astype(jnp.bfloat16)
                made = jnp.dot(
                    weights, lanes_of(held, g * TURNS, TURNS), preferred_element_type=jnp.float32
                )
                for t in range(TURNS):
                    g1 = made[:groups, t * LANES : (t + 1) * LANES]
                    g2 = made[groups:, t * LANES : (t + 1) * LANES]
                    if g == 0:
                        value = jnp.where(odd, g2, g1)
                    else:
                        value = g1 + sign * pltpu.roll(g2, LANES // 2, 1)
                    start = (g * TURNS + t) * groups
                    planes[start : start + groups, :] = value
                if g < TAIL:
                    tail(g, weights)

    @pl.when(step > 0)
    def _():
        block, span, _ = out_ref.shape
        first = (step - 1) * block
        back = back_ref[...]
        values = []
        for c in range(block):
            turned = planes[pl.ds(first + c, CHUNKS, stride=groups), :].T
            for s in range(2):
                at = 2 * s * span
                values.append(
                    jnp.concatenate([turned[at : at + span], turned[at + span : at + 2 * span]], 1)
                )
        value = jnp.concatenate(values, 0)
        high = value.astype(jnp.bfloat16)
        low = (value - high.astype(jnp.float32)).astype(jnp.bfloat16)
        both = jnp.dot(
            jnp.concatenate([high, low], 0), back, preferred_element_type=jnp.float32
        )
        rows = value.shape[0]
        placed = both[:rows] + both[rows:]
        for c in range(block):
            for s in range(2):
                at = (2 * c + s) * span
                out_ref[c, :, s * HARM : (s + 1) * HARM] = placed[at : at + span]


def sums(blocks, mixes, cands, back, groups, span):
    number = len(blocks)
    count = blocks[0].shape[1]
    total = number * count
    size = blocks[0].size * number
    block = 8
    whole = lambda i: (0, 0)
    return pl.pallas_call(
        functools.partial(sums_body, number=number, pieces=len(mixes)),
        grid=(1 + groups // block,),
        in_specs=[
            *[pl.BlockSpec(memory_space=pl.ANY)] * number,
            *[pl.BlockSpec(array.shape, whole) for array in (*mixes, *cands, back)],
        ],
        out_specs=[
            pl.BlockSpec((block, span, 2 * HARM), lambda i: (jnp.maximum(i - 1, 0), 0, 0)),
            pl.BlockSpec((1, groups), whole),
        ],
        out_shape=[
            jax.ShapeDtypeStruct((groups, span, 2 * HARM), jnp.float32),
            jax.ShapeDtypeStruct((1, groups), jnp.float32),
        ],
        scratch_shapes=[
            pltpu.VMEM((COEF, total), jnp.float32),
            pltpu.VMEM((2 * CAND_OWN, total), jnp.float32),
            pltpu.VMEM((CHUNKS * groups, LANES), jnp.float32),
            pltpu.VMEM((number, *blocks[0].shape), jnp.bfloat16),
            pltpu.SemaphoreType.DMA((len(RANGES), number)),
        ],
        compiler_params=pltpu.CompilerParams(vmem_limit_bytes=60 << 20),
        cost_estimate=pl.CostEstimate(
            flops=4 * size * groups,
            bytes_accessed=2 * size + 8 * groups * span * HARM,
            transcendentals=0,
        ),
        name="sums",
    )(*blocks, *mixes, *cands, back)


def hop(value, axis, distance):
    size = lax.axis_size(axis)
    return lax.ppermute(value, axis, [(i, i ^ distance) for i in range(size)])


def after(value, *others):
    return lax.optimization_barrier((value, *others))[0]


def direct(own):
    n_cls = lax.axis_size("cls")
    return {1 << bit: hop(own, "cls", 1 << bit) for bit in range(1, n_cls.bit_length() - 1)}


def relayed(known, d, *others):
    n_cls = lax.axis_size("cls")
    for j in sorted(range(2, n_cls, 2), key=lambda j: bin(j).count("1")):
        if j not in known:
            bits = [bit for bit in range(1, n_cls.bit_length()) if j >> bit & 1]
            way = 1 << bits[d % len(bits)]
            known[j] = hop(after(known[j ^ way], *others), "cls", way)
    return known


def paired(known, each, last):
    n_cls = lax.axis_size("cls")
    for j in range(0, n_cls, 2):
        others = last if j == n_cls - 2 else each
        block = after(known[j], *others) if others else known[j]
        known[j + 1] = hop(block, "cls", 1)
    return [known[j] for j in range(n_cls)]


def gather_device(particles, references, owner_groups, class_order):
    n_cls, n_prt = lax.axis_size("cls"), lax.axis_size("prt")
    cls, prt = lax.axis_index("cls"), lax.axis_index("prt")
    count, cycles, width = particles.shape
    groups = references.shape[0]
    span = cycles // n_prt
    back = jnp.asarray(unselector(), jnp.bfloat16)
    table = jnp.asarray(rotation_table())
    picks = class_order[:, :, :CAND_OWN].reshape(count, OWN_TOP * CAND_OWN)
    meta = jnp.concatenate([owner_groups, picks], 1)
    cls, prt = (index.reshape(1).astype(jnp.int32) for index in (cls, prt))
    outgoing = []
    for first in range(0, n_prt, 2):
        distances = tuple(range(first, min(first + 2, n_prt)))
        place = after(prt, outgoing[0]) if outgoing else prt
        outgoing += arrange_particles(
            place, particles, meta, n_prt, distances
        )
    arrived = [outgoing[0]]
    known = [{0: arrived[0], **direct(arrived[0])}]
    for d in range(1, min(n_prt, 3)):
        arrived.append(hop(outgoing[d], "prt", d))
    early = after(arrived[1], outgoing[-1])
    known.append({0: early, **direct(early)})
    relayed(known[0], 0, outgoing[-1])
    place = after(prt, *arrived[1:2], *[known[0][1 << b] for b in range(1, n_cls.bit_length() - 1)])
    arranged, norms = arrange_references(references, place, n_prt)
    for d in range(2, n_prt):
        if d > 2:
            arrived.append(hop(after(outgoing[d], arrived[d - 1], arranged), "prt", d))
        own = after(arrived[d], arranged) if d == 2 else arrived[d]
        known.append({0: own, **direct(own)})
    for d in range(1, n_prt, 2):
        relayed(known[d], d)
    scale = 2.0 / math.sqrt(cycles * width)
    coefs, cands, sent, blocks = [], [], [], []
    for d in range(n_prt):
        waits = []
        if n_prt > 3:
            waits = [[known[1][2]], [arrived[3], known[2][n_cls // 2]], [known[3][2]], []][min(d, 3)]
        if d and d % 2 == 0:
            relayed(known[d], d, coefs[0])
        each = [arranged, known[1][n_cls // 2]] if d == 0 else coefs[:1] if d < 3 else []
        last = coefs[-1:] + (sent[1:] if d == n_prt - 1 else [])
        blocks.append(paired(known[d], each, last))
        ready = after(arranged, *waits) if waits else arranged
        coef, cand = cross_coefficients(blocks[d], ready, norms, cls)
        coefs.append(coef)
        sent.append(hop(coef, "prt", d) if d else coef)
        cands.append(cand)
    score, stat = scores(sent, cands[0], table, scale)
    stats = lax.all_gather(stat.reshape(1, *stat.shape), "cls", axis=0, tiled=True)
    mix, log_norm = mixed_weights(cls, score, cands[0], stats, table, count)
    mixes = [hop(mix, "prt", d) if d else mix for d in range(n_prt)]
    class_sums, class_weights = sums(
        [block for piece in blocks for block in piece], mixes, cands, back, groups, span
    )
    own = log_norm[0]
    return class_sums, class_weights[0], own


def per_device(particles, references, owner_groups, class_order):
    n_cls, n_prt = lax.axis_size("cls"), lax.axis_size("prt")
    count, cycles, _ = particles.shape
    groups = references.shape[0]
    cap = max(2, 2 * count * OWN_TOP // n_cls)
    powers = n_cls & (n_cls - 1) == 0 and n_prt & (n_prt - 1) == 0
    fits = 4 * cycles == LANES * n_prt and n_cls * CAND_OWN <= LANES and groups % 16 == 0 and n_cls >= 4 and n_prt >= 4
    fits = fits and powers and n_cls * count == LANES
    plan = gather_device if cap >= count and fits else dispatch_device
    return plan(particles, references, owner_groups, class_order)


def solution(mesh):
    in_specs = (
        P(("cls", "prt"), None, None),
        P("cls", None, None),
        P(("cls", "prt"), None),
        P(("cls", "prt"), None, None),
    )
    out_specs = (P("cls", "prt", None), P("cls"), P(("cls", "prt")))
    return jax.shard_map(
        per_device, mesh=mesh, in_specs=in_specs, out_specs=out_specs, check_vma=False
    )
```

```python
import functools
import math

import jax
import jax.numpy as jnp
import numpy as np
from jax import lax
from jax.experimental import pallas as pl
from jax.experimental.pallas import tpu as pltpu
from jax.sharding import PartitionSpec as P

CYCLES = 128
HARM = 256
ROTS = 36
OWN_TOP = 4
CAND_OWN = 4


lowest = -1e30


def spectral_tables():
    harmonic = jnp.arange(HARM, dtype=jnp.float32)
    angles = 2.0 * math.pi * jnp.arange(ROTS, dtype=jnp.float32) / ROTS
    phase = harmonic[:, None] * angles[None, :]
    forward = jnp.concatenate([jnp.cos(phase), jnp.sin(phase)], 0)
    backward = jnp.concatenate([jnp.cos(phase), -jnp.sin(phase)], 0).T
    return (forward, backward)


def class_accumulate(lanes, mixed):
    l_re = lanes[..., :HARM]
    l_im = lanes[..., HARM:]
    y_re = mixed[..., :HARM]
    y_im = mixed[..., HARM:]
    s_re = jnp.einsum("lrm,lcm->crm", l_re, y_re, preferred_element_type=jnp.float32) - jnp.einsum(
        "lrm,lcm->crm", l_im, y_im, preferred_element_type=jnp.float32
    )
    s_im = jnp.einsum("lrm,lcm->crm", l_re, y_im, preferred_element_type=jnp.float32) + jnp.einsum(
        "lrm,lcm->crm", l_im, y_re, preferred_element_type=jnp.float32
    )
    return jnp.concatenate([s_re, s_im], -1)


def dispatch_device(particles, references, owner_groups, class_order):
    n_cls = lax.axis_size("cls")
    count = particles.shape[0]
    groups = references.shape[0]
    cap = max(2, 2 * count * OWN_TOP // n_cls)
    slots = n_cls * cap
    width = 2 * HARM
    flat_owner = owner_groups.reshape(-1)
    owner_hot = (flat_owner[:, None] == jnp.arange(n_cls, dtype=jnp.int32)[None, :]).astype(
        jnp.int32
    )
    before = jnp.cumsum(owner_hot, axis=0) - owner_hot
    rank = jnp.sum(before * owner_hot, axis=1)
    slot_of = flat_owner * cap + rank
    match = slot_of[None, :] == jnp.arange(slots, dtype=jnp.int32)[:, None]
    member = jnp.any(match.reshape(slots, count, OWN_TOP), axis=2)
    filled = jnp.any(member, axis=1)
    dispatch = member.astype(jnp.bfloat16)
    outgoing = jnp.dot(
        dispatch, particles.reshape(count, CYCLES * width), preferred_element_type=jnp.float32
    )
    outgoing = outgoing.astype(jnp.bfloat16).reshape(n_cls, cap, CYCLES, width)
    match_int = match.astype(jnp.int32)
    picks = class_order[:, :, :CAND_OWN].reshape(count * OWN_TOP, CAND_OWN)
    slot_cand = jnp.where(filled[:, None], jnp.dot(match_int, picks), -1)
    owner_rows = jnp.repeat(jnp.arange(count, dtype=jnp.int32), OWN_TOP)
    slot_pid = jnp.where(filled, jnp.dot(match_int, owner_rows), -1)
    labels_out = jnp.concatenate([slot_cand, slot_pid[:, None]], 1).reshape(
        n_cls, cap, CAND_OWN + 1
    )
    arrived, labels = (
        lax.all_to_all(outgoing, "cls", split_axis=0, concat_axis=0, tiled=True),
        lax.all_to_all(labels_out, "cls", split_axis=0, concat_axis=0, tiled=True),
    )
    lanes = arrived.reshape(slots, CYCLES, width)
    labels = labels.reshape(slots, CAND_OWN + 1)
    forward, backward = spectral_tables()
    scale = 2.0 / math.sqrt(CYCLES * width)
    norms = jnp.sum(jnp.square(references.astype(jnp.float32)), axis=(1, 2))
    l_re = lanes[..., :HARM]
    l_im = lanes[..., HARM:]
    r_re = references[..., :HARM]
    r_im = references[..., HARM:]
    x_re = jnp.einsum("lrm,crm->lcm", l_re, r_re, preferred_element_type=jnp.float32) + jnp.einsum(
        "lrm,crm->lcm", l_im, r_im, preferred_element_type=jnp.float32
    )
    x_im = jnp.einsum("lrm,crm->lcm", l_im, r_re, preferred_element_type=jnp.float32) - jnp.einsum(
        "lrm,crm->lcm", l_re, r_im, preferred_element_type=jnp.float32
    )
    cross = jnp.concatenate([x_re, x_im], -1)
    corr = jnp.dot(
        cross.reshape(slots * groups, width), forward, precision=lax.Precision.HIGHEST
    ).reshape(slots, groups, ROTS)
    score = (corr - 0.5 * norms[None, :, None]) * scale
    candidate = jnp.any(
        labels[:, :CAND_OWN, None] == jnp.arange(groups, dtype=jnp.int32)[None, None, :], axis=1
    )
    part_max = jnp.max(jnp.where(candidate[:, :, None], score, lowest), axis=(1, 2))
    part_sum = jnp.sum(
        jnp.where(candidate[:, :, None], jnp.exp(score - part_max[:, None, None]), 0.0), axis=(1, 2)
    )
    sender_ids = labels[:, CAND_OWN].astype(jnp.float32)
    table_max, table_sum, table_ids = (
        lax.all_gather(part_max.reshape(1, n_cls, cap), "cls", axis=0, tiled=True),
        lax.all_gather(part_sum.reshape(1, n_cls, cap), "cls", axis=0, tiled=True),
        lax.all_gather(sender_ids.reshape(1, n_cls, cap), "cls", axis=0, tiled=True),
    )
    local_ids = jnp.arange(count, dtype=jnp.float32)
    hit = table_ids[..., None] == local_ids
    top = jnp.max(jnp.where(hit, table_max[..., None], lowest), axis=(0, 2))
    total = jnp.sum(
        jnp.where(
            hit, table_sum[..., None] * jnp.exp(table_max[..., None] - top[None, :, None, :]), 0.0
        ),
        axis=(0, 2),
    )
    table_norm = top + jnp.log(total)
    slot_ids = labels[:, CAND_OWN].reshape(n_cls, cap)
    slot_norm = jnp.sum(
        jnp.where(
            slot_ids[..., None] == jnp.arange(count, dtype=jnp.int32), table_norm[:, None, :], 0.0
        ),
        axis=2,
    ).reshape(slots)
    own_norm = lax.dynamic_index_in_dim(table_norm, lax.axis_index("cls"), 0, keepdims=False)
    weight = jnp.where(candidate[:, :, None], jnp.exp(score - slot_norm[:, None, None]), 0.0)
    mixed = (
        jnp.dot(weight.reshape(slots * groups, ROTS), backward, precision=lax.Precision.HIGHEST)
        .astype(jnp.bfloat16)
        .reshape(slots, groups, width)
    )
    class_weights = lax.psum(jnp.sum(weight, axis=(0, 2)), "prt")
    partial_sums = class_accumulate(lanes, mixed)
    class_sums = lax.psum_scatter(partial_sums, "prt", scatter_dimension=1, tiled=True)
    return (class_sums, class_weights, own_norm)


LANES = 128


def harmonic_plan():
    half = ROTS // 2
    turns = HARM // ROTS
    tail = HARM - turns * ROTS
    chunk_of = np.zeros(HARM, np.int32)
    side_of = np.zeros(HARM, np.int32)
    for m in range(HARM):
        turn, rest = divmod(m, ROTS)
        if turn == turns:
            chunk_of[m] = half * turns + rest // 2
            side_of[m] = rest % 2
        elif rest < half:
            chunk_of[m] = rest * turns + turn
        else:
            chunk_of[m] = ((ROTS - rest) % half) * turns + turn
            side_of[m] = 1
    return half, turns, tail, chunk_of, side_of


HALF, TURNS, TAIL, CHUNK_OF, SIDE_OF = harmonic_plan()
BODY = HALF * TURNS
CHUNKS = BODY + TAIL // 2
EXTRA = TAIL // 2 + 1
COEF = 2 * HALF * CAND_OWN
RANGE = 6
RANGES = ((BODY, CHUNKS + 1),) + tuple(
    (first * TURNS, (first + RANGE) * TURNS) for first in range(0, HALF, RANGE)
)


def selector():
    return (np.arange(CHUNKS)[:, None] == CHUNK_OF[None, :]).astype(np.float32)


def unselector():
    sel = selector()
    return np.concatenate([sel * (SIDE_OF == 0), sel * (SIDE_OF == 1)], 0)


def rotation_table():
    table = np.zeros((HALF, 2, CAND_OWN, ROTS, CAND_OWN))
    angle = 2.0 * np.pi * np.arange(ROTS) / ROTS
    for g in range(HALF):
        first = np.cos(g * angle)
        second = np.cos(HALF * angle) if g == 0 else np.sin(g * angle)
        for q in range(CAND_OWN):
            table[g, 0, q, :, q] = first
            table[g, 1, q, :, q] = second
    return table.reshape(COEF, ROTS * CAND_OWN).astype(np.float32)


def nt_dot(a, b):
    return lax.dot_general(a, b, (((1,), (1,)), ((), ())), preferred_element_type=jnp.float32)


def selector_masks():
    m = lax.broadcasted_iota(jnp.int32, (1, HARM), 1)
    turn = jnp.zeros((1, HARM), jnp.int32)
    for t in range(1, TURNS + 1):
        turn += jnp.where(m >= t * ROTS, 1, 0)
    rest = m - ROTS * turn
    back = jnp.where(rest == HALF, 0, ROTS - rest)
    chunk = jnp.where(rest < HALF, rest, back) * TURNS + turn
    side = jnp.where(rest < HALF, 0, 1)
    chunk = jnp.where(turn == TURNS, BODY + rest // 2, chunk)
    side = jnp.where(turn == TURNS, rest % 2, side)
    rows = lax.broadcasted_iota(jnp.int32, (CHUNKS, HARM), 0)
    sel = jnp.where(rows == chunk, 1.0, 0.0).astype(jnp.bfloat16)
    sides = lax.broadcasted_iota(jnp.int32, (2, HARM), 0)
    masks = jnp.where(sides == side, 1.0, 0.0).astype(jnp.bfloat16)
    return sel, masks


def masked_stack(piece, masks):
    parts = []
    for s in range(2):
        for b in range(2):
            parts.append(piece[:, s * HARM : (s + 1) * HARM] * masks[b : b + 1])
    return jnp.concatenate(parts, 0)


def repeat(number, step, body, carry):
    def several(i, carry):
        for u in range(step):
            carry = body(i * step + u, carry)
        return carry

    return lax.fori_loop(0, number // step, several, carry)


def particle_body(at_ref, x_ref, meta_ref, *refs, distances, n_prt):
    outs, scr = refs[:-1], refs[-1]
    count, cycles, _ = x_ref.shape
    number = len(outs)
    span = cycles // n_prt
    sel, masks = selector_masks()

    def one(n, carry):
        parts = []
        for d in distances:
            start = pl.multiple_of((at_ref[0] ^ d) * span, span)
            parts.append(masked_stack(x_ref[n, pl.ds(start, span), :], masks))
        w = jnp.concatenate(parts, 0)
        y = nt_dot(sel, w)
        for p in range(number):
            scr[p, pl.ds(pl.multiple_of(n * CHUNKS, CHUNKS), CHUNKS), :] = y[
                :, p * LANES : (p + 1) * LANES
            ]
        return carry

    repeat(count, 4, one, 0)

    def two(c, carry):
        for p in range(number):
            outs[p][c] = scr[p, pl.ds(c, count, stride=CHUNKS), :].astype(jnp.bfloat16)
        return carry

    repeat(CHUNKS, 8, two, 0)
    lane = lax.broadcasted_iota(jnp.int32, (count, LANES), 1)
    label = jnp.full((count, LANES), -1, jnp.int32)
    for t in range(OWN_TOP):
        mine = (lane // CAND_OWN) == meta_ref[:, t : t + 1]
        for q in range(CAND_OWN):
            at = OWN_TOP + t * CAND_OWN + q
            label = jnp.where(
                mine & (lane % CAND_OWN == q), meta_ref[:, at : at + 1], label
            )
    label = label.astype(jnp.float32).astype(jnp.bfloat16)
    for p in range(number):
        outs[p][CHUNKS] = label


def arrange_particles(prt, particles, meta, n_prt, distances):
    count = particles.shape[0]
    number = len(distances)
    size = particles.size * number // n_prt
    return pl.pallas_call(
        functools.partial(particle_body, distances=distances, n_prt=n_prt),
        in_specs=[pl.BlockSpec(memory_space=pltpu.SMEM)] + [pl.BlockSpec(memory_space=pltpu.VMEM)] * 2,
        out_shape=[jax.ShapeDtypeStruct((CHUNKS + 1, count, LANES), jnp.bfloat16)] * number,
        scratch_shapes=[pltpu.VMEM((number, count * CHUNKS, LANES), jnp.float32)],
        compiler_params=pltpu.CompilerParams(vmem_limit_bytes=32 << 20),
        cost_estimate=pl.CostEstimate(
            flops=size * 2 * CHUNKS, bytes_accessed=size * 4, transcendentals=0
        ),
        name="arrange_particles",
    )(prt, particles, meta)


def reference_body(at_ref, x_ref, out_ref, norm_ref, scr):
    rows = x_ref.shape[0]
    sel, masks = selector_masks()
    step = 4

    def one(n, carry):
        w = jnp.concatenate([masked_stack(x_ref[n * step + i], masks) for i in range(step)], 0)
        y = nt_dot(sel, w)
        for i in range(step):
            scr[pl.ds(pl.multiple_of((n * step + i) * CHUNKS, CHUNKS), CHUNKS), :] = y[
                :, i * LANES : (i + 1) * LANES
            ]
        return carry

    repeat(rows // step, 2, one, 0)

    def two(c, carry):
        value = scr[pl.ds(c, rows, stride=CHUNKS), :]
        out_ref[c] = value.astype(jnp.bfloat16)
        return carry + value * value

    norm_ref[...] = repeat(CHUNKS, 8, two, jnp.zeros((rows, LANES), jnp.float32))


def arrange_references(references, prt, n_prt):
    groups, cycles, width = references.shape
    span = cycles // n_prt
    block = 16
    return pl.pallas_call(
        reference_body,
        grid_spec=pltpu.PrefetchScalarGridSpec(
            num_scalar_prefetch=1,
            grid=(groups // block,),
            in_specs=[
                pl.BlockSpec((block, span, width), lambda i, at: (i, at[0], 0)),
            ],
            out_specs=[
                pl.BlockSpec((CHUNKS, block, LANES), lambda i, at: (0, i, 0)),
                pl.BlockSpec((block, LANES), lambda i, at: (i, 0)),
            ],
            scratch_shapes=[pltpu.VMEM((block * CHUNKS, LANES), jnp.float32)],
        ),
        out_shape=[
            jax.ShapeDtypeStruct((CHUNKS, groups, LANES), jnp.bfloat16),
            jax.ShapeDtypeStruct((groups, LANES), jnp.float32),
        ],
        compiler_params=pltpu.CompilerParams(vmem_limit_bytes=60 << 20),
        cost_estimate=pl.CostEstimate(
            flops=groups * span * width * 2 * CHUNKS,
            bytes_accessed=groups * span * width * 4,
            transcendentals=0,
        ),
        name="arrange_references",
    )(prt, references)


def lane_signs():
    lane = lax.broadcasted_iota(jnp.int32, (1, LANES), 1)
    quarter = LANES // 4
    imag = lane >= 2 * quarter
    odd = (lane // quarter) % 2 == 1
    return imag, odd


def lanes_of(held, first, number):
    parts = []
    for i in range(number):
        parts.append(jnp.concatenate([held[j, first + i] for j in range(held.shape[0])], 0))
    return jnp.concatenate(parts, 1) if number > 1 else parts[0]


def fetch(blocks, held, sems):
    copies = []
    for r, (first, last) in enumerate(RANGES):
        chunks = pl.ds(first, last - first)
        copies.append(
            [
                pltpu.make_async_copy(block.at[chunks], held.at[j, chunks], sems.at[r, j])
                for j, block in enumerate(blocks)
            ]
        )
    for group in copies:
        for copy in group:
            copy.start()
    return copies


def hot_masks(cand, groups):
    rows = lax.broadcasted_iota(jnp.int32, (groups, cand.shape[1]), 0).astype(jnp.float32)
    return [rows == cand[q : q + 1] for q in range(CAND_OWN)]


def residue_weights(q_ref, g):
    imag, odd = lane_signs()
    sign = jnp.where(imag == odd, -1.0, 1.0)
    first, second = [], []
    for i in range(TURNS):
        q = q_ref[g * TURNS + i].astype(jnp.float32)
        turned = pltpu.roll(q, LANES // 2, 1) * sign
        if g == 0:
            first.append(jnp.where(odd, 0.0, q))
            second.append(jnp.where(odd, q, 0.0))
        else:
            first.append(q)
            second.append(turned)
    return jnp.concatenate(
        [jnp.concatenate(first, 1), jnp.concatenate(second, 1)], 0
    ).astype(jnp.bfloat16)


def chosen_rows(acc, cand):
    groups = acc.shape[0] // 2
    hot = hot_masks(cand, groups)
    rows = []
    for ab in range(2):
        part = acc[ab * groups : (ab + 1) * groups, :]
        for q in range(CAND_OWN):
            rows.append(jnp.sum(jnp.where(hot[q], part, 0.0), axis=0, keepdims=True))
    return jnp.concatenate(rows, 0)


def cross_body(at_ref, *refs):
    blocks = refs[:-6]
    q_ref, norm_ref, coef_ref, cand_ref, held, sems = refs[-6:]
    groups = q_ref.shape[1]
    imag, odd = lane_signs()
    copies = fetch(blocks, held, sems)
    for copy in copies[0]:
        copy.wait()
    label = lanes_of(held, CHUNKS, 1).astype(jnp.float32).T
    row = lax.broadcasted_iota(jnp.int32, label.shape, 0)
    base = at_ref[0] * CAND_OWN
    for q in range(CAND_OWN):
        cand_ref[q : q + 1, :] = jnp.sum(
            jnp.where(row == base + q, label, 0.0), axis=0, keepdims=True
        )
    cand_ref[CAND_OWN:, :] = jnp.full(
        (cand_ref.shape[0] - CAND_OWN, cand_ref.shape[1]), -1.0, jnp.float32
    )

    def tail(i):
        q = q_ref[BODY + i // 2].astype(jnp.float32)
        keep = odd if i % 2 else ~odd
        a = jnp.where(keep, q, 0.0)
        turned = pltpu.roll(q, LANES // 2, 1) * jnp.where(imag, 1.0, -1.0)
        b = jnp.where(keep, turned, 0.0)
        if i == 0:
            b = jnp.zeros_like(b)
        w = jnp.concatenate([a, b], 0).astype(jnp.bfloat16)
        return nt_dot(w, lanes_of(held, BODY + i // 2, 1))

    for r in range(1, len(RANGES)):
        for copy in copies[r]:
            copy.wait()

        for g in range((r - 1) * RANGE, r * RANGE):
            acc = nt_dot(residue_weights(q_ref, g), lanes_of(held, g * TURNS, TURNS))
            if g < TAIL:
                acc += tail(g)
            if g == 0:
                half_norm = 0.5 * jnp.sum(norm_ref[...], axis=1, keepdims=True)
                acc = jnp.concatenate([acc[:groups] - half_norm, acc[groups:]], 0)
            block = 2 * CAND_OWN
            coef_ref[g * block : (g + 1) * block, :] = chosen_rows(acc, cand_ref[...])


def cross_coefficients(blocks, arranged, norms, cls):
    number = len(blocks)
    count = blocks[0].shape[1]
    groups = arranged.shape[1]
    total = number * count
    size = blocks[0].size * number
    block = 2 * CAND_OWN
    return pl.pallas_call(
        cross_body,
        in_specs=[pl.BlockSpec(memory_space=pltpu.SMEM)]
        + [pl.BlockSpec(memory_space=pl.ANY)] * number
        + [pl.BlockSpec(memory_space=pltpu.VMEM)] * 2,
        out_shape=[
            jax.ShapeDtypeStruct((COEF, total), jnp.float32),
            jax.ShapeDtypeStruct((block, total), jnp.float32),
        ],
        scratch_shapes=[
            pltpu.VMEM((number, *blocks[0].shape), jnp.bfloat16),
            pltpu.SemaphoreType.DMA((len(RANGES), number)),
        ],
        compiler_params=pltpu.CompilerParams(vmem_limit_bytes=60 << 20),
        cost_estimate=pl.CostEstimate(
            flops=4 * size * groups, bytes_accessed=2 * size, transcendentals=0
        ),
        name="cross_coefficients",
    )(cls, *blocks, arranged, norms)


def score_body(*refs, scale):
    *coefs, cand_ref, table_ref, score_ref, stat_ref = refs
    corr = lax.dot_general(
        table_ref[...],
        functools.reduce(jnp.add, [ref[...] for ref in coefs]),
        (((0,), (0,)), ((), ())),
        precision=lax.Precision.HIGHEST,
        preferred_element_type=jnp.float32,
    )
    score = jnp.where(cand_ref[0:1, :] >= 0.0, corr * scale, lowest)
    top = jnp.max(score, axis=0, keepdims=True)
    total = jnp.sum(jnp.exp(score - top), axis=0, keepdims=True)
    score_ref[...] = score
    stat_ref[0:1, :] = top
    stat_ref[1:2, :] = jnp.where(cand_ref[0:1, :] >= 0.0, total, 0.0)


def scores(coefs, cand, table, scale):
    total = cand.shape[1]
    return pl.pallas_call(
        functools.partial(score_body, scale=scale),
        out_shape=[
            jax.ShapeDtypeStruct((ROTS * CAND_OWN, total), jnp.float32),
            jax.ShapeDtypeStruct((2, total), jnp.float32),
        ],
        name="scores",
    )(*coefs, cand, table)


def swap_blocks(x, distance, width):
    lane = lax.broadcasted_iota(jnp.int32, x.shape, 1)
    bit = 1
    while bit <= distance:
        if distance & bit:
            shift = bit * width
            down = pltpu.roll(x, shift, 1)
            up = pltpu.roll(x, x.shape[1] - shift, 1)
            x = jnp.where((lane // shift) % 2 == 1, down, up)
        bit *= 2
    return x


def weights_body(at_ref, score_ref, cand_ref, stat_ref, table_ref, mix_ref, norm_ref):
    n_cls, _, total = stat_ref.shape
    width = total // n_cls
    tops, parts = [], []
    for e in range(n_cls):
        table = stat_ref[at_ref[0] ^ e]
        table = swap_blocks(jnp.concatenate([table] * 4, 0), e, width)
        tops.append(table[0:1])
        parts.append(table[1:2])
    top = functools.reduce(jnp.maximum, tops)
    summed = jnp.zeros_like(top)
    for other, part in zip(tops, parts):
        summed += part * jnp.exp(other - top)
    log_norm = top + jnp.log(summed)
    norm_ref[...] = log_norm[:, : norm_ref.shape[1]]
    weight = jnp.where(cand_ref[0:1, :] >= 0.0, jnp.exp(score_ref[...] - log_norm), 0.0)
    mix_ref[...] = lax.dot_general(
        table_ref[...],
        weight,
        (((1,), (0,)), ((), ())),
        precision=lax.Precision.HIGHEST,
        preferred_element_type=jnp.float32,
    )


def mixed_weights(cls, score, cand, stats, table, count):
    total = score.shape[1]
    return pl.pallas_call(
        weights_body,
        in_specs=[pl.BlockSpec(memory_space=pltpu.SMEM)] + [pl.BlockSpec(memory_space=pltpu.VMEM)] * 4,
        out_shape=[
            jax.ShapeDtypeStruct((COEF, total), jnp.float32),
            jax.ShapeDtypeStruct((1, count), jnp.float32),
        ],
        name="mixed_weights",
    )(cls, score, cand, stats, table)


def sums_body(*refs, number, pieces):
    blocks = refs[:number]
    refs = refs[number:]
    mixes, cands = refs[:pieces], refs[pieces : 2 * pieces]
    back_ref, out_ref, weight_ref, mix, cand, planes, held, sems = refs[2 * pieces :]
    step = pl.program_id(0)
    groups = weight_ref.shape[1]
    total = mix.shape[1]
    imag, odd = lane_signs()

    @pl.when(step == 0)
    def _():
        copies = fetch(blocks, held, sems)
        mixed = jnp.concatenate([ref[...] for ref in mixes], 1)
        chosen = jnp.concatenate([ref[...] for ref in cands], 1)
        hot = hot_masks(chosen, groups)
        summed = jnp.zeros((groups, total), jnp.float32)
        for q in range(CAND_OWN):
            summed += jnp.where(hot[q], mixed[q : q + 1], 0.0)
        weight_ref[...] = lax.dot_general(
            jnp.ones((1, total), jnp.float32),
            summed,
            (((1,), (1,)), ((), ())),
            precision=lax.Precision.HIGHEST,
            preferred_element_type=jnp.float32,
        )
        mix[...] = mixed
        cand[...] = chosen
        sign = jnp.where(imag == odd, 1.0, -1.0)
        for copy in copies[0]:
            copy.wait()

        def tail(t, weights):
            made = jnp.dot(
                weights, lanes_of(held, BODY + t // 2, 1), preferred_element_type=jnp.float32
            )
            g1, g2 = made[:groups], made[groups:]
            value = g1
            if t > 0:
                value = g1 + jnp.where(imag, -1.0, 1.0) * pltpu.roll(g2, LANES // 2, 1)
            rows = pl.ds((BODY + t // 2) * groups, groups)
            if t % 2:
                value = jnp.where(odd, value, planes[rows, :])
            planes[rows, :] = value

        for r in range(1, len(RANGES)):
            for copy in copies[r]:
                copy.wait()

            hot = hot_masks(cand[...], groups)
            block = 2 * CAND_OWN
            for g in range((r - 1) * RANGE, r * RANGE):
                mine = mix[g * block : (g + 1) * block, :]
                halves = []
                for ab in range(2):
                    dense = jnp.zeros((groups, total), jnp.float32)
                    for q in range(CAND_OWN):
                        at = ab * CAND_OWN + q
                        dense = jnp.where(hot[q], mine[at : at + 1], dense)
                    halves.append(dense)
                weights = jnp.concatenate(halves, 0).astype(jnp.bfloat16)
                made = jnp.dot(
                    weights, lanes_of(held, g * TURNS, TURNS), preferred_element_type=jnp.float32
                )
                for t in range(TURNS):
                    g1 = made[:groups, t * LANES : (t + 1) * LANES]
                    g2 = made[groups:, t * LANES : (t + 1) * LANES]
                    if g == 0:
                        value = jnp.where(odd, g2, g1)
                    else:
                        value = g1 + sign * pltpu.roll(g2, LANES // 2, 1)
                    start = (g * TURNS + t) * groups
                    planes[start : start + groups, :] = value
                if g < TAIL:
                    tail(g, weights)

    @pl.when(step > 0)
    def _():
        block, span, _ = out_ref.shape
        first = (step - 1) * block
        back = back_ref[...]
        values = []
        for c in range(block):
            turned = planes[pl.ds(first + c, CHUNKS, stride=groups), :].T
            for s in range(2):
                at = 2 * s * span
                values.append(
                    jnp.concatenate([turned[at : at + span], turned[at + span : at + 2 * span]], 1)
                )
        value = jnp.concatenate(values, 0)
        high = value.astype(jnp.bfloat16)
        low = (value - high.astype(jnp.float32)).astype(jnp.bfloat16)
        both = jnp.dot(
            jnp.concatenate([high, low], 0), back, preferred_element_type=jnp.float32
        )
        rows = value.shape[0]
        placed = both[:rows] + both[rows:]
        for c in range(block):
            for s in range(2):
                at = (2 * c + s) * span
                out_ref[c, :, s * HARM : (s + 1) * HARM] = placed[at : at + span]


def sums(blocks, mixes, cands, back, groups, span):
    number = len(blocks)
    count = blocks[0].shape[1]
    total = number * count
    size = blocks[0].size * number
    block = 16
    whole = lambda i: (0, 0)
    return pl.pallas_call(
        functools.partial(sums_body, number=number, pieces=len(mixes)),
        grid=(1 + groups // block,),
        in_specs=[
            *[pl.BlockSpec(memory_space=pl.ANY)] * number,
            *[pl.BlockSpec(array.shape, whole) for array in (*mixes, *cands, back)],
        ],
        out_specs=[
            pl.BlockSpec((block, span, 2 * HARM), lambda i: (jnp.maximum(i - 1, 0), 0, 0)),
            pl.BlockSpec((1, groups), whole),
        ],
        out_shape=[
            jax.ShapeDtypeStruct((groups, span, 2 * HARM), jnp.float32),
            jax.ShapeDtypeStruct((1, groups), jnp.float32),
        ],
        scratch_shapes=[
            pltpu.VMEM((COEF, total), jnp.float32),
            pltpu.VMEM((2 * CAND_OWN, total), jnp.float32),
            pltpu.VMEM((CHUNKS * groups, LANES), jnp.float32),
            pltpu.VMEM((number, *blocks[0].shape), jnp.bfloat16),
            pltpu.SemaphoreType.DMA((len(RANGES), number)),
        ],
        compiler_params=pltpu.CompilerParams(vmem_limit_bytes=60 << 20),
        cost_estimate=pl.CostEstimate(
            flops=4 * size * groups,
            bytes_accessed=2 * size + 8 * groups * span * HARM,
            transcendentals=0,
        ),
        name="sums",
    )(*blocks, *mixes, *cands, back)


def hop(value, axis, distance):
    size = lax.axis_size(axis)
    return lax.ppermute(value, axis, [(i, i ^ distance) for i in range(size)])


def after(value, *others):
    return lax.optimization_barrier((value, *others))[0]


def direct(own):
    n_cls = lax.axis_size("cls")
    return {1 << bit: hop(own, "cls", 1 << bit) for bit in range(1, n_cls.bit_length() - 1)}


def relayed(known, d, *others):
    n_cls = lax.axis_size("cls")
    for j in sorted(range(2, n_cls, 2), key=lambda j: bin(j).count("1")):
        if j not in known:
            bits = [bit for bit in range(1, n_cls.bit_length()) if j >> bit & 1]
            way = 1 << bits[d % len(bits)]
            known[j] = hop(after(known[j ^ way], *others), "cls", way)
    return known


def paired(known, each, last):
    n_cls = lax.axis_size("cls")
    for j in range(0, n_cls, 2):
        others = last if j == n_cls - 2 else each
        block = after(known[j], *others) if others else known[j]
        known[j + 1] = hop(block, "cls", 1)
    return [known[j] for j in range(n_cls)]


def gather_device(particles, references, owner_groups, class_order):
    n_cls, n_prt = lax.axis_size("cls"), lax.axis_size("prt")
    cls, prt = lax.axis_index("cls"), lax.axis_index("prt")
    count, cycles, width = particles.shape
    groups = references.shape[0]
    span = cycles // n_prt
    back = jnp.asarray(unselector(), jnp.bfloat16)
    table = jnp.asarray(rotation_table())
    picks = class_order[:, :, :CAND_OWN].reshape(count, OWN_TOP * CAND_OWN)
    meta = jnp.concatenate([owner_groups, picks], 1)
    cls, prt = (index.reshape(1).astype(jnp.int32) for index in (cls, prt))
    outgoing = []
    for first in range(0, n_prt, 2):
        distances = tuple(range(first, min(first + 2, n_prt)))
        place = after(prt, outgoing[0]) if outgoing else prt
        outgoing += arrange_particles(
            place, particles, meta, n_prt, distances
        )
    arrived = [outgoing[0]]
    known = [{0: arrived[0], **direct(arrived[0])}]
    for d in range(1, min(n_prt, 3)):
        arrived.append(hop(outgoing[d], "prt", d))
    early = after(arrived[1], outgoing[-1])
    known.append({0: early, **direct(early)})
    relayed(known[0], 0, outgoing[-1])
    place = after(prt, *arrived[1:2], *[known[0][1 << b] for b in range(1, n_cls.bit_length() - 1)])
    arranged, norms = arrange_references(references, place, n_prt)
    for d in range(2, n_prt):
        if d > 2:
            arrived.append(hop(after(outgoing[d], arrived[d - 1], arranged), "prt", d))
        own = after(arrived[d], arranged) if d == 2 else arrived[d]
        known.append({0: own, **direct(own)})
    for d in range(1, n_prt, 2):
        relayed(known[d], d)
    scale = 2.0 / math.sqrt(cycles * width)
    coefs, cands, sent, blocks = [], [], [], []
    for d in range(n_prt):
        waits = []
        if n_prt > 3:
            waits = [[known[1][2]], [arrived[3], known[2][n_cls // 2]], [known[3][2]], []][min(d, 3)]
        if d and d % 2 == 0:
            relayed(known[d], d, coefs[0])
        each = [arranged, known[1][n_cls // 2]] if d == 0 else coefs[:1] if d < 3 else []
        blocks.append(paired(known[d], each, coefs[-1:]))
        ready = after(arranged, *waits) if waits else arranged
        coef, cand = cross_coefficients(blocks[d], ready, norms, cls)
        coefs.append(coef)
        sent.append(hop(coef, "prt", d) if d else coef)
        cands.append(cand)
    score, stat = scores(sent, cands[0], table, scale)
    stats = lax.all_gather(stat.reshape(1, *stat.shape), "cls", axis=0, tiled=True)
    mix, log_norm = mixed_weights(cls, score, cands[0], stats, table, count)
    mixes = [hop(mix, "prt", d) if d else mix for d in range(n_prt)]
    class_sums, class_weights = sums(
        [block for piece in blocks for block in piece], mixes, cands, back, groups, span
    )
    own = log_norm[0]
    return class_sums, class_weights[0], own


def per_device(particles, references, owner_groups, class_order):
    n_cls, n_prt = lax.axis_size("cls"), lax.axis_size("prt")
    count, cycles, _ = particles.shape
    groups = references.shape[0]
    cap = max(2, 2 * count * OWN_TOP // n_cls)
    powers = n_cls & (n_cls - 1) == 0 and n_prt & (n_prt - 1) == 0
    fits = 4 * cycles == LANES * n_prt and n_cls * CAND_OWN <= LANES and groups % 16 == 0 and n_cls >= 4 and n_prt >= 4
    fits = fits and powers and n_cls * count == LANES
    plan = gather_device if cap >= count and fits else dispatch_device
    return plan(particles, references, owner_groups, class_order)


def solution(mesh):
    in_specs = (
        P(("cls", "prt"), None, None),
        P("cls", None, None),
        P(("cls", "prt"), None),
        P(("cls", "prt"), None, None),
    )
    out_specs = (P("cls", "prt", None), P("cls"), P(("cls", "prt")))
    return jax.shard_map(
        per_device, mesh=mesh, in_specs=in_specs, out_specs=out_specs, check_vma=False
    )
```
